32 devices in a mesh: row: 4 (over x, core), col: 8 (over z, y).
Axes of the slice: x: 2, y: 2, z: 4, core: 2. Of those that a mesh axis runs over, the one named last changes fastest.
Arguments:
- covariance: float32 [8192, 8192], P('row', 'col'), may hold values from -12 to 12, as said below
- noise_var: float32 [64, 128], P('row'), may hold values from 0.1 to 1
- wind_table: float32 [16, 2], replicated, may hold values from -0.7 to 0.7
- diffusivity: float32 [16], replicated, may hold values from 0.01 to 0.05
- wind_index: int32 [3, 64], replicated, may hold values from 0 to 15
Outputs:
- predicted_spread_matrix: float32 [8192, 8192], P('row', 'col')
- operator_times_prior: bfloat16 [8192, 8192], P('row', 'col')
The draws below stay inside these ranges and needn't reach their ends.
Inputs may be any that keep to these rules, and one draw needn't show every extreme that they name: covariance is symmetric: entry (a, b) equals entry (b, a) exactly.
All inputs are finite; a program needn't handle non-finite values.
Results may differ from the reference program's by a relative error of at most 0.0025.
Values may be sent and summed in bfloat16 or wider, within the bound.
No kernel may reach another device: no remote copies, remote signals or barrier semaphores. Data moves between devices by JAX's collectives and lax.ppermute only.
A program may use at most 192 MiB of HBM per device.

```python
import math
import jax
import jax.numpy as jnp
from jax import lax

NLAT = 64
NLON = 128
STEPS = 3
TABLE = 16
MATRIX_ORDER = 8192


def draw_covariance(key, part):
    size = NLAT * NLON
    key_noise = jax.random.fold_in(jax.random.fold_in(key, 11), 0)
    raw = jnp.clip(jax.random.normal(key_noise, (size, size), jnp.float32), -6.0, 6.0) * 0.3
    sym = (raw + raw.T) * 0.5
    index_all = jnp.arange(size)
    sym = sym.at[index_all, index_all].add(1.0)
    return sym


def with_ends(drawn, rng, low, top_value):
    extent = drawn.shape
    index_at = [jax.random.randint(jax.random.fold_in(rng, axis), (), 0, extent[axis]) for axis in range(len(extent))]
    drawn = drawn.at[tuple(index_at)].set(low)
    longest = extent.index(max(extent))
    index_at[longest] = (index_at[longest] + 1) % extent[longest]
    return drawn.at[tuple(index_at)].set(top_value)


def shard_levels(rng, dims, cuts, low, top_value):
    def one(axis_at, parts):
        heights = jax.random.uniform(jax.random.fold_in(jax.random.fold_in(rng, 6), axis_at), (parts,), jnp.float32, low / len(cuts), top_value / len(cuts))
        return jnp.repeat(jnp.exp(heights), dims[axis_at] // parts).reshape((-1,) + (1,) * (len(dims) - axis_at - 1))

    factor_of = one(*cuts[0])
    for cut in cuts[1:]:
        factor_of = factor_of * one(*cut)
    return factor_of


def setup_inputs(seed: int = 0) -> dict:
    keys = jax.random.split(jax.random.key(seed), 6)
    return {
        "covariance": draw_covariance(jax.random.fold_in(keys[5], 71), 0),
        "noise_var": jnp.clip(jnp.exp(math.log(1.0) - 2.3025851 * jax.random.uniform(keys[1], (NLAT, NLON), jnp.float32) ** shard_levels(keys[1], (NLAT, NLON), ((0, 4),), -0.2, 0.2)), 0.1, 1.0),
        "wind_table": jnp.clip(jax.random.uniform(keys[2], (TABLE, 2), jnp.float32, -0.7, 0.7), -0.7, 0.7),
        "diffusivity": jnp.clip(jax.random.uniform(keys[3], (TABLE,), jnp.float32, 0.01, 0.05), 0.01, 0.05),
        "wind_index": with_ends(jax.random.randint(keys[4], (STEPS, NLAT), 0, TABLE), jax.random.fold_in(keys[4], 1), 0, TABLE - 1).astype(jnp.int32),
    }


def stencil_terms(zonal_cour, merid_cour, diffuse):
    middle_weight = 1.0 - zonal_cour * zonal_cour - merid_cour * merid_cour - 4.0 * diffuse
    eastward_weight = 0.5 * zonal_cour * zonal_cour - 0.5 * zonal_cour + diffuse
    west_w = 0.5 * zonal_cour * zonal_cour + 0.5 * zonal_cour + diffuse
    north_w = 0.5 * merid_cour * merid_cour - 0.5 * merid_cour + diffuse
    south_w = 0.5 * merid_cour * merid_cour + 0.5 * merid_cour + diffuse
    return jnp.stack([middle_weight, eastward_weight, west_w, north_w, south_w])


def stencil_weights(wind_table, diffusivity, wind_index):
    courant = wind_table[wind_index]
    return stencil_terms(courant[..., 0], courant[..., 1], diffusivity[wind_index])


def advance(values, weights, step_no):
    middle_weight = weights[0, step_no][:, None, None]
    eastward_weight = weights[1, step_no][:, None, None]
    west_w = weights[2, step_no][:, None, None]
    north_w = weights[3, step_no][:, None, None]
    south_w = weights[4, step_no][:, None, None]
    padded = jnp.pad(values, ((1, 1), (0, 0), (0, 0)))
    return (middle_weight * values + eastward_weight * jnp.roll(values, -1, 1) + west_w * jnp.roll(values, 1, 1)
            + north_w * padded[2:] + south_w * padded[:-2])


def reference(covariance, noise_var, wind_table, diffusivity, wind_index):
    weights = stencil_weights(wind_table, diffusivity, wind_index)
    count_of_blocks = NLAT // 4
    width_per_block = 4 * NLON

    def propagate(columns):
        values = columns.reshape(NLAT, NLON, width_per_block)
        for step_no in range(STEPS):
            values = advance(values, weights, step_no)
        return values.reshape(MATRIX_ORDER, width_per_block)

    def forward(columns):
        return propagate(columns).astype(jnp.bfloat16)

    column_blocks = covariance.reshape(MATRIX_ORDER, count_of_blocks, width_per_block).transpose(1, 0, 2)
    product_blocks = lax.map(forward, column_blocks)
    operator_times_prior = product_blocks.transpose(1, 0, 2).reshape(MATRIX_ORDER, MATRIX_ORDER)
    noise_flat = noise_var.reshape(MATRIX_ORDER)

    def backward(pair):
        s_rows, start = pair
        output_matrix = propagate(s_rows.T.astype(jnp.float32))
        on_diag = jnp.arange(MATRIX_ORDER, dtype=jnp.int32)[:, None] == (start + jnp.arange(width_per_block, dtype=jnp.int32))[None, :]
        return output_matrix + jnp.where(on_diag, noise_flat[:, None], jnp.zeros((), jnp.float32))

    blocks_by_row = operator_times_prior.reshape(count_of_blocks, width_per_block, MATRIX_ORDER)
    starts = jnp.arange(count_of_blocks, dtype=jnp.int32) * width_per_block
    prior_matrix_tiles = lax.map(backward, (blocks_by_row, starts))
    predicted_spread_matrix = prior_matrix_tiles.transpose(1, 0, 2).reshape(MATRIX_ORDER, MATRIX_ORDER)
    return predicted_spread_matrix, operator_times_prior
```

```python
import functools

import jax
import jax.numpy as jnp
from jax import lax
from jax.experimental import pallas as pl
from jax.experimental.pallas import tpu as pltpu
from jax.sharding import PartitionSpec as P

F32 = jnp.float32
BF16 = jnp.bfloat16
VMEM_LIMIT = 40 * 1024 * 1024


def params():
    return pltpu.CompilerParams(vmem_limit_bytes=VMEM_LIMIT)


def stencil_terms(zonal_cour, merid_cour, diffuse):
    middle_weight = 1.0 - zonal_cour * zonal_cour - merid_cour * merid_cour - 4.0 * diffuse
    eastward_weight = 0.5 * zonal_cour * zonal_cour - 0.5 * zonal_cour + diffuse
    west_w = 0.5 * zonal_cour * zonal_cour + 0.5 * zonal_cour + diffuse
    north_w = 0.5 * merid_cour * merid_cour - 0.5 * merid_cour + diffuse
    south_w = 0.5 * merid_cour * merid_cour + 0.5 * merid_cour + diffuse
    return jnp.stack([middle_weight, eastward_weight, west_w, north_w, south_w])


def looked_up(wind_table, diffusivity, wind_index):
    table_ids = jnp.arange(wind_table.shape[0], dtype=jnp.int32)
    one_hot = (wind_index[:, :, None] == table_ids[None, None, :]).astype(F32)
    courant = jnp.einsum("sly,yc->slc", one_hot, wind_table, precision=lax.Precision.HIGHEST)
    diffuse = jnp.einsum("sly,y->sl", one_hot, diffusivity, precision=lax.Precision.HIGHEST)
    return stencil_terms(courant[..., 0], courant[..., 1], diffuse)


def stepped(planes, weight, steps, axis):
    size = planes[0].shape[axis]
    for step_no in range(steps):
        fresh = []
        for i in range(1, len(planes) - 1):
            c, e, w, n, s = [weight(member, step_no, i + step_no) for member in range(5)]
            u = planes[i]
            fresh.append(
                c * u
                + e * pltpu.roll(u, size - 1, axis)
                + w * pltpu.roll(u, 1, axis)
                + n * planes[i + 1]
                + s * planes[i - 1]
            )
        planes = fresh
    return planes


def edge_at(i, near, lat_rows):
    return jnp.where(i < near, i, i + (lat_rows - 2 * near))


def pack_edges(covariance, near, halo, nlon):
    rows, cols = covariance.shape
    lat_rows = rows // nlon
    wide = halo * nlon
    count = 2 * near

    def kernel(p_ref, first_ref, last_ref, top_ref, bottom_ref):
        i = pl.program_id(0)
        first_ref[...] = p_ref[:, :wide].astype(BF16)
        last_ref[...] = p_ref[:, cols - wide :].astype(BF16)

        @pl.when(i < halo)
        def _():
            top_ref[...] = p_ref[...].astype(BF16)

        @pl.when(i >= count - halo)
        def _():
            bottom_ref[...] = p_ref[...].astype(BF16)

    return pl.pallas_call(
        kernel,
        grid=(count,),
        in_specs=[pl.BlockSpec((nlon, cols), lambda i: (edge_at(i, near, lat_rows), 0))],
        out_specs=[
            pl.BlockSpec((nlon, wide), lambda i: (i, 0)),
            pl.BlockSpec((nlon, wide), lambda i: (i, 0)),
            pl.BlockSpec((nlon, cols), lambda i: (jnp.minimum(i, halo - 1), 0)),
            pl.BlockSpec((nlon, cols), lambda i: (jnp.maximum(i - (count - halo), 0), 0)),
        ],
        out_shape=[
            jax.ShapeDtypeStruct((count * nlon, wide), BF16),
            jax.ShapeDtypeStruct((count * nlon, wide), BF16),
            jax.ShapeDtypeStruct((wide, cols), BF16),
            jax.ShapeDtypeStruct((wide, cols), BF16),
        ],
        compiler_params=params(),
        cost_estimate=pl.CostEstimate(
            flops=count * nlon * cols, bytes_accessed=count * nlon * cols * 6, transcendentals=0
        ),
        name="pack_edges",
    )(covariance)


def pack_middle(covariance, where, own, halo, nlon):
    rows, cols = covariance.shape
    wide = halo * nlon

    def kernel(where_ref, p_ref, first_ref, last_ref):
        first_ref[...] = p_ref[:, :wide].astype(BF16)
        last_ref[...] = p_ref[:, cols - wide :].astype(BF16)

    return pl.pallas_call(
        kernel,
        grid_spec=pltpu.PrefetchScalarGridSpec(
            num_scalar_prefetch=1,
            grid=(own,),
            in_specs=[pl.BlockSpec((nlon, cols), lambda i, at: (at[0] + i, 0))],
            out_specs=[
                pl.BlockSpec((nlon, wide), lambda i, at: (i, 0)),
                pl.BlockSpec((nlon, wide), lambda i, at: (i, 0)),
            ],
        ),
        out_shape=[jax.ShapeDtypeStruct((own * nlon, wide), BF16)] * 2,
        compiler_params=params(),
        cost_estimate=pl.CostEstimate(
            flops=own * nlon * cols, bytes_accessed=own * nlon * cols * 6, transcendentals=0
        ),
        name="pack_middle",
    )(where, covariance)


def pack_mirror(covariance, where, own, halo, nlon):
    rows, cols = covariance.shape
    wide = halo * nlon

    def kernel(where_ref, left_ref, right_ref, left_out, right_out):
        start = where_ref[2]
        for a in range(own):
            lanes = pl.ds(pl.multiple_of((start + a) * nlon, nlon), nlon)
            out_rows = pl.ds(a * nlon, nlon)
            left_out[out_rows, :] = left_ref[:, lanes].T.astype(BF16)
            right_out[out_rows, :] = right_ref[:, lanes].T.astype(BF16)

    return pl.pallas_call(
        kernel,
        grid_spec=pltpu.PrefetchScalarGridSpec(
            num_scalar_prefetch=1,
            grid=(halo,),
            in_specs=[
                pl.BlockSpec((nlon, cols), lambda j, at: (at[0] + j, 0)),
                pl.BlockSpec((nlon, cols), lambda j, at: (at[1] + j, 0)),
            ],
            out_specs=[
                pl.BlockSpec((own * nlon, nlon), lambda j, at: (0, j)),
                pl.BlockSpec((own * nlon, nlon), lambda j, at: (0, j)),
            ],
        ),
        out_shape=[jax.ShapeDtypeStruct((own * nlon, wide), BF16)] * 2,
        compiler_params=params(),
        cost_estimate=pl.CostEstimate(
            flops=2 * wide * own * nlon, bytes_accessed=2 * wide * cols * 6, transcendentals=0
        ),
        name="pack_mirror",
    )(where, covariance, covariance)


def columns_operator(covariance, left, right, weights, where, steps, nlon, near=None, held=None):
    rows, cols = covariance.shape
    lat_rows, lats = rows // nlon, cols // nlon
    wide = steps * nlon
    count = left.shape[0] // nlon
    padded = lats + 2 * steps
    group = 16

    def kernel(where_ref, weight_ref, p_ref, left_ref, right_ref, *rest):
        outs = rest if held is None else rest[1:]
        t_ref = outs[0]

        def weight(member, step_no, lat):
            return weight_ref[(member * steps + step_no) * padded + lat]

        def body(g, carry):
            at = pl.ds(pl.multiple_of(g * group, group), group)
            planes = [left_ref[at, k * nlon : (k + 1) * nlon].astype(F32) for k in range(steps)]
            planes += [p_ref[at, k * nlon : (k + 1) * nlon] for k in range(lats)]
            planes += [right_ref[at, k * nlon : (k + 1) * nlon].astype(F32) for k in range(steps)]
            for k, plane in enumerate(stepped(planes, weight, steps, 1)):
                t_ref[at, k * nlon : (k + 1) * nlon] = plane.astype(BF16)
            return carry

        lax.fori_loop(0, nlon // group, body, 0)
        if held is None:
            i = pl.program_id(0)

            @pl.when(i < steps)
            def _():
                outs[1][...] = t_ref[...]

            @pl.when(i >= count - steps)
            def _():
                outs[2][...] = t_ref[...]

    if held is None:
        lat_at = lambda i, at: (edge_at(i, near, lat_rows), 0)
    else:
        lat_at = lambda i, at: (at[0] + i, 0)
    in_specs = [
        pl.BlockSpec(memory_space=pltpu.SMEM),
        pl.BlockSpec((nlon, cols), lat_at),
        pl.BlockSpec((nlon, wide), lambda i, at: (i, 0)),
        pl.BlockSpec((nlon, wide), lambda i, at: (i, 0)),
    ]
    out_specs = [pl.BlockSpec((nlon, cols), lat_at)]
    out_shape = [jax.ShapeDtypeStruct((rows, cols), BF16)]
    operands = [where, weights, covariance, left, right]
    aliases = {}
    if held is None:
        out_specs += [
            pl.BlockSpec((nlon, cols), lambda i, at: (jnp.minimum(i, steps - 1), 0)),
            pl.BlockSpec((nlon, cols), lambda i, at: (jnp.maximum(i - (count - steps), 0), 0)),
        ]
        out_shape += [jax.ShapeDtypeStruct((wide, cols), BF16)] * 2
    else:
        in_specs.append(pl.BlockSpec(memory_space=pl.ANY))
        operands.append(held)
        aliases = {5: 0}
    return pl.pallas_call(
        kernel,
        grid_spec=pltpu.PrefetchScalarGridSpec(
            num_scalar_prefetch=1, grid=(count,), in_specs=in_specs, out_specs=out_specs
        ),
        out_shape=out_shape,
        input_output_aliases=aliases,
        compiler_params=params(),
        cost_estimate=pl.CostEstimate(
            flops=27 * count * nlon * cols, bytes_accessed=count * nlon * cols * 8, transcendentals=0
        ),
        name="columns_operator",
    )(*operands)


def rows_operator(values, top, bottom, weights, steps, nlon, out_dtype, noise=None, diagonal=None):
    rows, cols = values.shape
    lat_rows = rows // nlon
    wide = steps * nlon
    padded = lat_rows + 2 * steps

    def kernel(weight_ref, x_ref, top_ref, bottom_ref, *rest):
        extra, (out_ref, *scratch) = rest[: 0 if noise is None else 2], rest[0 if noise is None else 2 :]

        def weight(member, step_no, lat):
            return weight_ref[(member * steps + step_no) * padded + lat]

        def first(i):
            if i < steps:
                return top_ref[i * nlon : (i + 1) * nlon, :].astype(F32)
            if i < steps + lat_rows:
                return x_ref[(i - steps) * nlon : (i - steps + 1) * nlon, :].astype(F32)
            i = i - steps - lat_rows
            return bottom_ref[i * nlon : (i + 1) * nlon, :].astype(F32)

        source = first
        for step_no in range(steps):
            span = padded - 2 * (step_no + 1)
            last = step_no == steps - 1
            target = out_ref if last else scratch[step_no]
            south, here = source(0), source(1)
            for i in range(span):
                north = source(i + 2)
                c, e, w, n, s = [weight(member, step_no, i + 1 + step_no) for member in range(5)]
                fresh = (
                    c * here
                    + e * pltpu.roll(here, nlon - 1, 0)
                    + w * pltpu.roll(here, 1, 0)
                    + n * north
                    + s * south
                )
                target[i * nlon : (i + 1) * nlon, :] = fresh.astype(target.dtype)
                south, here = here, north
            if not last:
                source = lambda i, ref=target: ref[i * nlon : (i + 1) * nlon, :]

        if noise is not None:
            diagonal_ref, noise_ref = extra
            lat = diagonal_ref[0] + pl.program_id(0)

            @pl.when(jnp.logical_and(lat >= 0, lat < lat_rows))
            def _():
                at = pl.ds(pl.multiple_of(lat * nlon, nlon), nlon)
                eye = lax.broadcasted_iota(jnp.int32, (nlon, nlon), 0) == lax.broadcasted_iota(
                    jnp.int32, (nlon, nlon), 1
                )
                out_ref[at, :] += jnp.where(eye, noise_ref[pl.ds(lat, 1), :], 0.0)

    in_specs = [
        pl.BlockSpec(memory_space=pltpu.SMEM),
        pl.BlockSpec((rows, nlon), lambda j: (0, j)),
        pl.BlockSpec((wide, nlon), lambda j: (0, j)),
        pl.BlockSpec((wide, nlon), lambda j: (0, j)),
    ]
    operands = [weights, values, top, bottom]
    if noise is not None:
        in_specs += [pl.BlockSpec(memory_space=pltpu.SMEM), pl.BlockSpec(noise.shape, lambda j: (0, 0))]
        operands += [diagonal, noise]
    return pl.pallas_call(
        kernel,
        grid=(cols // nlon,),
        in_specs=in_specs,
        out_specs=pl.BlockSpec((rows, nlon), lambda j: (0, j)),
        out_shape=jax.ShapeDtypeStruct((rows, cols), out_dtype),
        scratch_shapes=[
            pltpu.VMEM(((padded - 2 * (step_no + 1)) * nlon, nlon), F32) for step_no in range(steps - 1)
        ],
        compiler_params=params(),
        cost_estimate=pl.CostEstimate(
            flops=27 * rows * cols, bytes_accessed=rows * cols * 6, transcendentals=0
        ),
        name="rows_operator",
    )(*operands)


def shifted(block, axis, by):
    size = lax.axis_size(axis)
    pairs = [(i, i + by) for i in range(size) if 0 <= i + by < size]
    return lax.ppermute(block, axis, pairs)


def gathered(first, last, axis, dim, unit, halo, own):
    before, after = [], []
    need, hop = halo, 1
    while need > 0:
        take = min(own, need)
        size = first.shape[dim]
        before.insert(0, shifted(lax.slice_in_dim(last, size - take * unit, size, axis=dim), axis, hop))
        after.append(shifted(lax.slice_in_dim(first, 0, take * unit, axis=dim), axis, -hop))
        need, hop = need - take, hop + 1
    join = lambda parts: parts[0] if len(parts) == 1 else jnp.concatenate(parts, axis=dim)
    return join(before), join(after)


def mirror_pairs(n_row, n_col, side):
    pairs = []
    for a in range(n_row):
        for b in range(n_col):
            to = 2 * a + (1 - b % 2) + side
            if 0 <= to < n_col:
                pairs.append((a * n_col + b, (b // 2) * n_col + to))
    return pairs


def body(covariance, noise_var, wind_table, diffusivity, wind_index):
    rows_dev, cols_dev = covariance.shape
    lat_rows, nlon = noise_var.shape
    steps, nlat = wind_index.shape
    lats = cols_dev // nlon
    n_row, n_col = lax.axis_size("row"), lax.axis_size("col")
    row_id, col_id = lax.axis_index("row"), lax.axis_index("col")
    own = min(lats - steps, lat_rows // 2 - steps, lats // 2)
    mirrored = lat_rows == 2 * lats and own > 0

    if not mirrored:
        return plain_body(covariance, noise_var, wind_table, diffusivity, wind_index)

    near = lat_rows // 2 - own
    middle = lat_rows // 2
    parity = col_id % 2
    first_e, last_e, top, bottom = pack_edges(covariance, near, steps, nlon)
    left_e = shifted(last_e, "col", 1)
    right_e = shifted(first_e, "col", -1)
    p_top = shifted(bottom, "row", 1)
    p_bottom = shifted(top, "row", -1)
    by_parity = lambda even, odd: jnp.where(parity == 0, even, odd).astype(jnp.int32)
    mirror_at = by_parity(middle - own, middle).reshape(1)
    direct_at = by_parity(middle, middle - own).reshape(1)
    first_d, last_d = pack_middle(covariance, mirror_at, own, steps, nlon)
    left_d = shifted(last_d, "col", 1)
    right_d = shifted(first_d, "col", -1)
    base = (1 - parity) * lats
    sources = jnp.stack([base + lats - steps, base, by_parity(lats - own, 0)]).astype(jnp.int32)
    left_m, right_m = pack_mirror(covariance, sources, own, steps, nlon)
    left_m = lax.ppermute(left_m, ("row", "col"), mirror_pairs(n_row, n_col, 1))
    right_m = lax.ppermute(right_m, ("row", "col"), mirror_pairs(n_row, n_col, -1))

    weights = looked_up(wind_table, diffusivity, wind_index)
    padded_w = jnp.pad(weights, ((0, 0), (0, 0), (steps, steps)))
    row_w = lax.dynamic_slice_in_dim(padded_w, row_id * lat_rows, lat_rows + 2 * steps, 2).reshape(-1)
    col_w = lax.dynamic_slice_in_dim(padded_w, col_id * lats, lats + 2 * steps, 2).reshape(-1)

    operator_times_prior = rows_operator(covariance, p_top, p_bottom, row_w, steps, nlon, BF16)

    mirror, t_first, t_last = columns_operator(
        covariance, left_e, right_e, col_w, mirror_at, steps, nlon, near=near
    )
    t_top = shifted(t_last, "row", 1)
    t_bottom = shifted(t_first, "row", -1)
    (mirror,) = columns_operator(covariance, left_m, right_m, col_w, mirror_at, steps, nlon, held=mirror)
    (mirror,) = columns_operator(covariance, left_d, right_d, col_w, direct_at, steps, nlon, held=mirror)
    diagonal = (col_id * lats - row_id * lat_rows).astype(jnp.int32).reshape(1)
    predicted_spread_matrix = rows_operator(
        mirror, t_top, t_bottom, row_w, steps, nlon, F32, noise_var, diagonal
    )
    return (predicted_spread_matrix, operator_times_prior)


def plain_body(covariance, noise_var, wind_table, diffusivity, wind_index):
    rows_dev, cols_dev = covariance.shape
    lat_rows, nlon = noise_var.shape
    steps, nlat = wind_index.shape
    lats = cols_dev // nlon
    row_id, col_id = lax.axis_index("row"), lax.axis_index("col")
    sent = covariance.astype(BF16)
    left, right = gathered(sent, sent, "col", 1, nlon, steps, lats)
    p_top, p_bottom = gathered(sent, sent, "row", 0, nlon, steps, lat_rows)
    weights = looked_up(wind_table, diffusivity, wind_index)
    padded_w = jnp.pad(weights, ((0, 0), (0, 0), (steps, steps)))
    row_w = lax.dynamic_slice_in_dim(padded_w, row_id * lat_rows, lat_rows + 2 * steps, 2).reshape(-1)
    col_w = lax.dynamic_slice_in_dim(padded_w, col_id * lats, lats + 2 * steps, 2).reshape(-1)
    operator_times_prior = rows_operator(covariance, p_top, p_bottom, row_w, steps, nlon, BF16)
    unused = jnp.zeros((1,), jnp.int32)
    held = jnp.zeros((rows_dev, cols_dev), BF16)
    (mirror,) = columns_operator(covariance, left, right, col_w, unused, steps, nlon, held=held)
    t_top, t_bottom = gathered(mirror, mirror, "row", 0, nlon, steps, lat_rows)
    diagonal = (col_id * lats - row_id * lat_rows).astype(jnp.int32).reshape(1)
    predicted_spread_matrix = rows_operator(
        mirror, t_top, t_bottom, row_w, steps, nlon, F32, noise_var, diagonal
    )
    return (predicted_spread_matrix, operator_times_prior)


def solution(mesh):
    in_specs = (P("row", "col"), P("row", None), P(), P(), P())
    out_specs = (P("row", "col"), P("row", "col"))
    return jax.shard_map(body, mesh=mesh, in_specs=in_specs, out_specs=out_specs, check_vma=False)
```

```python
import functools

import jax
import jax.numpy as jnp
from jax import lax
from jax.experimental import pallas as pl
from jax.experimental.pallas import tpu as pltpu
from jax.sharding import PartitionSpec as P

F32 = jnp.float32
BF16 = jnp.bfloat16
VMEM_LIMIT = 63 * 1024 * 1024


def params():
    return pltpu.CompilerParams(vmem_limit_bytes=VMEM_LIMIT)


def cost(work):
    return pl.CostEstimate(flops=work, bytes_accessed=work, transcendentals=0)


def stencil_terms(zonal_cour, merid_cour, diffuse):
    middle_weight = 1.0 - zonal_cour * zonal_cour - merid_cour * merid_cour - 4.0 * diffuse
    eastward_weight = 0.5 * zonal_cour * zonal_cour - 0.5 * zonal_cour + diffuse
    west_w = 0.5 * zonal_cour * zonal_cour + 0.5 * zonal_cour + diffuse
    north_w = 0.5 * merid_cour * merid_cour - 0.5 * merid_cour + diffuse
    south_w = 0.5 * merid_cour * merid_cour + 0.5 * merid_cour + diffuse
    return jnp.stack([middle_weight, eastward_weight, west_w, north_w, south_w])


def looked_up(wind_table, diffusivity, wind_index):
    table_ids = jnp.arange(wind_table.shape[0], dtype=jnp.int32)
    one_hot = (wind_index[:, :, None] == table_ids[None, None, :]).astype(F32)
    courant = jnp.einsum("sly,yc->slc", one_hot, wind_table, precision=lax.Precision.HIGHEST)
    diffuse = jnp.einsum("sly,y->sl", one_hot, diffusivity, precision=lax.Precision.HIGHEST)
    return stencil_terms(courant[..., 0], courant[..., 1], diffuse)


def sweep(source, lats, weight, steps, axis, scratch, out):
    for step_no in range(steps):
        last = step_no == steps - 1
        target = out if last else scratch[step_no]
        south, here = source(0), source(1)
        size = here.shape[axis]
        for i in range(lats + 2 * (steps - step_no - 1)):
            north = source(i + 2)
            c, e, w, n, s = [weight(member, step_no, i + 1 + step_no) for member in range(5)]
            fresh = (
                c * here
                + e * pltpu.roll(here, size - 1, axis)
                + w * pltpu.roll(here, 1, axis)
                + n * north
                + s * south
            )
            target(i, fresh)
            south, here = here, north
        if not last:
            source = scratch[step_no]


def plane_view(ref, axis, size):
    def view(i, value=None):
        at = pl.ds(i * size, size)
        index = (at, slice(None)) if axis == 0 else (slice(None), at)
        if value is None:
            return ref[index].astype(F32)
        ref[index] = value.astype(ref.dtype)

    return view


def joined(before, middle, after, steps, lats):
    def view(i):
        if i < steps:
            return before(i)
        if i < steps + lats:
            return middle(i - steps)
        return after(i - steps - lats)

    return view


def edge_at(i, near, own):
    return jnp.where(i < near, i, i + own)


def pack_direct(covariance, where, near, own, halo, nlon):
    rows, cols = covariance.shape
    lat_rows = rows // nlon
    wide = halo * nlon
    count = 2 * near + own

    def kernel(where_ref, p_ref, last_ref, outer_ref, inner_ref, top_ref, bottom_ref):
        i = pl.program_id(0)
        inner = jnp.logical_and(i >= near, i < near + own)
        last_ref[...] = p_ref[:, cols - wide :].astype(BF16)

        @pl.when(jnp.logical_not(inner))
        def _():
            outer_ref[...] = p_ref[:, :wide].astype(BF16)

        @pl.when(inner)
        def _():
            inner_ref[...] = p_ref[:, :wide].astype(BF16)

        @pl.when(i < halo)
        def _():
            top_ref[...] = p_ref[...].astype(BF16)

        @pl.when(i >= count - halo)
        def _():
            bottom_ref[...] = p_ref[...].astype(BF16)

    def lat_at(i, at):
        inner = at[0] + i - near
        outer = jnp.where(i < near, i, i + lat_rows - count)
        return (jnp.where(jnp.logical_and(i >= near, i < near + own), inner, outer), 0)

    def outer_at(i, at):
        return (jnp.where(i < near, i, jnp.maximum(i - own, near - 1)), 0)

    return pl.pallas_call(
        kernel,
        grid_spec=pltpu.PrefetchScalarGridSpec(
            num_scalar_prefetch=1,
            grid=(count,),
            in_specs=[pl.BlockSpec((nlon, cols), lat_at)],
            out_specs=[
                pl.BlockSpec((nlon, wide), lambda i, at: (i, 0)),
                pl.BlockSpec((nlon, wide), outer_at),
                pl.BlockSpec((nlon, wide), lambda i, at: (jnp.clip(i - near, 0, own - 1), 0)),
                pl.BlockSpec((nlon, cols), lambda i, at: (jnp.minimum(i, halo - 1), 0)),
                pl.BlockSpec((nlon, cols), lambda i, at: (jnp.maximum(i - (count - halo), 0), 0)),
            ],
        ),
        out_shape=[
            jax.ShapeDtypeStruct((count * nlon, wide), BF16),
            jax.ShapeDtypeStruct((2 * near * nlon, wide), BF16),
            jax.ShapeDtypeStruct((own * nlon, wide), BF16),
            jax.ShapeDtypeStruct((wide, cols), BF16),
            jax.ShapeDtypeStruct((wide, cols), BF16),
        ],
        compiler_params=params(),
        cost_estimate=cost(1),
        name="pack_direct",
    )(where, covariance)


def pack_mirror(covariance, where, own, halo, nlon):
    rows, cols = covariance.shape
    wide = halo * nlon

    def kernel(where_ref, left_ref, right_ref, left_out, right_out):
        start = where_ref[2]
        for a in range(own):
            lanes = pl.ds(pl.multiple_of((start + a) * nlon, nlon), nlon)
            out_rows = pl.ds(a * nlon, nlon)
            left_out[out_rows, :] = left_ref[:, lanes].T.astype(BF16)
            right_out[out_rows, :] = right_ref[:, lanes].T.astype(BF16)

    return pl.pallas_call(
        kernel,
        grid_spec=pltpu.PrefetchScalarGridSpec(
            num_scalar_prefetch=1,
            grid=(halo,),
            in_specs=[
                pl.BlockSpec((nlon, cols), lambda j, at: (at[0] + j, 0)),
                pl.BlockSpec((nlon, cols), lambda j, at: (at[1] + j, 0)),
            ],
            out_specs=[
                pl.BlockSpec((own * nlon, nlon), lambda j, at: (0, j)),
                pl.BlockSpec((own * nlon, nlon), lambda j, at: (0, j)),
            ],
        ),
        out_shape=[jax.ShapeDtypeStruct((own * nlon, wide), BF16)] * 2,
        compiler_params=params(),
        cost_estimate=cost(1),
        name="pack_mirror",
    )(where, covariance, covariance)


def columns_operator(
    covariance, left, right, weights, where, steps, nlon, count, lat_at, left_at, right_at, held=None, work=1
):
    rows, cols = covariance.shape
    lats = cols // nlon
    wide = steps * nlon
    padded = lats + 2 * steps

    def kernel(where_ref, weight_ref, p_ref, left_ref, right_ref, *rest):
        outs = rest[: len(rest) - (steps - 1)] if held is None else rest[1 : len(rest) - (steps - 1)]
        scratch = rest[len(rest) - (steps - 1) :]
        t_ref = outs[0]

        def weight(member, step_no, lat):
            return weight_ref[(member * steps + step_no) * padded + lat]

        view = lambda ref: plane_view(ref, 1, nlon)
        source = joined(view(left_ref), view(p_ref), view(right_ref), steps, lats)
        sweep(source, lats, weight, steps, 1, [view(ref) for ref in scratch], view(t_ref))
        if held is None:
            i = pl.program_id(0)

            @pl.when(i < steps)
            def _():
                outs[1][...] = t_ref[...]

            @pl.when(i >= count - steps)
            def _():
                outs[2][...] = t_ref[...]

    in_specs = [
        pl.BlockSpec(memory_space=pltpu.SMEM),
        pl.BlockSpec((nlon, cols), lambda i, at: (lat_at(i, at), 0)),
        pl.BlockSpec((nlon, wide), lambda i, at: (left_at(i), 0)),
        pl.BlockSpec((nlon, wide), lambda i, at: (right_at(i), 0)),
    ]
    out_specs = [pl.BlockSpec((nlon, cols), lambda i, at: (lat_at(i, at), 0))]
    out_shape = [jax.ShapeDtypeStruct((rows, cols), BF16)]
    operands = [where, weights, covariance, left, right]
    aliases = {}
    if held is None:
        out_specs += [
            pl.BlockSpec((nlon, cols), lambda i, at: (jnp.minimum(i, steps - 1), 0)),
            pl.BlockSpec((nlon, cols), lambda i, at: (jnp.maximum(i - (count - steps), 0), 0)),
        ]
        out_shape += [jax.ShapeDtypeStruct((wide, cols), BF16)] * 2
    else:
        in_specs.append(pl.BlockSpec(memory_space=pl.ANY))
        operands.append(held)
        aliases = {5: 0}
    return pl.pallas_call(
        kernel,
        grid_spec=pltpu.PrefetchScalarGridSpec(
            num_scalar_prefetch=1,
            grid=(count,),
            in_specs=in_specs,
            out_specs=out_specs,
            scratch_shapes=[
                pltpu.VMEM((nlon, (padded - 2 * (step_no + 1)) * nlon), F32) for step_no in range(steps - 1)
            ],
        ),
        out_shape=out_shape,
        input_output_aliases=aliases,
        compiler_params=params(),
        cost_estimate=cost(work),
        name="columns_operator",
    )(*operands)


def rows_operator(values, top, bottom, weights, steps, nlon, out_dtype, noise=None, diagonal=None):
    rows, cols = values.shape
    lat_rows = rows // nlon
    wide = steps * nlon
    padded = lat_rows + 2 * steps

    def kernel(weight_ref, x_ref, top_ref, bottom_ref, *rest):
        extra, (out_ref, *scratch) = rest[: 0 if noise is None else 2], rest[0 if noise is None else 2 :]

        def weight(member, step_no, lat):
            return weight_ref[(member * steps + step_no) * padded + lat]

        view = lambda ref: plane_view(ref, 0, nlon)
        source = joined(view(top_ref), view(x_ref), view(bottom_ref), steps, lat_rows)
        sweep(source, lat_rows, weight, steps, 0, [view(ref) for ref in scratch], view(out_ref))

        if noise is not None:
            diagonal_ref, noise_ref = extra
            lat = diagonal_ref[0] + pl.program_id(0)

            @pl.when(jnp.logical_and(lat >= 0, lat < lat_rows))
            def _():
                at = pl.ds(pl.multiple_of(lat * nlon, nlon), nlon)
                eye = lax.broadcasted_iota(jnp.int32, (nlon, nlon), 0) == lax.broadcasted_iota(
                    jnp.int32, (nlon, nlon), 1
                )
                out_ref[at, :] += jnp.where(eye, noise_ref[pl.ds(lat, 1), :], 0.0)

    in_specs = [
        pl.BlockSpec(memory_space=pltpu.SMEM),
        pl.BlockSpec((rows, nlon), lambda j: (0, j)),
        pl.BlockSpec((wide, nlon), lambda j: (0, j)),
        pl.BlockSpec((wide, nlon), lambda j: (0, j)),
    ]
    operands = [weights, values, top, bottom]
    if noise is not None:
        in_specs += [pl.BlockSpec(memory_space=pltpu.SMEM), pl.BlockSpec(noise.shape, lambda j: (0, 0))]
        operands += [diagonal, noise]
    return pl.pallas_call(
        kernel,
        grid=(cols // nlon,),
        in_specs=in_specs,
        out_specs=pl.BlockSpec((rows, nlon), lambda j: (0, j)),
        out_shape=jax.ShapeDtypeStruct((rows, cols), out_dtype),
        scratch_shapes=[
            pltpu.VMEM(((padded - 2 * (step_no + 1)) * nlon, nlon), F32) for step_no in range(steps - 1)
        ],
        compiler_params=params(),
        cost_estimate=cost(1),
        name="rows_operator",
    )(*operands)


def shifted(block, axis, by):
    size = lax.axis_size(axis)
    pairs = [(i, i + by) for i in range(size) if 0 <= i + by < size]
    return lax.ppermute(block, axis, pairs)


def gathered(first, last, axis, dim, unit, halo, own):
    before, after = [], []
    need, hop = halo, 1
    while need > 0:
        take = min(own, need)
        size = first.shape[dim]
        before.insert(0, shifted(lax.slice_in_dim(last, size - take * unit, size, axis=dim), axis, hop))
        after.append(shifted(lax.slice_in_dim(first, 0, take * unit, axis=dim), axis, -hop))
        need, hop = need - take, hop + 1
    join = lambda parts: parts[0] if len(parts) == 1 else jnp.concatenate(parts, axis=dim)
    return join(before), join(after)


def mirror_pairs(n_row, n_col, side):
    pairs = []
    for a in range(n_row):
        for b in range(n_col):
            to = 2 * a + (1 - b % 2) + side
            if 0 <= to < n_col:
                pairs.append((a * n_col + b, (b // 2) * n_col + to))
    return pairs


def body(covariance, noise_var, wind_table, diffusivity, wind_index):
    rows_dev, cols_dev = covariance.shape
    lat_rows, nlon = noise_var.shape
    steps, nlat = wind_index.shape
    lats = cols_dev // nlon
    n_row, n_col = lax.axis_size("row"), lax.axis_size("col")
    row_id, col_id = lax.axis_index("row"), lax.axis_index("col")
    own = min(lats - steps, lat_rows // 2 - steps, lats // 2)
    mirrored = lat_rows == 2 * lats and own > 0

    if not mirrored:
        return plain_body(covariance, noise_var, wind_table, diffusivity, wind_index)

    near = lat_rows // 2 - own
    middle = lat_rows // 2
    parity = col_id % 2
    by_parity = lambda even, odd: jnp.where(parity == 0, even, odd).astype(jnp.int32)
    mirror_at = by_parity(middle - own, middle).reshape(1)
    direct_at = by_parity(middle, middle - own).reshape(1)
    last, first_outer, first_inner, top, bottom = pack_direct(covariance, mirror_at, near, own, steps, nlon)
    left = shifted(last, "col", 1)
    right_outer = shifted(first_outer, "col", -1)
    p_top = shifted(bottom, "row", 1)
    p_bottom = shifted(top, "row", -1)

    base = (1 - parity) * lats
    sources = jnp.stack([base + lats - steps, base, by_parity(lats - own, 0)]).astype(jnp.int32)
    sources, top = lax.optimization_barrier((sources, top))
    left_m, right_m = pack_mirror(covariance, sources, own, steps, nlon)
    left_m, right_m, first_inner, wind_index, p_top, p_bottom = lax.optimization_barrier(
        (left_m, right_m, first_inner, wind_index, p_top, p_bottom)
    )
    left_m = lax.ppermute(left_m, ("row", "col"), mirror_pairs(n_row, n_col, 1))
    right_m = lax.ppermute(right_m, ("row", "col"), mirror_pairs(n_row, n_col, -1))
    right_inner = shifted(first_inner, "col", -1)

    weights = looked_up(wind_table, diffusivity, wind_index)
    padded_w = jnp.pad(weights, ((0, 0), (0, 0), (steps, steps)))
    row_w = lax.dynamic_slice_in_dim(padded_w, row_id * lat_rows, lat_rows + 2 * steps, 2).reshape(-1)
    col_w = lax.dynamic_slice_in_dim(padded_w, col_id * lats, lats + 2 * steps, 2).reshape(-1)

    operator_times_prior = rows_operator(covariance, p_top, p_bottom, row_w, steps, nlon, BF16)
    operator_times_prior, right_outer = lax.optimization_barrier((operator_times_prior, right_outer))
    same = lambda i: i
    inner_at = lambda i, at: at[0] + i
    mirror, t_first, t_last = columns_operator(
        covariance, left, right_outer, col_w, mirror_at, steps, nlon, 2 * near,
        lambda i, at: edge_at(i, near, 2 * own), lambda i: edge_at(i, near, own), same,
    )
    t_top = shifted(t_last, "row", 1)
    t_bottom = shifted(t_first, "row", -1)
    (mirror,) = columns_operator(
        covariance, left_m, right_m, col_w, mirror_at, steps, nlon, own, inner_at, same, same, mirror
    )
    (mirror,) = columns_operator(
        covariance, left, right_inner, col_w, direct_at, steps, nlon, own, inner_at,
        lambda i: i + near, same, mirror, 10 ** 13,
    )
    diagonal = (col_id * lats - row_id * lat_rows).astype(jnp.int32).reshape(1)
    predicted_spread_matrix = rows_operator(
        mirror, t_top, t_bottom, row_w, steps, nlon, F32, noise_var, diagonal
    )
    return (predicted_spread_matrix, operator_times_prior)


def plain_body(covariance, noise_var, wind_table, diffusivity, wind_index):
    rows_dev, cols_dev = covariance.shape
    lat_rows, nlon = noise_var.shape
    steps, nlat = wind_index.shape
    lats = cols_dev // nlon
    row_id, col_id = lax.axis_index("row"), lax.axis_index("col")
    sent = covariance.astype(BF16)
    left, right = gathered(sent, sent, "col", 1, nlon, steps, lats)
    p_top, p_bottom = gathered(sent, sent, "row", 0, nlon, steps, lat_rows)
    weights = looked_up(wind_table, diffusivity, wind_index)
    padded_w = jnp.pad(weights, ((0, 0), (0, 0), (steps, steps)))
    row_w = lax.dynamic_slice_in_dim(padded_w, row_id * lat_rows, lat_rows + 2 * steps, 2).reshape(-1)
    col_w = lax.dynamic_slice_in_dim(padded_w, col_id * lats, lats + 2 * steps, 2).reshape(-1)
    operator_times_prior = rows_operator(covariance, p_top, p_bottom, row_w, steps, nlon, BF16)
    unused = jnp.zeros((1,), jnp.int32)
    held = jnp.zeros((rows_dev, cols_dev), BF16)
    same = lambda i: i
    (mirror,) = columns_operator(
        covariance, left, right, col_w, unused, steps, nlon, lat_rows, lambda i, at: i, same, same, held
    )
    t_top, t_bottom = gathered(mirror, mirror, "row", 0, nlon, steps, lat_rows)
    diagonal = (col_id * lats - row_id * lat_rows).astype(jnp.int32).reshape(1)
    predicted_spread_matrix = rows_operator(
        mirror, t_top, t_bottom, row_w, steps, nlon, F32, noise_var, diagonal
    )
    return (predicted_spread_matrix, operator_times_prior)


def solution(mesh):
    in_specs = (P("row", "col"), P("row", None), P(), P(), P())
    out_specs = (P("row", "col"), P("row", "col"))
    return jax.shard_map(body, mesh=mesh, in_specs=in_specs, out_specs=out_specs, check_vma=False)
```

```python
import functools

import jax
import jax.numpy as jnp
from jax import lax
from jax.experimental import pallas as pl
from jax.experimental.pallas import tpu as pltpu
from jax.sharding import PartitionSpec as P

F32 = jnp.float32
BF16 = jnp.bfloat16
VMEM_LIMIT = 63 * 1024 * 1024


def params():
    return pltpu.CompilerParams(vmem_limit_bytes=VMEM_LIMIT)


def cost(work):
    return pl.CostEstimate(flops=work, bytes_accessed=work, transcendentals=0)


def stencil_terms(zonal_cour, merid_cour, diffuse):
    middle_weight = 1.0 - zonal_cour * zonal_cour - merid_cour * merid_cour - 4.0 * diffuse
    eastward_weight = 0.5 * zonal_cour * zonal_cour - 0.5 * zonal_cour + diffuse
    west_w = 0.5 * zonal_cour * zonal_cour + 0.5 * zonal_cour + diffuse
    north_w = 0.5 * merid_cour * merid_cour - 0.5 * merid_cour + diffuse
    south_w = 0.5 * merid_cour * merid_cour + 0.5 * merid_cour + diffuse
    return jnp.stack([middle_weight, eastward_weight, west_w, north_w, south_w])


def looked_up(wind_table, diffusivity, wind_index):
    table_ids = jnp.arange(wind_table.shape[0], dtype=jnp.int32)
    one_hot = (wind_index[:, :, None] == table_ids[None, None, :]).astype(F32)
    courant = jnp.einsum("sly,yc->slc", one_hot, wind_table, precision=lax.Precision.HIGHEST)
    diffuse = jnp.einsum("sly,y->sl", one_hot, diffusivity, precision=lax.Precision.HIGHEST)
    return stencil_terms(courant[..., 0], courant[..., 1], diffuse)


def sweep(source, lats, weight, steps, axis, scratch, out):
    for step_no in range(steps):
        last = step_no == steps - 1
        target = out if last else scratch[step_no]
        south, here = source(0), source(1)
        size = here.shape[axis]
        for i in range(lats + 2 * (steps - step_no - 1)):
            north = source(i + 2)
            c, e, w, n, s = [weight(member, step_no, i + 1 + step_no) for member in range(5)]
            fresh = (
                c * here
                + e * pltpu.roll(here, size - 1, axis)
                + w * pltpu.roll(here, 1, axis)
                + n * north
                + s * south
            )
            target(i, fresh)
            south, here = here, north
        if not last:
            source = scratch[step_no]


def plane_view(ref, axis, size):
    def view(i, value=None):
        at = pl.ds(i * size, size)
        index = (at, slice(None)) if axis == 0 else (slice(None), at)
        if value is None:
            return ref[index].astype(F32)
        ref[index] = value.astype(ref.dtype)

    return view


def joined(before, middle, after, steps, lats):
    def view(i):
        if i < steps:
            return before(i)
        if i < steps + lats:
            return middle(i - steps)
        return after(i - steps - lats)

    return view


def edge_at(i, near, own):
    return jnp.where(i < near, i, i + own)


def pack(covariance, where, near, own, halo, nlon):
    rows, cols = covariance.shape
    wide = halo * nlon
    outer, span = near * nlon, own * nlon
    direct = [(0, outer, 0, 0), (0, outer, outer, rows - outer), (2, span, 0, None)]
    made_shapes = [(2 * outer, wide)] * 2 + [(span, wide)] * 4 + [(wide, cols)] * 2
    got_shapes = [(size, wide) for _, size, _, _ in direct for _ in range(2)]
    got_shapes += [(wide, span)] * 2 + [(wide, cols)] * 2

    def kernel(where_ref, p_ref, *refs):
        outs, got, made, in_sem, out_sem = refs[:8], refs[8:18], refs[18:26], refs[26], refs[27]
        lat = lambda k: pl.multiple_of(where_ref[k] * nlon, nlon)
        sources = []
        for _, size, _, start in direct:
            at = pl.ds(lat(0) if start is None else start, size)
            sources += [p_ref.at[at, pl.ds(lane, wide)] for lane in (0, cols - wide)]
        sources += [p_ref.at[pl.ds(lat(k), wide), pl.ds(lat(3), span)] for k in (1, 2)]
        sources += [p_ref.at[pl.ds(start, wide), :] for start in (0, rows - wide)]
        loads = [
            pltpu.make_async_copy(source, got[k], in_sem.at[k]) for k, source in enumerate(sources)
        ]
        for load in loads:
            load.start()
        stores = []

        def store(k, row, size):
            at = pl.ds(row, size)
            stores.append(
                pltpu.make_async_copy(made[k].at[at, :], outs[k].at[at, :], out_sem.at[len(stores)])
            )
            stores[-1].start()

        for k, (first_out, size, row, _) in enumerate(direct):
            for side in range(2):
                loads[2 * k + side].wait()
                made[first_out + side][row : row + size, :] = got[2 * k + side][...].astype(BF16)
                store(first_out + side, row, size)
        for k in range(2):
            loads[6 + k].wait()
            for j in range(halo):
                for a in range(own):
                    block = got[6 + k][j * nlon : (j + 1) * nlon, a * nlon : (a + 1) * nlon]
                    made[4 + k][a * nlon : (a + 1) * nlon, j * nlon : (j + 1) * nlon] = block.T.astype(BF16)
            store(4 + k, 0, span)
        for k in range(2):
            loads[8 + k].wait()
            made[6 + k][...] = got[8 + k][...].astype(BF16)
            store(6 + k, 0, wide)
        for copy in stores:
            copy.wait()

    return pl.pallas_call(
        kernel,
        in_specs=[pl.BlockSpec(memory_space=pltpu.SMEM), pl.BlockSpec(memory_space=pl.ANY)],
        out_specs=[pl.BlockSpec(memory_space=pl.ANY)] * 8,
        out_shape=[jax.ShapeDtypeStruct(shape, BF16) for shape in made_shapes],
        scratch_shapes=[pltpu.VMEM(shape, F32) for shape in got_shapes]
        + [pltpu.VMEM(shape, BF16) for shape in made_shapes]
        + [pltpu.SemaphoreType.DMA((10,)), pltpu.SemaphoreType.DMA((10,))],
        compiler_params=params(),
        cost_estimate=cost(1),
        name="pack",
    )(where, covariance)


def columns_operator(
    covariance, left, right, weights, where, steps, nlon, count, lat_at, left_at, right_at, held=None, work=1
):
    rows, cols = covariance.shape
    lats = cols // nlon
    wide = steps * nlon
    padded = lats + 2 * steps

    def kernel(where_ref, weight_ref, p_ref, left_ref, right_ref, *rest):
        outs = rest[: len(rest) - (steps - 1)] if held is None else rest[1 : len(rest) - (steps - 1)]
        scratch = rest[len(rest) - (steps - 1) :]
        t_ref = outs[0]

        def weight(member, step_no, lat):
            return weight_ref[(member * steps + step_no) * padded + lat]

        view = lambda ref: plane_view(ref, 1, nlon)
        source = joined(view(left_ref), view(p_ref), view(right_ref), steps, lats)
        sweep(source, lats, weight, steps, 1, [view(ref) for ref in scratch], view(t_ref))
        if held is None:
            i = pl.program_id(0)

            @pl.when(i < steps)
            def _():
                outs[1][...] = t_ref[...]

            @pl.when(i >= count - steps)
            def _():
                outs[2][...] = t_ref[...]

    in_specs = [
        pl.BlockSpec(memory_space=pltpu.SMEM),
        pl.BlockSpec((nlon, cols), lambda i, at: (lat_at(i, at), 0)),
        pl.BlockSpec((nlon, wide), lambda i, at: (left_at(i), 0)),
        pl.BlockSpec((nlon, wide), lambda i, at: (right_at(i), 0)),
    ]
    out_specs = [pl.BlockSpec((nlon, cols), lambda i, at: (lat_at(i, at), 0))]
    out_shape = [jax.ShapeDtypeStruct((rows, cols), BF16)]
    operands = [where, weights, covariance, left, right]
    aliases = {}
    if held is None:
        out_specs += [
            pl.BlockSpec((nlon, cols), lambda i, at: (jnp.minimum(i, steps - 1), 0)),
            pl.BlockSpec((nlon, cols), lambda i, at: (jnp.maximum(i - (count - steps), 0), 0)),
        ]
        out_shape += [jax.ShapeDtypeStruct((wide, cols), BF16)] * 2
    else:
        in_specs.append(pl.BlockSpec(memory_space=pl.ANY))
        operands.append(held)
        aliases = {5: 0}
    return pl.pallas_call(
        kernel,
        grid_spec=pltpu.PrefetchScalarGridSpec(
            num_scalar_prefetch=1,
            grid=(count,),
            in_specs=in_specs,
            out_specs=out_specs,
            scratch_shapes=[
                pltpu.VMEM((nlon, (padded - 2 * (step_no + 1)) * nlon), F32) for step_no in range(steps - 1)
            ],
        ),
        out_shape=out_shape,
        input_output_aliases=aliases,
        compiler_params=params(),
        cost_estimate=cost(work),
        name="columns_operator",
    )(*operands)


def rows_operator(values, top, bottom, weights, steps, nlon, out_dtype, noise=None, diagonal=None):
    rows, cols = values.shape
    lat_rows = rows // nlon
    wide = steps * nlon
    padded = lat_rows + 2 * steps

    def kernel(weight_ref, x_ref, top_ref, bottom_ref, *rest):
        extra, (out_ref, *scratch) = rest[: 0 if noise is None else 2], rest[0 if noise is None else 2 :]

        def weight(member, step_no, lat):
            return weight_ref[(member * steps + step_no) * padded + lat]

        view = lambda ref: plane_view(ref, 0, nlon)
        source = joined(view(top_ref), view(x_ref), view(bottom_ref), steps, lat_rows)
        sweep(source, lat_rows, weight, steps, 0, [view(ref) for ref in scratch], view(out_ref))

        if noise is not None:
            diagonal_ref, noise_ref = extra
            lat = diagonal_ref[0] + pl.program_id(0)

            @pl.when(jnp.logical_and(lat >= 0, lat < lat_rows))
            def _():
                at = pl.ds(pl.multiple_of(lat * nlon, nlon), nlon)
                eye = lax.broadcasted_iota(jnp.int32, (nlon, nlon), 0) == lax.broadcasted_iota(
                    jnp.int32, (nlon, nlon), 1
                )
                out_ref[at, :] += jnp.where(eye, noise_ref[pl.ds(lat, 1), :], 0.0)

    in_specs = [
        pl.BlockSpec(memory_space=pltpu.SMEM),
        pl.BlockSpec((rows, nlon), lambda j: (0, j)),
        pl.BlockSpec((wide, nlon), lambda j: (0, j)),
        pl.BlockSpec((wide, nlon), lambda j: (0, j)),
    ]
    operands = [weights, values, top, bottom]
    if noise is not None:
        in_specs += [pl.BlockSpec(memory_space=pltpu.SMEM), pl.BlockSpec(noise.shape, lambda j: (0, 0))]
        operands += [diagonal, noise]
    return pl.pallas_call(
        kernel,
        grid=(cols // nlon,),
        in_specs=in_specs,
        out_specs=pl.BlockSpec((rows, nlon), lambda j: (0, j)),
        out_shape=jax.ShapeDtypeStruct((rows, cols), out_dtype),
        scratch_shapes=[
            pltpu.VMEM(((padded - 2 * (step_no + 1)) * nlon, nlon), F32) for step_no in range(steps - 1)
        ],
        compiler_params=params(),
        cost_estimate=cost(1),
        name="rows_operator",
    )(*operands)


def shifted(block, axis, by):
    size = lax.axis_size(axis)
    pairs = [(i, i + by) for i in range(size) if 0 <= i + by < size]
    return lax.ppermute(block, axis, pairs)


def gathered(first, last, axis, dim, unit, halo, own):
    before, after = [], []
    need, hop = halo, 1
    while need > 0:
        take = min(own, need)
        size = first.shape[dim]
        before.insert(0, shifted(lax.slice_in_dim(last, size - take * unit, size, axis=dim), axis, hop))
        after.append(shifted(lax.slice_in_dim(first, 0, take * unit, axis=dim), axis, -hop))
        need, hop = need - take, hop + 1
    join = lambda parts: parts[0] if len(parts) == 1 else jnp.concatenate(parts, axis=dim)
    return join(before), join(after)


def mirror_pairs(n_row, n_col, side):
    pairs = []
    for a in range(n_row):
        for b in range(n_col):
            to = 2 * a + (1 - b % 2) + side
            if 0 <= to < n_col:
                pairs.append((a * n_col + b, (b // 2) * n_col + to))
    return pairs


def body(covariance, noise_var, wind_table, diffusivity, wind_index):
    rows_dev, cols_dev = covariance.shape
    lat_rows, nlon = noise_var.shape
    steps, nlat = wind_index.shape
    lats = cols_dev // nlon
    n_row, n_col = lax.axis_size("row"), lax.axis_size("col")
    row_id, col_id = lax.axis_index("row"), lax.axis_index("col")
    own = min(lats - steps, lat_rows // 2 - steps, lats // 2)
    mirrored = lat_rows == 2 * lats and own > 0

    if not mirrored:
        return plain_body(covariance, noise_var, wind_table, diffusivity, wind_index)

    near = lat_rows // 2 - own
    middle = lat_rows // 2
    parity = col_id % 2
    by_parity = lambda even, odd: jnp.where(parity == 0, even, odd).astype(jnp.int32)
    mirror_at = by_parity(middle - own, middle).reshape(1)
    direct_at = by_parity(middle, middle - own).reshape(1)
    base = (1 - parity) * lats
    sources = jnp.stack([mirror_at[0], base + lats - steps, base, by_parity(lats - own, 0)]).astype(jnp.int32)
    first, last, first_inner, last_inner, left_m, right_m, top, bottom = pack(
        covariance, sources, near, own, steps, nlon
    )
    left = shifted(last, "col", 1)
    right = shifted(first, "col", -1)
    left_m = lax.ppermute(left_m, ("row", "col"), mirror_pairs(n_row, n_col, 1))
    right_m = lax.ppermute(right_m, ("row", "col"), mirror_pairs(n_row, n_col, -1))
    p_top = shifted(bottom, "row", 1)
    p_top, top, wind_index = lax.optimization_barrier((p_top, top, wind_index))
    p_bottom = shifted(top, "row", -1)

    weights = looked_up(wind_table, diffusivity, wind_index)
    padded_w = jnp.pad(weights, ((0, 0), (0, 0), (steps, steps)))
    row_w = lax.dynamic_slice_in_dim(padded_w, row_id * lat_rows, lat_rows + 2 * steps, 2).reshape(-1)
    col_w = lax.dynamic_slice_in_dim(padded_w, col_id * lats, lats + 2 * steps, 2).reshape(-1)

    operator_times_prior = rows_operator(covariance, p_top, p_bottom, row_w, steps, nlon, BF16)
    operator_times_prior, left, right, first_inner, last_inner = lax.optimization_barrier(
        (operator_times_prior, left, right, first_inner, last_inner)
    )
    left_inner = shifted(last_inner, "col", 1)
    right_inner = shifted(first_inner, "col", -1)
    same = lambda i: i
    inner_at = lambda i, at: at[0] + i
    mirror, t_first, t_last = columns_operator(
        covariance, left, right, col_w, mirror_at, steps, nlon, 2 * near,
        lambda i, at: edge_at(i, near, 2 * own), same, same,
    )
    t_top = shifted(t_last, "row", 1)
    t_first, left_m = lax.optimization_barrier((t_first, left_m))
    t_bottom = shifted(t_first, "row", -1)
    (mirror,) = columns_operator(
        covariance, left_m, right_m, col_w, mirror_at, steps, nlon, own, inner_at, same, same, mirror
    )
    (mirror,) = columns_operator(
        covariance, left_inner, right_inner, col_w, direct_at, steps, nlon, own, inner_at, same, same, mirror,
        10 ** 13,
    )
    diagonal = (col_id * lats - row_id * lat_rows).astype(jnp.int32).reshape(1)
    predicted_spread_matrix = rows_operator(
        mirror, t_top, t_bottom, row_w, steps, nlon, F32, noise_var, diagonal
    )
    return (predicted_spread_matrix, operator_times_prior)


def plain_body(covariance, noise_var, wind_table, diffusivity, wind_index):
    rows_dev, cols_dev = covariance.shape
    lat_rows, nlon = noise_var.shape
    steps, nlat = wind_index.shape
    lats = cols_dev // nlon
    row_id, col_id = lax.axis_index("row"), lax.axis_index("col")
    sent = covariance.astype(BF16)
    left, right = gathered(sent, sent, "col", 1, nlon, steps, lats)
    p_top, p_bottom = gathered(sent, sent, "row", 0, nlon, steps, lat_rows)
    weights = looked_up(wind_table, diffusivity, wind_index)
    padded_w = jnp.pad(weights, ((0, 0), (0, 0), (steps, steps)))
    row_w = lax.dynamic_slice_in_dim(padded_w, row_id * lat_rows, lat_rows + 2 * steps, 2).reshape(-1)
    col_w = lax.dynamic_slice_in_dim(padded_w, col_id * lats, lats + 2 * steps, 2).reshape(-1)
    operator_times_prior = rows_operator(covariance, p_top, p_bottom, row_w, steps, nlon, BF16)
    unused = jnp.zeros((1,), jnp.int32)
    held = jnp.zeros((rows_dev, cols_dev), BF16)
    same = lambda i: i
    (mirror,) = columns_operator(
        covariance, left, right, col_w, unused, steps, nlon, lat_rows, lambda i, at: i, same, same, held
    )
    t_top, t_bottom = gathered(mirror, mirror, "row", 0, nlon, steps, lat_rows)
    diagonal = (col_id * lats - row_id * lat_rows).astype(jnp.int32).reshape(1)
    predicted_spread_matrix = rows_operator(
        mirror, t_top, t_bottom, row_w, steps, nlon, F32, noise_var, diagonal
    )
    return (predicted_spread_matrix, operator_times_prior)


def solution(mesh):
    in_specs = (P("row", "col"), P("row", None), P(), P(), P())
    out_specs = (P("row", "col"), P("row", "col"))
    return jax.shard_map(body, mesh=mesh, in_specs=in_specs, out_specs=out_specs, check_vma=False)
```

```python
import functools

import jax
import jax.numpy as jnp
from jax import lax
from jax.experimental import pallas as pl
from jax.experimental.pallas import tpu as pltpu
from jax.sharding import PartitionSpec as P

F32 = jnp.float32
BF16 = jnp.bfloat16
VMEM_LIMIT = 63 * 1024 * 1024


def params():
    return pltpu.CompilerParams(vmem_limit_bytes=VMEM_LIMIT)


def cost(work):
    return pl.CostEstimate(flops=work, bytes_accessed=work, transcendentals=0)


def stencil_terms(zonal_cour, merid_cour, diffuse):
    middle_weight = 1.0 - zonal_cour * zonal_cour - merid_cour * merid_cour - 4.0 * diffuse
    eastward_weight = 0.5 * zonal_cour * zonal_cour - 0.5 * zonal_cour + diffuse
    west_w = 0.5 * zonal_cour * zonal_cour + 0.5 * zonal_cour + diffuse
    north_w = 0.5 * merid_cour * merid_cour - 0.5 * merid_cour + diffuse
    south_w = 0.5 * merid_cour * merid_cour + 0.5 * merid_cour + diffuse
    return jnp.stack([middle_weight, eastward_weight, west_w, north_w, south_w])


def looked_up(wind_table, diffusivity, wind_index):
    table_ids = jnp.arange(wind_table.shape[0], dtype=jnp.int32)
    one_hot = (wind_index[:, :, None] == table_ids[None, None, :]).astype(F32)
    courant = jnp.einsum("sly,yc->slc", one_hot, wind_table, precision=lax.Precision.HIGHEST)
    diffuse = jnp.einsum("sly,y->sl", one_hot, diffusivity, precision=lax.Precision.HIGHEST)
    return stencil_terms(courant[..., 0], courant[..., 1], diffuse)


def split(values):
    high = values.astype(BF16)
    return high, (values - high.astype(F32)).astype(BF16)


def circulant(row):
    size = row.shape[1]
    return pltpu.roll(jnp.broadcast_to(row, (size, size)), 0, 1, stride=1, stride_axis=0)


def product(left, right):
    return jnp.dot(left, right, preferred_element_type=F32)


def composed(weight_ref, steps, lats):
    nlon = weight_ref.shape[-1]
    padded = lats + 2 * steps
    lane = lax.broadcasted_iota(jnp.int32, (padded, nlon), 1)
    rows = {0: (lane == 0).astype(F32)}
    for step_no in range(steps):
        low, high = step_no + 1, padded - step_no - 1
        c, e, w, n, s = [weight_ref[member * steps + step_no, low:high, :] for member in range(5)]
        size = high - low
        fresh = {}
        for d in range(-step_no - 1, step_no + 2):
            terms = []
            if d in rows:
                here = rows[d][1 : 1 + size]
                terms += [c * here, e * pltpu.roll(here, 1, 1), w * pltpu.roll(here, nlon - 1, 1)]
            if d - 1 in rows:
                terms.append(n * rows[d - 1][2 : 2 + size])
            if d + 1 in rows:
                terms.append(s * rows[d + 1][0:size])
            fresh[d] = functools.reduce(lambda x, y: x + y, terms)
        rows = fresh
    return rows


def stencil_rows(row_seights, col_seights, steps, lat_rows, lats, nlon):
    def kernel(row_ref, col_ref, row_out, col_out):
        for ref, out, size in ((row_ref, row_out, lat_rows), (col_ref, col_out, lats)):
            for d, value in composed(ref, steps, size).items():
                out[d + steps] = value

    return pl.pallas_call(
        kernel,
        out_shape=[
            jax.ShapeDtypeStruct((2 * steps + 1, size, nlon), F32) for size in (lat_rows, lats)
        ],
        compiler_params=params(),
        cost_estimate=cost(1),
        name="stencil_rows",
    )(row_seights, col_seights)


def pack(covariance, where, near, own, halo, nlon):
    rows, cols = covariance.shape
    wide = halo * nlon
    outer, span = near * nlon, own * nlon
    direct = [(0, outer, 0, 0), (0, outer, outer, rows - outer), (2, span, 0, None)]
    made_shapes = [(2 * outer, wide)] * 2 + [(span, wide)] * 4 + [(wide, cols)] * 2
    got_shapes = [(size, wide) for _, size, _, _ in direct for _ in range(2)]
    got_shapes += [(wide, span)] * 2 + [(wide, cols)] * 2

    def kernel(where_ref, p_ref, *refs):
        outs, got, made, in_sem, out_sem = refs[:8], refs[8:18], refs[18:26], refs[26], refs[27]
        lat = lambda k: pl.multiple_of(where_ref[k] * nlon, nlon)
        sources = []
        for _, size, _, start in direct:
            at = pl.ds(lat(0) if start is None else start, size)
            sources += [p_ref.at[at, pl.ds(lane, wide)] for lane in (0, cols - wide)]
        sources += [p_ref.at[pl.ds(lat(k), wide), pl.ds(lat(3), span)] for k in (1, 2)]
        sources += [p_ref.at[pl.ds(start, wide), :] for start in (0, rows - wide)]
        loads = [
            pltpu.make_async_copy(source, got[k], in_sem.at[k]) for k, source in enumerate(sources)
        ]
        for load in loads:
            load.start()
        stores = []

        def store(k, row, size):
            at = pl.ds(row, size)
            stores.append(
                pltpu.make_async_copy(made[k].at[at, :], outs[k].at[at, :], out_sem.at[len(stores)])
            )
            stores[-1].start()

        for k, (first_out, size, row, _) in enumerate(direct):
            for side in range(2):
                loads[2 * k + side].wait()
                made[first_out + side][row : row + size, :] = got[2 * k + side][...].astype(BF16)
                store(first_out + side, row, size)
        for k in range(2):
            loads[6 + k].wait()
            for j in range(halo):
                for a in range(own):
                    block = got[6 + k][j * nlon : (j + 1) * nlon, a * nlon : (a + 1) * nlon]
                    made[4 + k][a * nlon : (a + 1) * nlon, j * nlon : (j + 1) * nlon] = block.T.astype(BF16)
            store(4 + k, 0, span)
        for k in range(2):
            loads[8 + k].wait()
            made[6 + k][...] = got[8 + k][...].astype(BF16)
            store(6 + k, 0, wide)
        for copy in stores:
            copy.wait()

    return pl.pallas_call(
        kernel,
        in_specs=[pl.BlockSpec(memory_space=pltpu.SMEM), pl.BlockSpec(memory_space=pl.ANY)],
        out_specs=[pl.BlockSpec(memory_space=pl.ANY)] * 8,
        out_shape=[jax.ShapeDtypeStruct(shape, BF16) for shape in made_shapes],
        scratch_shapes=[pltpu.VMEM(shape, F32) for shape in got_shapes]
        + [pltpu.VMEM(shape, BF16) for shape in made_shapes]
        + [pltpu.SemaphoreType.DMA((10,)), pltpu.SemaphoreType.DMA((10,))],
        compiler_params=params(),
        cost_estimate=cost(1),
        name="pack",
    )(where, covariance)


def columns_operator(
    covariance, left, right, stencil, where, steps, nlon, count, pair_at, left_at, right_at, held=None, work=1
):
    rows, cols = covariance.shape
    lats = cols // nlon
    wide = steps * nlon
    size = 2 * nlon
    span = 2 * steps * nlon
    pairs = lats // 2

    def kernel(where_ref, stencil_ref, p_ref, left_ref, right_ref, *rest):
        outs, (high_ref, low_ref, b_high, b_low) = rest[:-4], rest[-4:]
        if held is not None:
            outs = outs[1:]
        t_ref = outs[0]
        i = pl.program_id(0)

        @pl.when(i == 0)
        def _():
            low_ref[:, :wide] = jnp.zeros((size, wide), BF16)
            low_ref[:, wide + cols :] = jnp.zeros((size, wide), BF16)
            for q in range(pairs):
                for a in range(2):
                    for k in range(2 * steps):
                        d = k - (steps - 1) - a
                        high, low = split(circulant(stencil_ref[d + steps, 2 * q + a : 2 * q + a + 1, :]))
                        at = pl.ds(q * span + k * nlon, nlon)
                        b_high[at, a * nlon : (a + 1) * nlon] = high
                        b_low[at, a * nlon : (a + 1) * nlon] = low

        high_ref[:, :wide] = left_ref[...]
        high_ref[:, wide + cols :] = right_ref[...]
        high, low = split(p_ref[...])
        high_ref[:, wide : wide + cols] = high
        low_ref[:, wide : wide + cols] = low
        for q in range(pairs):
            start = (2 * q + 1) * nlon
            window, rest_of = high_ref[:, start : start + span], low_ref[:, start : start + span]
            of = pl.ds(q * span, span)
            total = product(window, b_high[of, :]) + product(window, b_low[of, :])
            total += product(rest_of, b_high[of, :])
            for a, unit, d in ((0, 2 * q, -steps), (1, 2 * q + 2 * steps + 1, steps)):
                far = slice(unit * nlon, (unit + 1) * nlon)
                weight = jnp.sum(stencil_ref[d + steps, 2 * q + a : 2 * q + a + 1, :], axis=1, keepdims=True)
                far_values = high_ref[:, far].astype(F32) + low_ref[:, far].astype(F32)
                value = total[:, a * nlon : (a + 1) * nlon] + weight * far_values
                t_ref[:, (2 * q + a) * nlon : (2 * q + a + 1) * nlon] = value.astype(BF16)
        if held is None:
            done = 0
            for block in range(-(-wide // size)):
                part = min(size, wide - done)

                @pl.when(i == block)
                def _(done=done, part=part):
                    outs[1][done : done + part, :] = t_ref[:part, :]

                @pl.when(i == count - 1 - block)
                def _(done=done, part=part):
                    outs[2][wide - done - part : wide - done, :] = t_ref[size - part :, :]

                done += part

    in_specs = [
        pl.BlockSpec(stencil.shape, lambda i, at: (0, 0, 0)),
        pl.BlockSpec((size, cols), lambda i, at: (pair_at(i, at), 0)),
        pl.BlockSpec((size, wide), lambda i, at: (left_at(i), 0)),
        pl.BlockSpec((size, wide), lambda i, at: (right_at(i), 0)),
    ]
    out_specs = [pl.BlockSpec((size, cols), lambda i, at: (pair_at(i, at), 0))]
    out_shape = [jax.ShapeDtypeStruct((rows, cols), BF16)]
    operands = [where, stencil, covariance, left, right]
    aliases = {}
    if held is None:
        out_specs += [pl.BlockSpec((wide, cols), lambda i, at: (0, 0))] * 2
        out_shape += [jax.ShapeDtypeStruct((wide, cols), BF16)] * 2
    else:
        in_specs.append(pl.BlockSpec(memory_space=pl.ANY))
        operands.append(held)
        aliases = {5: 0}
    return pl.pallas_call(
        kernel,
        grid_spec=pltpu.PrefetchScalarGridSpec(
            num_scalar_prefetch=1,
            grid=(count,),
            in_specs=in_specs,
            out_specs=out_specs,
            scratch_shapes=[pltpu.VMEM((size, cols + 2 * wide), BF16)] * 2
            + [pltpu.VMEM((pairs * span, size), BF16)] * 2,
        ),
        out_shape=out_shape,
        input_output_aliases=aliases,
        compiler_params=params(),
        cost_estimate=cost(work),
        name="columns_operator",
    )(*operands)


def rows_operator(values, top, bottom, stencil, steps, nlon, out_dtype, noise=None, diagonal=None):
    rows, cols = values.shape
    lat_rows = rows // nlon
    wide = steps * nlon
    size = 2 * nlon
    span = 2 * steps * nlon
    pairs = lat_rows // 2
    ahead = (steps + 1) // 2
    exact = values.dtype == BF16
    chunk = min(cols, 256)

    def kernel(stencil_ref, x_ref, top_ref, bottom_ref, *rest):
        extra, rest = (rest[:2], rest[2:]) if noise is not None else ((), rest)
        out_ref, a_high, a_low, high_ref = rest[:4]
        low_ref = None if exact else rest[4]
        g = pl.program_id(0)

        @pl.when(g == 0)
        def _():
            high_ref[:wide, :] = top_ref[...]
            high_ref[wide + rows :, :] = bottom_ref[...]
            if not exact:
                low_ref[:wide, :] = jnp.zeros((wide, cols), BF16)
                low_ref[wide + rows :, :] = jnp.zeros((wide, cols), BF16)

        @pl.when(g < pairs)
        def _():
            at = pl.ds(pl.multiple_of(wide + g * size, nlon), size)
            if exact:
                high_ref[at, :] = x_ref[...]
            else:
                high_ref[at, :], low_ref[at, :] = split(x_ref[...])

        @pl.when(g >= ahead)
        def _():
            p = g - ahead
            row = lambda d, a: stencil_ref[d + steps, pl.ds(2 * p + a, 1), :]
            for a in range(2):
                for k in range(2 * steps):
                    high, low = split(circulant(row(k - (steps - 1) - a, a)))
                    a_high[a * nlon : (a + 1) * nlon, k * nlon : (k + 1) * nlon] = high
                    a_low[a * nlon : (a + 1) * nlon, k * nlon : (k + 1) * nlon] = low
            unit = lambda k: pl.multiple_of((2 * p + k) * nlon, nlon)
            for lane in range(0, cols, chunk):
                lanes = slice(lane, lane + chunk)
                window = high_ref[pl.ds(unit(1), span), lanes]
                total = product(a_high[...], window) + product(a_low[...], window)
                if not exact:
                    total += product(a_high[...], low_ref[pl.ds(unit(1), span), lanes])
                for a, k, d in ((0, 0, -steps), (1, 2 * steps + 1, steps)):
                    far = high_ref[pl.ds(unit(k), nlon), lanes].astype(F32)
                    if not exact:
                        far += low_ref[pl.ds(unit(k), nlon), lanes].astype(F32)
                    weight = jnp.sum(row(d, a), axis=1, keepdims=True)
                    value = total[a * nlon : (a + 1) * nlon, :] + weight * far
                    out_ref[a * nlon : (a + 1) * nlon, lanes] = value.astype(out_dtype)
            if noise is not None:
                diagonal_ref, noise_ref = extra
                for a in range(2):
                    lat = 2 * p + a - diagonal_ref[0]

                    @pl.when(jnp.logical_and(lat >= 0, lat < cols // nlon))
                    def _(a=a, lat=lat):
                        lanes = pl.ds(pl.multiple_of(lat * nlon, nlon), nlon)
                        eye = lax.broadcasted_iota(jnp.int32, (nlon, nlon), 0) == lax.broadcasted_iota(
                            jnp.int32, (nlon, nlon), 1
                        )
                        added = jnp.where(eye, noise_ref[pl.ds(2 * p + a, 1), :], 0.0)
                        out_ref[a * nlon : (a + 1) * nlon, lanes] += added

    in_specs = [
        pl.BlockSpec(stencil.shape, lambda g: (0, 0, 0)),
        pl.BlockSpec((size, cols), lambda g: (jnp.minimum(g, pairs - 1), 0)),
        pl.BlockSpec((wide, cols), lambda g: (0, 0)),
        pl.BlockSpec((wide, cols), lambda g: (0, 0)),
    ]
    operands = [stencil, values, top, bottom]
    if noise is not None:
        in_specs += [pl.BlockSpec(memory_space=pltpu.SMEM), pl.BlockSpec(noise.shape, lambda g: (0, 0))]
        operands += [diagonal, noise]
    return pl.pallas_call(
        kernel,
        grid=(pairs + ahead,),
        in_specs=in_specs,
        out_specs=pl.BlockSpec((size, cols), lambda g: (jnp.maximum(g - ahead, 0), 0)),
        out_shape=jax.ShapeDtypeStruct((rows, cols), out_dtype),
        scratch_shapes=[pltpu.VMEM((size, span), BF16)] * 2
        + [pltpu.VMEM((rows + 2 * wide, cols), BF16)] * (1 if exact else 2),
        compiler_params=params(),
        cost_estimate=cost(1),
        name="rows_operator",
    )(*operands)


def shifted(block, axis, by):
    size = lax.axis_size(axis)
    pairs = [(i, i + by) for i in range(size) if 0 <= i + by < size]
    return lax.ppermute(block, axis, pairs)


def gathered(first, last, axis, dim, unit, halo, own):
    before, after = [], []
    need, hop = halo, 1
    while need > 0:
        take = min(own, need)
        size = first.shape[dim]
        before.insert(0, shifted(lax.slice_in_dim(last, size - take * unit, size, axis=dim), axis, hop))
        after.append(shifted(lax.slice_in_dim(first, 0, take * unit, axis=dim), axis, -hop))
        need, hop = need - take, hop + 1
    join = lambda parts: parts[0] if len(parts) == 1 else jnp.concatenate(parts, axis=dim)
    return join(before), join(after)


def mirror_pairs(n_row, n_col, side):
    pairs = []
    for a in range(n_row):
        for b in range(n_col):
            to = 2 * a + (1 - b % 2) + side
            if 0 <= to < n_col:
                pairs.append((a * n_col + b, (b // 2) * n_col + to))
    return pairs


def device_stencils(wind_table, diffusivity, wind_index, lat_rows, lats, nlon):
    steps = wind_index.shape[0]
    weights = looked_up(wind_table, diffusivity, wind_index)
    padded = jnp.pad(weights, ((0, 0), (0, 0), (steps, steps)))
    turned = padded[jnp.array([0, 2, 1, 3, 4])]

    def local(of, axis, count):
        part = lax.dynamic_slice_in_dim(of, lax.axis_index(axis) * count, count + 2 * steps, 2)
        part = part.reshape(5 * steps, count + 2 * steps, 1)
        return jnp.broadcast_to(part, part.shape[:2] + (nlon,))

    return stencil_rows(local(padded, "row", lat_rows), local(turned, "col", lats), steps, lat_rows, lats, nlon)


def body(covariance, noise_var, wind_table, diffusivity, wind_index):
    rows_dev, cols_dev = covariance.shape
    lat_rows, nlon = noise_var.shape
    steps, nlat = wind_index.shape
    lats = cols_dev // nlon
    n_row, n_col = lax.axis_size("row"), lax.axis_size("col")
    row_id, col_id = lax.axis_index("row"), lax.axis_index("col")
    own = lat_rows // 4
    mirrored = lat_rows == 2 * lats and own % 2 == 0 and own >= steps and own <= lats - steps

    if not mirrored:
        return plain_body(covariance, noise_var, wind_table, diffusivity, wind_index)

    near = lat_rows // 2 - own
    middle = lat_rows // 2
    parity = col_id % 2
    by_parity = lambda even, odd: jnp.where(parity == 0, even, odd).astype(jnp.int32)
    mirror_at = by_parity(middle - own, middle).reshape(1)
    direct_at = by_parity(middle, middle - own).reshape(1)
    base = (1 - parity) * lats
    sources = jnp.stack([mirror_at[0], base + lats - steps, base, by_parity(lats - own, 0)]).astype(jnp.int32)
    first, last, first_inner, last_inner, left_m, right_m, top, bottom = pack(
        covariance, sources, near, own, steps, nlon
    )
    left = shifted(last, "col", 1)
    right = shifted(first, "col", -1)
    left_m = lax.ppermute(left_m, ("row", "col"), mirror_pairs(n_row, n_col, 1))
    right_m = lax.ppermute(right_m, ("row", "col"), mirror_pairs(n_row, n_col, -1))
    p_top = shifted(bottom, "row", 1)
    p_top, top, wind_index = lax.optimization_barrier((p_top, top, wind_index))
    p_bottom = shifted(top, "row", -1)

    row_s, col_s = device_stencils(wind_table, diffusivity, wind_index, lat_rows, lats, nlon)

    operator_times_prior = rows_operator(covariance, p_top, p_bottom, row_s, steps, nlon, BF16)
    operator_times_prior, left, right, first_inner, last_inner = lax.optimization_barrier(
        (operator_times_prior, left, right, first_inner, last_inner)
    )
    left_inner = shifted(last_inner, "col", 1)
    right_inner = shifted(first_inner, "col", -1)
    same = lambda i: i
    inner_at = lambda i, at: at[0] // 2 + i
    mirror, t_first, t_last = columns_operator(
        covariance, left, right, col_s, mirror_at, steps, nlon, near,
        lambda i, at: jnp.where(i < near // 2, i, i + own), same, same,
    )
    t_top = shifted(t_last, "row", 1)
    t_first, left_m = lax.optimization_barrier((t_first, left_m))
    t_bottom = shifted(t_first, "row", -1)
    (mirror,) = columns_operator(
        covariance, left_m, right_m, col_s, mirror_at, steps, nlon, own // 2, inner_at, same, same, mirror
    )
    (mirror,) = columns_operator(
        covariance, left_inner, right_inner, col_s, direct_at, steps, nlon, own // 2, inner_at, same, same, mirror,
        10 ** 13,
    )
    diagonal = (col_id * lats - row_id * lat_rows).astype(jnp.int32).reshape(1)
    predicted_spread_matrix = rows_operator(
        mirror, t_top, t_bottom, row_s, steps, nlon, F32, noise_var, diagonal
    )
    return (predicted_spread_matrix, operator_times_prior)


def plain_body(covariance, noise_var, wind_table, diffusivity, wind_index):
    rows_dev, cols_dev = covariance.shape
    lat_rows, nlon = noise_var.shape
    steps, nlat = wind_index.shape
    lats = cols_dev // nlon
    row_id, col_id = lax.axis_index("row"), lax.axis_index("col")
    sent = covariance.astype(BF16)
    left, right = gathered(sent, sent, "col", 1, nlon, steps, lats)
    p_top, p_bottom = gathered(sent, sent, "row", 0, nlon, steps, lat_rows)
    row_s, col_s = device_stencils(wind_table, diffusivity, wind_index, lat_rows, lats, nlon)
    operator_times_prior = rows_operator(covariance, p_top, p_bottom, row_s, steps, nlon, BF16)
    unused = jnp.zeros((1,), jnp.int32)
    held = jnp.zeros((rows_dev, cols_dev), BF16)
    same = lambda i: i
    (mirror,) = columns_operator(
        covariance, left, right, col_s, unused, steps, nlon, lat_rows // 2, lambda i, at: i, same, same, held
    )
    t_top, t_bottom = gathered(mirror, mirror, "row", 0, nlon, steps, lat_rows)
    diagonal = (col_id * lats - row_id * lat_rows).astype(jnp.int32).reshape(1)
    predicted_spread_matrix = rows_operator(
        mirror, t_top, t_bottom, row_s, steps, nlon, F32, noise_var, diagonal
    )
    return (predicted_spread_matrix, operator_times_prior)


def solution(mesh):
    in_specs = (P("row", "col"), P("row", None), P(), P(), P())
    out_specs = (P("row", "col"), P("row", "col"))
    return jax.shard_map(body, mesh=mesh, in_specs=in_specs, out_specs=out_specs, check_vma=False)
```

```python
import functools

import jax
import jax.numpy as jnp
from jax import lax
from jax.experimental import pallas as pl
from jax.experimental.pallas import tpu as pltpu
from jax.sharding import PartitionSpec as P

F32 = jnp.float32
BF16 = jnp.bfloat16
VMEM_LIMIT = 63 * 1024 * 1024


def params():
    return pltpu.CompilerParams(vmem_limit_bytes=VMEM_LIMIT)


def cost(work):
    return pl.CostEstimate(flops=work, bytes_accessed=work, transcendentals=0)


def stencil_terms(zonal_cour, merid_cour, diffuse):
    middle_weight = 1.0 - zonal_cour * zonal_cour - merid_cour * merid_cour - 4.0 * diffuse
    eastward_weight = 0.5 * zonal_cour * zonal_cour - 0.5 * zonal_cour + diffuse
    west_w = 0.5 * zonal_cour * zonal_cour + 0.5 * zonal_cour + diffuse
    north_w = 0.5 * merid_cour * merid_cour - 0.5 * merid_cour + diffuse
    south_w = 0.5 * merid_cour * merid_cour + 0.5 * merid_cour + diffuse
    return jnp.stack([middle_weight, eastward_weight, west_w, north_w, south_w])


def looked_up(wind_table, diffusivity, wind_index):
    table_ids = jnp.arange(wind_table.shape[0], dtype=jnp.int32)
    one_hot = (wind_index[:, :, None] == table_ids[None, None, :]).astype(F32)
    courant = jnp.einsum("sly,yc->slc", one_hot, wind_table, precision=lax.Precision.HIGHEST)
    diffuse = jnp.einsum("sly,y->sl", one_hot, diffusivity, precision=lax.Precision.HIGHEST)
    return stencil_terms(courant[..., 0], courant[..., 1], diffuse)


def split(values):
    high = values.astype(BF16)
    return high, (values - high.astype(F32)).astype(BF16)


def circulant(row):
    size = row.shape[1]
    return pltpu.roll(jnp.broadcast_to(row, (size, size)), 0, 1, stride=1, stride_axis=0)


def product(left, right):
    return jnp.dot(left, right, preferred_element_type=F32)


def composed(weight_ref, steps, lats):
    nlon = weight_ref.shape[-1]
    padded = lats + 2 * steps
    lane = lax.broadcasted_iota(jnp.int32, (padded, nlon), 1)
    rows = {0: (lane == 0).astype(F32)}
    for step_no in range(steps):
        low, high = step_no + 1, padded - step_no - 1
        c, e, w, n, s = [weight_ref[member * steps + step_no, low:high, :] for member in range(5)]
        size = high - low
        fresh = {}
        for d in range(-step_no - 1, step_no + 2):
            terms = []
            if d in rows:
                here = rows[d][1 : 1 + size]
                terms += [c * here, e * pltpu.roll(here, 1, 1), w * pltpu.roll(here, nlon - 1, 1)]
            if d - 1 in rows:
                terms.append(n * rows[d - 1][2 : 2 + size])
            if d + 1 in rows:
                terms.append(s * rows[d + 1][0:size])
            fresh[d] = functools.reduce(lambda x, y: x + y, terms)
        rows = fresh
    return rows


def stencil_rows(row_seights, col_seights, steps, lat_rows, lats, nlon):
    def kernel(row_ref, col_ref, row_out, col_out):
        for ref, out, size in ((row_ref, row_out, lat_rows), (col_ref, col_out, lats)):
            for d, value in composed(ref, steps, size).items():
                out[d + steps] = value

    return pl.pallas_call(
        kernel,
        out_shape=[
            jax.ShapeDtypeStruct((2 * steps + 1, size, nlon), F32) for size in (lat_rows, lats)
        ],
        compiler_params=params(),
        cost_estimate=cost(1),
        name="stencil_rows",
    )(row_seights, col_seights)


def pack(covariance, where, near, own, halo, nlon):
    rows, cols = covariance.shape
    wide = halo * nlon
    outer, span = near * nlon, own * nlon
    direct = [(0, outer, 0, 0), (0, outer, outer, rows - outer), (2, span, 0, None)]
    made_shapes = [(2 * outer, wide)] * 2 + [(span, wide)] * 4 + [(wide, cols)] * 2
    got_shapes = [(size, wide) for _, size, _, _ in direct for _ in range(2)]
    got_shapes += [(wide, span)] * 2 + [(wide, cols)] * 2

    def kernel(where_ref, p_ref, *refs):
        outs, got, made, in_sem, out_sem = refs[:8], refs[8:18], refs[18:26], refs[26], refs[27]
        lat = lambda k: pl.multiple_of(where_ref[k] * nlon, nlon)
        sources = []
        for _, size, _, start in direct:
            at = pl.ds(lat(0) if start is None else start, size)
            sources += [p_ref.at[at, pl.ds(lane, wide)] for lane in (0, cols - wide)]
        sources += [p_ref.at[pl.ds(lat(k), wide), pl.ds(lat(3), span)] for k in (1, 2)]
        sources += [p_ref.at[pl.ds(start, wide), :] for start in (0, rows - wide)]
        loads = [
            pltpu.make_async_copy(source, got[k], in_sem.at[k]) for k, source in enumerate(sources)
        ]
        for load in loads:
            load.start()
        stores = []

        def store(k, row, size):
            at = pl.ds(row, size)
            stores.append(
                pltpu.make_async_copy(made[k].at[at, :], outs[k].at[at, :], out_sem.at[len(stores)])
            )
            stores[-1].start()

        for k, (first_out, size, row, _) in enumerate(direct):
            for side in range(2):
                loads[2 * k + side].wait()
                made[first_out + side][row : row + size, :] = got[2 * k + side][...].astype(BF16)
                store(first_out + side, row, size)
        for k in range(2):
            loads[6 + k].wait()
            for j in range(halo):
                for a in range(own):
                    block = got[6 + k][j * nlon : (j + 1) * nlon, a * nlon : (a + 1) * nlon]
                    made[4 + k][a * nlon : (a + 1) * nlon, j * nlon : (j + 1) * nlon] = block.T.astype(BF16)
            store(4 + k, 0, span)
        for k in range(2):
            loads[8 + k].wait()
            made[6 + k][...] = got[8 + k][...].astype(BF16)
            store(6 + k, 0, wide)
        for copy in stores:
            copy.wait()

    return pl.pallas_call(
        kernel,
        in_specs=[pl.BlockSpec(memory_space=pltpu.SMEM), pl.BlockSpec(memory_space=pl.ANY)],
        out_specs=[pl.BlockSpec(memory_space=pl.ANY)] * 8,
        out_shape=[jax.ShapeDtypeStruct(shape, BF16) for shape in made_shapes],
        scratch_shapes=[pltpu.VMEM(shape, F32) for shape in got_shapes]
        + [pltpu.VMEM(shape, BF16) for shape in made_shapes]
        + [pltpu.SemaphoreType.DMA((10,)), pltpu.SemaphoreType.DMA((10,))],
        compiler_params=params(),
        cost_estimate=cost(1),
        name="pack",
    )(where, covariance)


def columns_operator(
    covariance, left, right, stencil, where, unit, steps, nlon, count, block_at, held=None, work=1
):
    rows, cols = covariance.shape
    lats = cols // nlon
    wide = steps * nlon
    size = unit * nlon
    span = 2 * steps * nlon
    pairs = lats // 2

    def kernel(where_ref, stencil_ref, p_ref, left_ref, right_ref, *rest):
        outs, (data_ref, b_high, b_low) = rest[:-3], rest[-3:]
        if held is not None:
            outs = outs[1:]
        t_ref = outs[0]
        i = pl.program_id(0)

        @pl.when(i == 0)
        def _():
            data_ref[size:, :wide] = jnp.zeros((size, wide), BF16)
            data_ref[size:, wide + cols :] = jnp.zeros((size, wide), BF16)
            for q in range(pairs):
                for a in range(2):
                    for k in range(2 * steps):
                        d = k - (steps - 1) - a
                        high, low = split(circulant(stencil_ref[d + steps, 2 * q + a : 2 * q + a + 1, :]))
                        at = pl.ds(q * span + k * nlon, nlon)
                        b_high[at, a * nlon : (a + 1) * nlon] = high
                        b_low[at, a * nlon : (a + 1) * nlon] = low

        data_ref[:size, :wide] = left_ref[...]
        data_ref[:size, wide + cols :] = right_ref[...]
        data_ref[:size, wide : wide + cols], data_ref[size:, wide : wide + cols] = split(p_ref[...])
        for q in range(pairs):
            window = slice((2 * q + 1) * nlon, (2 * q + 1) * nlon + span)
            of = pl.ds(q * span, span)
            both = product(data_ref[:, window], b_high[of, :])
            total = both[:size] + both[size:] + product(data_ref[:size, window], b_low[of, :])
            for a, k, d in ((0, 2 * q, -steps), (1, 2 * q + 2 * steps + 1, steps)):
                far = slice(k * nlon, (k + 1) * nlon)
                weight = jnp.sum(stencil_ref[d + steps, 2 * q + a : 2 * q + a + 1, :], axis=1, keepdims=True)
                far_values = data_ref[:size, far].astype(F32) + data_ref[size:, far].astype(F32)
                value = total[:, a * nlon : (a + 1) * nlon] + weight * far_values
                t_ref[:, (2 * q + a) * nlon : (2 * q + a + 1) * nlon] = value.astype(BF16)
        if held is None:

            @pl.when(i == 0)
            def _():
                outs[1][...] = t_ref[:wide, :]

            @pl.when(i == count - 1)
            def _():
                outs[2][...] = t_ref[size - wide :, :]

    in_specs = [
        pl.BlockSpec(stencil.shape, lambda i, at: (0, 0, 0)),
        pl.BlockSpec((size, cols), lambda i, at: (block_at(i, at), 0)),
        pl.BlockSpec((size, wide), lambda i, at: (i, 0)),
        pl.BlockSpec((size, wide), lambda i, at: (i, 0)),
    ]
    out_specs = [pl.BlockSpec((size, cols), lambda i, at: (block_at(i, at), 0))]
    out_shape = [jax.ShapeDtypeStruct((rows, cols), BF16)]
    operands = [where, stencil, covariance, left, right]
    aliases = {}
    if held is None:
        out_specs += [pl.BlockSpec((wide, cols), lambda i, at: (0, 0))] * 2
        out_shape += [jax.ShapeDtypeStruct((wide, cols), BF16)] * 2
    else:
        in_specs.append(pl.BlockSpec(memory_space=pl.ANY))
        operands.append(held)
        aliases = {5: 0}
    return pl.pallas_call(
        kernel,
        grid_spec=pltpu.PrefetchScalarGridSpec(
            num_scalar_prefetch=1,
            grid=(count,),
            in_specs=in_specs,
            out_specs=out_specs,
            scratch_shapes=[pltpu.VMEM((2 * size, cols + 2 * wide), BF16)]
            + [pltpu.VMEM((pairs * span, size), BF16)] * 2,
        ),
        out_shape=out_shape,
        input_output_aliases=aliases,
        compiler_params=params(),
        cost_estimate=cost(work),
        name="columns_operator",
    )(*operands)


def rows_operator(values, top, bottom, stencil, steps, nlon, out_dtype, noise=None, diagonal=None):
    rows, cols = values.shape
    lat_rows = rows // nlon
    wide = steps * nlon
    size = 2 * nlon
    span = 2 * steps * nlon
    pairs = lat_rows // 2
    ahead = (steps + 1) // 2
    exact = values.dtype == BF16
    chunk = min(cols, 256)

    def kernel(stencil_ref, x_ref, top_ref, bottom_ref, *rest):
        extra, rest = (rest[:2], rest[2:]) if noise is not None else ((), rest)
        out_ref, a_ref, high_ref = rest[:3]
        low_ref = None if exact else rest[3]
        g = pl.program_id(0)

        @pl.when(g == 0)
        def _():
            high_ref[:wide, :] = top_ref[...]
            high_ref[wide + rows :, :] = bottom_ref[...]
            if not exact:
                low_ref[:wide, :] = jnp.zeros((wide, cols), BF16)
                low_ref[wide + rows :, :] = jnp.zeros((wide, cols), BF16)

        @pl.when(g < pairs)
        def _():
            at = pl.ds(pl.multiple_of(wide + g * size, nlon), size)
            if exact:
                high_ref[at, :] = x_ref[...]
            else:
                high_ref[at, :], low_ref[at, :] = split(x_ref[...])

        @pl.when(g >= ahead)
        def _():
            p = g - ahead
            row = lambda d, a: stencil_ref[d + steps, pl.ds(2 * p + a, 1), :]
            for a in range(2):
                for k in range(2 * steps):
                    high, low = split(circulant(row(k - (steps - 1) - a, a)))
                    a_ref[a * nlon : (a + 1) * nlon, k * nlon : (k + 1) * nlon] = high
                    a_ref[size + a * nlon : size + (a + 1) * nlon, k * nlon : (k + 1) * nlon] = low
            unit = lambda k: pl.multiple_of((2 * p + k) * nlon, nlon)
            for lane in range(0, cols, chunk):
                lanes = slice(lane, lane + chunk)
                window = high_ref[pl.ds(unit(1), span), lanes]
                both = product(a_ref[...], window)
                total = both[:size] + both[size:]
                if not exact:
                    total += product(a_ref[:size, :], low_ref[pl.ds(unit(1), span), lanes])
                for a, k, d in ((0, 0, -steps), (1, 2 * steps + 1, steps)):
                    far = high_ref[pl.ds(unit(k), nlon), lanes].astype(F32)
                    if not exact:
                        far += low_ref[pl.ds(unit(k), nlon), lanes].astype(F32)
                    weight = jnp.sum(row(d, a), axis=1, keepdims=True)
                    value = total[a * nlon : (a + 1) * nlon, :] + weight * far
                    out_ref[a * nlon : (a + 1) * nlon, lanes] = value.astype(out_dtype)
            if noise is not None:
                diagonal_ref, noise_ref = extra
                for a in range(2):
                    lat = 2 * p + a - diagonal_ref[0]

                    @pl.when(jnp.logical_and(lat >= 0, lat < cols // nlon))
                    def _(a=a, lat=lat):
                        lanes = pl.ds(pl.multiple_of(lat * nlon, nlon), nlon)
                        eye = lax.broadcasted_iota(jnp.int32, (nlon, nlon), 0) == lax.broadcasted_iota(
                            jnp.int32, (nlon, nlon), 1
                        )
                        added = jnp.where(eye, noise_ref[pl.ds(2 * p + a, 1), :], 0.0)
                        out_ref[a * nlon : (a + 1) * nlon, lanes] += added

    in_specs = [
        pl.BlockSpec(stencil.shape, lambda g: (0, 0, 0)),
        pl.BlockSpec((size, cols), lambda g: (jnp.minimum(g, pairs - 1), 0)),
        pl.BlockSpec((wide, cols), lambda g: (0, 0)),
        pl.BlockSpec((wide, cols), lambda g: (0, 0)),
    ]
    operands = [stencil, values, top, bottom]
    if noise is not None:
        in_specs += [pl.BlockSpec(memory_space=pltpu.SMEM), pl.BlockSpec(noise.shape, lambda g: (0, 0))]
        operands += [diagonal, noise]
    return pl.pallas_call(
        kernel,
        grid=(pairs + ahead,),
        in_specs=in_specs,
        out_specs=pl.BlockSpec((size, cols), lambda g: (jnp.maximum(g - ahead, 0), 0)),
        out_shape=jax.ShapeDtypeStruct((rows, cols), out_dtype),
        scratch_shapes=[pltpu.VMEM((2 * size, span), BF16)]
        + [pltpu.VMEM((rows + 2 * wide, cols), BF16)] * (1 if exact else 2),
        compiler_params=params(),
        cost_estimate=cost(1),
        name="rows_operator",
    )(*operands)


def shifted(block, axis, by):
    size = lax.axis_size(axis)
    pairs = [(i, i + by) for i in range(size) if 0 <= i + by < size]
    return lax.ppermute(block, axis, pairs)


def gathered(first, last, axis, dim, unit, halo, own):
    before, after = [], []
    need, hop = halo, 1
    while need > 0:
        take = min(own, need)
        size = first.shape[dim]
        before.insert(0, shifted(lax.slice_in_dim(last, size - take * unit, size, axis=dim), axis, hop))
        after.append(shifted(lax.slice_in_dim(first, 0, take * unit, axis=dim), axis, -hop))
        need, hop = need - take, hop + 1
    join = lambda parts: parts[0] if len(parts) == 1 else jnp.concatenate(parts, axis=dim)
    return join(before), join(after)


def mirror_pairs(n_row, n_col, side):
    pairs = []
    for a in range(n_row):
        for b in range(n_col):
            to = 2 * a + (1 - b % 2) + side
            if 0 <= to < n_col:
                pairs.append((a * n_col + b, (b // 2) * n_col + to))
    return pairs


def device_stencils(wind_table, diffusivity, wind_index, lat_rows, lats, nlon):
    steps = wind_index.shape[0]
    weights = looked_up(wind_table, diffusivity, wind_index)
    padded = jnp.pad(weights, ((0, 0), (0, 0), (steps, steps)))
    turned = padded[jnp.array([0, 2, 1, 3, 4])]

    def local(of, axis, count):
        part = lax.dynamic_slice_in_dim(of, lax.axis_index(axis) * count, count + 2 * steps, 2)
        part = part.reshape(5 * steps, count + 2 * steps, 1)
        return jnp.broadcast_to(part, part.shape[:2] + (nlon,))

    return stencil_rows(local(padded, "row", lat_rows), local(turned, "col", lats), steps, lat_rows, lats, nlon)


def body(covariance, noise_var, wind_table, diffusivity, wind_index):
    rows_dev, cols_dev = covariance.shape
    lat_rows, nlon = noise_var.shape
    steps, nlat = wind_index.shape
    lats = cols_dev // nlon
    n_row, n_col = lax.axis_size("row"), lax.axis_size("col")
    row_id, col_id = lax.axis_index("row"), lax.axis_index("col")
    own = lat_rows // 4
    mirrored = lat_rows == 2 * lats and own % 2 == 0 and own >= steps and own <= lats - steps

    if not mirrored:
        return plain_body(covariance, noise_var, wind_table, diffusivity, wind_index)

    near = lat_rows // 2 - own
    middle = lat_rows // 2
    parity = col_id % 2
    by_parity = lambda even, odd: jnp.where(parity == 0, even, odd).astype(jnp.int32)
    mirror_at = by_parity(middle - own, middle).reshape(1)
    direct_at = by_parity(middle, middle - own).reshape(1)
    base = (1 - parity) * lats
    sources = jnp.stack([mirror_at[0], base + lats - steps, base, by_parity(lats - own, 0)]).astype(jnp.int32)
    first, last, first_inner, last_inner, left_m, right_m, top, bottom = pack(
        covariance, sources, near, own, steps, nlon
    )
    left = shifted(last, "col", 1)
    right = shifted(first, "col", -1)
    p_top = shifted(bottom, "row", 1)
    p_bottom = shifted(top, "row", -1)
    left_m, right_m, p_top, wind_index = lax.optimization_barrier((left_m, right_m, p_top, wind_index))
    left_m = lax.ppermute(left_m, ("row", "col"), mirror_pairs(n_row, n_col, 1))
    right_m = lax.ppermute(right_m, ("row", "col"), mirror_pairs(n_row, n_col, -1))

    row_s, col_s = device_stencils(wind_table, diffusivity, wind_index, lat_rows, lats, nlon)

    operator_times_prior = rows_operator(covariance, p_top, p_bottom, row_s, steps, nlon, BF16)
    operator_times_prior, left, right, first_inner, last_inner = lax.optimization_barrier(
        (operator_times_prior, left, right, first_inner, last_inner)
    )
    left_inner = shifted(last_inner, "col", 1)
    right_inner = shifted(first_inner, "col", -1)
    mirror, t_first, t_last = columns_operator(
        covariance, left, right, col_s, mirror_at, near, steps, nlon, 2, lambda i, at: i * (lat_rows // near - 1)
    )
    t_top = shifted(t_last, "row", 1)
    t_first, left_m = lax.optimization_barrier((t_first, left_m))
    t_bottom = shifted(t_first, "row", -1)
    inner_at = lambda i, at: at[0] // own + i
    (mirror,) = columns_operator(
        covariance, left_m, right_m, col_s, mirror_at, own, steps, nlon, 1, inner_at, mirror
    )
    (mirror,) = columns_operator(
        covariance, left_inner, right_inner, col_s, direct_at, own, steps, nlon, 1, inner_at, mirror, 10 ** 13
    )
    diagonal = (col_id * lats - row_id * lat_rows).astype(jnp.int32).reshape(1)
    predicted_spread_matrix = rows_operator(
        mirror, t_top, t_bottom, row_s, steps, nlon, F32, noise_var, diagonal
    )
    return (predicted_spread_matrix, operator_times_prior)


def plain_body(covariance, noise_var, wind_table, diffusivity, wind_index):
    rows_dev, cols_dev = covariance.shape
    lat_rows, nlon = noise_var.shape
    steps, nlat = wind_index.shape
    lats = cols_dev // nlon
    row_id, col_id = lax.axis_index("row"), lax.axis_index("col")
    sent = covariance.astype(BF16)
    left, right = gathered(sent, sent, "col", 1, nlon, steps, lats)
    p_top, p_bottom = gathered(sent, sent, "row", 0, nlon, steps, lat_rows)
    row_s, col_s = device_stencils(wind_table, diffusivity, wind_index, lat_rows, lats, nlon)
    operator_times_prior = rows_operator(covariance, p_top, p_bottom, row_s, steps, nlon, BF16)
    unused = jnp.zeros((1,), jnp.int32)
    held = jnp.zeros((rows_dev, cols_dev), BF16)
    (mirror,) = columns_operator(
        covariance, left, right, col_s, unused, 2, steps, nlon, lat_rows // 2, lambda i, at: i, held
    )
    t_top, t_bottom = gathered(mirror, mirror, "row", 0, nlon, steps, lat_rows)
    diagonal = (col_id * lats - row_id * lat_rows).astype(jnp.int32).reshape(1)
    predicted_spread_matrix = rows_operator(
        mirror, t_top, t_bottom, row_s, steps, nlon, F32, noise_var, diagonal
    )
    return (predicted_spread_matrix, operator_times_prior)


def solution(mesh):
    in_specs = (P("row", "col"), P("row", None), P(), P(), P())
    out_specs = (P("row", "col"), P("row", "col"))
    return jax.shard_map(body, mesh=mesh, in_specs=in_specs, out_specs=out_specs, check_vma=False)
```

```python
import functools

import jax
import jax.numpy as jnp
from jax import lax
from jax.experimental import pallas as pl
from jax.experimental.pallas import tpu as pltpu
from jax.sharding import PartitionSpec as P

F32 = jnp.float32
BF16 = jnp.bfloat16
VMEM_LIMIT = 63 * 1024 * 1024


def params():
    return pltpu.CompilerParams(vmem_limit_bytes=VMEM_LIMIT)


def cost(work):
    return pl.CostEstimate(flops=work, bytes_accessed=work, transcendentals=0)


def stencil_terms(zonal_cour, merid_cour, diffuse):
    middle_weight = 1.0 - zonal_cour * zonal_cour - merid_cour * merid_cour - 4.0 * diffuse
    eastward_weight = 0.5 * zonal_cour * zonal_cour - 0.5 * zonal_cour + diffuse
    west_w = 0.5 * zonal_cour * zonal_cour + 0.5 * zonal_cour + diffuse
    north_w = 0.5 * merid_cour * merid_cour - 0.5 * merid_cour + diffuse
    south_w = 0.5 * merid_cour * merid_cour + 0.5 * merid_cour + diffuse
    return middle_weight, eastward_weight, west_w, north_w, south_w


def split(values):
    high = values.astype(BF16)
    return high, (values - high.astype(F32)).astype(BF16)


def circulant(row):
    size, group = row.shape[1], 8
    first = pltpu.roll(jnp.broadcast_to(row, (group, size)), 0, 1, stride=1, stride_axis=0)
    return jnp.concatenate([first] + [pltpu.roll(first, at, 1) for at in range(group, size, group)], axis=0)


def product(left, right):
    return jnp.dot(left, right, preferred_element_type=F32)


def composed(terms, lats, nlon):
    steps = len(terms)
    padded = lats + 2 * steps
    lane = lax.broadcasted_iota(jnp.int32, (padded, nlon), 1)
    rows = {0: (lane == 0).astype(F32)}
    for step_no in range(steps):
        low, high = step_no + 1, padded - step_no - 1
        c, e, w, n, s = [term[low:high] for term in terms[step_no]]
        size = high - low
        fresh = {}
        for d in range(-step_no - 1, step_no + 2):
            parts = []
            if d in rows:
                here = rows[d][1 : 1 + size]
                parts += [c * here, e * pltpu.roll(here, 1, 1), w * pltpu.roll(here, nlon - 1, 1)]
            if d - 1 in rows:
                parts.append(n * rows[d - 1][2 : 2 + size])
            if d + 1 in rows:
                parts.append(s * rows[d + 1][0:size])
            fresh[d] = functools.reduce(lambda x, y: x + y, parts)
        rows = fresh
    return rows


def stencil_rows(wind_table, diffusivity, wind_index, row_lat, col_lat, lat_rows, lats, nlon):
    steps = wind_index.shape[0]
    table = wind_table.shape[0]
    padded = jnp.pad(wind_index, ((0, 0), (steps, steps)), constant_values=-1)

    def local(first, count):
        part = lax.dynamic_slice_in_dim(padded, first, count + 2 * steps, 1)
        return jnp.broadcast_to(part[:, :, None], part.shape + (nlon,))

    def kernel(table_ref, diffuse_ref, row_ref, col_ref, row_out, col_out):
        for ref, out, size, turned in ((row_ref, row_out, lat_rows, False), (col_ref, col_out, lats, True)):
            terms = []
            for step_no in range(steps):
                index = ref[step_no]
                zonal = merid = diffuse = jnp.zeros(index.shape, F32)
                for entry in range(table):
                    here = index == entry
                    zonal = jnp.where(here, table_ref[2 * entry], zonal)
                    merid = jnp.where(here, table_ref[2 * entry + 1], merid)
                    diffuse = jnp.where(here, diffuse_ref[entry], diffuse)
                c, e, w, n, s = [
                    jnp.where(index >= 0, term, 0.0) for term in stencil_terms(zonal, merid, diffuse)
                ]
                terms.append((c, w, e, n, s) if turned else (c, e, w, n, s))
            for d, value in composed(terms, size, nlon).items():
                out[d + steps] = value

    return pl.pallas_call(
        kernel,
        in_specs=[pl.BlockSpec(memory_space=pltpu.SMEM)] * 2 + [pl.BlockSpec(memory_space=pltpu.VMEM)] * 2,
        out_shape=[
            jax.ShapeDtypeStruct((2 * steps + 1, size, nlon), F32) for size in (lat_rows, lats)
        ],
        compiler_params=params(),
        cost_estimate=cost(1),
        name="stencil_rows",
    )(wind_table.reshape(-1), diffusivity, local(row_lat, lat_rows), local(col_lat, lats))


def packed(covariance, where, pieces):
    outs = 1 + max(piece[4] for piece in pieces)

    def placed(piece):
        _, size, _, width, _, _, turn = piece
        return (width, size) if turn else (size, width)

    out_shapes = [None] * outs
    for piece in pieces:
        shape = placed(piece)
        out_shapes[piece[4]] = (max(piece[5] + shape[0], (out_shapes[piece[4]] or (0,))[0]), shape[1])

    def kernel(where_ref, p_ref, *refs):
        count = len(pieces)
        results, got, made = refs[:outs], refs[outs : outs + count], refs[outs + count : outs + 2 * count]
        in_sem, out_sem = refs[outs + 2 * count :]
        start = lambda at: pl.multiple_of(where_ref[at[0]], 128) if isinstance(at, tuple) else at
        loads = []
        for k, (row, size, col, width, _, _, _) in enumerate(pieces):
            source = p_ref.at[pl.ds(start(row), size), pl.ds(start(col), width)]
            loads.append(pltpu.make_async_copy(source, got[k], in_sem.at[k]))
            loads[-1].start()
        stores = []
        for k, piece in enumerate(pieces):
            loads[k].wait()
            turn, shape = piece[6], placed(piece)
            if turn:
                for a in range(0, shape[0], turn):
                    for b in range(0, shape[1], turn):
                        made[k][a : a + turn, b : b + turn] = got[k][b : b + turn, a : a + turn].T.astype(BF16)
            else:
                made[k][...] = got[k][...].astype(BF16)
            target = results[piece[4]].at[pl.ds(piece[5], shape[0]), :]
            stores.append(pltpu.make_async_copy(made[k], target, out_sem.at[k]))
            stores[-1].start()
        for copy in stores:
            copy.wait()

    return pl.pallas_call(
        kernel,
        in_specs=[pl.BlockSpec(memory_space=pltpu.SMEM), pl.BlockSpec(memory_space=pl.ANY)],
        out_specs=[pl.BlockSpec(memory_space=pl.ANY)] * outs,
        out_shape=[jax.ShapeDtypeStruct(shape, BF16) for shape in out_shapes],
        scratch_shapes=[pltpu.VMEM(piece[1:4:2], F32) for piece in pieces]
        + [pltpu.VMEM(placed(piece), BF16) for piece in pieces]
        + [pltpu.SemaphoreType.DMA((len(pieces),)), pltpu.SemaphoreType.DMA((len(pieces),))],
        compiler_params=params(),
        cost_estimate=cost(1),
        name="packed",
    )(where, covariance)


def columns_operator(
    covariance, left, right, stencil, where, unit, steps, nlon, count, block_at, held=None, work=1
):
    rows, cols = covariance.shape
    lats = cols // nlon
    wide = steps * nlon
    size = unit * nlon
    span = 2 * steps * nlon
    pairs = lats // 2

    def kernel(where_ref, stencil_ref, p_ref, left_ref, right_ref, *rest):
        outs, (data_ref, b_high, b_low) = rest[:-3], rest[-3:]
        if held is not None:
            outs = outs[1:]
        t_ref = outs[0]
        i = pl.program_id(0)

        @pl.when(i == 0)
        def _():
            data_ref[size:, :wide] = jnp.zeros((size, wide), BF16)
            data_ref[size:, wide + cols :] = jnp.zeros((size, wide), BF16)
            for q in range(pairs):
                for a in range(2):
                    for k in range(2 * steps):
                        d = k - (steps - 1) - a
                        high, low = split(circulant(stencil_ref[d + steps, 2 * q + a : 2 * q + a + 1, :]))
                        at = pl.ds(q * span + k * nlon, nlon)
                        b_high[at, a * nlon : (a + 1) * nlon] = high
                        b_low[at, a * nlon : (a + 1) * nlon] = low

        data_ref[:size, :wide] = left_ref[...]
        data_ref[:size, wide + cols :] = right_ref[...]
        data_ref[:size, wide : wide + cols], data_ref[size:, wide : wide + cols] = split(p_ref[...])
        for q in range(pairs):
            window = slice((2 * q + 1) * nlon, (2 * q + 1) * nlon + span)
            of = pl.ds(q * span, span)
            both = product(data_ref[:, window], b_high[of, :])
            total = both[:size] + both[size:] + product(data_ref[:size, window], b_low[of, :])
            for a, k, d in ((0, 2 * q, -steps), (1, 2 * q + 2 * steps + 1, steps)):
                far = slice(k * nlon, (k + 1) * nlon)
                weight = jnp.sum(stencil_ref[d + steps, 2 * q + a : 2 * q + a + 1, :], axis=1, keepdims=True)
                far_values = data_ref[:size, far].astype(F32) + data_ref[size:, far].astype(F32)
                value = total[:, a * nlon : (a + 1) * nlon] + weight * far_values
                t_ref[:, (2 * q + a) * nlon : (2 * q + a + 1) * nlon] = value.astype(BF16)
        if held is None:

            @pl.when(i == 0)
            def _():
                outs[1][...] = t_ref[:wide, :]

            @pl.when(i == count - 1)
            def _():
                outs[2][...] = t_ref[size - wide :, :]

    in_specs = [
        pl.BlockSpec(stencil.shape, lambda i, at: (0, 0, 0)),
        pl.BlockSpec((size, cols), lambda i, at: (block_at(i, at), 0)),
        pl.BlockSpec((size, wide), lambda i, at: (i, 0)),
        pl.BlockSpec((size, wide), lambda i, at: (i, 0)),
    ]
    out_specs = [pl.BlockSpec((size, cols), lambda i, at: (block_at(i, at), 0))]
    out_shape = [jax.ShapeDtypeStruct((rows, cols), BF16)]
    operands = [where, stencil, covariance, left, right]
    aliases = {}
    if held is None:
        out_specs += [pl.BlockSpec((wide, cols), lambda i, at: (0, 0))] * 2
        out_shape += [jax.ShapeDtypeStruct((wide, cols), BF16)] * 2
    else:
        in_specs.append(pl.BlockSpec(memory_space=pl.ANY))
        operands.append(held)
        aliases = {5: 0}
    return pl.pallas_call(
        kernel,
        grid_spec=pltpu.PrefetchScalarGridSpec(
            num_scalar_prefetch=1,
            grid=(count,),
            in_specs=in_specs,
            out_specs=out_specs,
            scratch_shapes=[pltpu.VMEM((2 * size, cols + 2 * wide), BF16)]
            + [pltpu.VMEM((pairs * span, size), BF16)] * 2,
        ),
        out_shape=out_shape,
        input_output_aliases=aliases,
        compiler_params=params(),
        cost_estimate=cost(work),
        name="columns_operator",
    )(*operands)


def rows_operator(values, top, bottom, stencil, steps, nlon, out_dtype, noise=None, diagonal=None):
    rows, cols = values.shape
    lat_rows = rows // nlon
    wide = steps * nlon
    size = 2 * nlon
    span = 2 * steps * nlon
    pairs = lat_rows // 2
    ahead = min((steps + 1) // 2, pairs - 1)
    exact = values.dtype == BF16
    chunk = min(cols, 256)

    def kernel(stencil_ref, x_ref, top_ref, bottom_ref, *rest):
        extra, rest = (rest[:2], rest[2:]) if noise is not None else ((), rest)
        out_ref, a_ref, high_ref, sem = rest[:4]
        raw_ref, low_ref = (None, None) if exact else rest[4:]
        p = pl.program_id(0)

        def load(q):
            here = pl.ds(pl.multiple_of(q * size, size), size)
            there = pl.ds(pl.multiple_of(wide + q * size, nlon), size)
            target = high_ref.at[there, :] if exact else raw_ref.at[here, :]
            return pltpu.make_async_copy(x_ref.at[here, :], target, sem.at[q])

        def ready(q):
            load(q).wait()
            if not exact:
                there = pl.ds(pl.multiple_of(wide + q * size, nlon), size)
                here = pl.ds(pl.multiple_of(q * size, size), size)
                high_ref[there, :], low_ref[there, :] = split(raw_ref[here, :])

        @pl.when(p == 0)
        def _():
            halos = [
                pltpu.make_async_copy(top_ref, high_ref.at[:wide, :], sem.at[pairs]),
                pltpu.make_async_copy(bottom_ref, high_ref.at[wide + rows :, :], sem.at[pairs + 1]),
            ]
            for halo in halos:
                halo.start()
            for q in range(pairs):
                load(q).start()
            if not exact:
                low_ref[:wide, :] = jnp.zeros((wide, cols), BF16)
                low_ref[wide + rows :, :] = jnp.zeros((wide, cols), BF16)
            for halo in halos:
                halo.wait()
            for q in range(ahead):
                ready(q)

        @pl.when(p + ahead < pairs)
        def _():
            ready(p + ahead)

        row = lambda d, a: stencil_ref[d + steps, pl.ds(2 * p + a, 1), :]
        for a in range(2):
            for k in range(2 * steps):
                high, low = split(circulant(row(k - (steps - 1) - a, a)))
                a_ref[a * nlon : (a + 1) * nlon, k * nlon : (k + 1) * nlon] = high
                a_ref[size + a * nlon : size + (a + 1) * nlon, k * nlon : (k + 1) * nlon] = low
        unit = lambda k: pl.multiple_of((2 * p + k) * nlon, nlon)
        for lane in range(0, cols, chunk):
            lanes = slice(lane, lane + chunk)
            window = high_ref[pl.ds(unit(1), span), lanes]
            both = product(a_ref[...], window)
            total = both[:size] + both[size:]
            if not exact:
                total += product(a_ref[:size, :], low_ref[pl.ds(unit(1), span), lanes])
            for a, k, d in ((0, 0, -steps), (1, 2 * steps + 1, steps)):
                far = high_ref[pl.ds(unit(k), nlon), lanes].astype(F32)
                if not exact:
                    far += low_ref[pl.ds(unit(k), nlon), lanes].astype(F32)
                weight = jnp.sum(row(d, a), axis=1, keepdims=True)
                value = total[a * nlon : (a + 1) * nlon, :] + weight * far
                out_ref[a * nlon : (a + 1) * nlon, lanes] = value.astype(out_dtype)
        if noise is not None:
            diagonal_ref, noise_ref = extra
            for a in range(2):
                lat = 2 * p + a - diagonal_ref[0]

                @pl.when(jnp.logical_and(lat >= 0, lat < cols // nlon))
                def _(a=a, lat=lat):
                    lanes = pl.ds(pl.multiple_of(lat * nlon, nlon), nlon)
                    eye = lax.broadcasted_iota(jnp.int32, (nlon, nlon), 0) == lax.broadcasted_iota(
                        jnp.int32, (nlon, nlon), 1
                    )
                    added = jnp.where(eye, noise_ref[pl.ds(2 * p + a, 1), :], 0.0)
                    out_ref[a * nlon : (a + 1) * nlon, lanes] += added

    in_specs = [
        pl.BlockSpec(stencil.shape, lambda g: (0, 0, 0)),
        pl.BlockSpec(memory_space=pl.ANY),
        pl.BlockSpec(memory_space=pl.ANY),
        pl.BlockSpec(memory_space=pl.ANY),
    ]
    operands = [stencil, values, top, bottom]
    if noise is not None:
        in_specs += [pl.BlockSpec(memory_space=pltpu.SMEM), pl.BlockSpec(noise.shape, lambda g: (0, 0))]
        operands += [diagonal, noise]
    return pl.pallas_call(
        kernel,
        grid=(pairs,),
        in_specs=in_specs,
        out_specs=pl.BlockSpec((size, cols), lambda g: (g, 0)),
        out_shape=jax.ShapeDtypeStruct((rows, cols), out_dtype),
        scratch_shapes=[pltpu.VMEM((2 * size, span), BF16)]
        + [pltpu.VMEM((rows + 2 * wide, cols), BF16), pltpu.SemaphoreType.DMA((pairs + 2,))]
        + ([] if exact else [pltpu.VMEM((rows, cols), F32), pltpu.VMEM((rows + 2 * wide, cols), BF16)]),
        compiler_params=params(),
        cost_estimate=cost(1),
        name="rows_operator",
    )(*operands)


def shifted(block, axis, by):
    size = lax.axis_size(axis)
    pairs = [(i, i + by) for i in range(size) if 0 <= i + by < size]
    return lax.ppermute(block, axis, pairs)


def gathered(first, last, axis, dim, unit, halo, own):
    before, after = [], []
    need, hop = halo, 1
    while need > 0:
        take = min(own, need)
        size = first.shape[dim]
        before.insert(0, shifted(lax.slice_in_dim(last, size - take * unit, size, axis=dim), axis, hop))
        after.append(shifted(lax.slice_in_dim(first, 0, take * unit, axis=dim), axis, -hop))
        need, hop = need - take, hop + 1
    join = lambda parts: parts[0] if len(parts) == 1 else jnp.concatenate(parts, axis=dim)
    return join(before), join(after)


def mirror_pairs(n_row, n_col, side):
    pairs = []
    for a in range(n_row):
        for b in range(n_col):
            to = 2 * a + (1 - b % 2) + side
            if 0 <= to < n_col:
                pairs.append((a * n_col + b, (b // 2) * n_col + to))
    return pairs


def body(covariance, noise_var, wind_table, diffusivity, wind_index):
    rows_dev, cols_dev = covariance.shape
    lat_rows, nlon = noise_var.shape
    steps, nlat = wind_index.shape
    lats = cols_dev // nlon
    n_row, n_col = lax.axis_size("row"), lax.axis_size("col")
    row_id, col_id = lax.axis_index("row"), lax.axis_index("col")
    own = lat_rows // 4
    mirrored = lat_rows == 2 * lats and own % 2 == 0 and own >= steps and own <= lats - steps

    if not mirrored:
        return plain_body(covariance, noise_var, wind_table, diffusivity, wind_index)

    near = lat_rows // 2 - own
    middle = lat_rows // 2
    parity = col_id % 2
    by_parity = lambda even, odd: jnp.where(parity == 0, even, odd).astype(jnp.int32)
    mirror_at = by_parity(middle - own, middle).reshape(1)
    direct_at = by_parity(middle, middle - own).reshape(1)
    base = (1 - parity) * lats
    sources = nlon * jnp.stack([mirror_at[0], base + lats - steps, base, by_parity(lats - own, 0)]).astype(jnp.int32)
    outer, inner, wide = near * nlon, own * nlon, steps * nlon
    ends = (0, cols_dev - wide)
    pieces = [
        (row, outer, lane, wide, k, there, 0)
        for row, there in ((0, 0), (rows_dev - outer, outer))
        for k, lane in enumerate(ends)
    ]
    pieces += [(row, wide, 0, cols_dev, k + 2, 0, 0) for k, row in enumerate((0, rows_dev - wide))]
    pieces += [((k + 1,), wide, (3,), inner, k + 4, 0, nlon) for k in range(2)]
    pieces += [((0,), inner, lane, wide, k + 6, 0, 0) for k, lane in enumerate(ends)]
    first, last, top, bottom, left_m, right_m, first_inner, last_inner = packed(covariance, sources, pieces)
    left = shifted(last, "col", 1)
    right = shifted(first, "col", -1)
    p_top = shifted(bottom, "row", 1)
    p_bottom = shifted(top, "row", -1)
    left_m, right_m, first_inner, wind_index, p_top = lax.optimization_barrier(
        (left_m, right_m, first_inner, wind_index, p_top)
    )
    left_m = lax.ppermute(left_m, ("row", "col"), mirror_pairs(n_row, n_col, 1))
    right_m = lax.ppermute(right_m, ("row", "col"), mirror_pairs(n_row, n_col, -1))
    right_inner = shifted(first_inner, "col", -1)

    row_s, col_s = stencil_rows(
        wind_table, diffusivity, wind_index, row_id * lat_rows, col_id * lats, lat_rows, lats, nlon
    )

    operator_times_prior = rows_operator(covariance, p_top, p_bottom, row_s, steps, nlon, BF16)
    operator_times_prior, left, right, last_inner = lax.optimization_barrier(
        (operator_times_prior, left, right, last_inner)
    )
    left_inner = shifted(last_inner, "col", 1)
    mirror, t_first, t_last = columns_operator(
        covariance, left, right, col_s, mirror_at, near, steps, nlon, 2, lambda i, at: i * (lat_rows // near - 1)
    )
    t_top = shifted(t_last, "row", 1)
    t_first, left_m = lax.optimization_barrier((t_first, left_m))
    t_bottom = shifted(t_first, "row", -1)
    inner_at = lambda i, at: at[0] // own + i
    (mirror,) = columns_operator(
        covariance, left_m, right_m, col_s, mirror_at, own, steps, nlon, 1, inner_at, mirror
    )
    (mirror,) = columns_operator(
        covariance, left_inner, right_inner, col_s, direct_at, own, steps, nlon, 1, inner_at, mirror, 10 ** 13
    )
    diagonal = (col_id * lats - row_id * lat_rows).astype(jnp.int32).reshape(1)
    predicted_spread_matrix = rows_operator(
        mirror, t_top, t_bottom, row_s, steps, nlon, F32, noise_var, diagonal
    )
    return (predicted_spread_matrix, operator_times_prior)


def plain_body(covariance, noise_var, wind_table, diffusivity, wind_index):
    rows_dev, cols_dev = covariance.shape
    lat_rows, nlon = noise_var.shape
    steps, nlat = wind_index.shape
    lats = cols_dev // nlon
    row_id, col_id = lax.axis_index("row"), lax.axis_index("col")
    sent = covariance.astype(BF16)
    left, right = gathered(sent, sent, "col", 1, nlon, steps, lats)
    p_top, p_bottom = gathered(sent, sent, "row", 0, nlon, steps, lat_rows)
    row_s, col_s = stencil_rows(
        wind_table, diffusivity, wind_index, row_id * lat_rows, col_id * lats, lat_rows, lats, nlon
    )
    operator_times_prior = rows_operator(covariance, p_top, p_bottom, row_s, steps, nlon, BF16)
    unused = jnp.zeros((1,), jnp.int32)
    held = jnp.zeros((rows_dev, cols_dev), BF16)
    (mirror,) = columns_operator(
        covariance, left, right, col_s, unused, 2, steps, nlon, lat_rows // 2, lambda i, at: i, held
    )
    t_top, t_bottom = gathered(mirror, mirror, "row", 0, nlon, steps, lat_rows)
    diagonal = (col_id * lats - row_id * lat_rows).astype(jnp.int32).reshape(1)
    predicted_spread_matrix = rows_operator(
        mirror, t_top, t_bottom, row_s, steps, nlon, F32, noise_var, diagonal
    )
    return (predicted_spread_matrix, operator_times_prior)


def solution(mesh):
    in_specs = (P("row", "col"), P("row", None), P(), P(), P())
    out_specs = (P("row", "col"), P("row", "col"))
    return jax.shard_map(body, mesh=mesh, in_specs=in_specs, out_specs=out_specs, check_vma=False)
```

```python
import functools

import jax
import jax.numpy as jnp
from jax import lax
from jax.experimental import pallas as pl
from jax.experimental.pallas import tpu as pltpu
from jax.sharding import PartitionSpec as P

F32 = jnp.float32
BF16 = jnp.bfloat16
VMEM_LIMIT = 63 * 1024 * 1024


def params():
    return pltpu.CompilerParams(vmem_limit_bytes=VMEM_LIMIT)


def cost(work):
    return pl.CostEstimate(flops=work, bytes_accessed=work, transcendentals=0)


def stencil_terms(zonal_cour, merid_cour, diffuse):
    middle_weight = 1.0 - zonal_cour * zonal_cour - merid_cour * merid_cour - 4.0 * diffuse
    eastward_weight = 0.5 * zonal_cour * zonal_cour - 0.5 * zonal_cour + diffuse
    west_w = 0.5 * zonal_cour * zonal_cour + 0.5 * zonal_cour + diffuse
    north_w = 0.5 * merid_cour * merid_cour - 0.5 * merid_cour + diffuse
    south_w = 0.5 * merid_cour * merid_cour + 0.5 * merid_cour + diffuse
    return middle_weight, eastward_weight, west_w, north_w, south_w


def split(values):
    high = values.astype(BF16)
    return high, (values - high.astype(F32)).astype(BF16)


def circulant(row):
    size, group = row.shape[1], 8
    first = pltpu.roll(jnp.broadcast_to(row, (group, size)), 0, 1, stride=1, stride_axis=0)
    return jnp.concatenate([first] + [pltpu.roll(first, at, 1) for at in range(group, size, group)], axis=0)


def product(left, right):
    return jnp.dot(left, right, preferred_element_type=F32)


def composed(terms, lats, nlon):
    steps = len(terms)
    padded = lats + 2 * steps
    lane = lax.broadcasted_iota(jnp.int32, (padded, nlon), 1)
    rows = {0: (lane == 0).astype(F32)}
    for step_no in range(steps):
        low, high = step_no + 1, padded - step_no - 1
        c, e, w, n, s = [term[low:high] for term in terms[step_no]]
        size = high - low
        fresh = {}
        for d in range(-step_no - 1, step_no + 2):
            parts = []
            if d in rows:
                here = rows[d][1 : 1 + size]
                parts += [c * here, e * pltpu.roll(here, 1, 1), w * pltpu.roll(here, nlon - 1, 1)]
            if d - 1 in rows:
                parts.append(n * rows[d - 1][2 : 2 + size])
            if d + 1 in rows:
                parts.append(s * rows[d + 1][0:size])
            fresh[d] = functools.reduce(lambda x, y: x + y, parts)
        rows = fresh
    return rows


def stencil_rows(wind_table, diffusivity, wind_index, row_lat, col_lat, lat_rows, lats, nlon):
    steps = wind_index.shape[0]
    table = wind_table.shape[0]
    padded = jnp.pad(wind_index, ((0, 0), (steps, steps)), constant_values=-1)

    def local(first, count):
        part = lax.dynamic_slice_in_dim(padded, first, count + 2 * steps, 1)
        return jnp.broadcast_to(part[:, :, None], part.shape + (nlon,))

    def kernel(table_ref, diffuse_ref, row_ref, col_ref, row_out, col_out):
        for ref, out, size, turned in ((row_ref, row_out, lat_rows, False), (col_ref, col_out, lats, True)):
            terms = []
            for step_no in range(steps):
                index = ref[step_no]
                zonal = merid = diffuse = jnp.zeros(index.shape, F32)
                for entry in range(table):
                    here = index == entry
                    zonal = jnp.where(here, table_ref[2 * entry], zonal)
                    merid = jnp.where(here, table_ref[2 * entry + 1], merid)
                    diffuse = jnp.where(here, diffuse_ref[entry], diffuse)
                c, e, w, n, s = [
                    jnp.where(index >= 0, term, 0.0) for term in stencil_terms(zonal, merid, diffuse)
                ]
                terms.append((c, w, e, n, s) if turned else (c, e, w, n, s))
            for d, value in composed(terms, size, nlon).items():
                out[d + steps] = value

    return pl.pallas_call(
        kernel,
        in_specs=[pl.BlockSpec(memory_space=pltpu.SMEM)] * 2 + [pl.BlockSpec(memory_space=pltpu.VMEM)] * 2,
        out_shape=[
            jax.ShapeDtypeStruct((2 * steps + 1, size, nlon), F32) for size in (lat_rows, lats)
        ],
        compiler_params=params(),
        cost_estimate=cost(1),
        name="stencil_rows",
    )(wind_table.reshape(-1), diffusivity, local(row_lat, lat_rows), local(col_lat, lats))


def packed(covariance, where, pieces):
    outs = 1 + max(piece[4] for piece in pieces)

    def placed(piece):
        _, size, _, width, _, _, turn = piece
        return (width, size) if turn else (size, width)

    out_shapes = [None] * outs
    for piece in pieces:
        shape = placed(piece)
        out_shapes[piece[4]] = (max(piece[5] + shape[0], (out_shapes[piece[4]] or (0,))[0]), shape[1])

    def kernel(where_ref, p_ref, *refs):
        count = len(pieces)
        results, got, made = refs[:outs], refs[outs : outs + count], refs[outs + count : outs + 2 * count]
        in_sem, out_sem = refs[outs + 2 * count :]
        start = lambda at: pl.multiple_of(where_ref[at[0]], 128) if isinstance(at, tuple) else at
        loads = []
        for k, (row, size, col, width, _, _, _) in enumerate(pieces):
            source = p_ref.at[pl.ds(start(row), size), pl.ds(start(col), width)]
            loads.append(pltpu.make_async_copy(source, got[k], in_sem.at[k]))
            loads[-1].start()
        stores = []
        for k, piece in enumerate(pieces):
            loads[k].wait()
            turn, shape = piece[6], placed(piece)
            if turn:
                for a in range(0, shape[0], turn):
                    for b in range(0, shape[1], turn):
                        made[k][a : a + turn, b : b + turn] = got[k][b : b + turn, a : a + turn].T.astype(BF16)
            else:
                made[k][...] = got[k][...].astype(BF16)
            target = results[piece[4]].at[pl.ds(piece[5], shape[0]), :]
            stores.append(pltpu.make_async_copy(made[k], target, out_sem.at[k]))
            stores[-1].start()
        for copy in stores:
            copy.wait()

    return pl.pallas_call(
        kernel,
        in_specs=[pl.BlockSpec(memory_space=pltpu.SMEM), pl.BlockSpec(memory_space=pl.ANY)],
        out_specs=[pl.BlockSpec(memory_space=pl.ANY)] * outs,
        out_shape=[jax.ShapeDtypeStruct(shape, BF16) for shape in out_shapes],
        scratch_shapes=[pltpu.VMEM(piece[1:4:2], F32) for piece in pieces]
        + [pltpu.VMEM(placed(piece), BF16) for piece in pieces]
        + [pltpu.SemaphoreType.DMA((len(pieces),)), pltpu.SemaphoreType.DMA((len(pieces),))],
        compiler_params=params(),
        cost_estimate=cost(1),
        name="packed",
    )(where, covariance)


def columns_operator(
    covariance, left, right, stencil, where, unit, steps, nlon, count, block_at, held=None, ends=False, work=1
):
    rows, cols = covariance.shape
    lats = cols // nlon
    wide = steps * nlon
    size = unit * nlon
    span = 2 * steps * nlon
    pairs = lats // 2

    def kernel(where_ref, stencil_ref, p_ref, left_ref, right_ref, *rest):
        outs, (data_ref, b_ref) = rest[:-2], rest[-2:]
        if held is not None:
            outs = outs[1:]
        t_ref = outs[0]
        i = pl.program_id(0)

        @pl.when(i == 0)
        def _():
            data_ref[size:, :wide] = jnp.zeros((size, wide), BF16)
            data_ref[size:, wide + cols :] = jnp.zeros((size, wide), BF16)
            for q in range(pairs):
                for a in range(2):
                    for k in range(2 * steps):
                        d = k - (steps - 1) - a
                        high, low = split(circulant(stencil_ref[d + steps, 2 * q + a : 2 * q + a + 1, :]))
                        for part, value in enumerate((high, high, low)):
                            at = pl.ds((3 * q + part) * span + k * nlon, nlon)
                            b_ref[at, a * nlon : (a + 1) * nlon] = value

        data_ref[:size, :wide] = left_ref[...]
        data_ref[:size, wide + cols :] = right_ref[...]
        data_ref[:size, wide : wide + cols], data_ref[size:, wide : wide + cols] = split(p_ref[...])
        for q in range(pairs):
            window = slice((2 * q + 1) * nlon, (2 * q + 1) * nlon + span)
            high, low = data_ref[:size, window], data_ref[size:, window]
            total = product(jnp.concatenate([high, low, high], axis=1), b_ref[pl.ds(3 * q * span, 3 * span), :])
            for a, k, d in ((0, 2 * q, -steps), (1, 2 * q + 2 * steps + 1, steps)):
                far = slice(k * nlon, (k + 1) * nlon)
                weight = jnp.sum(stencil_ref[d + steps, 2 * q + a : 2 * q + a + 1, :], axis=1, keepdims=True)
                far_values = data_ref[:size, far].astype(F32) + data_ref[size:, far].astype(F32)
                value = total[:, a * nlon : (a + 1) * nlon] + weight * far_values
                t_ref[:, (2 * q + a) * nlon : (2 * q + a + 1) * nlon] = value.astype(BF16)
        if ends:

            @pl.when(i == 0)
            def _():
                outs[1][...] = t_ref[:wide, :]

            @pl.when(i == count - 1)
            def _():
                outs[2][...] = t_ref[size - wide :, :]

    in_specs = [
        pl.BlockSpec(stencil.shape, lambda i, at: (0, 0, 0)),
        pl.BlockSpec((size, cols), lambda i, at: (block_at(i, at), 0)),
        pl.BlockSpec((size, wide), lambda i, at: (i, 0)),
        pl.BlockSpec((size, wide), lambda i, at: (i, 0)),
    ]
    out_specs = [pl.BlockSpec((size, cols), lambda i, at: (block_at(i, at), 0))]
    out_shape = [jax.ShapeDtypeStruct((rows, cols), BF16)]
    operands = [where, stencil, covariance, left, right]
    aliases = {}
    if ends:
        out_specs += [pl.BlockSpec((wide, cols), lambda i, at: (0, 0))] * 2
        out_shape += [jax.ShapeDtypeStruct((wide, cols), BF16)] * 2
    if held is not None:
        in_specs.append(pl.BlockSpec(memory_space=pl.ANY))
        operands.append(held)
        aliases = {5: 0}
    return pl.pallas_call(
        kernel,
        grid_spec=pltpu.PrefetchScalarGridSpec(
            num_scalar_prefetch=1,
            grid=(count,),
            in_specs=in_specs,
            out_specs=out_specs,
            scratch_shapes=[pltpu.VMEM((2 * size, cols + 2 * wide), BF16)]
            + [pltpu.VMEM((3 * pairs * span, 2 * nlon), BF16)],
        ),
        out_shape=out_shape,
        input_output_aliases=aliases,
        compiler_params=params(),
        cost_estimate=cost(work),
        name="columns_operator",
    )(*operands)


def rows_operator(values, top, bottom, stencil, steps, nlon, out_dtype, noise=None, diagonal=None):
    rows, cols = values.shape
    lat_rows = rows // nlon
    wide = steps * nlon
    size = 2 * nlon
    span = 2 * steps * nlon
    pairs = lat_rows // 2
    ahead = min((steps + 1) // 2, pairs - 1)
    exact = values.dtype == BF16
    chunk = min(cols, 512)

    def kernel(stencil_ref, x_ref, top_ref, bottom_ref, *rest):
        extra, rest = (rest[:2], rest[2:]) if noise is not None else ((), rest)
        out_ref, a_ref, high_ref, sem = rest[:4]
        raw_ref, low_ref = (None, None) if exact else rest[4:]
        p = pl.program_id(0)

        def load(q):
            here = pl.ds(pl.multiple_of(q * size, size), size)
            there = pl.ds(pl.multiple_of(wide + q * size, nlon), size)
            target = high_ref.at[there, :] if exact else raw_ref.at[here, :]
            return pltpu.make_async_copy(x_ref.at[here, :], target, sem.at[q])

        def ready(q):
            load(q).wait()
            if not exact:
                there = pl.ds(pl.multiple_of(wide + q * size, nlon), size)
                here = pl.ds(pl.multiple_of(q * size, size), size)
                high_ref[there, :], low_ref[there, :] = split(raw_ref[here, :])

        @pl.when(p == 0)
        def _():
            halos = [
                pltpu.make_async_copy(top_ref, high_ref.at[:wide, :], sem.at[pairs]),
                pltpu.make_async_copy(bottom_ref, high_ref.at[wide + rows :, :], sem.at[pairs + 1]),
            ]
            for halo in halos:
                halo.start()
            for q in range(pairs):
                load(q).start()
            if not exact:
                low_ref[:wide, :] = jnp.zeros((wide, cols), BF16)
                low_ref[wide + rows :, :] = jnp.zeros((wide, cols), BF16)
            for halo in halos:
                halo.wait()
            for q in range(ahead):
                ready(q)

        @pl.when(p + ahead < pairs)
        def _():
            ready(p + ahead)

        row = lambda d, a: stencil_ref[d + steps, pl.ds(2 * p + a, 1), :]
        for a in range(2):
            for k in range(2 * steps):
                high, low = split(circulant(row(k - (steps - 1) - a, a)))
                for part, value in enumerate((high, low) if exact else (high, low, high)):
                    lane = part * span + k * nlon
                    a_ref[a * nlon : (a + 1) * nlon, lane : lane + nlon] = value
        unit = lambda k: pl.multiple_of((2 * p + k) * nlon, nlon)
        for lane in range(0, cols, chunk):
            lanes = slice(lane, lane + chunk)
            window = high_ref[pl.ds(unit(1), span), lanes]
            parts = [window, window]
            if not exact:
                parts.append(low_ref[pl.ds(unit(1), span), lanes])
            total = product(a_ref[...], jnp.concatenate(parts, axis=0))
            for a, k, d in ((0, 0, -steps), (1, 2 * steps + 1, steps)):
                far = high_ref[pl.ds(unit(k), nlon), lanes].astype(F32)
                if not exact:
                    far += low_ref[pl.ds(unit(k), nlon), lanes].astype(F32)
                weight = jnp.sum(row(d, a), axis=1, keepdims=True)
                value = total[a * nlon : (a + 1) * nlon, :] + weight * far
                out_ref[a * nlon : (a + 1) * nlon, lanes] = value.astype(out_dtype)
        if noise is not None:
            diagonal_ref, noise_ref = extra
            for a in range(2):
                lat = 2 * p + a - diagonal_ref[0]

                @pl.when(jnp.logical_and(lat >= 0, lat < cols // nlon))
                def _(a=a, lat=lat):
                    lanes = pl.ds(pl.multiple_of(lat * nlon, nlon), nlon)
                    eye = lax.broadcasted_iota(jnp.int32, (nlon, nlon), 0) == lax.broadcasted_iota(
                        jnp.int32, (nlon, nlon), 1
                    )
                    added = jnp.where(eye, noise_ref[pl.ds(2 * p + a, 1), :], 0.0)
                    out_ref[a * nlon : (a + 1) * nlon, lanes] += added

    in_specs = [
        pl.BlockSpec(stencil.shape, lambda g: (0, 0, 0)),
        pl.BlockSpec(memory_space=pl.ANY),
        pl.BlockSpec(memory_space=pl.ANY),
        pl.BlockSpec(memory_space=pl.ANY),
    ]
    operands = [stencil, values, top, bottom]
    if noise is not None:
        in_specs += [pl.BlockSpec(memory_space=pltpu.SMEM), pl.BlockSpec(noise.shape, lambda g: (0, 0))]
        operands += [diagonal, noise]
    return pl.pallas_call(
        kernel,
        grid=(pairs,),
        in_specs=in_specs,
        out_specs=pl.BlockSpec((size, cols), lambda g: (g, 0)),
        out_shape=jax.ShapeDtypeStruct((rows, cols), out_dtype),
        scratch_shapes=[pltpu.VMEM((size, (2 if exact else 3) * span), BF16)]
        + [pltpu.VMEM((rows + 2 * wide, cols), BF16), pltpu.SemaphoreType.DMA((pairs + 2,))]
        + ([] if exact else [pltpu.VMEM((rows, cols), F32), pltpu.VMEM((rows + 2 * wide, cols), BF16)]),
        compiler_params=params(),
        cost_estimate=cost(1),
        name="rows_operator",
    )(*operands)


def shifted(block, axis, by):
    size = lax.axis_size(axis)
    pairs = [(i, i + by) for i in range(size) if 0 <= i + by < size]
    return lax.ppermute(block, axis, pairs)


def gathered(first, last, axis, dim, unit, halo, own):
    before, after = [], []
    need, hop = halo, 1
    while need > 0:
        take = min(own, need)
        size = first.shape[dim]
        before.insert(0, shifted(lax.slice_in_dim(last, size - take * unit, size, axis=dim), axis, hop))
        after.append(shifted(lax.slice_in_dim(first, 0, take * unit, axis=dim), axis, -hop))
        need, hop = need - take, hop + 1
    join = lambda parts: parts[0] if len(parts) == 1 else jnp.concatenate(parts, axis=dim)
    return join(before), join(after)


def mirror_pairs(n_row, n_col, side):
    pairs = []
    for a in range(n_row):
        for b in range(n_col):
            to = 2 * a + (1 - b % 2) + side
            if 0 <= to < n_col:
                pairs.append((a * n_col + b, (b // 2) * n_col + to))
    return pairs


def body(covariance, noise_var, wind_table, diffusivity, wind_index):
    rows_dev, cols_dev = covariance.shape
    lat_rows, nlon = noise_var.shape
    steps, nlat = wind_index.shape
    lats = cols_dev // nlon
    n_row, n_col = lax.axis_size("row"), lax.axis_size("col")
    row_id, col_id = lax.axis_index("row"), lax.axis_index("col")
    own = lat_rows // 4
    mirrored = lat_rows == 2 * lats and own % 2 == 0 and own >= steps and own <= lats - steps

    if not mirrored:
        return plain_body(covariance, noise_var, wind_table, diffusivity, wind_index)

    near = lat_rows // 2 - own
    middle = lat_rows // 2
    parity = col_id % 2
    by_parity = lambda even, odd: jnp.where(parity == 0, even, odd).astype(jnp.int32)
    mirror_at = by_parity(middle - own, middle).reshape(1)
    direct_at = by_parity(middle, middle - own).reshape(1)
    base = (1 - parity) * lats
    sources = nlon * jnp.stack([mirror_at[0], base + lats - steps, base, by_parity(lats - own, 0)]).astype(jnp.int32)
    outer, inner, wide = near * nlon, own * nlon, steps * nlon
    ends = (0, cols_dev - wide)
    pieces = [
        (row, outer, lane, wide, k, there, 0)
        for row, there in ((0, 0), (rows_dev - outer, outer))
        for k, lane in enumerate(ends)
    ]
    pieces += [(row, wide, 0, cols_dev, k + 2, 0, 0) for k, row in enumerate((0, rows_dev - wide))]
    pieces += [((k + 1,), wide, (3,), inner, k + 4, 0, nlon) for k in range(2)]
    pieces += [((0,), inner, lane, wide, k + 6, 0, 0) for k, lane in enumerate(ends)]
    first, last, top, bottom, left_m, right_m, first_inner, last_inner = packed(covariance, sources, pieces)
    left = shifted(last, "col", 1)
    right = shifted(first, "col", -1)
    p_top = shifted(bottom, "row", 1)
    p_bottom = shifted(top, "row", -1)
    left_m, right_m, wind_index, p_top = lax.optimization_barrier((left_m, right_m, wind_index, p_top))
    left_m = lax.ppermute(left_m, ("row", "col"), mirror_pairs(n_row, n_col, 1))
    right_m = lax.ppermute(right_m, ("row", "col"), mirror_pairs(n_row, n_col, -1))

    row_s, col_s = stencil_rows(
        wind_table, diffusivity, wind_index, row_id * lat_rows, col_id * lats, lat_rows, lats, nlon
    )

    operator_times_prior = rows_operator(covariance, p_top, p_bottom, row_s, steps, nlon, BF16)
    operator_times_prior, left_m = lax.optimization_barrier((operator_times_prior, left_m))
    inner_at = lambda i, at: at[0] // own + i
    (mirror,) = columns_operator(
        covariance, left_m, right_m, col_s, mirror_at, own, steps, nlon, 1, inner_at
    )
    mirror, left, right, first_inner, last_inner = lax.optimization_barrier(
        (mirror, left, right, first_inner, last_inner)
    )
    left_inner = shifted(last_inner, "col", 1)
    right_inner = shifted(first_inner, "col", -1)
    mirror, t_first, t_last = columns_operator(
        covariance, left, right, col_s, mirror_at, near, steps, nlon, 2,
        lambda i, at: i * (lat_rows // near - 1), mirror, True,
    )
    t_top = shifted(t_last, "row", 1)
    t_bottom = shifted(t_first, "row", -1)
    (mirror,) = columns_operator(
        covariance, left_inner, right_inner, col_s, direct_at, own, steps, nlon, 1, inner_at, mirror, False,
        10 ** 13,
    )
    diagonal = (col_id * lats - row_id * lat_rows).astype(jnp.int32).reshape(1)
    predicted_spread_matrix = rows_operator(
        mirror, t_top, t_bottom, row_s, steps, nlon, F32, noise_var, diagonal
    )
    return (predicted_spread_matrix, operator_times_prior)


def plain_body(covariance, noise_var, wind_table, diffusivity, wind_index):
    rows_dev, cols_dev = covariance.shape
    lat_rows, nlon = noise_var.shape
    steps, nlat = wind_index.shape
    lats = cols_dev // nlon
    row_id, col_id = lax.axis_index("row"), lax.axis_index("col")
    sent = covariance.astype(BF16)
    left, right = gathered(sent, sent, "col", 1, nlon, steps, lats)
    p_top, p_bottom = gathered(sent, sent, "row", 0, nlon, steps, lat_rows)
    row_s, col_s = stencil_rows(
        wind_table, diffusivity, wind_index, row_id * lat_rows, col_id * lats, lat_rows, lats, nlon
    )
    operator_times_prior = rows_operator(covariance, p_top, p_bottom, row_s, steps, nlon, BF16)
    unused = jnp.zeros((1,), jnp.int32)
    held = jnp.zeros((rows_dev, cols_dev), BF16)
    (mirror,) = columns_operator(
        covariance, left, right, col_s, unused, 2, steps, nlon, lat_rows // 2, lambda i, at: i, held
    )
    t_top, t_bottom = gathered(mirror, mirror, "row", 0, nlon, steps, lat_rows)
    diagonal = (col_id * lats - row_id * lat_rows).astype(jnp.int32).reshape(1)
    predicted_spread_matrix = rows_operator(
        mirror, t_top, t_bottom, row_s, steps, nlon, F32, noise_var, diagonal
    )
    return (predicted_spread_matrix, operator_times_prior)


def solution(mesh):
    in_specs = (P("row", "col"), P("row", None), P(), P(), P())
    out_specs = (P("row", "col"), P("row", "col"))
    return jax.shard_map(body, mesh=mesh, in_specs=in_specs, out_specs=out_specs, check_vma=False)
```

```python
import functools

import jax
import jax.numpy as jnp
from jax import lax
from jax.experimental import pallas as pl
from jax.experimental.pallas import tpu as pltpu
from jax.sharding import PartitionSpec as P

F32 = jnp.float32
BF16 = jnp.bfloat16
VMEM_LIMIT = 63 * 1024 * 1024


def params():
    return pltpu.CompilerParams(vmem_limit_bytes=VMEM_LIMIT)


def cost(work):
    return pl.CostEstimate(flops=work, bytes_accessed=work, transcendentals=0)


def stencil_terms(zonal_cour, merid_cour, diffuse):
    middle_weight = 1.0 - zonal_cour * zonal_cour - merid_cour * merid_cour - 4.0 * diffuse
    eastward_weight = 0.5 * zonal_cour * zonal_cour - 0.5 * zonal_cour + diffuse
    west_w = 0.5 * zonal_cour * zonal_cour + 0.5 * zonal_cour + diffuse
    north_w = 0.5 * merid_cour * merid_cour - 0.5 * merid_cour + diffuse
    south_w = 0.5 * merid_cour * merid_cour + 0.5 * merid_cour + diffuse
    return middle_weight, eastward_weight, west_w, north_w, south_w


def split(values):
    high = values.astype(BF16)
    return high, (values - high.astype(F32)).astype(BF16)


def circulant(row):
    size, group = row.shape[1], 8
    first = pltpu.roll(jnp.broadcast_to(row, (group, size)), 0, 1, stride=1, stride_axis=0)
    return jnp.concatenate([first] + [pltpu.roll(first, at, 1) for at in range(group, size, group)], axis=0)


def product(left, right):
    return jnp.dot(left, right, preferred_element_type=F32)


def composed(terms, lats, nlon):
    steps = len(terms)
    padded = lats + 2 * steps
    lane = lax.broadcasted_iota(jnp.int32, (padded, nlon), 1)
    rows = {0: (lane == 0).astype(F32)}
    for step_no in range(steps):
        low, high = step_no + 1, padded - step_no - 1
        c, e, w, n, s = [term[low:high] for term in terms[step_no]]
        size = high - low
        fresh = {}
        for d in range(-step_no - 1, step_no + 2):
            parts = []
            if d in rows:
                here = rows[d][1 : 1 + size]
                parts += [c * here, e * pltpu.roll(here, 1, 1), w * pltpu.roll(here, nlon - 1, 1)]
            if d - 1 in rows:
                parts.append(n * rows[d - 1][2 : 2 + size])
            if d + 1 in rows:
                parts.append(s * rows[d + 1][0:size])
            fresh[d] = functools.reduce(lambda x, y: x + y, parts)
        rows = fresh
    return rows


def stencil_rows(wind_table, diffusivity, wind_index, row_lat, col_lat, lat_rows, lats, nlon):
    steps = wind_index.shape[0]
    table = wind_table.shape[0]
    padded = jnp.pad(wind_index, ((0, 0), (steps, steps)), constant_values=-1)

    def local(first, count):
        part = lax.dynamic_slice_in_dim(padded, first, count + 2 * steps, 1)
        return jnp.broadcast_to(part[:, :, None], part.shape + (nlon,))

    def kernel(table_ref, diffuse_ref, row_ref, col_ref, row_out, col_out):
        for ref, out, size, turned in ((row_ref, row_out, lat_rows, False), (col_ref, col_out, lats, True)):
            terms = []
            for step_no in range(steps):
                index = ref[step_no]
                zonal = merid = diffuse = jnp.zeros(index.shape, F32)
                for entry in range(table):
                    here = index == entry
                    zonal = jnp.where(here, table_ref[2 * entry], zonal)
                    merid = jnp.where(here, table_ref[2 * entry + 1], merid)
                    diffuse = jnp.where(here, diffuse_ref[entry], diffuse)
                c, e, w, n, s = [
                    jnp.where(index >= 0, term, 0.0) for term in stencil_terms(zonal, merid, diffuse)
                ]
                terms.append((c, w, e, n, s) if turned else (c, e, w, n, s))
            for d, value in composed(terms, size, nlon).items():
                out[d + steps] = value

    return pl.pallas_call(
        kernel,
        in_specs=[pl.BlockSpec(memory_space=pltpu.SMEM)] * 2 + [pl.BlockSpec(memory_space=pltpu.VMEM)] * 2,
        out_shape=[
            jax.ShapeDtypeStruct((2 * steps + 1, size, nlon), F32) for size in (lat_rows, lats)
        ],
        compiler_params=params(),
        cost_estimate=cost(1),
        name="stencil_rows",
    )(wind_table.reshape(-1), diffusivity, local(row_lat, lat_rows), local(col_lat, lats))


def packed(covariance, where, pieces):
    outs = 1 + max(piece[4] for piece in pieces)

    def placed(piece):
        _, size, _, width, _, _, turn = piece
        return (width, size) if turn else (size, width)

    out_shapes = [None] * outs
    for piece in pieces:
        shape = placed(piece)
        out_shapes[piece[4]] = (max(piece[5] + shape[0], (out_shapes[piece[4]] or (0,))[0]), shape[1])

    def kernel(where_ref, p_ref, *refs):
        count = len(pieces)
        results, got, made = refs[:outs], refs[outs : outs + count], refs[outs + count : outs + 2 * count]
        in_sem, out_sem = refs[outs + 2 * count :]
        start = lambda at: pl.multiple_of(where_ref[at[0]], 128) if isinstance(at, tuple) else at
        loads = []
        for k, (row, size, col, width, _, _, _) in enumerate(pieces):
            source = p_ref.at[pl.ds(start(row), size), pl.ds(start(col), width)]
            loads.append(pltpu.make_async_copy(source, got[k], in_sem.at[k]))
            loads[-1].start()
        stores = []
        for k, piece in enumerate(pieces):
            loads[k].wait()
            turn, shape = piece[6], placed(piece)
            if turn:
                for a in range(0, shape[0], turn):
                    for b in range(0, shape[1], turn):
                        made[k][a : a + turn, b : b + turn] = got[k][b : b + turn, a : a + turn].T.astype(BF16)
            else:
                made[k][...] = got[k][...].astype(BF16)
            target = results[piece[4]].at[pl.ds(piece[5], shape[0]), :]
            stores.append(pltpu.make_async_copy(made[k], target, out_sem.at[k]))
            stores[-1].start()
        for copy in stores:
            copy.wait()

    return pl.pallas_call(
        kernel,
        in_specs=[pl.BlockSpec(memory_space=pltpu.SMEM), pl.BlockSpec(memory_space=pl.ANY)],
        out_specs=[pl.BlockSpec(memory_space=pl.ANY)] * outs,
        out_shape=[jax.ShapeDtypeStruct(shape, BF16) for shape in out_shapes],
        scratch_shapes=[pltpu.VMEM(piece[1:4:2], F32) for piece in pieces]
        + [pltpu.VMEM(placed(piece), BF16) for piece in pieces]
        + [pltpu.SemaphoreType.DMA((len(pieces),)), pltpu.SemaphoreType.DMA((len(pieces),))],
        compiler_params=params(),
        cost_estimate=cost(1),
        name="packed",
    )(where, covariance)


def columns_operator(
    covariance, halos, stencil, where, unit, steps, nlon, count, block_at, held=None, ends=False, work=1
):
    rows, cols = covariance.shape
    lats = cols // nlon
    wide = steps * nlon
    size = unit * nlon
    span = 2 * steps * nlon
    pairs = lats // 2

    def kernel(where_ref, stencil_ref, p_ref, *rest):
        halo_refs, rest = rest[: 2 * len(halos)], rest[2 * len(halos) :]
        outs, (data_ref, b_high, b_low) = rest[:-3], rest[-3:]
        if held is not None:
            outs = outs[1:]
        t_ref = outs[0]
        i = pl.program_id(0)
        col_odd, row_odd = where_ref[2] != 0, where_ref[3] != 0

        @pl.when(i == 0)
        def _():
            data_ref[size:, :wide] = jnp.zeros((size, wide), BF16)
            data_ref[size:, wide + cols :] = jnp.zeros((size, wide), BF16)
            for q in range(pairs):
                for a in range(2):
                    for k in range(2 * steps):
                        d = k - (steps - 1) - a
                        high, low = split(circulant(stencil_ref[d + steps, 2 * q + a : 2 * q + a + 1, :]))
                        at = pl.ds(q * span + k * nlon, nlon)
                        b_high[at, a * nlon : (a + 1) * nlon] = high
                        b_low[at, a * nlon : (a + 1) * nlon] = low

        for k in range(len(halos)):
            even_ref, odd_ref = halo_refs[2 * k : 2 * k + 2]
            chosen = i >= 0 if len(halos) == 1 else i == k

            @pl.when(jnp.logical_and(chosen, col_odd))
            def _(even_ref=even_ref, odd_ref=odd_ref):
                data_ref[:size, :wide] = even_ref[...]
                data_ref[:size, wide + cols :] = odd_ref[...]

            @pl.when(jnp.logical_and(chosen, jnp.logical_not(col_odd)))
            def _(even_ref=even_ref, odd_ref=odd_ref):
                data_ref[:size, :wide] = odd_ref[...]
                data_ref[:size, wide + cols :] = even_ref[...]

        data_ref[:size, wide : wide + cols], data_ref[size:, wide : wide + cols] = split(p_ref[...])
        for q in range(pairs):
            window = slice((2 * q + 1) * nlon, (2 * q + 1) * nlon + span)
            of = pl.ds(q * span, span)
            both = product(data_ref[:, window], b_high[of, :])
            total = both[:size] + both[size:] + product(data_ref[:size, window], b_low[of, :])
            for a, k, d in ((0, 2 * q, -steps), (1, 2 * q + 2 * steps + 1, steps)):
                far = slice(k * nlon, (k + 1) * nlon)
                weight = jnp.sum(stencil_ref[d + steps, 2 * q + a : 2 * q + a + 1, :], axis=1, keepdims=True)
                far_values = data_ref[:size, far].astype(F32) + data_ref[size:, far].astype(F32)
                value = total[:, a * nlon : (a + 1) * nlon] + weight * far_values
                t_ref[:, (2 * q + a) * nlon : (2 * q + a + 1) * nlon] = value.astype(BF16)
        if ends:
            for odd in range(2):
                is_odd = row_odd if odd else jnp.logical_not(row_odd)

                @pl.when(jnp.logical_and(i == 0, is_odd))
                def _(odd=odd):
                    outs[2 - odd][...] = t_ref[:wide, :]

                @pl.when(jnp.logical_and(i == count - 1, is_odd))
                def _(odd=odd):
                    outs[1 + odd][...] = t_ref[size - wide :, :]

    halo_at = (lambda i, at: (i, 0)) if len(halos) == 1 else (lambda i, at: (0, 0))
    in_specs = [
        pl.BlockSpec(stencil.shape, lambda i, at: (0, 0, 0)),
        pl.BlockSpec((size, cols), lambda i, at: (block_at(i, at), 0)),
    ] + [pl.BlockSpec((size, wide), halo_at)] * (2 * len(halos))
    out_specs = [pl.BlockSpec((size, cols), lambda i, at: (block_at(i, at), 0))]
    out_shape = [jax.ShapeDtypeStruct((rows, cols), BF16)]
    operands = [where, stencil, covariance] + [array for pair in halos for array in pair]
    aliases = {}
    if ends:
        out_specs += [pl.BlockSpec((wide, cols), lambda i, at: (0, 0))] * 2
        out_shape += [jax.ShapeDtypeStruct((wide, cols), BF16)] * 2
    if held is not None:
        in_specs.append(pl.BlockSpec(memory_space=pl.ANY))
        aliases = {len(operands): 0}
        operands.append(held)
    return pl.pallas_call(
        kernel,
        grid_spec=pltpu.PrefetchScalarGridSpec(
            num_scalar_prefetch=1,
            grid=(count,),
            in_specs=in_specs,
            out_specs=out_specs,
            scratch_shapes=[pltpu.VMEM((2 * size, cols + 2 * wide), BF16)]
            + [pltpu.VMEM((pairs * span, 2 * nlon), BF16)] * 2,
        ),
        out_shape=out_shape,
        input_output_aliases=aliases,
        compiler_params=params(),
        cost_estimate=cost(work),
        name="columns_operator",
    )(*operands)


def rows_operator(values, even, odd, stencil, where, steps, nlon, out_dtype, blocks=None, noise=None):
    rows, cols = values.shape
    lat_rows = rows // nlon
    wide = steps * nlon
    size = 2 * nlon
    span = 2 * steps * nlon
    pairs = lat_rows // 2
    group = 2 if pairs % 2 == 0 else 1
    ahead = (steps + 1) // 2
    exact = values.dtype == BF16
    makes = blocks is None
    chunk = min(cols, 256)

    def kernel(where_ref, stencil_ref, x_ref, even_ref, odd_ref, *rest):
        if makes:
            out_ref, a_ref = rest[:2]
        else:
            a_ref, noise_ref, out_ref = rest[:3]
        high_ref, sem = rest[2 if makes else 3 :][:2]
        raw_ref, low_ref = (None, None) if exact else rest[-2:]
        step = pl.program_id(0)

        def load(q):
            here = pl.ds(pl.multiple_of(q * size, size), size)
            there = pl.ds(pl.multiple_of(wide + q * size, nlon), size)
            target = high_ref.at[there, :] if exact else raw_ref.at[here, :]
            return pltpu.make_async_copy(x_ref.at[here, :], target, sem.at[q])

        def ready(q):
            load(q).wait()
            if not exact:
                there = pl.ds(pl.multiple_of(wide + q * size, nlon), size)
                here = pl.ds(pl.multiple_of(q * size, size), size)
                high_ref[there, :], low_ref[there, :] = split(raw_ref[here, :])

        @pl.when(step == 0)
        def _():
            is_odd = where_ref[3]
            at_even = pl.ds(pl.multiple_of((1 - is_odd) * (wide + rows), nlon), wide)
            at_odd = pl.ds(pl.multiple_of(is_odd * (wide + rows), nlon), wide)
            halos = [
                pltpu.make_async_copy(even_ref, high_ref.at[at_even, :], sem.at[pairs]),
                pltpu.make_async_copy(odd_ref, high_ref.at[at_odd, :], sem.at[pairs + 1]),
            ]
            for halo in halos:
                halo.start()
            for q in range(pairs):
                load(q).start()
            if not exact:
                low_ref[:wide, :] = jnp.zeros((wide, cols), BF16)
                low_ref[wide + rows :, :] = jnp.zeros((wide, cols), BF16)
            for halo in halos:
                halo.wait()
            for q in range(min(ahead, pairs)):
                ready(q)

        for j in range(group):
            q = step * group + j + ahead

            @pl.when(q < pairs)
            def _(q=q):
                ready(q)

        row = lambda j, d, a: stencil_ref[d + steps, pl.ds(2 * (step * group + j) + a, 1), :]
        if makes:
            for j in range(group):
                for a in range(2):
                    for k in range(2 * steps):
                        high, low = split(circulant(row(j, k - (steps - 1) - a, a)))
                        top = 2 * j * size + a * nlon
                        a_ref[top : top + nlon, k * nlon : (k + 1) * nlon] = high
                        a_ref[top + size : top + size + nlon, k * nlon : (k + 1) * nlon] = low
        for j in range(group):
            unit = lambda k: pl.multiple_of((2 * (step * group + j) + k) * nlon, nlon)
            weights = [jnp.sum(row(j, d, a), axis=1, keepdims=True) for a, d in ((0, -steps), (1, steps))]
            top = 2 * j * size
            for lane in range(0, cols, chunk):
                lanes = slice(lane, lane + chunk)
                both = product(a_ref[top : top + 2 * size, :], high_ref[pl.ds(unit(1), span), lanes])
                total = both[:size] + both[size:]
                if not exact:
                    total += product(a_ref[top : top + size, :], low_ref[pl.ds(unit(1), span), lanes])
                for a, k in ((0, 0), (1, 2 * steps + 1)):
                    far = high_ref[pl.ds(unit(k), nlon), lanes].astype(F32)
                    if not exact:
                        far += low_ref[pl.ds(unit(k), nlon), lanes].astype(F32)
                    value = total[a * nlon : (a + 1) * nlon, :] + weights[a] * far
                    out_ref[j * size + a * nlon : j * size + (a + 1) * nlon, lanes] = value.astype(out_dtype)
        if noise is not None:
            for a in range(2 * group):
                lat = 2 * group * step + a - where_ref[4]

                @pl.when(jnp.logical_and(lat >= 0, lat < cols // nlon))
                def _(a=a, lat=lat):
                    lanes = pl.ds(pl.multiple_of(lat * nlon, nlon), nlon)
                    eye = lax.broadcasted_iota(jnp.int32, (nlon, nlon), 0) == lax.broadcasted_iota(
                        jnp.int32, (nlon, nlon), 1
                    )
                    added = jnp.where(eye, noise_ref[pl.ds(2 * group * step + a, 1), :], 0.0)
                    out_ref[a * nlon : (a + 1) * nlon, lanes] += added

    in_specs = [pl.BlockSpec(stencil.shape, lambda g, at: (0, 0, 0))] + [pl.BlockSpec(memory_space=pl.ANY)] * 3
    operands = [where, stencil, values, even, odd]
    out_specs = [pl.BlockSpec((group * size, cols), lambda g, at: (g, 0))]
    out_shape = [jax.ShapeDtypeStruct((rows, cols), out_dtype)]
    blocks_spec = pl.BlockSpec((2 * group * size, span), lambda g, at: (g, 0))
    if makes:
        out_specs.append(blocks_spec)
        out_shape.append(jax.ShapeDtypeStruct((2 * rows, span), BF16))
    else:
        in_specs += [blocks_spec, pl.BlockSpec(noise.shape, lambda g, at: (0, 0))]
        operands += [blocks, noise]
    return pl.pallas_call(
        kernel,
        grid_spec=pltpu.PrefetchScalarGridSpec(
            num_scalar_prefetch=1,
            grid=(pairs // group,),
            in_specs=in_specs,
            out_specs=out_specs,
            scratch_shapes=[pltpu.VMEM((rows + 2 * wide, cols), BF16), pltpu.SemaphoreType.DMA((pairs + 2,))]
            + ([] if exact else [pltpu.VMEM((rows, cols), F32), pltpu.VMEM((rows + 2 * wide, cols), BF16)]),
        ),
        out_shape=out_shape,
        compiler_params=params(),
        cost_estimate=cost(1),
        name="rows_operator",
    )(*operands)


def shifted(block, axis, by):
    size = lax.axis_size(axis)
    pairs = [(i, i + by) for i in range(size) if 0 <= i + by < size]
    return lax.ppermute(block, axis, pairs)


def gathered(first, last, axis, dim, unit, halo, own):
    before, after = [], []
    need, hop = halo, 1
    while need > 0:
        take = min(own, need)
        size = first.shape[dim]
        before.insert(0, shifted(lax.slice_in_dim(last, size - take * unit, size, axis=dim), axis, hop))
        after.append(shifted(lax.slice_in_dim(first, 0, take * unit, axis=dim), axis, -hop))
        need, hop = need - take, hop + 1
    join = lambda parts: parts[0] if len(parts) == 1 else jnp.concatenate(parts, axis=dim)
    return join(before), join(after)


def exchanged(block, axis, odd):
    pairs = []
    for i in range(odd, lax.axis_size(axis) - 1, 2):
        pairs += [(i, i + 1), (i + 1, i)]
    return lax.ppermute(block, axis, pairs)


def mirrored(block, odd):
    n_row, n_col = lax.axis_size("row"), lax.axis_size("col")
    pairs = []
    for a in range(n_row):
        for b in range(n_col):
            to = 2 * a + (1 - b % 2) + (1 if (b + odd) % 2 else -1)
            if 0 <= to < n_col:
                pairs.append((a * n_col + b, (b // 2) * n_col + to))
    return lax.ppermute(block, ("row", "col"), pairs)


def body(covariance, noise_var, wind_table, diffusivity, wind_index):
    rows_dev, cols_dev = covariance.shape
    lat_rows, nlon = noise_var.shape
    steps, nlat = wind_index.shape
    lats = cols_dev // nlon
    row_id, col_id = lax.axis_index("row"), lax.axis_index("col")
    own = lat_rows // 4
    fits = lat_rows == 2 * lats and own % 2 == 0 and own >= steps and own <= lats - steps
    if not fits or lax.axis_size("col") != 2 * lax.axis_size("row"):
        return plain_body(covariance, noise_var, wind_table, diffusivity, wind_index)

    near = lat_rows // 2 - own
    middle = lat_rows // 2
    outer, inner, wide = near * nlon, own * nlon, steps * nlon
    pick = lambda parity, even, odd: even + parity * (odd - even)
    col_odd, row_odd = col_id % 2, row_id % 2
    mirror_at, direct_at = pick(col_odd, middle - own, middle), pick(col_odd, middle, middle - own)
    diagonal = col_id * lats - row_id * lat_rows
    where = jnp.stack([mirror_at // own, direct_at // own, col_odd, row_odd, diagonal]).astype(jnp.int32)
    sources = jnp.stack(
        [
            mirror_at * nlon,
            pick(col_odd, lats, lats - steps) * nlon,
            pick(col_odd, 2 * lats - steps, 0) * nlon,
            pick(col_odd, lats - own, 0) * nlon,
            pick(col_odd, cols_dev - wide, 0),
            pick(col_odd, 0, cols_dev - wide),
            pick(row_odd, rows_dev - wide, 0),
            pick(row_odd, 0, rows_dev - wide),
        ]
    ).astype(jnp.int32)
    pieces = [
        (row, outer, (4 + k,), wide, k, there, 0)
        for row, there in ((0, 0), (rows_dev - outer, outer))
        for k in range(2)
    ]
    pieces += [((6 + k,), wide, 0, cols_dev, k + 2, 0, 0) for k in range(2)]
    pieces += [((1 + k,), wide, (3,), inner, k + 4, 0, nlon) for k in range(2)]
    pieces += [((0,), inner, (4 + k,), wide, k + 6, 0, 0) for k in range(2)]
    sent = packed(covariance, sources, pieces)
    outers, ends, mirrors, inners = [list(sent[k : k + 2]) for k in range(0, 8, 2)]
    outers = [exchanged(piece, "col", k) for k, piece in enumerate(outers)]
    ends = [exchanged(piece, "row", k) for k, piece in enumerate(ends)]
    mirrors[0], mirrors[1], wind_index, ends[0] = lax.optimization_barrier(
        (mirrors[0], mirrors[1], wind_index, ends[0])
    )
    mirrors = [mirrored(piece, k) for k, piece in enumerate(mirrors)]

    row_s, col_s = stencil_rows(
        wind_table, diffusivity, wind_index, row_id * lat_rows, col_id * lats, lat_rows, lats, nlon
    )
    operator_times_prior, blocks = rows_operator(covariance, *ends, row_s, where, steps, nlon, BF16)
    operator_times_prior, outers, inners = lax.optimization_barrier((operator_times_prior, outers, inners))
    inners = [exchanged(piece, "col", k) for k, piece in enumerate(inners)]
    mirror, *ends = columns_operator(
        covariance, [outers], col_s, where, near, steps, nlon, 2, lambda i, at: i * (lat_rows // near - 1),
        None, True,
    )
    ends = [exchanged(piece, "row", k) for k, piece in enumerate(ends)]
    (mirror,) = columns_operator(
        covariance, [mirrors, inners], col_s, where, own, steps, nlon, 2, lambda i, at: at[i], mirror, False,
        10 ** 13,
    )
    (predicted_spread_matrix,) = rows_operator(
        mirror, *ends, row_s, where, steps, nlon, F32, blocks, noise_var
    )
    return (predicted_spread_matrix, operator_times_prior)


def plain_body(covariance, noise_var, wind_table, diffusivity, wind_index):
    rows_dev, cols_dev = covariance.shape
    lat_rows, nlon = noise_var.shape
    steps, nlat = wind_index.shape
    lats = cols_dev // nlon
    row_id, col_id = lax.axis_index("row"), lax.axis_index("col")
    sent = covariance.astype(BF16)
    sides = gathered(sent, sent, "col", 1, nlon, steps, lats)
    ends = gathered(sent, sent, "row", 0, nlon, steps, lat_rows)
    row_s, col_s = stencil_rows(
        wind_table, diffusivity, wind_index, row_id * lat_rows, col_id * lats, lat_rows, lats, nlon
    )
    where = jnp.stack([0, 0, 1, 1, col_id * lats - row_id * lat_rows]).astype(jnp.int32)
    operator_times_prior, blocks = rows_operator(covariance, *ends, row_s, where, steps, nlon, BF16)
    (mirror,) = columns_operator(
        covariance, [sides], col_s, where, 2, steps, nlon, lat_rows // 2, lambda i, at: i
    )
    ends = gathered(mirror, mirror, "row", 0, nlon, steps, lat_rows)
    (predicted_spread_matrix,) = rows_operator(
        mirror, *ends, row_s, where, steps, nlon, F32, blocks, noise_var
    )
    return (predicted_spread_matrix, operator_times_prior)


def solution(mesh):
    in_specs = (P("row", "col"), P("row", None), P(), P(), P())
    out_specs = (P("row", "col"), P("row", "col"))
    return jax.shard_map(body, mesh=mesh, in_specs=in_specs, out_specs=out_specs, check_vma=False)
```

```python
import functools

import jax
import jax.numpy as jnp
from jax import lax
from jax.experimental import pallas as pl
from jax.experimental.pallas import tpu as pltpu
from jax.sharding import PartitionSpec as P

F32 = jnp.float32
BF16 = jnp.bfloat16
VMEM_LIMIT = 63 * 1024 * 1024


def params():
    return pltpu.CompilerParams(vmem_limit_bytes=VMEM_LIMIT)


def cost(work):
    return pl.CostEstimate(flops=work, bytes_accessed=work, transcendentals=0)


def stencil_terms(zonal_cour, merid_cour, diffuse):
    middle_weight = 1.0 - zonal_cour * zonal_cour - merid_cour * merid_cour - 4.0 * diffuse
    eastward_weight = 0.5 * zonal_cour * zonal_cour - 0.5 * zonal_cour + diffuse
    west_w = 0.5 * zonal_cour * zonal_cour + 0.5 * zonal_cour + diffuse
    north_w = 0.5 * merid_cour * merid_cour - 0.5 * merid_cour + diffuse
    south_w = 0.5 * merid_cour * merid_cour + 0.5 * merid_cour + diffuse
    return middle_weight, eastward_weight, west_w, north_w, south_w


def split(values):
    high = values.astype(BF16)
    return high, (values - high.astype(F32)).astype(BF16)


def circulant(row):
    size = row.shape[1]
    return pltpu.roll(jnp.broadcast_to(row, (size, size)), 0, 1, stride=1, stride_axis=0)


def product(left, right):
    return jnp.dot(left, right, preferred_element_type=F32)


def composed(terms, lats, nlon):
    steps = len(terms)
    padded = lats + 2 * steps
    lane = lax.broadcasted_iota(jnp.int32, (padded, nlon), 1)
    rows = {0: (lane == 0).astype(F32)}
    for step_no in range(steps):
        low, high = step_no + 1, padded - step_no - 1
        c, e, w, n, s = [term[low:high] for term in terms[step_no]]
        size = high - low
        fresh = {}
        for d in range(-step_no - 1, step_no + 2):
            parts = []
            if d in rows:
                here = rows[d][1 : 1 + size]
                parts += [c * here, e * pltpu.roll(here, 1, 1), w * pltpu.roll(here, nlon - 1, 1)]
            if d - 1 in rows:
                parts.append(n * rows[d - 1][2 : 2 + size])
            if d + 1 in rows:
                parts.append(s * rows[d + 1][0:size])
            fresh[d] = functools.reduce(lambda x, y: x + y, parts)
        rows = fresh
    return rows


def stencils(wind_table, diffusivity, wind_index, where, lat_rows, lats, nlon):
    steps, nlat = wind_index.shape
    sizes = (lat_rows, lats)
    span = 2 * steps * nlon
    pairs = lats // 2

    def kernel(table_ref, diffuse_ref, index_ref, where_ref, row_out, col_out, high_out, low_out, *scratch):
        for side, out in enumerate((row_out, col_out)):
            looked_up = scratch[side]
            terms = []
            for step_no in range(steps):
                for i in range(sizes[side] + 2 * steps):
                    lat = where_ref[5 + side] + i - steps
                    inside = jnp.logical_and(lat >= 0, lat < nlat)
                    entry = index_ref[step_no, jnp.clip(lat, 0, nlat - 1)]
                    values = (table_ref[entry, 0], table_ref[entry, 1], diffuse_ref[entry], inside.astype(F32))
                    for k, value in enumerate(values):
                        looked_up[k, i : i + 1, :] = jnp.full((1, nlon), value, F32)
                here = looked_up[3] > 0.5
                c, e, w, n, s = [
                    jnp.where(here, term, 0.0)
                    for term in stencil_terms(looked_up[0], looked_up[1], looked_up[2])
                ]
                terms.append((c, w, e, n, s) if side else (c, e, w, n, s))
            for d, value in composed(terms, sizes[side], nlon).items():
                out[d + steps] = value
        for q in range(pairs):
            for a in range(2):
                for k in range(2 * steps):
                    d = k - (steps - 1) - a
                    high, low = split(circulant(col_out[d + steps, 2 * q + a : 2 * q + a + 1, :]))
                    at = pl.ds(q * span + k * nlon, nlon)
                    high_out[at, a * nlon : (a + 1) * nlon] = high
                    low_out[at, a * nlon : (a + 1) * nlon] = low

    return pl.pallas_call(
        kernel,
        in_specs=[pl.BlockSpec(memory_space=pltpu.SMEM)] * 4,
        out_shape=[jax.ShapeDtypeStruct((2 * steps + 1, size, nlon), F32) for size in sizes]
        + [jax.ShapeDtypeStruct((pairs * span, 2 * nlon), BF16)] * 2,
        scratch_shapes=[pltpu.VMEM((4, size + 2 * steps, nlon), F32) for size in sizes],
        compiler_params=params(),
        cost_estimate=cost(1),
        name="stencils",
    )(wind_table, diffusivity, wind_index, where)


def packed(covariance, where, pieces):
    outs = 1 + max(piece[4] for piece in pieces)

    def placed(piece):
        _, size, _, width, _, _, turn = piece
        return (width, size) if turn else (size, width)

    out_shapes = [None] * outs
    for piece in pieces:
        shape = placed(piece)
        out_shapes[piece[4]] = (max(piece[5] + shape[0], (out_shapes[piece[4]] or (0,))[0]), shape[1])

    def kernel(where_ref, p_ref, *refs):
        count = len(pieces)
        results, got, made = refs[:outs], refs[outs : outs + count], refs[outs + count : outs + 2 * count]
        in_sem, out_sem = refs[outs + 2 * count :]
        start = lambda at: pl.multiple_of(where_ref[at[0]], 128) if isinstance(at, tuple) else at
        loads = []
        for k, (row, size, col, width, _, _, _) in enumerate(pieces):
            source = p_ref.at[pl.ds(start(row), size), pl.ds(start(col), width)]
            loads.append(pltpu.make_async_copy(source, got[k], in_sem.at[k]))
            loads[-1].start()
        stores = []
        for k, piece in enumerate(pieces):
            loads[k].wait()
            turn, shape = piece[6], placed(piece)
            if turn:
                for a in range(0, shape[0], turn):
                    for b in range(0, shape[1], turn):
                        made[k][a : a + turn, b : b + turn] = got[k][b : b + turn, a : a + turn].T.astype(BF16)
            else:
                made[k][...] = got[k][...].astype(BF16)
            target = results[piece[4]].at[pl.ds(piece[5], shape[0]), :]
            stores.append(pltpu.make_async_copy(made[k], target, out_sem.at[k]))
            stores[-1].start()
        for copy in stores:
            copy.wait()

    return pl.pallas_call(
        kernel,
        in_specs=[pl.BlockSpec(memory_space=pltpu.SMEM), pl.BlockSpec(memory_space=pl.ANY)],
        out_specs=[pl.BlockSpec(memory_space=pl.ANY)] * outs,
        out_shape=[jax.ShapeDtypeStruct(shape, BF16) for shape in out_shapes],
        scratch_shapes=[pltpu.VMEM(piece[1:4:2], F32) for piece in pieces]
        + [pltpu.VMEM(placed(piece), BF16) for piece in pieces]
        + [pltpu.SemaphoreType.DMA((len(pieces),)), pltpu.SemaphoreType.DMA((len(pieces),))],
        compiler_params=params(),
        cost_estimate=cost(1),
        name="packed",
    )(where, covariance)


def columns_operator(
    covariance, halos, stencil, blocks, where, unit, steps, nlon, count, block_at, held=None, ends=False, work=1
):
    rows, cols = covariance.shape
    lats = cols // nlon
    wide = steps * nlon
    size = unit * nlon
    span = 2 * steps * nlon
    pairs = lats // 2

    def kernel(where_ref, stencil_ref, p_ref, *rest):
        halo_refs, rest = rest[: 2 * len(halos)], rest[2 * len(halos) :]
        (b_high, b_low), outs, data_ref = rest[:2], rest[2:-1], rest[-1]
        if held is not None:
            outs = outs[1:]
        t_ref = outs[0]
        i = pl.program_id(0)
        col_odd, row_odd = where_ref[2] != 0, where_ref[3] != 0

        @pl.when(i == 0)
        def _():
            data_ref[size:, :wide] = jnp.zeros((size, wide), BF16)
            data_ref[size:, wide + cols :] = jnp.zeros((size, wide), BF16)

        for k in range(len(halos)):
            even_ref, odd_ref = halo_refs[2 * k : 2 * k + 2]
            chosen = i >= 0 if len(halos) == 1 else i == k

            @pl.when(jnp.logical_and(chosen, col_odd))
            def _(even_ref=even_ref, odd_ref=odd_ref):
                data_ref[:size, :wide] = even_ref[...]
                data_ref[:size, wide + cols :] = odd_ref[...]

            @pl.when(jnp.logical_and(chosen, jnp.logical_not(col_odd)))
            def _(even_ref=even_ref, odd_ref=odd_ref):
                data_ref[:size, :wide] = odd_ref[...]
                data_ref[:size, wide + cols :] = even_ref[...]

        data_ref[:size, wide : wide + cols], data_ref[size:, wide : wide + cols] = split(p_ref[...])
        for q in range(pairs):
            window = slice((2 * q + 1) * nlon, (2 * q + 1) * nlon + span)
            of = pl.ds(q * span, span)
            both = product(data_ref[:, window], b_high[of, :])
            total = both[:size] + both[size:] + product(data_ref[:size, window], b_low[of, :])
            for a, k, d in ((0, 2 * q, -steps), (1, 2 * q + 2 * steps + 1, steps)):
                far = slice(k * nlon, (k + 1) * nlon)
                weight = jnp.sum(stencil_ref[d + steps, 2 * q + a : 2 * q + a + 1, :], axis=1, keepdims=True)
                far_values = data_ref[:size, far].astype(F32) + data_ref[size:, far].astype(F32)
                value = total[:, a * nlon : (a + 1) * nlon] + weight * far_values
                t_ref[:, (2 * q + a) * nlon : (2 * q + a + 1) * nlon] = value.astype(BF16)
        if ends:
            for odd in range(2):
                is_odd = row_odd if odd else jnp.logical_not(row_odd)

                @pl.when(jnp.logical_and(i == 0, is_odd))
                def _(odd=odd):
                    outs[2 - odd][...] = t_ref[:wide, :]

                @pl.when(jnp.logical_and(i == count - 1, is_odd))
                def _(odd=odd):
                    outs[1 + odd][...] = t_ref[size - wide :, :]

    halo_at = (lambda i, at: (i, 0)) if len(halos) == 1 else (lambda i, at: (0, 0))
    in_specs = [
        pl.BlockSpec(stencil.shape, lambda i, at: (0, 0, 0)),
        pl.BlockSpec((size, cols), lambda i, at: (block_at(i, at), 0)),
    ]
    in_specs += [pl.BlockSpec((size, wide), halo_at)] * (2 * len(halos))
    in_specs += [pl.BlockSpec(block.shape, lambda i, at: (0, 0)) for block in blocks]
    out_specs = [pl.BlockSpec((size, cols), lambda i, at: (block_at(i, at), 0))]
    out_shape = [jax.ShapeDtypeStruct((rows, cols), BF16)]
    operands = [where, stencil, covariance] + [array for pair in halos for array in pair] + list(blocks)
    aliases = {}
    if ends:
        out_specs += [pl.BlockSpec((wide, cols), lambda i, at: (0, 0))] * 2
        out_shape += [jax.ShapeDtypeStruct((wide, cols), BF16)] * 2
    if held is not None:
        in_specs.append(pl.BlockSpec(memory_space=pl.ANY))
        aliases = {len(operands): 0}
        operands.append(held)
    return pl.pallas_call(
        kernel,
        grid_spec=pltpu.PrefetchScalarGridSpec(
            num_scalar_prefetch=1,
            grid=(count,),
            in_specs=in_specs,
            out_specs=out_specs,
            scratch_shapes=[pltpu.VMEM((2 * size, cols + 2 * wide), BF16)],
        ),
        out_shape=out_shape,
        input_output_aliases=aliases,
        compiler_params=params(),
        cost_estimate=cost(work),
        name="columns_operator",
    )(*operands)


def rows_operator(values, even, odd, stencil, where, steps, nlon, out_dtype, blocks=None, noise=None):
    rows, cols = values.shape
    lat_rows = rows // nlon
    wide = steps * nlon
    size = 2 * nlon
    span = 2 * steps * nlon
    pairs = lat_rows // 2
    group = 2 if pairs % 2 == 0 else 1
    ahead = (steps + 1) // 2
    exact = values.dtype == BF16
    makes = blocks is None
    chunk = min(cols, 256)

    def kernel(where_ref, stencil_ref, x_ref, even_ref, odd_ref, *rest):
        if makes:
            out_ref, a_ref = rest[:2]
        else:
            a_ref, noise_ref, out_ref = rest[:3]
        high_ref, sem = rest[2 if makes else 3 :][:2]
        raw_ref, low_ref = (None, None) if exact else rest[-2:]
        step = pl.program_id(0)

        def load(q):
            here = pl.ds(pl.multiple_of(q * size, size), size)
            there = pl.ds(pl.multiple_of(wide + q * size, nlon), size)
            target = high_ref.at[there, :] if exact else raw_ref.at[here, :]
            return pltpu.make_async_copy(x_ref.at[here, :], target, sem.at[q])

        def ready(q):
            load(q).wait()
            if not exact:
                there = pl.ds(pl.multiple_of(wide + q * size, nlon), size)
                here = pl.ds(pl.multiple_of(q * size, size), size)
                high_ref[there, :], low_ref[there, :] = split(raw_ref[here, :])

        @pl.when(step == 0)
        def _():
            is_odd = where_ref[3]
            at_even = pl.ds(pl.multiple_of((1 - is_odd) * (wide + rows), nlon), wide)
            at_odd = pl.ds(pl.multiple_of(is_odd * (wide + rows), nlon), wide)
            halos = [
                pltpu.make_async_copy(even_ref, high_ref.at[at_even, :], sem.at[pairs]),
                pltpu.make_async_copy(odd_ref, high_ref.at[at_odd, :], sem.at[pairs + 1]),
            ]
            for halo in halos:
                halo.start()
            for q in range(pairs):
                load(q).start()
            if not exact:
                low_ref[:wide, :] = jnp.zeros((wide, cols), BF16)
                low_ref[wide + rows :, :] = jnp.zeros((wide, cols), BF16)
            for halo in halos:
                halo.wait()
            for q in range(min(ahead, pairs)):
                ready(q)

        for j in range(group):
            q = step * group + j + ahead

            @pl.when(q < pairs)
            def _(q=q):
                ready(q)

        row = lambda j, d, a: stencil_ref[d + steps, pl.ds(2 * (step * group + j) + a, 1), :]
        if makes:
            for j in range(group):
                for a in range(2):
                    for k in range(2 * steps):
                        high, low = split(circulant(row(j, k - (steps - 1) - a, a)))
                        top = 2 * j * size + a * nlon
                        a_ref[top : top + nlon, k * nlon : (k + 1) * nlon] = high
                        a_ref[top + size : top + size + nlon, k * nlon : (k + 1) * nlon] = low
        for j in range(group):
            unit = lambda k: pl.multiple_of((2 * (step * group + j) + k) * nlon, nlon)
            weights = [jnp.sum(row(j, d, a), axis=1, keepdims=True) for a, d in ((0, -steps), (1, steps))]
            top = 2 * j * size
            for lane in range(0, cols, chunk):
                lanes = slice(lane, lane + chunk)
                both = product(a_ref[top : top + 2 * size, :], high_ref[pl.ds(unit(1), span), lanes])
                total = both[:size] + both[size:]
                if not exact:
                    total += product(a_ref[top : top + size, :], low_ref[pl.ds(unit(1), span), lanes])
                for a, k in ((0, 0), (1, 2 * steps + 1)):
                    far = high_ref[pl.ds(unit(k), nlon), lanes].astype(F32)
                    if not exact:
                        far += low_ref[pl.ds(unit(k), nlon), lanes].astype(F32)
                    value = total[a * nlon : (a + 1) * nlon, :] + weights[a] * far
                    out_ref[j * size + a * nlon : j * size + (a + 1) * nlon, lanes] = value.astype(out_dtype)
        if noise is not None:
            for a in range(2 * group):
                lat = 2 * group * step + a - where_ref[4]

                @pl.when(jnp.logical_and(lat >= 0, lat < cols // nlon))
                def _(a=a, lat=lat):
                    lanes = pl.ds(pl.multiple_of(lat * nlon, nlon), nlon)
                    eye = lax.broadcasted_iota(jnp.int32, (nlon, nlon), 0) == lax.broadcasted_iota(
                        jnp.int32, (nlon, nlon), 1
                    )
                    added = jnp.where(eye, noise_ref[pl.ds(2 * group * step + a, 1), :], 0.0)
                    out_ref[a * nlon : (a + 1) * nlon, lanes] += added

    in_specs = [pl.BlockSpec(stencil.shape, lambda g, at: (0, 0, 0))] + [pl.BlockSpec(memory_space=pl.ANY)] * 3
    operands = [where, stencil, values, even, odd]
    out_specs = [pl.BlockSpec((group * size, cols), lambda g, at: (g, 0))]
    out_shape = [jax.ShapeDtypeStruct((rows, cols), out_dtype)]
    blocks_spec = pl.BlockSpec((2 * group * size, span), lambda g, at: (g, 0))
    if makes:
        out_specs.append(blocks_spec)
        out_shape.append(jax.ShapeDtypeStruct((2 * rows, span), BF16))
    else:
        in_specs += [blocks_spec, pl.BlockSpec(noise.shape, lambda g, at: (0, 0))]
        operands += [blocks, noise]
    return pl.pallas_call(
        kernel,
        grid_spec=pltpu.PrefetchScalarGridSpec(
            num_scalar_prefetch=1,
            grid=(pairs // group,),
            in_specs=in_specs,
            out_specs=out_specs,
            scratch_shapes=[pltpu.VMEM((rows + 2 * wide, cols), BF16), pltpu.SemaphoreType.DMA((pairs + 2,))]
            + ([] if exact else [pltpu.VMEM((rows, cols), F32), pltpu.VMEM((rows + 2 * wide, cols), BF16)]),
        ),
        out_shape=out_shape,
        compiler_params=params(),
        cost_estimate=cost(1),
        name="rows_operator",
    )(*operands)


def shifted(block, axis, by):
    size = lax.axis_size(axis)
    pairs = [(i, i + by) for i in range(size) if 0 <= i + by < size]
    return lax.ppermute(block, axis, pairs)


def gathered(first, last, axis, dim, unit, halo, own):
    before, after = [], []
    need, hop = halo, 1
    while need > 0:
        take = min(own, need)
        size = first.shape[dim]
        before.insert(0, shifted(lax.slice_in_dim(last, size - take * unit, size, axis=dim), axis, hop))
        after.append(shifted(lax.slice_in_dim(first, 0, take * unit, axis=dim), axis, -hop))
        need, hop = need - take, hop + 1
    join = lambda parts: parts[0] if len(parts) == 1 else jnp.concatenate(parts, axis=dim)
    return join(before), join(after)


def exchanged(block, axis, odd):
    pairs = []
    for i in range(odd, lax.axis_size(axis) - 1, 2):
        pairs += [(i, i + 1), (i + 1, i)]
    return lax.ppermute(block, axis, pairs)


def mirrored(block, odd):
    n_row, n_col = lax.axis_size("row"), lax.axis_size("col")
    pairs = []
    for a in range(n_row):
        for b in range(n_col):
            to = 2 * a + (1 - b % 2) + (1 if (b + odd) % 2 else -1)
            if 0 <= to < n_col:
                pairs.append((a * n_col + b, (b // 2) * n_col + to))
    return lax.ppermute(block, ("row", "col"), pairs)


def body(covariance, noise_var, wind_table, diffusivity, wind_index):
    rows_dev, cols_dev = covariance.shape
    lat_rows, nlon = noise_var.shape
    steps, nlat = wind_index.shape
    lats = cols_dev // nlon
    row_id, col_id = lax.axis_index("row"), lax.axis_index("col")
    own = lat_rows // 4
    fits = lat_rows == 2 * lats and own % 2 == 0 and own >= steps and own <= lats - steps
    if not fits or lax.axis_size("col") != 2 * lax.axis_size("row"):
        return plain_body(covariance, noise_var, wind_table, diffusivity, wind_index)

    near = lat_rows // 2 - own
    middle = lat_rows // 2
    outer, inner, wide = near * nlon, own * nlon, steps * nlon
    pick = lambda parity, even, odd: even + parity * (odd - even)
    col_odd, row_odd = col_id % 2, row_id % 2
    mirror_at, direct_at = pick(col_odd, middle - own, middle), pick(col_odd, middle, middle - own)
    diagonal = col_id * lats - row_id * lat_rows
    where = jnp.stack(
        [
            mirror_at // own,
            direct_at // own,
            col_odd,
            row_odd,
            diagonal,
            row_id * lat_rows,
            col_id * lats,
            mirror_at * nlon,
            pick(col_odd, lats, lats - steps) * nlon,
            pick(col_odd, 2 * lats - steps, 0) * nlon,
            pick(col_odd, lats - own, 0) * nlon,
            pick(col_odd, cols_dev - wide, 0),
            pick(col_odd, 0, cols_dev - wide),
            pick(row_odd, rows_dev - wide, 0),
            pick(row_odd, 0, rows_dev - wide),
        ]
    ).astype(jnp.int32)
    pieces = [
        (row, outer, (11 + k,), wide, k, there, 0)
        for row, there in ((0, 0), (rows_dev - outer, outer))
        for k in range(2)
    ]
    pieces += [((13 + k,), wide, 0, cols_dev, k + 2, 0, 0) for k in range(2)]
    pieces += [((8 + k,), wide, (10,), inner, k + 4, 0, nlon) for k in range(2)]
    pieces += [((7,), inner, (11 + k,), wide, k + 6, 0, 0) for k in range(2)]
    sent = packed(covariance, where, pieces)
    outers, ends, mirrors, inners = [list(sent[k : k + 2]) for k in range(0, 8, 2)]
    outers = [exchanged(piece, "col", k) for k, piece in enumerate(outers)]
    ends = [exchanged(piece, "row", k) for k, piece in enumerate(ends)]
    mirrors[0], mirrors[1], wind_index, ends[0] = lax.optimization_barrier(
        (mirrors[0], mirrors[1], wind_index, ends[0])
    )
    mirrors = [mirrored(piece, k) for k, piece in enumerate(mirrors)]

    row_s, col_s, *col_blocks = stencils(wind_table, diffusivity, wind_index, where, lat_rows, lats, nlon)
    operator_times_prior, blocks = rows_operator(covariance, *ends, row_s, where, steps, nlon, BF16)
    operator_times_prior, outers, inners = lax.optimization_barrier((operator_times_prior, outers, inners))
    inners = [exchanged(piece, "col", k) for k, piece in enumerate(inners)]
    mirror, *ends = columns_operator(
        covariance, [outers], col_s, col_blocks, where, near, steps, nlon, 2, lambda i, at: i * (lat_rows // near - 1),
        None, True,
    )
    ends = [exchanged(piece, "row", k) for k, piece in enumerate(ends)]
    (mirror,) = columns_operator(
        covariance, [mirrors, inners], col_s, col_blocks, where, own, steps, nlon, 2, lambda i, at: at[i], mirror, False,
        10 ** 13,
    )
    (predicted_spread_matrix,) = rows_operator(
        mirror, *ends, row_s, where, steps, nlon, F32, blocks, noise_var
    )
    return (predicted_spread_matrix, operator_times_prior)


def plain_body(covariance, noise_var, wind_table, diffusivity, wind_index):
    rows_dev, cols_dev = covariance.shape
    lat_rows, nlon = noise_var.shape
    steps, nlat = wind_index.shape
    lats = cols_dev // nlon
    row_id, col_id = lax.axis_index("row"), lax.axis_index("col")
    sent = covariance.astype(BF16)
    sides = gathered(sent, sent, "col", 1, nlon, steps, lats)
    ends = gathered(sent, sent, "row", 0, nlon, steps, lat_rows)
    firsts = (row_id * lat_rows, col_id * lats)
    where = jnp.stack([0, 0, 1, 1, firsts[1] - firsts[0], *firsts]).astype(jnp.int32)
    row_s, col_s, *col_blocks = stencils(wind_table, diffusivity, wind_index, where, lat_rows, lats, nlon)
    operator_times_prior, blocks = rows_operator(covariance, *ends, row_s, where, steps, nlon, BF16)
    (mirror,) = columns_operator(
        covariance, [sides], col_s, col_blocks, where, 2, steps, nlon, lat_rows // 2, lambda i, at: i
    )
    ends = gathered(mirror, mirror, "row", 0, nlon, steps, lat_rows)
    (predicted_spread_matrix,) = rows_operator(
        mirror, *ends, row_s, where, steps, nlon, F32, blocks, noise_var
    )
    return (predicted_spread_matrix, operator_times_prior)


def solution(mesh):
    in_specs = (P("row", "col"), P("row", None), P(), P(), P())
    out_specs = (P("row", "col"), P("row", "col"))
    return jax.shard_map(body, mesh=mesh, in_specs=in_specs, out_specs=out_specs, check_vma=False)
```

```python
import functools

import jax
import jax.numpy as jnp
from jax import lax
from jax.experimental import pallas as pl
from jax.experimental.pallas import tpu as pltpu
from jax.sharding import PartitionSpec as P

F32 = jnp.float32
BF16 = jnp.bfloat16
VMEM_LIMIT = 63 * 1024 * 1024


def params():
    return pltpu.CompilerParams(vmem_limit_bytes=VMEM_LIMIT)


def cost(work):
    return pl.CostEstimate(flops=work, bytes_accessed=work, transcendentals=0)


def stencil_terms(zonal_cour, merid_cour, diffuse):
    middle_weight = 1.0 - zonal_cour * zonal_cour - merid_cour * merid_cour - 4.0 * diffuse
    eastward_weight = 0.5 * zonal_cour * zonal_cour - 0.5 * zonal_cour + diffuse
    west_w = 0.5 * zonal_cour * zonal_cour + 0.5 * zonal_cour + diffuse
    north_w = 0.5 * merid_cour * merid_cour - 0.5 * merid_cour + diffuse
    south_w = 0.5 * merid_cour * merid_cour + 0.5 * merid_cour + diffuse
    return middle_weight, eastward_weight, west_w, north_w, south_w


def split(values):
    high = values.astype(BF16)
    return high, (values - high.astype(F32)).astype(BF16)


def circulant(row):
    size = row.shape[1]
    return pltpu.roll(jnp.broadcast_to(row, (size, size)), 0, 1, stride=1, stride_axis=0)


def product(left, right):
    return jnp.dot(left, right, preferred_element_type=F32)


def composed(terms, lats, nlon):
    steps = len(terms)
    padded = lats + 2 * steps
    lane = lax.broadcasted_iota(jnp.int32, (padded, nlon), 1)
    rows = {0: (lane == 0).astype(F32)}
    for step_no in range(steps):
        low, high = step_no + 1, padded - step_no - 1
        c, e, w, n, s = [term[low:high] for term in terms[step_no]]
        size = high - low
        fresh = {}
        for d in range(-step_no - 1, step_no + 2):
            parts = []
            if d in rows:
                here = rows[d][1 : 1 + size]
                parts += [c * here, e * pltpu.roll(here, 1, 1), w * pltpu.roll(here, nlon - 1, 1)]
            if d - 1 in rows:
                parts.append(n * rows[d - 1][2 : 2 + size])
            if d + 1 in rows:
                parts.append(s * rows[d + 1][0:size])
            fresh[d] = functools.reduce(lambda x, y: x + y, parts)
        rows = fresh
    return rows


def swept(planes, weights):
    for step_no, (c, e, w, n, s) in enumerate(weights):
        fresh = []
        for i in range(1, len(planes) - 1):
            at, u = i + step_no, planes[i]
            nlon = u.shape[1]
            fresh.append(
                c(at) * u
                + e(at) * pltpu.roll(u, nlon - 1, 1)
                + w(at) * pltpu.roll(u, 1, 1)
                + n(at) * planes[i + 1]
                + s(at) * planes[i - 1]
            )
        planes = fresh
    return planes


def stencils(wind_table, diffusivity, wind_index, where, lat_rows, lats, nlon):
    steps, nlat = wind_index.shape
    sizes = (lat_rows, lats)
    span = 2 * steps * nlon
    pairs = lats // 2

    def kernel(
        table_ref, diffuse_ref, index_ref, where_ref, row_out, col_out, high_out, low_out, step_out, *scratch
    ):
        for side, out in enumerate((row_out, col_out)):
            looked_up = scratch[side]
            terms = []
            for step_no in range(steps):
                for i in range(sizes[side] + 2 * steps):
                    lat = where_ref[5 + side] + i - steps
                    inside = jnp.logical_and(lat >= 0, lat < nlat)
                    entry = index_ref[step_no, jnp.clip(lat, 0, nlat - 1)]
                    values = (table_ref[entry, 0], table_ref[entry, 1], diffuse_ref[entry], inside.astype(F32))
                    for k, value in enumerate(values):
                        looked_up[k, i : i + 1, :] = jnp.full((1, nlon), value, F32)
                here = looked_up[3] > 0.5
                c, e, w, n, s = [
                    jnp.where(here, term, 0.0)
                    for term in stencil_terms(looked_up[0], looked_up[1], looked_up[2])
                ]
                terms.append((c, w, e, n, s) if side else (c, e, w, n, s))
                if side:
                    for member, value in enumerate((c, e, w, n, s)):
                        step_out[5 * step_no + member] = value
            for d, value in composed(terms, sizes[side], nlon).items():
                out[d + steps] = value
        for q in range(pairs):
            for a in range(2):
                for k in range(2 * steps):
                    d = k - (steps - 1) - a
                    high, low = split(circulant(col_out[d + steps, 2 * q + a : 2 * q + a + 1, :]))
                    at = pl.ds(q * span + k * nlon, nlon)
                    high_out[at, a * nlon : (a + 1) * nlon] = high
                    low_out[at, a * nlon : (a + 1) * nlon] = low

    return pl.pallas_call(
        kernel,
        in_specs=[pl.BlockSpec(memory_space=pltpu.SMEM)] * 4,
        out_shape=[jax.ShapeDtypeStruct((2 * steps + 1, size, nlon), F32) for size in sizes]
        + [jax.ShapeDtypeStruct((pairs * span, 2 * nlon), BF16)] * 2
        + [jax.ShapeDtypeStruct((5 * steps, lats + 2 * steps, nlon), F32)],
        scratch_shapes=[pltpu.VMEM((4, size + 2 * steps, nlon), F32) for size in sizes],
        compiler_params=params(),
        cost_estimate=cost(1),
        name="stencils",
    )(wind_table, diffusivity, wind_index, where)


def packed(covariance, where, pieces):
    outs = 1 + max(piece[4] for piece in pieces)

    def placed(piece):
        _, size, _, width, _, _, turn = piece
        return (width, size) if turn else (size, width)

    out_shapes = [None] * outs
    for piece in pieces:
        shape = placed(piece)
        out_shapes[piece[4]] = (max(piece[5] + shape[0], (out_shapes[piece[4]] or (0,))[0]), shape[1])

    def kernel(where_ref, p_ref, *refs):
        count = len(pieces)
        results, got, made = refs[:outs], refs[outs : outs + count], refs[outs + count : outs + 2 * count]
        in_sem, out_sem = refs[outs + 2 * count :]
        start = lambda at: pl.multiple_of(where_ref[at[0]], 128) if isinstance(at, tuple) else at
        loads = []
        for k, (row, size, col, width, _, _, _) in enumerate(pieces):
            source = p_ref.at[pl.ds(start(row), size), pl.ds(start(col), width)]
            loads.append(pltpu.make_async_copy(source, got[k], in_sem.at[k]))
            loads[-1].start()
        stores = []
        for k, piece in enumerate(pieces):
            loads[k].wait()
            turn, shape = piece[6], placed(piece)
            if turn:
                for a in range(0, shape[0], turn):
                    for b in range(0, shape[1], turn):
                        made[k][a : a + turn, b : b + turn] = got[k][b : b + turn, a : a + turn].T.astype(BF16)
            else:
                made[k][...] = got[k][...].astype(BF16)
            target = results[piece[4]].at[pl.ds(piece[5], shape[0]), :]
            stores.append(pltpu.make_async_copy(made[k], target, out_sem.at[k]))
            stores[-1].start()
        for copy in stores:
            copy.wait()

    return pl.pallas_call(
        kernel,
        in_specs=[pl.BlockSpec(memory_space=pltpu.SMEM), pl.BlockSpec(memory_space=pl.ANY)],
        out_specs=[pl.BlockSpec(memory_space=pl.ANY)] * outs,
        out_shape=[jax.ShapeDtypeStruct(shape, BF16) for shape in out_shapes],
        scratch_shapes=[pltpu.VMEM(piece[1:4:2], F32) for piece in pieces]
        + [pltpu.VMEM(placed(piece), BF16) for piece in pieces]
        + [pltpu.SemaphoreType.DMA((len(pieces),)), pltpu.SemaphoreType.DMA((len(pieces),))],
        compiler_params=params(),
        cost_estimate=cost(1),
        name="packed",
    )(where, covariance)


def columns_operator(
    covariance, halos, stencil, blocks, where, unit, steps, nlon, count, block_at, held=None, ends=False, work=1
):
    rows, cols = covariance.shape
    lats = cols // nlon
    wide = steps * nlon
    size = unit * nlon
    span = 2 * steps * nlon
    pairs = lats // 2
    part = nlon // 2
    upper = size - part * (3 * size // (8 * part))

    def kernel(where_ref, stencil_ref, p_ref, *rest):
        halo_refs, rest = rest[: 2 * len(halos)], rest[2 * len(halos) :]
        (b_high, b_low, step_ref), outs, data_ref = rest[:3], rest[3:-1], rest[-1]
        if held is not None:
            outs = outs[1:]
        t_ref = outs[0]
        i = pl.program_id(0)
        col_odd, row_odd = where_ref[2] != 0, where_ref[3] != 0

        @pl.when(i == 0)
        def _():
            data_ref[size:, :wide] = jnp.zeros((size, wide), BF16)
            data_ref[size:, wide + cols :] = jnp.zeros((size, wide), BF16)

        for k in range(len(halos)):
            even_ref, odd_ref = halo_refs[2 * k : 2 * k + 2]
            chosen = i >= 0 if len(halos) == 1 else i == k

            @pl.when(jnp.logical_and(chosen, col_odd))
            def _(even_ref=even_ref, odd_ref=odd_ref):
                data_ref[:size, :wide] = even_ref[...]
                data_ref[:size, wide + cols :] = odd_ref[...]

            @pl.when(jnp.logical_and(chosen, jnp.logical_not(col_odd)))
            def _(even_ref=even_ref, odd_ref=odd_ref):
                data_ref[:size, :wide] = odd_ref[...]
                data_ref[:size, wide + cols :] = even_ref[...]

        data_ref[:upper, wide : wide + cols], data_ref[size : size + upper, wide : wide + cols] = split(
            p_ref[:upper, :]
        )
        weights = [
            [
                lambda at, k=5 * step_no + member: step_ref[k, at : at + 1, :]
                for member in range(5)
            ]
            for step_no in range(steps)
        ]
        starts = list(range(upper, size, part))
        for q in range(max(pairs, len(starts))):
            if q < pairs:
                window = slice((2 * q + 1) * nlon, (2 * q + 1) * nlon + span)
                of = pl.ds(q * span, span)
                total = product(data_ref[:upper, window], b_high[of, :])
                total += product(data_ref[size : size + upper, window], b_high[of, :])
                total += product(data_ref[:upper, window], b_low[of, :])
                for a, k, d in ((0, 2 * q, -steps), (1, 2 * q + 2 * steps + 1, steps)):
                    far = slice(k * nlon, (k + 1) * nlon)
                    row = stencil_ref[d + steps, 2 * q + a : 2 * q + a + 1, :]
                    weight = jnp.sum(row, axis=1, keepdims=True)
                    far_values = data_ref[:upper, far].astype(F32) + data_ref[size : size + upper, far].astype(F32)
                    value = total[:, a * nlon : (a + 1) * nlon] + weight * far_values
                    t_ref[:upper, (2 * q + a) * nlon : (2 * q + a + 1) * nlon] = value.astype(BF16)
            if q < len(starts):
                rows_at = slice(starts[q], starts[q] + part)
                planes = []
                for k in range(lats + 2 * steps):
                    if steps <= k < steps + lats:
                        planes.append(p_ref[rows_at, (k - steps) * nlon : (k - steps + 1) * nlon])
                    else:
                        planes.append(data_ref[rows_at, k * nlon : (k + 1) * nlon].astype(F32))
                for k, plane in enumerate(swept(planes, weights)):
                    t_ref[rows_at, k * nlon : (k + 1) * nlon] = plane.astype(BF16)
        if ends:
            for odd in range(2):
                is_odd = row_odd if odd else jnp.logical_not(row_odd)

                @pl.when(jnp.logical_and(i == 0, is_odd))
                def _(odd=odd):
                    outs[2 - odd][...] = t_ref[:wide, :]

                @pl.when(jnp.logical_and(i == count - 1, is_odd))
                def _(odd=odd):
                    outs[1 + odd][...] = t_ref[size - wide :, :]

    halo_at = (lambda i, at: (i, 0)) if len(halos) == 1 else (lambda i, at: (0, 0))
    in_specs = [
        pl.BlockSpec(stencil.shape, lambda i, at: (0, 0, 0)),
        pl.BlockSpec((size, cols), lambda i, at: (block_at(i, at), 0)),
    ]
    in_specs += [pl.BlockSpec((size, wide), halo_at)] * (2 * len(halos))
    in_specs += [pl.BlockSpec(block.shape, lambda i, at, n=block.ndim: (0,) * n) for block in blocks]
    out_specs = [pl.BlockSpec((size, cols), lambda i, at: (block_at(i, at), 0))]
    out_shape = [jax.ShapeDtypeStruct((rows, cols), BF16)]
    operands = [where, stencil, covariance] + [array for pair in halos for array in pair] + list(blocks)
    aliases = {}
    if ends:
        out_specs += [pl.BlockSpec((wide, cols), lambda i, at: (0, 0))] * 2
        out_shape += [jax.ShapeDtypeStruct((wide, cols), BF16)] * 2
    if held is not None:
        in_specs.append(pl.BlockSpec(memory_space=pl.ANY))
        aliases = {len(operands): 0}
        operands.append(held)
    return pl.pallas_call(
        kernel,
        grid_spec=pltpu.PrefetchScalarGridSpec(
            num_scalar_prefetch=1,
            grid=(count,),
            in_specs=in_specs,
            out_specs=out_specs,
            scratch_shapes=[pltpu.VMEM((2 * size, cols + 2 * wide), BF16)],
        ),
        out_shape=out_shape,
        input_output_aliases=aliases,
        compiler_params=params(),
        cost_estimate=cost(work),
        name="columns_operator",
    )(*operands)


def rows_operator(values, even, odd, stencil, where, steps, nlon, out_dtype, blocks=None, noise=None):
    rows, cols = values.shape
    lat_rows = rows // nlon
    wide = steps * nlon
    size = 2 * nlon
    span = 2 * steps * nlon
    pairs = lat_rows // 2
    group = 2 if pairs % 2 == 0 else 1
    ahead = (steps + 1) // 2
    exact = values.dtype == BF16
    makes = blocks is None
    chunk = min(cols, 256)

    def kernel(where_ref, stencil_ref, x_ref, even_ref, odd_ref, *rest):
        if makes:
            out_ref, a_ref = rest[:2]
        else:
            a_ref, noise_ref, out_ref = rest[:3]
        high_ref, sem = rest[2 if makes else 3 :][:2]
        raw_ref, low_ref = (None, None) if exact else rest[-2:]
        step = pl.program_id(0)

        def load(q):
            here = pl.ds(pl.multiple_of(q * size, size), size)
            there = pl.ds(pl.multiple_of(wide + q * size, nlon), size)
            target = high_ref.at[there, :] if exact else raw_ref.at[here, :]
            return pltpu.make_async_copy(x_ref.at[here, :], target, sem.at[q])

        def ready(q):
            load(q).wait()
            if not exact:
                there = pl.ds(pl.multiple_of(wide + q * size, nlon), size)
                here = pl.ds(pl.multiple_of(q * size, size), size)
                high_ref[there, :], low_ref[there, :] = split(raw_ref[here, :])

        @pl.when(step == 0)
        def _():
            is_odd = where_ref[3]
            at_even = pl.ds(pl.multiple_of((1 - is_odd) * (wide + rows), nlon), wide)
            at_odd = pl.ds(pl.multiple_of(is_odd * (wide + rows), nlon), wide)
            halos = [
                pltpu.make_async_copy(even_ref, high_ref.at[at_even, :], sem.at[pairs]),
                pltpu.make_async_copy(odd_ref, high_ref.at[at_odd, :], sem.at[pairs + 1]),
            ]
            for halo in halos:
                halo.start()
            for q in range(pairs):
                load(q).start()
            if not exact:
                low_ref[:wide, :] = jnp.zeros((wide, cols), BF16)
                low_ref[wide + rows :, :] = jnp.zeros((wide, cols), BF16)
            for halo in halos:
                halo.wait()
            for q in range(min(ahead, pairs)):
                ready(q)

        for j in range(group):
            q = step * group + j + ahead

            @pl.when(q < pairs)
            def _(q=q):
                ready(q)

        row = lambda j, d, a: stencil_ref[d + steps, pl.ds(2 * (step * group + j) + a, 1), :]
        if makes:
            for j in range(group):
                for a in range(2):
                    for k in range(2 * steps):
                        high, low = split(circulant(row(j, k - (steps - 1) - a, a)))
                        top = 2 * j * size + a * nlon
                        a_ref[top : top + nlon, k * nlon : (k + 1) * nlon] = high
                        a_ref[top + size : top + size + nlon, k * nlon : (k + 1) * nlon] = low
        for j in range(group):
            unit = lambda k: pl.multiple_of((2 * (step * group + j) + k) * nlon, nlon)
            weights = [jnp.sum(row(j, d, a), axis=1, keepdims=True) for a, d in ((0, -steps), (1, steps))]
            top = 2 * j * size
            for lane in range(0, cols, chunk):
                lanes = slice(lane, lane + chunk)
                both = product(a_ref[top : top + 2 * size, :], high_ref[pl.ds(unit(1), span), lanes])
                total = both[:size] + both[size:]
                if not exact:
                    total += product(a_ref[top : top + size, :], low_ref[pl.ds(unit(1), span), lanes])
                for a, k in ((0, 0), (1, 2 * steps + 1)):
                    far = high_ref[pl.ds(unit(k), nlon), lanes].astype(F32)
                    if not exact:
                        far += low_ref[pl.ds(unit(k), nlon), lanes].astype(F32)
                    value = total[a * nlon : (a + 1) * nlon, :] + weights[a] * far
                    out_ref[j * size + a * nlon : j * size + (a + 1) * nlon, lanes] = value.astype(out_dtype)
        if noise is not None:
            for a in range(2 * group):
                lat = 2 * group * step + a - where_ref[4]

                @pl.when(jnp.logical_and(lat >= 0, lat < cols // nlon))
                def _(a=a, lat=lat):
                    lanes = pl.ds(pl.multiple_of(lat * nlon, nlon), nlon)
                    eye = lax.broadcasted_iota(jnp.int32, (nlon, nlon), 0) == lax.broadcasted_iota(
                        jnp.int32, (nlon, nlon), 1
                    )
                    added = jnp.where(eye, noise_ref[pl.ds(2 * group * step + a, 1), :], 0.0)
                    out_ref[a * nlon : (a + 1) * nlon, lanes] += added

    in_specs = [pl.BlockSpec(stencil.shape, lambda g, at: (0, 0, 0))] + [pl.BlockSpec(memory_space=pl.ANY)] * 3
    operands = [where, stencil, values, even, odd]
    out_specs = [pl.BlockSpec((group * size, cols), lambda g, at: (g, 0))]
    out_shape = [jax.ShapeDtypeStruct((rows, cols), out_dtype)]
    blocks_spec = pl.BlockSpec((2 * group * size, span), lambda g, at: (g, 0))
    if makes:
        out_specs.append(blocks_spec)
        out_shape.append(jax.ShapeDtypeStruct((2 * rows, span), BF16))
    else:
        in_specs += [blocks_spec, pl.BlockSpec(noise.shape, lambda g, at: (0, 0))]
        operands += [blocks, noise]
    return pl.pallas_call(
        kernel,
        grid_spec=pltpu.PrefetchScalarGridSpec(
            num_scalar_prefetch=1,
            grid=(pairs // group,),
            in_specs=in_specs,
            out_specs=out_specs,
            scratch_shapes=[pltpu.VMEM((rows + 2 * wide, cols), BF16), pltpu.SemaphoreType.DMA((pairs + 2,))]
            + ([] if exact else [pltpu.VMEM((rows, cols), F32), pltpu.VMEM((rows + 2 * wide, cols), BF16)]),
        ),
        out_shape=out_shape,
        compiler_params=params(),
        cost_estimate=cost(1),
        name="rows_operator",
    )(*operands)


def shifted(block, axis, by):
    size = lax.axis_size(axis)
    pairs = [(i, i + by) for i in range(size) if 0 <= i + by < size]
    return lax.ppermute(block, axis, pairs)


def gathered(first, last, axis, dim, unit, halo, own):
    before, after = [], []
    need, hop = halo, 1
    while need > 0:
        take = min(own, need)
        size = first.shape[dim]
        before.insert(0, shifted(lax.slice_in_dim(last, size - take * unit, size, axis=dim), axis, hop))
        after.append(shifted(lax.slice_in_dim(first, 0, take * unit, axis=dim), axis, -hop))
        need, hop = need - take, hop + 1
    join = lambda parts: parts[0] if len(parts) == 1 else jnp.concatenate(parts, axis=dim)
    return join(before), join(after)


def exchanged(block, axis, odd):
    pairs = []
    for i in range(odd, lax.axis_size(axis) - 1, 2):
        pairs += [(i, i + 1), (i + 1, i)]
    return lax.ppermute(block, axis, pairs)


def mirrored(block, odd):
    n_row, n_col = lax.axis_size("row"), lax.axis_size("col")
    pairs = []
    for a in range(n_row):
        for b in range(n_col):
            to = 2 * a + (1 - b % 2) + (1 if (b + odd) % 2 else -1)
            if 0 <= to < n_col:
                pairs.append((a * n_col + b, (b // 2) * n_col + to))
    return lax.ppermute(block, ("row", "col"), pairs)


def body(covariance, noise_var, wind_table, diffusivity, wind_index):
    rows_dev, cols_dev = covariance.shape
    lat_rows, nlon = noise_var.shape
    steps, nlat = wind_index.shape
    lats = cols_dev // nlon
    row_id, col_id = lax.axis_index("row"), lax.axis_index("col")
    own = lat_rows // 4
    fits = lat_rows == 2 * lats and own % 2 == 0 and own >= steps and own <= lats - steps
    if not fits or lax.axis_size("col") != 2 * lax.axis_size("row"):
        return plain_body(covariance, noise_var, wind_table, diffusivity, wind_index)

    near = lat_rows // 2 - own
    middle = lat_rows // 2
    outer, inner, wide = near * nlon, own * nlon, steps * nlon
    pick = lambda parity, even, odd: even + parity * (odd - even)
    col_odd, row_odd = col_id % 2, row_id % 2
    mirror_at, direct_at = pick(col_odd, middle - own, middle), pick(col_odd, middle, middle - own)
    diagonal = col_id * lats - row_id * lat_rows
    where = jnp.stack(
        [
            mirror_at // own,
            direct_at // own,
            col_odd,
            row_odd,
            diagonal,
            row_id * lat_rows,
            col_id * lats,
            mirror_at * nlon,
            pick(col_odd, lats, lats - steps) * nlon,
            pick(col_odd, 2 * lats - steps, 0) * nlon,
            pick(col_odd, lats - own, 0) * nlon,
            pick(col_odd, cols_dev - wide, 0),
            pick(col_odd, 0, cols_dev - wide),
            pick(row_odd, rows_dev - wide, 0),
            pick(row_odd, 0, rows_dev - wide),
        ]
    ).astype(jnp.int32)
    pieces = [
        (row, outer, (11 + k,), wide, k, there, 0)
        for row, there in ((0, 0), (rows_dev - outer, outer))
        for k in range(2)
    ]
    pieces += [((13 + k,), wide, 0, cols_dev, k + 2, 0, 0) for k in range(2)]
    others = [((8 + k,), wide, (10,), inner, k, 0, nlon) for k in range(2)]
    others += [((7,), inner, (11 + k,), wide, k + 2, 0, 0) for k in range(2)]
    sent = packed(covariance, where, pieces)
    outers, ends = list(sent[:2]), list(sent[2:])
    outers = [exchanged(piece, "col", k) for k, piece in enumerate(outers)]
    ends = [exchanged(piece, "row", k) for k, piece in enumerate(ends)]
    late, ends[0] = lax.optimization_barrier((where, ends[0]))
    sent = packed(covariance, late, others)
    mirrors, inners = list(sent[:2]), list(sent[2:])
    mirrors[0], mirrors[1], wind_index, ends[0] = lax.optimization_barrier(
        (mirrors[0], mirrors[1], wind_index, ends[0])
    )
    mirrors = [mirrored(piece, k) for k, piece in enumerate(mirrors)]

    row_s, col_s, *col_blocks = stencils(wind_table, diffusivity, wind_index, where, lat_rows, lats, nlon)
    operator_times_prior, blocks = rows_operator(covariance, *ends, row_s, where, steps, nlon, BF16)
    operator_times_prior, outers, inners = lax.optimization_barrier((operator_times_prior, outers, inners))
    inners = [exchanged(piece, "col", k) for k, piece in enumerate(inners)]
    mirror, *ends = columns_operator(
        covariance, [outers], col_s, col_blocks, where, near, steps, nlon, 2, lambda i, at: i * (lat_rows // near - 1),
        None, True,
    )
    ends = [exchanged(piece, "row", k) for k, piece in enumerate(ends)]
    (mirror,) = columns_operator(
        covariance, [mirrors, inners], col_s, col_blocks, where, own, steps, nlon, 2, lambda i, at: at[i], mirror, False,
        10 ** 13,
    )
    (predicted_spread_matrix,) = rows_operator(
        mirror, *ends, row_s, where, steps, nlon, F32, blocks, noise_var
    )
    return (predicted_spread_matrix, operator_times_prior)


def plain_body(covariance, noise_var, wind_table, diffusivity, wind_index):
    rows_dev, cols_dev = covariance.shape
    lat_rows, nlon = noise_var.shape
    steps, nlat = wind_index.shape
    lats = cols_dev // nlon
    row_id, col_id = lax.axis_index("row"), lax.axis_index("col")
    sent = covariance.astype(BF16)
    sides = gathered(sent, sent, "col", 1, nlon, steps, lats)
    ends = gathered(sent, sent, "row", 0, nlon, steps, lat_rows)
    firsts = (row_id * lat_rows, col_id * lats)
    where = jnp.stack([0, 0, 1, 1, firsts[1] - firsts[0], *firsts]).astype(jnp.int32)
    row_s, col_s, *col_blocks = stencils(wind_table, diffusivity, wind_index, where, lat_rows, lats, nlon)
    operator_times_prior, blocks = rows_operator(covariance, *ends, row_s, where, steps, nlon, BF16)
    (mirror,) = columns_operator(
        covariance, [sides], col_s, col_blocks, where, 2, steps, nlon, lat_rows // 2, lambda i, at: i
    )
    ends = gathered(mirror, mirror, "row", 0, nlon, steps, lat_rows)
    (predicted_spread_matrix,) = rows_operator(
        mirror, *ends, row_s, where, steps, nlon, F32, blocks, noise_var
    )
    return (predicted_spread_matrix, operator_times_prior)


def solution(mesh):
    in_specs = (P("row", "col"), P("row", None), P(), P(), P())
    out_specs = (P("row", "col"), P("row", "col"))
    return jax.shard_map(body, mesh=mesh, in_specs=in_specs, out_specs=out_specs, check_vma=False)
```

```python
import functools

import jax
import jax.numpy as jnp
from jax import lax
from jax.experimental import pallas as pl
from jax.experimental.pallas import tpu as pltpu
from jax.sharding import PartitionSpec as P

F32 = jnp.float32
BF16 = jnp.bfloat16
VMEM_LIMIT = 63 * 1024 * 1024


def params():
    return pltpu.CompilerParams(vmem_limit_bytes=VMEM_LIMIT)


def cost(work):
    return pl.CostEstimate(flops=work, bytes_accessed=work, transcendentals=0)


def stencil_terms(zonal_cour, merid_cour, diffuse):
    middle_weight = 1.0 - zonal_cour * zonal_cour - merid_cour * merid_cour - 4.0 * diffuse
    eastward_weight = 0.5 * zonal_cour * zonal_cour - 0.5 * zonal_cour + diffuse
    west_w = 0.5 * zonal_cour * zonal_cour + 0.5 * zonal_cour + diffuse
    north_w = 0.5 * merid_cour * merid_cour - 0.5 * merid_cour + diffuse
    south_w = 0.5 * merid_cour * merid_cour + 0.5 * merid_cour + diffuse
    return middle_weight, eastward_weight, west_w, north_w, south_w


def split(values):
    high = values.astype(BF16)
    return high, (values - high.astype(F32)).astype(BF16)


def circulant(row):
    size = row.shape[1]
    return pltpu.roll(jnp.broadcast_to(row, (size, size)), 0, 1, stride=1, stride_axis=0)


def product(left, right):
    return jnp.dot(left, right, preferred_element_type=F32)


def composed(terms, lats, nlon):
    steps = len(terms)
    padded = lats + 2 * steps
    lane = lax.broadcasted_iota(jnp.int32, (padded, nlon), 1)
    rows = {0: (lane == 0).astype(F32)}
    for step_no in range(steps):
        low, high = step_no + 1, padded - step_no - 1
        c, e, w, n, s = [term[low:high] for term in terms[step_no]]
        size = high - low
        fresh = {}
        for d in range(-step_no - 1, step_no + 2):
            parts = []
            if d in rows:
                here = rows[d][1 : 1 + size]
                parts += [c * here, e * pltpu.roll(here, 1, 1), w * pltpu.roll(here, nlon - 1, 1)]
            if d - 1 in rows:
                parts.append(n * rows[d - 1][2 : 2 + size])
            if d + 1 in rows:
                parts.append(s * rows[d + 1][0:size])
            fresh[d] = functools.reduce(lambda x, y: x + y, parts)
        rows = fresh
    return rows


def swept(planes, weights):
    for step_no, (c, e, w, n, s) in enumerate(weights):
        fresh = []
        for i in range(1, len(planes) - 1):
            at, u = i + step_no, planes[i]
            nlon = u.shape[1]
            fresh.append(
                c(at) * u
                + e(at) * pltpu.roll(u, nlon - 1, 1)
                + w(at) * pltpu.roll(u, 1, 1)
                + n(at) * planes[i + 1]
                + s(at) * planes[i - 1]
            )
        planes = fresh
    return planes


def packing(pieces):
    def placed(piece):
        _, size, _, width, _, _, turn = piece
        return (width, size) if turn else (size, width)

    shapes = {}
    for piece in pieces:
        shape, out = placed(piece), piece[4]
        shapes[out] = (max(piece[5] + shape[0], shapes.get(out, (0,))[0]), shape[1])
    count = len(pieces)
    scratch = [pltpu.VMEM(piece[1:4:2], F32) for piece in pieces]
    scratch += [pltpu.VMEM(placed(piece), BF16) for piece in pieces]
    scratch += [pltpu.SemaphoreType.DMA((count,)), pltpu.SemaphoreType.DMA((count,))]

    def start(where_ref, p_ref, refs):
        first = lambda at: pl.multiple_of(where_ref[at[0]], 128) if isinstance(at, tuple) else at
        loads = []
        for k, (row, size, col, width, _, _, _) in enumerate(pieces):
            source = p_ref.at[pl.ds(first(row), size), pl.ds(first(col), width)]
            loads.append(pltpu.make_async_copy(source, refs[k], refs[2 * count].at[k]))
            loads[-1].start()
        return loads

    def finish(loads, results, refs):
        stores = []
        for k, piece in enumerate(pieces):
            loads[k].wait()
            got, made, turn, shape = refs[k], refs[count + k], piece[6], placed(piece)
            if turn:
                for a in range(0, shape[0], turn):
                    for b in range(0, shape[1], turn):
                        made[a : a + turn, b : b + turn] = got[b : b + turn, a : a + turn].T.astype(BF16)
            else:
                made[...] = got[...].astype(BF16)
            target = results[piece[4]].at[pl.ds(piece[5], shape[0]), :]
            stores.append(pltpu.make_async_copy(made, target, refs[2 * count + 1].at[k]))
            stores[-1].start()
        for copy in stores:
            copy.wait()

    return [jax.ShapeDtypeStruct(shapes[k], BF16) for k in range(len(shapes))], scratch, start, finish


def packed(covariance, where, pieces):
    out_shape, scratch, start, finish = packing(pieces)

    def kernel(where_ref, p_ref, *refs):
        results, refs = refs[: len(out_shape)], refs[len(out_shape) :]
        finish(start(where_ref, p_ref, refs), results, refs)

    return pl.pallas_call(
        kernel,
        in_specs=[pl.BlockSpec(memory_space=pltpu.SMEM), pl.BlockSpec(memory_space=pl.ANY)],
        out_specs=[pl.BlockSpec(memory_space=pl.ANY)] * len(out_shape),
        out_shape=out_shape,
        scratch_shapes=scratch,
        compiler_params=params(),
        cost_estimate=cost(1),
        name="packed",
    )(where, covariance)


def stencils(wind_table, diffusivity, wind_index, where, lat_rows, lats, nlon, covariance, pieces):
    steps, nlat = wind_index.shape
    sizes = (lat_rows, lats)
    span = 2 * steps * nlon
    pairs = lats // 2
    packs, pack_scratch, start, finish = packing(pieces)

    def kernel(table_ref, diffuse_ref, index_ref, where_ref, p_ref, *refs):
        row_out, col_out, high_out, low_out, step_out = refs[:5]
        results, scratch, refs = refs[5 : 5 + len(packs)], refs[5 + len(packs) :][:2], refs[7 + len(packs) :]
        loads = start(where_ref, p_ref, refs)
        for side, out in enumerate((row_out, col_out)):
            looked_up = scratch[side]
            terms = []
            for step_no in range(steps):
                for i in range(sizes[side] + 2 * steps):
                    lat = where_ref[5 + side] + i - steps
                    inside = jnp.logical_and(lat >= 0, lat < nlat)
                    entry = index_ref[step_no, jnp.clip(lat, 0, nlat - 1)]
                    values = (table_ref[0, entry], table_ref[1, entry], diffuse_ref[entry], inside.astype(F32))
                    for k, value in enumerate(values):
                        looked_up[k, i : i + 1, :] = jnp.full((1, nlon), value, F32)
                here = looked_up[3] > 0.5
                c, e, w, n, s = [
                    jnp.where(here, term, 0.0)
                    for term in stencil_terms(looked_up[0], looked_up[1], looked_up[2])
                ]
                terms.append((c, w, e, n, s) if side else (c, e, w, n, s))
                if side:
                    for member, value in enumerate((c, e, w, n, s)):
                        step_out[5 * step_no + member] = value
            for d, value in composed(terms, sizes[side], nlon).items():
                out[d + steps] = value
        for q in range(pairs):
            for a in range(2):
                for k in range(2 * steps):
                    d = k - (steps - 1) - a
                    high, low = split(circulant(col_out[d + steps, 2 * q + a : 2 * q + a + 1, :]))
                    at = pl.ds(q * span + k * nlon, nlon)
                    high_out[at, a * nlon : (a + 1) * nlon] = high
                    low_out[at, a * nlon : (a + 1) * nlon] = low
        finish(loads, results, refs)

    return pl.pallas_call(
        kernel,
        in_specs=[pl.BlockSpec(memory_space=pltpu.SMEM)] * 4 + [pl.BlockSpec(memory_space=pl.ANY)],
        out_specs=[pl.BlockSpec(memory_space=pltpu.VMEM)] * 5 + [pl.BlockSpec(memory_space=pl.ANY)] * len(packs),
        out_shape=[jax.ShapeDtypeStruct((2 * steps + 1, size, nlon), F32) for size in sizes]
        + [jax.ShapeDtypeStruct((pairs * span, 2 * nlon), BF16)] * 2
        + [jax.ShapeDtypeStruct((5 * steps, lats + 2 * steps, nlon), F32)]
        + packs,
        scratch_shapes=[pltpu.VMEM((4, size + 2 * steps, nlon), F32) for size in sizes]
        + pack_scratch,
        compiler_params=params(),
        cost_estimate=cost(1),
        name="stencils",
    )(wind_table.T, diffusivity, wind_index, where, covariance)


def columns_operator(
    covariance, halos, stencil, blocks, where, unit, steps, nlon, count, block_at, held=None, ends=False, work=1
):
    rows, cols = covariance.shape
    lats = cols // nlon
    wide = steps * nlon
    size = unit * nlon
    span = 2 * steps * nlon
    pairs = lats // 2
    part = nlon // 2
    upper = size - part * (3 * size // (8 * part))

    def kernel(where_ref, stencil_ref, p_ref, *rest):
        halo_refs, rest = rest[: 2 * len(halos)], rest[2 * len(halos) :]
        (b_high, b_low, step_ref), outs, data_ref = rest[:3], rest[3:-1], rest[-1]
        if held is not None:
            outs = outs[1:]
        t_ref = outs[0]
        i = pl.program_id(0)
        col_odd, row_odd = where_ref[2] != 0, where_ref[3] != 0

        @pl.when(i == 0)
        def _():
            data_ref[size:, :wide] = jnp.zeros((size, wide), BF16)
            data_ref[size:, wide + cols :] = jnp.zeros((size, wide), BF16)

        for k in range(len(halos)):
            even_ref, odd_ref = halo_refs[2 * k : 2 * k + 2]
            chosen = i >= 0 if len(halos) == 1 else i == k

            @pl.when(jnp.logical_and(chosen, col_odd))
            def _(even_ref=even_ref, odd_ref=odd_ref):
                data_ref[:size, :wide] = even_ref[...]
                data_ref[:size, wide + cols :] = odd_ref[...]

            @pl.when(jnp.logical_and(chosen, jnp.logical_not(col_odd)))
            def _(even_ref=even_ref, odd_ref=odd_ref):
                data_ref[:size, :wide] = odd_ref[...]
                data_ref[:size, wide + cols :] = even_ref[...]

        data_ref[:upper, wide : wide + cols], data_ref[size : size + upper, wide : wide + cols] = split(
            p_ref[:upper, :]
        )
        weights = [
            [
                lambda at, k=5 * step_no + member: step_ref[k, at : at + 1, :]
                for member in range(5)
            ]
            for step_no in range(steps)
        ]
        starts = list(range(upper, size, part))
        for q in range(max(pairs, len(starts))):
            if q < pairs:
                window = slice((2 * q + 1) * nlon, (2 * q + 1) * nlon + span)
                of = pl.ds(q * span, span)
                total = product(data_ref[:upper, window], b_high[of, :])
                total += product(data_ref[size : size + upper, window], b_high[of, :])
                total += product(data_ref[:upper, window], b_low[of, :])
                for a, k, d in ((0, 2 * q, -steps), (1, 2 * q + 2 * steps + 1, steps)):
                    far = slice(k * nlon, (k + 1) * nlon)
                    row = stencil_ref[d + steps, 2 * q + a : 2 * q + a + 1, :]
                    weight = jnp.sum(row, axis=1, keepdims=True)
                    far_values = data_ref[:upper, far].astype(F32) + data_ref[size : size + upper, far].astype(F32)
                    value = total[:, a * nlon : (a + 1) * nlon] + weight * far_values
                    t_ref[:upper, (2 * q + a) * nlon : (2 * q + a + 1) * nlon] = value.astype(BF16)
            if q < len(starts):
                rows_at = slice(starts[q], starts[q] + part)
                planes = []
                for k in range(lats + 2 * steps):
                    if steps <= k < steps + lats:
                        planes.append(p_ref[rows_at, (k - steps) * nlon : (k - steps + 1) * nlon])
                    else:
                        planes.append(data_ref[rows_at, k * nlon : (k + 1) * nlon].astype(F32))
                for k, plane in enumerate(swept(planes, weights)):
                    t_ref[rows_at, k * nlon : (k + 1) * nlon] = plane.astype(BF16)
        if ends:
            for odd in range(2):
                is_odd = row_odd if odd else jnp.logical_not(row_odd)

                @pl.when(jnp.logical_and(i == 0, is_odd))
                def _(odd=odd):
                    outs[2 - odd][...] = t_ref[:wide, :]

                @pl.when(jnp.logical_and(i == count - 1, is_odd))
                def _(odd=odd):
                    outs[1 + odd][...] = t_ref[size - wide :, :]

    halo_at = (lambda i, at: (i, 0)) if len(halos) == 1 else (lambda i, at: (0, 0))
    in_specs = [
        pl.BlockSpec(stencil.shape, lambda i, at: (0, 0, 0)),
        pl.BlockSpec((size, cols), lambda i, at: (block_at(i, at), 0)),
    ]
    in_specs += [pl.BlockSpec((size, wide), halo_at)] * (2 * len(halos))
    in_specs += [pl.BlockSpec(block.shape, lambda i, at, n=block.ndim: (0,) * n) for block in blocks]
    out_specs = [pl.BlockSpec((size, cols), lambda i, at: (block_at(i, at), 0))]
    out_shape = [jax.ShapeDtypeStruct((rows, cols), BF16)]
    operands = [where, stencil, covariance] + [array for pair in halos for array in pair] + list(blocks)
    aliases = {}
    if ends:
        out_specs += [pl.BlockSpec((wide, cols), lambda i, at: (0, 0))] * 2
        out_shape += [jax.ShapeDtypeStruct((wide, cols), BF16)] * 2
    if held is not None:
        in_specs.append(pl.BlockSpec(memory_space=pl.ANY))
        aliases = {len(operands): 0}
        operands.append(held)
    return pl.pallas_call(
        kernel,
        grid_spec=pltpu.PrefetchScalarGridSpec(
            num_scalar_prefetch=1,
            grid=(count,),
            in_specs=in_specs,
            out_specs=out_specs,
            scratch_shapes=[pltpu.VMEM((2 * size, cols + 2 * wide), BF16)],
        ),
        out_shape=out_shape,
        input_output_aliases=aliases,
        compiler_params=params(),
        cost_estimate=cost(work),
        name="columns_operator",
    )(*operands)


def rows_operator(values, even, odd, stencil, where, steps, nlon, out_dtype, blocks=None, noise=None):
    rows, cols = values.shape
    lat_rows = rows // nlon
    wide = steps * nlon
    size = 2 * nlon
    span = 2 * steps * nlon
    pairs = lat_rows // 2
    group = 2 if pairs % 2 == 0 else 1
    ahead = (steps + 1) // 2
    exact = values.dtype == BF16
    makes = blocks is None
    chunk = min(cols, 256)

    def kernel(where_ref, stencil_ref, x_ref, even_ref, odd_ref, *rest):
        if makes:
            out_ref, a_ref = rest[:2]
        else:
            a_ref, noise_ref, out_ref = rest[:3]
        high_ref, sem = rest[2 if makes else 3 :][:2]
        raw_ref, low_ref = (None, None) if exact else rest[-2:]
        step = pl.program_id(0)

        def load(q):
            here = pl.ds(pl.multiple_of(q * size, size), size)
            there = pl.ds(pl.multiple_of(wide + q * size, nlon), size)
            target = high_ref.at[there, :] if exact else raw_ref.at[here, :]
            return pltpu.make_async_copy(x_ref.at[here, :], target, sem.at[q])

        def ready(q):
            load(q).wait()
            if not exact:
                there = pl.ds(pl.multiple_of(wide + q * size, nlon), size)
                here = pl.ds(pl.multiple_of(q * size, size), size)
                high_ref[there, :], low_ref[there, :] = split(raw_ref[here, :])

        @pl.when(step == 0)
        def _():
            is_odd = where_ref[3]
            at_even = pl.ds(pl.multiple_of((1 - is_odd) * (wide + rows), nlon), wide)
            at_odd = pl.ds(pl.multiple_of(is_odd * (wide + rows), nlon), wide)
            halos = [
                pltpu.make_async_copy(even_ref, high_ref.at[at_even, :], sem.at[pairs]),
                pltpu.make_async_copy(odd_ref, high_ref.at[at_odd, :], sem.at[pairs + 1]),
            ]
            for halo in halos:
                halo.start()
            for q in range(pairs):
                load(q).start()
            if not exact:
                low_ref[:wide, :] = jnp.zeros((wide, cols), BF16)
                low_ref[wide + rows :, :] = jnp.zeros((wide, cols), BF16)
            for halo in halos:
                halo.wait()
            for q in range(min(ahead, pairs)):
                ready(q)

        for j in range(group):
            q = step * group + j + ahead

            @pl.when(q < pairs)
            def _(q=q):
                ready(q)

        row = lambda j, d, a: stencil_ref[d + steps, pl.ds(2 * (step * group + j) + a, 1), :]
        if makes:
            for j in range(group):
                for a in range(2):
                    for k in range(2 * steps):
                        high, low = split(circulant(row(j, k - (steps - 1) - a, a)))
                        top = 2 * j * size + a * nlon
                        a_ref[top : top + nlon, k * nlon : (k + 1) * nlon] = high
                        a_ref[top + size : top + size + nlon, k * nlon : (k + 1) * nlon] = low
        for j in range(group):
            unit = lambda k: pl.multiple_of((2 * (step * group + j) + k) * nlon, nlon)
            weights = [jnp.sum(row(j, d, a), axis=1, keepdims=True) for a, d in ((0, -steps), (1, steps))]
            top = 2 * j * size
            for lane in range(0, cols, chunk):
                lanes = slice(lane, lane + chunk)
                both = product(a_ref[top : top + 2 * size, :], high_ref[pl.ds(unit(1), span), lanes])
                total = both[:size] + both[size:]
                if not exact:
                    total += product(a_ref[top : top + size, :], low_ref[pl.ds(unit(1), span), lanes])
                for a, k in ((0, 0), (1, 2 * steps + 1)):
                    far = high_ref[pl.ds(unit(k), nlon), lanes].astype(F32)
                    if not exact:
                        far += low_ref[pl.ds(unit(k), nlon), lanes].astype(F32)
                    value = total[a * nlon : (a + 1) * nlon, :] + weights[a] * far
                    out_ref[j * size + a * nlon : j * size + (a + 1) * nlon, lanes] = value.astype(out_dtype)
        if noise is not None:
            for a in range(2 * group):
                lat = 2 * group * step + a - where_ref[4]

                @pl.when(jnp.logical_and(lat >= 0, lat < cols // nlon))
                def _(a=a, lat=lat):
                    lanes = pl.ds(pl.multiple_of(lat * nlon, nlon), nlon)
                    eye = lax.broadcasted_iota(jnp.int32, (nlon, nlon), 0) == lax.broadcasted_iota(
                        jnp.int32, (nlon, nlon), 1
                    )
                    added = jnp.where(eye, noise_ref[pl.ds(2 * group * step + a, 1), :], 0.0)
                    out_ref[a * nlon : (a + 1) * nlon, lanes] += added

    in_specs = [pl.BlockSpec(stencil.shape, lambda g, at: (0, 0, 0))] + [pl.BlockSpec(memory_space=pl.ANY)] * 3
    operands = [where, stencil, values, even, odd]
    out_specs = [pl.BlockSpec((group * size, cols), lambda g, at: (g, 0))]
    out_shape = [jax.ShapeDtypeStruct((rows, cols), out_dtype)]
    blocks_spec = pl.BlockSpec((2 * group * size, span), lambda g, at: (g, 0))
    if makes:
        out_specs.append(blocks_spec)
        out_shape.append(jax.ShapeDtypeStruct((2 * rows, span), BF16))
    else:
        in_specs += [blocks_spec, pl.BlockSpec(noise.shape, lambda g, at: (0, 0))]
        operands += [blocks, noise]
    return pl.pallas_call(
        kernel,
        grid_spec=pltpu.PrefetchScalarGridSpec(
            num_scalar_prefetch=1,
            grid=(pairs // group,),
            in_specs=in_specs,
            out_specs=out_specs,
            scratch_shapes=[pltpu.VMEM((rows + 2 * wide, cols), BF16), pltpu.SemaphoreType.DMA((pairs + 2,))]
            + ([] if exact else [pltpu.VMEM((rows, cols), F32), pltpu.VMEM((rows + 2 * wide, cols), BF16)]),
        ),
        out_shape=out_shape,
        compiler_params=params(),
        cost_estimate=cost(1),
        name="rows_operator",
    )(*operands)


def shifted(block, axis, by):
    size = lax.axis_size(axis)
    pairs = [(i, i + by) for i in range(size) if 0 <= i + by < size]
    return lax.ppermute(block, axis, pairs)


def gathered(first, last, axis, dim, unit, halo, own):
    before, after = [], []
    need, hop = halo, 1
    while need > 0:
        take = min(own, need)
        size = first.shape[dim]
        before.insert(0, shifted(lax.slice_in_dim(last, size - take * unit, size, axis=dim), axis, hop))
        after.append(shifted(lax.slice_in_dim(first, 0, take * unit, axis=dim), axis, -hop))
        need, hop = need - take, hop + 1
    join = lambda parts: parts[0] if len(parts) == 1 else jnp.concatenate(parts, axis=dim)
    return join(before), join(after)


def exchanged(block, axis, odd):
    pairs = []
    for i in range(odd, lax.axis_size(axis) - 1, 2):
        pairs += [(i, i + 1), (i + 1, i)]
    return lax.ppermute(block, axis, pairs)


def mirrored(block, odd):
    n_row, n_col = lax.axis_size("row"), lax.axis_size("col")
    pairs = []
    for a in range(n_row):
        for b in range(n_col):
            to = 2 * a + (1 - b % 2) + (1 if (b + odd) % 2 else -1)
            if 0 <= to < n_col:
                pairs.append((a * n_col + b, (b // 2) * n_col + to))
    return lax.ppermute(block, ("row", "col"), pairs)


def body(covariance, noise_var, wind_table, diffusivity, wind_index):
    rows_dev, cols_dev = covariance.shape
    lat_rows, nlon = noise_var.shape
    steps, nlat = wind_index.shape
    lats = cols_dev // nlon
    row_id, col_id = lax.axis_index("row"), lax.axis_index("col")
    own = lat_rows // 4
    fits = lat_rows == 2 * lats and own % 2 == 0 and own >= steps and own <= lats - steps
    if not fits or lax.axis_size("col") != 2 * lax.axis_size("row"):
        return plain_body(covariance, noise_var, wind_table, diffusivity, wind_index)

    near = lat_rows // 2 - own
    middle = lat_rows // 2
    outer, inner, wide = near * nlon, own * nlon, steps * nlon
    pick = lambda parity, even, odd: even + parity * (odd - even)
    col_odd, row_odd = col_id % 2, row_id % 2
    mirror_at, direct_at = pick(col_odd, middle - own, middle), pick(col_odd, middle, middle - own)
    diagonal = col_id * lats - row_id * lat_rows
    where = jnp.stack(
        [
            mirror_at // own,
            direct_at // own,
            col_odd,
            row_odd,
            diagonal,
            row_id * lat_rows,
            col_id * lats,
            mirror_at * nlon,
            pick(col_odd, lats, lats - steps) * nlon,
            pick(col_odd, 2 * lats - steps, 0) * nlon,
            pick(col_odd, lats - own, 0) * nlon,
            pick(col_odd, cols_dev - wide, 0),
            pick(col_odd, 0, cols_dev - wide),
            pick(row_odd, rows_dev - wide, 0),
            pick(row_odd, 0, rows_dev - wide),
        ]
    ).astype(jnp.int32)
    pieces = [
        (row, size, (11 + k,), wide, k, there, 0)
        for row, size, there in ((0, outer, 0), (rows_dev - outer, outer, outer), (0, 16, 2 * outer))
        for k in range(2)
    ]
    others = [((13 + k,), wide, 0, cols_dev, k, 0, 0) for k in range(2)]
    others += [((8 + k,), wide, (10,), inner, k + 2, 0, nlon) for k in range(2)]
    others += [((7,), inner, (11 + k,), wide, k + 4, 0, 0) for k in range(2)]
    outers = packed(covariance, where, pieces)
    outers = [exchanged(piece, "col", k) for k, piece in enumerate(outers)]
    row_s, col_s, *rest = stencils(
        wind_table, diffusivity, wind_index, where, lat_rows, lats, nlon, covariance, others
    )
    col_blocks, ends, mirrors, inners = rest[:3], rest[3:5], rest[5:7], rest[7:9]
    ends = [exchanged(piece, "row", k) for k, piece in enumerate(ends)]
    mirrors = [mirrored(piece, k) for k, piece in enumerate(mirrors)]

    operator_times_prior, blocks = rows_operator(covariance, *ends, row_s, where, steps, nlon, BF16)
    inners[0] = exchanged(inners[0], "col", 0)
    operator_times_prior, outers, inners[1] = lax.optimization_barrier(
        (operator_times_prior, outers, inners[1])
    )
    inners[1] = exchanged(inners[1], "col", 1)
    mirror, *ends = columns_operator(
        covariance, [outers], col_s, col_blocks, where, near, steps, nlon, 2, lambda i, at: i * (lat_rows // near - 1),
        None, True,
    )
    ends = [exchanged(piece, "row", k) for k, piece in enumerate(ends)]
    (mirror,) = columns_operator(
        covariance, [mirrors, inners], col_s, col_blocks, where, own, steps, nlon, 2, lambda i, at: at[i], mirror, False,
        10 ** 13,
    )
    (predicted_spread_matrix,) = rows_operator(
        mirror, *ends, row_s, where, steps, nlon, F32, blocks, noise_var
    )
    return (predicted_spread_matrix, operator_times_prior)


def plain_body(covariance, noise_var, wind_table, diffusivity, wind_index):
    rows_dev, cols_dev = covariance.shape
    lat_rows, nlon = noise_var.shape
    steps, nlat = wind_index.shape
    lats = cols_dev // nlon
    row_id, col_id = lax.axis_index("row"), lax.axis_index("col")
    sent = covariance.astype(BF16)
    sides = gathered(sent, sent, "col", 1, nlon, steps, lats)
    ends = gathered(sent, sent, "row", 0, nlon, steps, lat_rows)
    firsts = (row_id * lat_rows, col_id * lats)
    where = jnp.stack([0, 0, 1, 1, firsts[1] - firsts[0], *firsts]).astype(jnp.int32)
    row_s, col_s, *col_blocks = stencils(
        wind_table, diffusivity, wind_index, where, lat_rows, lats, nlon, covariance, []
    )
    operator_times_prior, blocks = rows_operator(covariance, *ends, row_s, where, steps, nlon, BF16)
    (mirror,) = columns_operator(
        covariance, [sides], col_s, col_blocks, where, 2, steps, nlon, lat_rows // 2, lambda i, at: i
    )
    ends = gathered(mirror, mirror, "row", 0, nlon, steps, lat_rows)
    (predicted_spread_matrix,) = rows_operator(
        mirror, *ends, row_s, where, steps, nlon, F32, blocks, noise_var
    )
    return (predicted_spread_matrix, operator_times_prior)


def solution(mesh):
    in_specs = (P("row", "col"), P("row", None), P(), P(), P())
    out_specs = (P("row", "col"), P("row", "col"))
    return jax.shard_map(body, mesh=mesh, in_specs=in_specs, out_specs=out_specs, check_vma=False)
```

```python
import functools

import jax
import jax.numpy as jnp
from jax import lax
from jax.experimental import pallas as pl
from jax.experimental.pallas import tpu as pltpu
from jax.sharding import PartitionSpec as P

F32 = jnp.float32
BF16 = jnp.bfloat16
VMEM_LIMIT = 63 * 1024 * 1024


def params():
    return pltpu.CompilerParams(vmem_limit_bytes=VMEM_LIMIT)


def cost(work):
    return pl.CostEstimate(flops=work, bytes_accessed=work, transcendentals=0)


def stencil_terms(zonal_cour, merid_cour, diffuse):
    middle_weight = 1.0 - zonal_cour * zonal_cour - merid_cour * merid_cour - 4.0 * diffuse
    eastward_weight = 0.5 * zonal_cour * zonal_cour - 0.5 * zonal_cour + diffuse
    west_w = 0.5 * zonal_cour * zonal_cour + 0.5 * zonal_cour + diffuse
    north_w = 0.5 * merid_cour * merid_cour - 0.5 * merid_cour + diffuse
    south_w = 0.5 * merid_cour * merid_cour + 0.5 * merid_cour + diffuse
    return middle_weight, eastward_weight, west_w, north_w, south_w


def split(values):
    high = values.astype(BF16)
    return high, (values - high.astype(F32)).astype(BF16)


def circulant(row):
    size = row.shape[1]
    return pltpu.roll(jnp.broadcast_to(row, (size, size)), 0, 1, stride=1, stride_axis=0)


def product(left, right):
    return jnp.dot(left, right, preferred_element_type=F32)


def composed(terms, lats, nlon):
    steps = len(terms)
    padded = lats + 2 * steps
    lane = lax.broadcasted_iota(jnp.int32, (padded, nlon), 1)
    rows = {0: (lane == 0).astype(F32)}
    for step_no in range(steps):
        low, high = step_no + 1, padded - step_no - 1
        c, e, w, n, s = [term[low:high] for term in terms[step_no]]
        size = high - low
        fresh = {}
        for d in range(-step_no - 1, step_no + 2):
            parts = []
            if d in rows:
                here = rows[d][1 : 1 + size]
                parts += [c * here, e * pltpu.roll(here, 1, 1), w * pltpu.roll(here, nlon - 1, 1)]
            if d - 1 in rows:
                parts.append(n * rows[d - 1][2 : 2 + size])
            if d + 1 in rows:
                parts.append(s * rows[d + 1][0:size])
            fresh[d] = functools.reduce(lambda x, y: x + y, parts)
        rows = fresh
    return rows


def swept(planes, weights):
    for step_no, (c, e, w, n, s) in enumerate(weights):
        fresh = []
        for i in range(1, len(planes) - 1):
            at, u = i + step_no, planes[i]
            nlon = u.shape[1]
            fresh.append(
                c(at) * u
                + e(at) * pltpu.roll(u, nlon - 1, 1)
                + w(at) * pltpu.roll(u, 1, 1)
                + n(at) * planes[i + 1]
                + s(at) * planes[i - 1]
            )
        planes = fresh
    return planes


def packing(pieces):
    def placed(piece):
        _, size, _, width, _, _, turn = piece
        return (width, size) if turn else (size, width)

    shapes = {}
    for piece in pieces:
        shape, out = placed(piece), piece[4]
        shapes[out] = (max(piece[5] + shape[0], shapes.get(out, (0,))[0]), shape[1])
    count = len(pieces)
    scratch = [pltpu.VMEM(piece[1:4:2], F32) for piece in pieces]
    scratch += [pltpu.VMEM(placed(piece), BF16) for piece in pieces]
    scratch += [pltpu.SemaphoreType.DMA((count,)), pltpu.SemaphoreType.DMA((count,))]

    def start(where_ref, p_ref, refs):
        first = lambda at: pl.multiple_of(where_ref[at[0]], 128) if isinstance(at, tuple) else at
        loads = []
        for k, (row, size, col, width, _, _, _) in enumerate(pieces):
            source = p_ref.at[pl.ds(first(row), size), pl.ds(first(col), width)]
            loads.append(pltpu.make_async_copy(source, refs[k], refs[2 * count].at[k]))
            loads[-1].start()
        return loads

    def finish(loads, results, refs):
        stores = []
        for k, piece in enumerate(pieces):
            loads[k].wait()
            got, made, turn, shape = refs[k], refs[count + k], piece[6], placed(piece)
            if turn:
                for a in range(0, shape[0], turn):
                    for b in range(0, shape[1], turn):
                        made[a : a + turn, b : b + turn] = got[b : b + turn, a : a + turn].T.astype(BF16)
            else:
                made[...] = got[...].astype(BF16)
            target = results[piece[4]].at[pl.ds(piece[5], shape[0]), :]
            stores.append(pltpu.make_async_copy(made, target, refs[2 * count + 1].at[k]))
            stores[-1].start()
        for copy in stores:
            copy.wait()

    return [jax.ShapeDtypeStruct(shapes[k], BF16) for k in range(len(shapes))], scratch, start, finish


def packed(covariance, where, pieces):
    out_shape, scratch, start, finish = packing(pieces)

    def kernel(where_ref, p_ref, *refs):
        results, refs = refs[: len(out_shape)], refs[len(out_shape) :]
        finish(start(where_ref, p_ref, refs), results, refs)

    return pl.pallas_call(
        kernel,
        in_specs=[pl.BlockSpec(memory_space=pltpu.SMEM), pl.BlockSpec(memory_space=pl.ANY)],
        out_specs=[pl.BlockSpec(memory_space=pl.ANY)] * len(out_shape),
        out_shape=out_shape,
        scratch_shapes=scratch,
        compiler_params=params(),
        cost_estimate=cost(1),
        name="packed",
    )(where, covariance)


def stencils(wind_table, diffusivity, wind_index, where, lat_rows, lats, nlon, covariance, pieces):
    steps, nlat = wind_index.shape
    sizes = (lat_rows, lats)
    span = 2 * steps * nlon
    pairs = lats // 2
    packs, pack_scratch, start, finish = packing(pieces)

    def kernel(table_ref, diffuse_ref, index_ref, where_ref, p_ref, *refs):
        row_out, col_out, high_out, low_out, step_out = refs[:5]
        results, scratch, refs = refs[5 : 5 + len(packs)], refs[5 + len(packs) :][:2], refs[7 + len(packs) :]
        loads = start(where_ref, p_ref, refs)
        for side, out in enumerate((row_out, col_out)):
            looked_up = scratch[side]
            terms = []
            for step_no in range(steps):
                for i in range(sizes[side] + 2 * steps):
                    lat = where_ref[5 + side] + i - steps
                    inside = jnp.logical_and(lat >= 0, lat < nlat)
                    entry = index_ref[step_no, jnp.clip(lat, 0, nlat - 1)]
                    values = (table_ref[0, entry], table_ref[1, entry], diffuse_ref[entry], inside.astype(F32))
                    for k, value in enumerate(values):
                        looked_up[k, i : i + 1, :] = jnp.full((1, nlon), value, F32)
                here = looked_up[3] > 0.5
                c, e, w, n, s = [
                    jnp.where(here, term, 0.0)
                    for term in stencil_terms(looked_up[0], looked_up[1], looked_up[2])
                ]
                terms.append((c, w, e, n, s) if side else (c, e, w, n, s))
                if side:
                    for member, value in enumerate((c, e, w, n, s)):
                        step_out[5 * step_no + member] = value
            for d, value in composed(terms, sizes[side], nlon).items():
                out[d + steps] = value
        for q in range(pairs):
            for a in range(2):
                for k in range(2 * steps):
                    d = k - (steps - 1) - a
                    high, low = split(circulant(col_out[d + steps, 2 * q + a : 2 * q + a + 1, :]))
                    at = pl.ds(q * span + k * nlon, nlon)
                    high_out[at, a * nlon : (a + 1) * nlon] = high
                    low_out[at, a * nlon : (a + 1) * nlon] = low
        finish(loads, results, refs)

    return pl.pallas_call(
        kernel,
        in_specs=[pl.BlockSpec(memory_space=pltpu.SMEM)] * 4 + [pl.BlockSpec(memory_space=pl.ANY)],
        out_specs=[pl.BlockSpec(memory_space=pltpu.VMEM)] * 5 + [pl.BlockSpec(memory_space=pl.ANY)] * len(packs),
        out_shape=[jax.ShapeDtypeStruct((2 * steps + 1, size, nlon), F32) for size in sizes]
        + [jax.ShapeDtypeStruct((pairs * span, 2 * nlon), BF16)] * 2
        + [jax.ShapeDtypeStruct((5 * steps, lats + 2 * steps, nlon), F32)]
        + packs,
        scratch_shapes=[pltpu.VMEM((4, size + 2 * steps, nlon), F32) for size in sizes]
        + pack_scratch,
        compiler_params=params(),
        cost_estimate=cost(1),
        name="stencils",
    )(wind_table.T, diffusivity, wind_index, where, covariance)


def columns_operator(
    covariance, halos, stencil, blocks, where, unit, steps, nlon, count, block_at, held=None, ends=False, work=1
):
    rows, cols = covariance.shape
    lats = cols // nlon
    wide = steps * nlon
    size = unit * nlon
    span = 2 * steps * nlon
    pairs = lats // 2
    part = nlon // 2
    upper = size - part * (3 * size // (8 * part))

    def kernel(where_ref, stencil_ref, p_ref, *rest):
        halo_refs, rest = rest[: 2 * len(halos)], rest[2 * len(halos) :]
        (b_high, b_low, step_ref), outs, data_ref = rest[:3], rest[3:-1], rest[-1]
        if held is not None:
            outs = outs[1:]
        t_ref = outs[0]
        i = pl.program_id(0)
        col_odd, row_odd = where_ref[2] != 0, where_ref[3] != 0

        @pl.when(i == 0)
        def _():
            data_ref[size:, :wide] = jnp.zeros((size, wide), BF16)
            data_ref[size:, wide + cols :] = jnp.zeros((size, wide), BF16)

        for k in range(len(halos)):
            even_ref, odd_ref = halo_refs[2 * k : 2 * k + 2]
            chosen = i >= 0 if len(halos) == 1 else i == k

            @pl.when(jnp.logical_and(chosen, col_odd))
            def _(even_ref=even_ref, odd_ref=odd_ref):
                data_ref[:size, :wide] = even_ref[...]
                data_ref[:size, wide + cols :] = odd_ref[...]

            @pl.when(jnp.logical_and(chosen, jnp.logical_not(col_odd)))
            def _(even_ref=even_ref, odd_ref=odd_ref):
                data_ref[:size, :wide] = odd_ref[...]
                data_ref[:size, wide + cols :] = even_ref[...]

        data_ref[:upper, wide : wide + cols], data_ref[size : size + upper, wide : wide + cols] = split(
            p_ref[:upper, :]
        )
        weights = [
            [
                lambda at, k=5 * step_no + member: step_ref[k, at : at + 1, :]
                for member in range(5)
            ]
            for step_no in range(steps)
        ]
        starts = list(range(upper, size, part))
        for q in range(max(pairs, len(starts))):
            if q < pairs:
                window = slice((2 * q + 1) * nlon, (2 * q + 1) * nlon + span)
                of = pl.ds(q * span, span)
                total = product(data_ref[:upper, window], b_high[of, :])
                total += product(data_ref[size : size + upper, window], b_high[of, :])
                total += product(data_ref[:upper, window], b_low[of, :])
                for a, k, d in ((0, 2 * q, -steps), (1, 2 * q + 2 * steps + 1, steps)):
                    far = slice(k * nlon, (k + 1) * nlon)
                    row = stencil_ref[d + steps, 2 * q + a : 2 * q + a + 1, :]
                    weight = jnp.sum(row, axis=1, keepdims=True)
                    far_values = data_ref[:upper, far].astype(F32) + data_ref[size : size + upper, far].astype(F32)
                    value = total[:, a * nlon : (a + 1) * nlon] + weight * far_values
                    t_ref[:upper, (2 * q + a) * nlon : (2 * q + a + 1) * nlon] = value.astype(BF16)
            if q < len(starts):
                rows_at = slice(starts[q], starts[q] + part)
                planes = []
                for k in range(lats + 2 * steps):
                    if steps <= k < steps + lats:
                        planes.append(p_ref[rows_at, (k - steps) * nlon : (k - steps + 1) * nlon])
                    else:
                        planes.append(data_ref[rows_at, k * nlon : (k + 1) * nlon].astype(F32))
                for k, plane in enumerate(swept(planes, weights)):
                    t_ref[rows_at, k * nlon : (k + 1) * nlon] = plane.astype(BF16)
        if ends:
            for odd in range(2):
                is_odd = row_odd if odd else jnp.logical_not(row_odd)

                @pl.when(jnp.logical_and(i == 0, is_odd))
                def _(odd=odd):
                    outs[2 - odd][...] = t_ref[:wide, :]

                @pl.when(jnp.logical_and(i == count - 1, is_odd))
                def _(odd=odd):
                    outs[1 + odd][...] = t_ref[size - wide :, :]

    halo_at = (lambda i, at: (i, 0)) if len(halos) == 1 else (lambda i, at: (0, 0))
    in_specs = [
        pl.BlockSpec(stencil.shape, lambda i, at: (0, 0, 0)),
        pl.BlockSpec((size, cols), lambda i, at: (block_at(i, at), 0)),
    ]
    in_specs += [pl.BlockSpec((size, wide), halo_at)] * (2 * len(halos))
    in_specs += [pl.BlockSpec(block.shape, lambda i, at, n=block.ndim: (0,) * n) for block in blocks]
    out_specs = [pl.BlockSpec((size, cols), lambda i, at: (block_at(i, at), 0))]
    out_shape = [jax.ShapeDtypeStruct((rows, cols), BF16)]
    operands = [where, stencil, covariance] + [array for pair in halos for array in pair] + list(blocks)
    aliases = {}
    if ends:
        out_specs += [pl.BlockSpec((wide, cols), lambda i, at: (0, 0))] * 2
        out_shape += [jax.ShapeDtypeStruct((wide, cols), BF16)] * 2
    if held is not None:
        in_specs.append(pl.BlockSpec(memory_space=pl.ANY))
        aliases = {len(operands): 0}
        operands.append(held)
    return pl.pallas_call(
        kernel,
        grid_spec=pltpu.PrefetchScalarGridSpec(
            num_scalar_prefetch=1,
            grid=(count,),
            in_specs=in_specs,
            out_specs=out_specs,
            scratch_shapes=[pltpu.VMEM((2 * size, cols + 2 * wide), BF16)],
        ),
        out_shape=out_shape,
        input_output_aliases=aliases,
        compiler_params=params(),
        cost_estimate=cost(work),
        name="columns_operator",
    )(*operands)


def rows_operator(values, even, odd, stencil, where, steps, nlon, out_dtype, blocks=None, noise=None):
    rows, cols = values.shape
    lat_rows = rows // nlon
    wide = steps * nlon
    size = 2 * nlon
    span = 2 * steps * nlon
    pairs = lat_rows // 2
    group = 2 if pairs % 2 == 0 else 1
    ahead = (steps + 1) // 2
    exact = values.dtype == BF16
    makes = blocks is None
    chunk = min(cols, 256)

    def kernel(where_ref, stencil_ref, x_ref, even_ref, odd_ref, *rest):
        if makes:
            out_ref, a_ref = rest[:2]
        else:
            a_ref, noise_ref, out_ref = rest[:3]
        high_ref, sem = rest[2 if makes else 3 :][:2]
        raw_ref, low_ref = (None, None) if exact else rest[-2:]
        step = pl.program_id(0)

        def load(q):
            here = pl.ds(pl.multiple_of(q * size, size), size)
            there = pl.ds(pl.multiple_of(wide + q * size, nlon), size)
            target = high_ref.at[there, :] if exact else raw_ref.at[here, :]
            return pltpu.make_async_copy(x_ref.at[here, :], target, sem.at[q])

        def ready(q):
            load(q).wait()
            if not exact:
                there = pl.ds(pl.multiple_of(wide + q * size, nlon), size)
                here = pl.ds(pl.multiple_of(q * size, size), size)
                high_ref[there, :], low_ref[there, :] = split(raw_ref[here, :])

        @pl.when(step == 0)
        def _():
            is_odd = where_ref[3]
            at_even = pl.ds(pl.multiple_of((1 - is_odd) * (wide + rows), nlon), wide)
            at_odd = pl.ds(pl.multiple_of(is_odd * (wide + rows), nlon), wide)
            halos = [
                pltpu.make_async_copy(even_ref, high_ref.at[at_even, :], sem.at[pairs]),
                pltpu.make_async_copy(odd_ref, high_ref.at[at_odd, :], sem.at[pairs + 1]),
            ]
            for halo in halos:
                halo.start()
            for q in range(pairs):
                load(q).start()
            if not exact:
                low_ref[:wide, :] = jnp.zeros((wide, cols), BF16)
                low_ref[wide + rows :, :] = jnp.zeros((wide, cols), BF16)
            for halo in halos:
                halo.wait()
            for q in range(min(ahead, pairs)):
                ready(q)

        for j in range(group):
            q = step * group + j + ahead

            @pl.when(q < pairs)
            def _(q=q):
                ready(q)

        row = lambda j, d, a: stencil_ref[d + steps, pl.ds(2 * (step * group + j) + a, 1), :]
        if makes:
            for j in range(group):
                for a in range(2):
                    for k in range(2 * steps):
                        high, low = split(circulant(row(j, k - (steps - 1) - a, a)))
                        top = 2 * j * size + a * nlon
                        a_ref[top : top + nlon, k * nlon : (k + 1) * nlon] = high
                        a_ref[top + size : top + size + nlon, k * nlon : (k + 1) * nlon] = low
        for j in range(group):
            unit = lambda k: pl.multiple_of((2 * (step * group + j) + k) * nlon, nlon)
            weights = [jnp.sum(row(j, d, a), axis=1, keepdims=True) for a, d in ((0, -steps), (1, steps))]
            top = 2 * j * size
            for lane in range(0, cols, chunk):
                lanes = slice(lane, lane + chunk)
                both = product(a_ref[top : top + 2 * size, :], high_ref[pl.ds(unit(1), span), lanes])
                total = both[:size] + both[size:]
                if not exact:
                    total += product(a_ref[top : top + size, :], low_ref[pl.ds(unit(1), span), lanes])
                for a, k in ((0, 0), (1, 2 * steps + 1)):
                    far = high_ref[pl.ds(unit(k), nlon), lanes].astype(F32)
                    if not exact:
                        far += low_ref[pl.ds(unit(k), nlon), lanes].astype(F32)
                    value = total[a * nlon : (a + 1) * nlon, :] + weights[a] * far
                    out_ref[j * size + a * nlon : j * size + (a + 1) * nlon, lanes] = value.astype(out_dtype)
        if noise is not None:
            for a in range(2 * group):
                lat = 2 * group * step + a - where_ref[4]

                @pl.when(jnp.logical_and(lat >= 0, lat < cols // nlon))
                def _(a=a, lat=lat):
                    lanes = pl.ds(pl.multiple_of(lat * nlon, nlon), nlon)
                    eye = lax.broadcasted_iota(jnp.int32, (nlon, nlon), 0) == lax.broadcasted_iota(
                        jnp.int32, (nlon, nlon), 1
                    )
                    added = jnp.where(eye, noise_ref[pl.ds(2 * group * step + a, 1), :], 0.0)
                    out_ref[a * nlon : (a + 1) * nlon, lanes] += added

    in_specs = [pl.BlockSpec(stencil.shape, lambda g, at: (0, 0, 0))] + [pl.BlockSpec(memory_space=pl.ANY)] * 3
    operands = [where, stencil, values, even, odd]
    out_specs = [pl.BlockSpec((group * size, cols), lambda g, at: (g, 0))]
    out_shape = [jax.ShapeDtypeStruct((rows, cols), out_dtype)]
    blocks_spec = pl.BlockSpec((2 * group * size, span), lambda g, at: (g, 0))
    if makes:
        out_specs.append(blocks_spec)
        out_shape.append(jax.ShapeDtypeStruct((2 * rows, span), BF16))
    else:
        in_specs += [blocks_spec, pl.BlockSpec(noise.shape, lambda g, at: (0, 0))]
        operands += [blocks, noise]
    return pl.pallas_call(
        kernel,
        grid_spec=pltpu.PrefetchScalarGridSpec(
            num_scalar_prefetch=1,
            grid=(pairs // group,),
            in_specs=in_specs,
            out_specs=out_specs,
            scratch_shapes=[pltpu.VMEM((rows + 2 * wide, cols), BF16), pltpu.SemaphoreType.DMA((pairs + 2,))]
            + ([] if exact else [pltpu.VMEM((rows, cols), F32), pltpu.VMEM((rows + 2 * wide, cols), BF16)]),
        ),
        out_shape=out_shape,
        compiler_params=params(),
        cost_estimate=cost(1),
        name="rows_operator",
    )(*operands)


def shifted(block, axis, by):
    size = lax.axis_size(axis)
    pairs = [(i, i + by) for i in range(size) if 0 <= i + by < size]
    return lax.ppermute(block, axis, pairs)


def gathered(first, last, axis, dim, unit, halo, own):
    before, after = [], []
    need, hop = halo, 1
    while need > 0:
        take = min(own, need)
        size = first.shape[dim]
        before.insert(0, shifted(lax.slice_in_dim(last, size - take * unit, size, axis=dim), axis, hop))
        after.append(shifted(lax.slice_in_dim(first, 0, take * unit, axis=dim), axis, -hop))
        need, hop = need - take, hop + 1
    join = lambda parts: parts[0] if len(parts) == 1 else jnp.concatenate(parts, axis=dim)
    return join(before), join(after)


def exchanged(block, axis, odd):
    pairs = []
    for i in range(odd, lax.axis_size(axis) - 1, 2):
        pairs += [(i, i + 1), (i + 1, i)]
    return lax.ppermute(block, axis, pairs)


def mirrored(block, odd):
    n_row, n_col = lax.axis_size("row"), lax.axis_size("col")
    pairs = []
    for a in range(n_row):
        for b in range(n_col):
            to = 2 * a + (1 - b % 2) + (1 if (b + odd) % 2 else -1)
            if 0 <= to < n_col:
                pairs.append((a * n_col + b, (b // 2) * n_col + to))
    return lax.ppermute(block, ("row", "col"), pairs)


def body(covariance, noise_var, wind_table, diffusivity, wind_index):
    rows_dev, cols_dev = covariance.shape
    lat_rows, nlon = noise_var.shape
    steps, nlat = wind_index.shape
    lats = cols_dev // nlon
    row_id, col_id = lax.axis_index("row"), lax.axis_index("col")
    own = lat_rows // 4
    fits = lat_rows == 2 * lats and own % 2 == 0 and own >= steps and own <= lats - steps
    if not fits or lax.axis_size("col") != 2 * lax.axis_size("row"):
        return plain_body(covariance, noise_var, wind_table, diffusivity, wind_index)

    near = lat_rows // 2 - own
    middle = lat_rows // 2
    outer, inner, wide = near * nlon, own * nlon, steps * nlon
    pick = lambda parity, even, odd: even + parity * (odd - even)
    col_odd, row_odd = col_id % 2, row_id % 2
    mirror_at, direct_at = pick(col_odd, middle - own, middle), pick(col_odd, middle, middle - own)
    diagonal = col_id * lats - row_id * lat_rows
    where = jnp.stack(
        [
            mirror_at // own,
            direct_at // own,
            col_odd,
            row_odd,
            diagonal,
            row_id * lat_rows,
            col_id * lats,
            mirror_at * nlon,
            pick(col_odd, lats, lats - steps) * nlon,
            pick(col_odd, 2 * lats - steps, 0) * nlon,
            pick(col_odd, lats - own, 0) * nlon,
            pick(col_odd, cols_dev - wide, 0),
            pick(col_odd, 0, cols_dev - wide),
            pick(row_odd, rows_dev - wide, 0),
            pick(row_odd, 0, rows_dev - wide),
        ]
    ).astype(jnp.int32)
    pieces = [
        (row, outer, (11 + k,), wide, k, there, 0)
        for row, there in ((0, 0), (rows_dev - outer, outer))
        for k in range(2)
    ]
    pieces += [((13 + k,), wide, 0, cols_dev, k + 2, 0, 0) for k in range(2)]
    others = [((8 + k,), wide, (10,), inner, k, 0, nlon) for k in range(2)]
    others += [((7,), inner, (11 + k,), wide, k + 2, 0, 0) for k in range(2)]
    sent = packed(covariance, where, pieces)
    outers, ends = list(sent[:2]), list(sent[2:])
    outers = [exchanged(piece, "col", k) for k, piece in enumerate(outers)]
    ends = [exchanged(piece, "row", k) for k, piece in enumerate(ends)]
    wind_index, ends[0] = lax.optimization_barrier((wind_index, ends[0]))
    row_s, col_s, *rest = stencils(
        wind_table, diffusivity, wind_index, where, lat_rows, lats, nlon, covariance, others
    )
    col_blocks, mirrors, inners = rest[:3], rest[3:5], rest[5:7]
    mirrors = [mirrored(piece, k) for k, piece in enumerate(mirrors)]

    operator_times_prior, blocks = rows_operator(covariance, *ends, row_s, where, steps, nlon, BF16)
    inners[0] = exchanged(inners[0], "col", 0)
    operator_times_prior, outers, inners[1] = lax.optimization_barrier(
        (operator_times_prior, outers, inners[1])
    )
    inners[1] = exchanged(inners[1], "col", 1)
    mirror, *ends = columns_operator(
        covariance, [outers], col_s, col_blocks, where, near, steps, nlon, 2, lambda i, at: i * (lat_rows // near - 1),
        None, True,
    )
    ends = [exchanged(piece, "row", k) for k, piece in enumerate(ends)]
    (mirror,) = columns_operator(
        covariance, [mirrors, inners], col_s, col_blocks, where, own, steps, nlon, 2, lambda i, at: at[i], mirror, False,
        10 ** 13,
    )
    (predicted_spread_matrix,) = rows_operator(
        mirror, *ends, row_s, where, steps, nlon, F32, blocks, noise_var
    )
    return (predicted_spread_matrix, operator_times_prior)


def plain_body(covariance, noise_var, wind_table, diffusivity, wind_index):
    rows_dev, cols_dev = covariance.shape
    lat_rows, nlon = noise_var.shape
    steps, nlat = wind_index.shape
    lats = cols_dev // nlon
    row_id, col_id = lax.axis_index("row"), lax.axis_index("col")
    sent = covariance.astype(BF16)
    sides = gathered(sent, sent, "col", 1, nlon, steps, lats)
    ends = gathered(sent, sent, "row", 0, nlon, steps, lat_rows)
    firsts = (row_id * lat_rows, col_id * lats)
    where = jnp.stack([0, 0, 1, 1, firsts[1] - firsts[0], *firsts]).astype(jnp.int32)
    row_s, col_s, *col_blocks = stencils(
        wind_table, diffusivity, wind_index, where, lat_rows, lats, nlon, covariance, []
    )
    operator_times_prior, blocks = rows_operator(covariance, *ends, row_s, where, steps, nlon, BF16)
    (mirror,) = columns_operator(
        covariance, [sides], col_s, col_blocks, where, 2, steps, nlon, lat_rows // 2, lambda i, at: i
    )
    ends = gathered(mirror, mirror, "row", 0, nlon, steps, lat_rows)
    (predicted_spread_matrix,) = rows_operator(
        mirror, *ends, row_s, where, steps, nlon, F32, blocks, noise_var
    )
    return (predicted_spread_matrix, operator_times_prior)


def solution(mesh):
    in_specs = (P("row", "col"), P("row", None), P(), P(), P())
    out_specs = (P("row", "col"), P("row", "col"))
    return jax.shard_map(body, mesh=mesh, in_specs=in_specs, out_specs=out_specs, check_vma=False)
```

```python
import functools

import jax
import jax.numpy as jnp
from jax import lax
from jax.experimental import pallas as pl
from jax.experimental.pallas import tpu as pltpu
from jax.sharding import PartitionSpec as P

F32 = jnp.float32
BF16 = jnp.bfloat16
VMEM_LIMIT = 63 * 1024 * 1024


def params():
    return pltpu.CompilerParams(vmem_limit_bytes=VMEM_LIMIT)


def cost(work):
    return pl.CostEstimate(flops=work, bytes_accessed=work, transcendentals=0)


def stencil_terms(zonal_cour, merid_cour, diffuse):
    middle_weight = 1.0 - zonal_cour * zonal_cour - merid_cour * merid_cour - 4.0 * diffuse
    eastward_weight = 0.5 * zonal_cour * zonal_cour - 0.5 * zonal_cour + diffuse
    west_w = 0.5 * zonal_cour * zonal_cour + 0.5 * zonal_cour + diffuse
    north_w = 0.5 * merid_cour * merid_cour - 0.5 * merid_cour + diffuse
    south_w = 0.5 * merid_cour * merid_cour + 0.5 * merid_cour + diffuse
    return middle_weight, eastward_weight, west_w, north_w, south_w


def split(values):
    high = values.astype(BF16)
    return high, (values - high.astype(F32)).astype(BF16)


def circulant(row):
    size = row.shape[1]
    return pltpu.roll(jnp.broadcast_to(row, (size, size)), 0, 1, stride=1, stride_axis=0)


def product(left, right):
    return jnp.dot(left, right, preferred_element_type=F32)


def composed(terms, lats, nlon):
    steps = len(terms)
    padded = lats + 2 * steps
    lane = lax.broadcasted_iota(jnp.int32, (padded, nlon), 1)
    rows = {0: (lane == 0).astype(F32)}
    for step_no in range(steps):
        low, high = step_no + 1, padded - step_no - 1
        c, e, w, n, s = [term[low:high] for term in terms[step_no]]
        size = high - low
        fresh = {}
        for d in range(-step_no - 1, step_no + 2):
            parts = []
            if d in rows:
                here = rows[d][1 : 1 + size]
                parts += [c * here, e * pltpu.roll(here, 1, 1), w * pltpu.roll(here, nlon - 1, 1)]
            if d - 1 in rows:
                parts.append(n * rows[d - 1][2 : 2 + size])
            if d + 1 in rows:
                parts.append(s * rows[d + 1][0:size])
            fresh[d] = functools.reduce(lambda x, y: x + y, parts)
        rows = fresh
    return rows


def swept(planes, weights):
    for step_no, (c, e, w, n, s) in enumerate(weights):
        fresh = []
        for i in range(1, len(planes) - 1):
            at, u = i + step_no, planes[i]
            nlon = u.shape[1]
            fresh.append(
                c(at) * u
                + e(at) * pltpu.roll(u, nlon - 1, 1)
                + w(at) * pltpu.roll(u, 1, 1)
                + n(at) * planes[i + 1]
                + s(at) * planes[i - 1]
            )
        planes = fresh
    return planes


def packing(pieces):
    def placed(piece):
        _, size, _, width, _, _, turn = piece
        return (width, size) if turn else (size, width)

    shapes = {}
    for piece in pieces:
        shape, out = placed(piece), piece[4]
        shapes[out] = (max(piece[5] + shape[0], shapes.get(out, (0,))[0]), shape[1])
    count = len(pieces)
    scratch = [pltpu.VMEM(piece[1:4:2], F32) for piece in pieces]
    scratch += [pltpu.VMEM(placed(piece), BF16) for piece in pieces]
    scratch += [pltpu.SemaphoreType.DMA((count,)), pltpu.SemaphoreType.DMA((count,))]

    def start(where_ref, p_ref, refs):
        first = lambda at: pl.multiple_of(where_ref[at[0]] + sum(at[1:]), 128) if isinstance(at, tuple) else at
        loads = []
        for k, (row, size, col, width, _, _, _) in enumerate(pieces):
            source = p_ref.at[pl.ds(first(row), size), pl.ds(first(col), width)]
            loads.append(pltpu.make_async_copy(source, refs[k], refs[2 * count].at[k]))
            loads[-1].start()
        return loads

    def finish(loads, results, refs):
        stores = []
        for k, piece in enumerate(pieces):
            loads[k].wait()
            got, made, turn, shape = refs[k], refs[count + k], piece[6], placed(piece)
            if turn:
                for a in range(0, shape[0], turn):
                    for b in range(0, shape[1], turn):
                        made[a : a + turn, b : b + turn] = got[b : b + turn, a : a + turn].T.astype(BF16)
            else:
                made[...] = got[...].astype(BF16)
            target = results[piece[4]].at[pl.ds(piece[5], shape[0]), :]
            stores.append(pltpu.make_async_copy(made, target, refs[2 * count + 1].at[k]))
            stores[-1].start()
        for copy in stores:
            copy.wait()

    return [jax.ShapeDtypeStruct(shapes[k], BF16) for k in range(len(shapes))], scratch, start, finish


def packed(covariance, where, pieces):
    out_shape, scratch, start, finish = packing(pieces)

    def kernel(where_ref, p_ref, *refs):
        results, refs = refs[: len(out_shape)], refs[len(out_shape) :]
        finish(start(where_ref, p_ref, refs), results, refs)

    return pl.pallas_call(
        kernel,
        in_specs=[pl.BlockSpec(memory_space=pltpu.SMEM), pl.BlockSpec(memory_space=pl.ANY)],
        out_specs=[pl.BlockSpec(memory_space=pl.ANY)] * len(out_shape),
        out_shape=out_shape,
        scratch_shapes=scratch,
        compiler_params=params(),
        cost_estimate=cost(1),
        name="packed",
    )(where, covariance)


def stencils(wind_table, diffusivity, wind_index, where, lat_rows, lats, nlon, covariance, pieces):
    steps, nlat = wind_index.shape
    sizes = (lat_rows, lats)
    span = 2 * steps * nlon
    pairs = lats // 2
    packs, pack_scratch, start, finish = packing(pieces)

    def kernel(table_ref, diffuse_ref, index_ref, where_ref, p_ref, *refs):
        row_out, col_out, high_out, low_out, step_out = refs[:5]
        results, scratch, refs = refs[5 : 5 + len(packs)], refs[5 + len(packs) :][:2], refs[7 + len(packs) :]
        loads = start(where_ref, p_ref, refs)
        for side, out in enumerate((row_out, col_out)):
            looked_up = scratch[side]
            terms = []
            for step_no in range(steps):
                for i in range(sizes[side] + 2 * steps):
                    lat = where_ref[5 + side] + i - steps
                    inside = jnp.logical_and(lat >= 0, lat < nlat)
                    entry = index_ref[step_no, jnp.clip(lat, 0, nlat - 1)]
                    values = (table_ref[0, entry], table_ref[1, entry], diffuse_ref[entry], inside.astype(F32))
                    for k, value in enumerate(values):
                        looked_up[k, i : i + 1, :] = jnp.full((1, nlon), value, F32)
                here = looked_up[3] > 0.5
                c, e, w, n, s = [
                    jnp.where(here, term, 0.0)
                    for term in stencil_terms(looked_up[0], looked_up[1], looked_up[2])
                ]
                terms.append((c, w, e, n, s) if side else (c, e, w, n, s))
                if side:
                    for member, value in enumerate((c, e, w, n, s)):
                        step_out[5 * step_no + member] = value
            for d, value in composed(terms, sizes[side], nlon).items():
                out[d + steps] = value
        for q in range(pairs):
            for a in range(2):
                for k in range(2 * steps):
                    d = k - (steps - 1) - a
                    high, low = split(circulant(col_out[d + steps, 2 * q + a : 2 * q + a + 1, :]))
                    at = pl.ds(q * span + k * nlon, nlon)
                    high_out[at, a * nlon : (a + 1) * nlon] = high
                    low_out[at, a * nlon : (a + 1) * nlon] = low
        finish(loads, results, refs)

    return pl.pallas_call(
        kernel,
        in_specs=[pl.BlockSpec(memory_space=pltpu.SMEM)] * 4 + [pl.BlockSpec(memory_space=pl.ANY)],
        out_specs=[pl.BlockSpec(memory_space=pltpu.VMEM)] * 5 + [pl.BlockSpec(memory_space=pl.ANY)] * len(packs),
        out_shape=[jax.ShapeDtypeStruct((2 * steps + 1, size, nlon), F32) for size in sizes]
        + [jax.ShapeDtypeStruct((pairs * span, 2 * nlon), BF16)] * 2
        + [jax.ShapeDtypeStruct((5 * steps, lats + 2 * steps, nlon), F32)]
        + packs,
        scratch_shapes=[pltpu.VMEM((4, size + 2 * steps, nlon), F32) for size in sizes]
        + pack_scratch,
        compiler_params=params(),
        cost_estimate=cost(1),
        name="stencils",
    )(wind_table.T, diffusivity, wind_index, where, covariance)


def columns_operator(
    covariance, halos, stencil, blocks, where, unit, steps, nlon, count, block_at, held=None, ends=False, work=1
):
    rows, cols = covariance.shape
    lats = cols // nlon
    wide = steps * nlon
    size = unit * nlon
    span = 2 * steps * nlon
    pairs = lats // 2
    part = nlon // 2
    upper = size - part * (3 * size // (8 * part))

    def kernel(where_ref, stencil_ref, p_ref, *rest):
        halo_refs, rest = rest[: 2 * len(halos)], rest[2 * len(halos) :]
        (b_high, b_low, step_ref), outs, data_ref = rest[:3], rest[3:-1], rest[-1]
        if held is not None:
            outs = outs[1:]
        t_ref = outs[0]
        i = pl.program_id(0)
        col_odd, row_odd = where_ref[2] != 0, where_ref[3] != 0

        @pl.when(i == 0)
        def _():
            data_ref[size:, :wide] = jnp.zeros((size, wide), BF16)
            data_ref[size:, wide + cols :] = jnp.zeros((size, wide), BF16)

        for k in range(len(halos)):
            even_ref, odd_ref = halo_refs[2 * k : 2 * k + 2]
            chosen = i >= 0 if len(halos) == 1 else i == k

            @pl.when(jnp.logical_and(chosen, col_odd))
            def _(even_ref=even_ref, odd_ref=odd_ref):
                data_ref[:size, :wide] = even_ref[...]
                data_ref[:size, wide + cols :] = odd_ref[...]

            @pl.when(jnp.logical_and(chosen, jnp.logical_not(col_odd)))
            def _(even_ref=even_ref, odd_ref=odd_ref):
                data_ref[:size, :wide] = odd_ref[...]
                data_ref[:size, wide + cols :] = even_ref[...]

        data_ref[:upper, wide : wide + cols], data_ref[size : size + upper, wide : wide + cols] = split(
            p_ref[:upper, :]
        )
        weights = [
            [
                lambda at, k=5 * step_no + member: step_ref[k, at : at + 1, :]
                for member in range(5)
            ]
            for step_no in range(steps)
        ]
        starts = list(range(upper, size, part))
        for q in range(max(pairs, len(starts))):
            if q < pairs:
                window = slice((2 * q + 1) * nlon, (2 * q + 1) * nlon + span)
                of = pl.ds(q * span, span)
                total = product(data_ref[:upper, window], b_high[of, :])
                total += product(data_ref[size : size + upper, window], b_high[of, :])
                total += product(data_ref[:upper, window], b_low[of, :])
                for a, k, d in ((0, 2 * q, -steps), (1, 2 * q + 2 * steps + 1, steps)):
                    far = slice(k * nlon, (k + 1) * nlon)
                    row = stencil_ref[d + steps, 2 * q + a : 2 * q + a + 1, :]
                    weight = jnp.sum(row, axis=1, keepdims=True)
                    far_values = data_ref[:upper, far].astype(F32) + data_ref[size : size + upper, far].astype(F32)
                    value = total[:, a * nlon : (a + 1) * nlon] + weight * far_values
                    t_ref[:upper, (2 * q + a) * nlon : (2 * q + a + 1) * nlon] = value.astype(BF16)
            if q < len(starts):
                rows_at = slice(starts[q], starts[q] + part)
                planes = []
                for k in range(lats + 2 * steps):
                    if steps <= k < steps + lats:
                        planes.append(p_ref[rows_at, (k - steps) * nlon : (k - steps + 1) * nlon])
                    else:
                        planes.append(data_ref[rows_at, k * nlon : (k + 1) * nlon].astype(F32))
                for k, plane in enumerate(swept(planes, weights)):
                    t_ref[rows_at, k * nlon : (k + 1) * nlon] = plane.astype(BF16)
        if ends:
            for odd in range(2):
                is_odd = row_odd if odd else jnp.logical_not(row_odd)

                @pl.when(jnp.logical_and(i == 0, is_odd))
                def _(odd=odd):
                    outs[2 - odd][...] = t_ref[:wide, :]

                @pl.when(jnp.logical_and(i == count - 1, is_odd))
                def _(odd=odd):
                    outs[1 + odd][...] = t_ref[size - wide :, :]

    halo_at = (lambda i, at: (i, 0)) if len(halos) == 1 else (lambda i, at: (0, 0))
    in_specs = [
        pl.BlockSpec(stencil.shape, lambda i, at: (0, 0, 0)),
        pl.BlockSpec((size, cols), lambda i, at: (block_at(i, at), 0)),
    ]
    in_specs += [pl.BlockSpec((size, wide), halo_at)] * (2 * len(halos))
    in_specs += [pl.BlockSpec(block.shape, lambda i, at, n=block.ndim: (0,) * n) for block in blocks]
    out_specs = [pl.BlockSpec((size, cols), lambda i, at: (block_at(i, at), 0))]
    out_shape = [jax.ShapeDtypeStruct((rows, cols), BF16)]
    operands = [where, stencil, covariance] + [array for pair in halos for array in pair] + list(blocks)
    aliases = {}
    if ends:
        out_specs += [pl.BlockSpec((wide, cols), lambda i, at: (0, 0))] * 2
        out_shape += [jax.ShapeDtypeStruct((wide, cols), BF16)] * 2
    if held is not None:
        in_specs.append(pl.BlockSpec(memory_space=pl.ANY))
        aliases = {len(operands): 0}
        operands.append(held)
    return pl.pallas_call(
        kernel,
        grid_spec=pltpu.PrefetchScalarGridSpec(
            num_scalar_prefetch=1,
            grid=(count,),
            in_specs=in_specs,
            out_specs=out_specs,
            scratch_shapes=[pltpu.VMEM((2 * size, cols + 2 * wide), BF16)],
        ),
        out_shape=out_shape,
        input_output_aliases=aliases,
        compiler_params=params(),
        cost_estimate=cost(work),
        name="columns_operator",
    )(*operands)


def rows_operator(values, even, odd, stencil, where, steps, nlon, out_dtype, blocks=None, noise=None):
    rows, cols = values.shape
    lat_rows = rows // nlon
    wide = steps * nlon
    size = 2 * nlon
    span = 2 * steps * nlon
    pairs = lat_rows // 2
    group = 2 if pairs % 2 == 0 else 1
    ahead = (steps + 1) // 2
    exact = values.dtype == BF16
    makes = blocks is None
    chunk = min(cols, 256)

    def kernel(where_ref, stencil_ref, x_ref, even_ref, odd_ref, *rest):
        if makes:
            out_ref, a_ref = rest[:2]
        else:
            a_ref, noise_ref, out_ref = rest[:3]
        high_ref, sem = rest[2 if makes else 3 :][:2]
        raw_ref, low_ref = (None, None) if exact else rest[-2:]
        step = pl.program_id(0)

        def load(q):
            here = pl.ds(pl.multiple_of(q * size, size), size)
            there = pl.ds(pl.multiple_of(wide + q * size, nlon), size)
            target = high_ref.at[there, :] if exact else raw_ref.at[here, :]
            return pltpu.make_async_copy(x_ref.at[here, :], target, sem.at[q])

        def ready(q):
            load(q).wait()
            if not exact:
                there = pl.ds(pl.multiple_of(wide + q * size, nlon), size)
                here = pl.ds(pl.multiple_of(q * size, size), size)
                high_ref[there, :], low_ref[there, :] = split(raw_ref[here, :])

        @pl.when(step == 0)
        def _():
            is_odd = where_ref[3]
            at_even = pl.ds(pl.multiple_of((1 - is_odd) * (wide + rows), nlon), wide)
            at_odd = pl.ds(pl.multiple_of(is_odd * (wide + rows), nlon), wide)
            halos = [
                pltpu.make_async_copy(even_ref, high_ref.at[at_even, :], sem.at[pairs]),
                pltpu.make_async_copy(odd_ref, high_ref.at[at_odd, :], sem.at[pairs + 1]),
            ]
            for halo in halos:
                halo.start()
            for q in range(pairs):
                load(q).start()
            if not exact:
                low_ref[:wide, :] = jnp.zeros((wide, cols), BF16)
                low_ref[wide + rows :, :] = jnp.zeros((wide, cols), BF16)
            for halo in halos:
                halo.wait()
            for q in range(min(ahead, pairs)):
                ready(q)

        for j in range(group):
            q = step * group + j + ahead

            @pl.when(q < pairs)
            def _(q=q):
                ready(q)

        row = lambda j, d, a: stencil_ref[d + steps, pl.ds(2 * (step * group + j) + a, 1), :]
        if makes:
            for j in range(group):
                for a in range(2):
                    for k in range(2 * steps):
                        high, low = split(circulant(row(j, k - (steps - 1) - a, a)))
                        top = 2 * j * size + a * nlon
                        a_ref[top : top + nlon, k * nlon : (k + 1) * nlon] = high
                        a_ref[top + size : top + size + nlon, k * nlon : (k + 1) * nlon] = low
        for j in range(group):
            unit = lambda k: pl.multiple_of((2 * (step * group + j) + k) * nlon, nlon)
            weights = [jnp.sum(row(j, d, a), axis=1, keepdims=True) for a, d in ((0, -steps), (1, steps))]
            top = 2 * j * size
            for lane in range(0, cols, chunk):
                lanes = slice(lane, lane + chunk)
                both = product(a_ref[top : top + 2 * size, :], high_ref[pl.ds(unit(1), span), lanes])
                total = both[:size] + both[size:]
                if not exact:
                    total += product(a_ref[top : top + size, :], low_ref[pl.ds(unit(1), span), lanes])
                for a, k in ((0, 0), (1, 2 * steps + 1)):
                    far = high_ref[pl.ds(unit(k), nlon), lanes].astype(F32)
                    if not exact:
                        far += low_ref[pl.ds(unit(k), nlon), lanes].astype(F32)
                    value = total[a * nlon : (a + 1) * nlon, :] + weights[a] * far
                    out_ref[j * size + a * nlon : j * size + (a + 1) * nlon, lanes] = value.astype(out_dtype)
        if noise is not None:
            for a in range(2 * group):
                lat = 2 * group * step + a - where_ref[4]

                @pl.when(jnp.logical_and(lat >= 0, lat < cols // nlon))
                def _(a=a, lat=lat):
                    lanes = pl.ds(pl.multiple_of(lat * nlon, nlon), nlon)
                    eye = lax.broadcasted_iota(jnp.int32, (nlon, nlon), 0) == lax.broadcasted_iota(
                        jnp.int32, (nlon, nlon), 1
                    )
                    added = jnp.where(eye, noise_ref[pl.ds(2 * group * step + a, 1), :], 0.0)
                    out_ref[a * nlon : (a + 1) * nlon, lanes] += added

    in_specs = [pl.BlockSpec(stencil.shape, lambda g, at: (0, 0, 0))] + [pl.BlockSpec(memory_space=pl.ANY)] * 3
    operands = [where, stencil, values, even, odd]
    out_specs = [pl.BlockSpec((group * size, cols), lambda g, at: (g, 0))]
    out_shape = [jax.ShapeDtypeStruct((rows, cols), out_dtype)]
    blocks_spec = pl.BlockSpec((2 * group * size, span), lambda g, at: (g, 0))
    if makes:
        out_specs.append(blocks_spec)
        out_shape.append(jax.ShapeDtypeStruct((2 * rows, span), BF16))
    else:
        in_specs += [blocks_spec, pl.BlockSpec(noise.shape, lambda g, at: (0, 0))]
        operands += [blocks, noise]
    return pl.pallas_call(
        kernel,
        grid_spec=pltpu.PrefetchScalarGridSpec(
            num_scalar_prefetch=1,
            grid=(pairs // group,),
            in_specs=in_specs,
            out_specs=out_specs,
            scratch_shapes=[pltpu.VMEM((rows + 2 * wide, cols), BF16), pltpu.SemaphoreType.DMA((pairs + 2,))]
            + ([] if exact else [pltpu.VMEM((rows, cols), F32), pltpu.VMEM((rows + 2 * wide, cols), BF16)]),
        ),
        out_shape=out_shape,
        compiler_params=params(),
        cost_estimate=cost(1),
        name="rows_operator",
    )(*operands)


def shifted(block, axis, by):
    size = lax.axis_size(axis)
    pairs = [(i, i + by) for i in range(size) if 0 <= i + by < size]
    return lax.ppermute(block, axis, pairs)


def gathered(first, last, axis, dim, unit, halo, own):
    before, after = [], []
    need, hop = halo, 1
    while need > 0:
        take = min(own, need)
        size = first.shape[dim]
        before.insert(0, shifted(lax.slice_in_dim(last, size - take * unit, size, axis=dim), axis, hop))
        after.append(shifted(lax.slice_in_dim(first, 0, take * unit, axis=dim), axis, -hop))
        need, hop = need - take, hop + 1
    join = lambda parts: parts[0] if len(parts) == 1 else jnp.concatenate(parts, axis=dim)
    return join(before), join(after)


def exchanged(block, axis, odd):
    pairs = []
    for i in range(odd, lax.axis_size(axis) - 1, 2):
        pairs += [(i, i + 1), (i + 1, i)]
    return lax.ppermute(block, axis, pairs)


def mirrored(block, odd):
    n_row, n_col = lax.axis_size("row"), lax.axis_size("col")
    pairs = []
    for a in range(n_row):
        for b in range(n_col):
            to = 2 * a + (1 - b % 2) + (1 if (b + odd) % 2 else -1)
            if 0 <= to < n_col:
                pairs.append((a * n_col + b, (b // 2) * n_col + to))
    return lax.ppermute(block, ("row", "col"), pairs)


def body(covariance, noise_var, wind_table, diffusivity, wind_index):
    rows_dev, cols_dev = covariance.shape
    lat_rows, nlon = noise_var.shape
    steps, nlat = wind_index.shape
    lats = cols_dev // nlon
    row_id, col_id = lax.axis_index("row"), lax.axis_index("col")
    own = lat_rows // 4
    fits = lat_rows == 2 * lats and own % 2 == 0 and own >= steps and own <= lats - steps
    if not fits or lax.axis_size("col") != 2 * lax.axis_size("row"):
        return plain_body(covariance, noise_var, wind_table, diffusivity, wind_index)

    near = lat_rows // 2 - own
    middle = lat_rows // 2
    outer, inner, wide = near * nlon, own * nlon, steps * nlon
    pick = lambda parity, even, odd: even + parity * (odd - even)
    col_odd, row_odd = col_id % 2, row_id % 2
    mirror_at, direct_at = pick(col_odd, middle - own, middle), pick(col_odd, middle, middle - own)
    diagonal = col_id * lats - row_id * lat_rows
    where = jnp.stack(
        [
            mirror_at // own,
            direct_at // own,
            col_odd,
            row_odd,
            diagonal,
            row_id * lat_rows,
            col_id * lats,
            mirror_at * nlon,
            pick(col_odd, lats, lats - steps) * nlon,
            pick(col_odd, 2 * lats - steps, 0) * nlon,
            pick(col_odd, lats - own, 0) * nlon,
            pick(col_odd, cols_dev - wide, 0),
            pick(col_odd, 0, cols_dev - wide),
            pick(row_odd, rows_dev - wide, 0),
            pick(row_odd, 0, rows_dev - wide),
        ]
    ).astype(jnp.int32)
    half = outer // 2
    spans = [(0, half, 0), (half, half, half)]
    spans += [(rows_dev - outer, half, outer), (rows_dev - half, half, outer + half), (0, 16, 2 * outer)]
    pieces = [(row, size, (11 + k,), wide, k, there, 0) for row, size, there in spans for k in range(2)]
    pieces += [((13 + k, j * nlon), nlon, 0, cols_dev, k + 2, j * nlon, 0) for k in range(2) for j in range(steps)]
    others = [((8 + k,), wide, (10,), inner, k, 0, nlon) for k in range(2)]
    others += [((7,), inner, (11 + k,), wide, k + 2, 0, 0) for k in range(2)]
    sent = packed(covariance, where, pieces)
    outers, ends = list(sent[:2]), list(sent[2:])
    outers = [exchanged(piece, "col", k) for k, piece in enumerate(outers)]
    ends = [exchanged(piece, "row", k) for k, piece in enumerate(ends)]
    row_s, col_s, *rest = stencils(
        wind_table, diffusivity, wind_index, where, lat_rows, lats, nlon, covariance, others
    )
    col_blocks, mirrors, inners = rest[:3], rest[3:5], rest[5:7]
    mirrors = [mirrored(piece, k) for k, piece in enumerate(mirrors)]

    operator_times_prior, blocks = rows_operator(covariance, *ends, row_s, where, steps, nlon, BF16)
    inners[0] = exchanged(inners[0], "col", 0)
    operator_times_prior, outers, inners[1] = lax.optimization_barrier(
        (operator_times_prior, outers, inners[1])
    )
    inners[1] = exchanged(inners[1], "col", 1)
    mirror, *ends = columns_operator(
        covariance, [outers], col_s, col_blocks, where, near, steps, nlon, 2, lambda i, at: i * (lat_rows // near - 1),
        None, True,
    )
    ends = [exchanged(piece, "row", k) for k, piece in enumerate(ends)]
    (mirror,) = columns_operator(
        covariance, [mirrors, inners], col_s, col_blocks, where, own, steps, nlon, 2, lambda i, at: at[i], mirror, False,
        10 ** 13,
    )
    (predicted_spread_matrix,) = rows_operator(
        mirror, *ends, row_s, where, steps, nlon, F32, blocks, noise_var
    )
    return (predicted_spread_matrix, operator_times_prior)


def plain_body(covariance, noise_var, wind_table, diffusivity, wind_index):
    rows_dev, cols_dev = covariance.shape
    lat_rows, nlon = noise_var.shape
    steps, nlat = wind_index.shape
    lats = cols_dev // nlon
    row_id, col_id = lax.axis_index("row"), lax.axis_index("col")
    sent = covariance.astype(BF16)
    sides = gathered(sent, sent, "col", 1, nlon, steps, lats)
    ends = gathered(sent, sent, "row", 0, nlon, steps, lat_rows)
    firsts = (row_id * lat_rows, col_id * lats)
    where = jnp.stack([0, 0, 1, 1, firsts[1] - firsts[0], *firsts]).astype(jnp.int32)
    row_s, col_s, *col_blocks = stencils(
        wind_table, diffusivity, wind_index, where, lat_rows, lats, nlon, covariance, []
    )
    operator_times_prior, blocks = rows_operator(covariance, *ends, row_s, where, steps, nlon, BF16)
    (mirror,) = columns_operator(
        covariance, [sides], col_s, col_blocks, where, 2, steps, nlon, lat_rows // 2, lambda i, at: i
    )
    ends = gathered(mirror, mirror, "row", 0, nlon, steps, lat_rows)
    (predicted_spread_matrix,) = rows_operator(
        mirror, *ends, row_s, where, steps, nlon, F32, blocks, noise_var
    )
    return (predicted_spread_matrix, operator_times_prior)


def solution(mesh):
    in_specs = (P("row", "col"), P("row", None), P(), P(), P())
    out_specs = (P("row", "col"), P("row", "col"))
    return jax.shard_map(body, mesh=mesh, in_specs=in_specs, out_specs=out_specs, check_vma=False)
```

```python
import functools

import jax
import jax.numpy as jnp
from jax import lax
from jax.experimental import pallas as pl
from jax.experimental.pallas import tpu as pltpu
from jax.sharding import PartitionSpec as P

F32 = jnp.float32
BF16 = jnp.bfloat16
VMEM_LIMIT = 63 * 1024 * 1024


def params():
    return pltpu.CompilerParams(vmem_limit_bytes=VMEM_LIMIT)


def cost(work):
    return pl.CostEstimate(flops=work, bytes_accessed=work, transcendentals=0)


def stencil_terms(zonal_cour, merid_cour, diffuse):
    middle_weight = 1.0 - zonal_cour * zonal_cour - merid_cour * merid_cour - 4.0 * diffuse
    eastward_weight = 0.5 * zonal_cour * zonal_cour - 0.5 * zonal_cour + diffuse
    west_w = 0.5 * zonal_cour * zonal_cour + 0.5 * zonal_cour + diffuse
    north_w = 0.5 * merid_cour * merid_cour - 0.5 * merid_cour + diffuse
    south_w = 0.5 * merid_cour * merid_cour + 0.5 * merid_cour + diffuse
    return middle_weight, eastward_weight, west_w, north_w, south_w


def split(values):
    high = values.astype(BF16)
    return high, (values - high.astype(F32)).astype(BF16)


def circulant(row):
    size = row.shape[1]
    return pltpu.roll(jnp.broadcast_to(row, (size, size)), 0, 1, stride=1, stride_axis=0)


def product(left, right):
    return jnp.dot(left, right, preferred_element_type=F32)


def composed(terms, lats, nlon):
    steps = len(terms)
    padded = lats + 2 * steps
    lane = lax.broadcasted_iota(jnp.int32, (padded, nlon), 1)
    rows = {0: (lane == 0).astype(F32)}
    for step_no in range(steps):
        low, high = step_no + 1, padded - step_no - 1
        c, e, w, n, s = [term[low:high] for term in terms[step_no]]
        size = high - low
        fresh = {}
        for d in range(-step_no - 1, step_no + 2):
            parts = []
            if d in rows:
                here = rows[d][1 : 1 + size]
                parts += [c * here, e * pltpu.roll(here, 1, 1), w * pltpu.roll(here, nlon - 1, 1)]
            if d - 1 in rows:
                parts.append(n * rows[d - 1][2 : 2 + size])
            if d + 1 in rows:
                parts.append(s * rows[d + 1][0:size])
            fresh[d] = functools.reduce(lambda x, y: x + y, parts)
        rows = fresh
    return rows


def swept(planes, weights):
    for step_no, (c, e, w, n, s) in enumerate(weights):
        fresh = []
        for i in range(1, len(planes) - 1):
            at, u = i + step_no, planes[i]
            nlon = u.shape[1]
            fresh.append(
                c(at) * u
                + e(at) * pltpu.roll(u, nlon - 1, 1)
                + w(at) * pltpu.roll(u, 1, 1)
                + n(at) * planes[i + 1]
                + s(at) * planes[i - 1]
            )
        planes = fresh
    return planes


def packing(pieces):
    def placed(piece):
        _, size, _, width, _, _, turn = piece
        return (width, size) if turn else (size, width)

    shapes = {}
    for piece in pieces:
        shape, out = placed(piece), piece[4]
        shapes[out] = (max(piece[5] + shape[0], shapes.get(out, (0,))[0]), shape[1])
    count = len(pieces)
    scratch = [pltpu.VMEM(piece[1:4:2], F32) for piece in pieces]
    scratch += [pltpu.VMEM(placed(piece), BF16) for piece in pieces]
    scratch += [pltpu.SemaphoreType.DMA((count,)), pltpu.SemaphoreType.DMA((count,))]

    def start(where_ref, p_ref, refs):
        first = lambda at: pl.multiple_of(where_ref[at[0]] + sum(at[1:]), 128) if isinstance(at, tuple) else at
        loads = []
        for k, (row, size, col, width, _, _, _) in enumerate(pieces):
            source = p_ref.at[pl.ds(first(row), size), pl.ds(first(col), width)]
            loads.append(pltpu.make_async_copy(source, refs[k], refs[2 * count].at[k]))
            loads[-1].start()
        return loads

    def finish(loads, results, refs):
        stores = []
        for k, piece in enumerate(pieces):
            loads[k].wait()
            got, made, turn, shape = refs[k], refs[count + k], piece[6], placed(piece)
            if turn:
                for a in range(0, shape[0], turn):
                    for b in range(0, shape[1], turn):
                        made[a : a + turn, b : b + turn] = got[b : b + turn, a : a + turn].T.astype(BF16)
            else:
                made[...] = got[...].astype(BF16)
            target = results[piece[4]].at[pl.ds(piece[5], shape[0]), :]
            stores.append(pltpu.make_async_copy(made, target, refs[2 * count + 1].at[k]))
            stores[-1].start()
        for copy in stores:
            copy.wait()

    return [jax.ShapeDtypeStruct(shapes[k], BF16) for k in range(len(shapes))], scratch, start, finish


def packed(covariance, where, pieces):
    out_shape, scratch, start, finish = packing(pieces)

    def kernel(where_ref, p_ref, *refs):
        results, refs = refs[: len(out_shape)], refs[len(out_shape) :]
        finish(start(where_ref, p_ref, refs), results, refs)

    return pl.pallas_call(
        kernel,
        in_specs=[pl.BlockSpec(memory_space=pltpu.SMEM), pl.BlockSpec(memory_space=pl.ANY)],
        out_specs=[pl.BlockSpec(memory_space=pl.ANY)] * len(out_shape),
        out_shape=out_shape,
        scratch_shapes=scratch,
        compiler_params=params(),
        cost_estimate=cost(1),
        name="packed",
    )(where, covariance)


def stencils(wind_table, diffusivity, wind_index, where, lat_rows, lats, nlon, covariance, pieces):
    steps, nlat = wind_index.shape
    sizes = (lat_rows, lats)
    span = 2 * steps * nlon
    pairs = lats // 2
    packs, pack_scratch, start, finish = packing(pieces)

    def kernel(table_ref, diffuse_ref, index_ref, where_ref, p_ref, *refs):
        row_out, col_out, high_out, low_out, step_out = refs[:5]
        results, scratch, refs = refs[5 : 5 + len(packs)], refs[5 + len(packs) :][:2], refs[7 + len(packs) :]
        loads = start(where_ref, p_ref, refs)
        for side, out in enumerate((row_out, col_out)):
            looked_up = scratch[side]
            terms = []
            for step_no in range(steps):
                for i in range(sizes[side] + 2 * steps):
                    lat = where_ref[5 + side] + i - steps
                    inside = jnp.logical_and(lat >= 0, lat < nlat)
                    entry = index_ref[step_no, jnp.clip(lat, 0, nlat - 1)]
                    values = (table_ref[0, entry], table_ref[1, entry], diffuse_ref[entry], inside.astype(F32))
                    for k, value in enumerate(values):
                        looked_up[k, i : i + 1, :] = jnp.full((1, nlon), value, F32)
                here = looked_up[3] > 0.5
                c, e, w, n, s = [
                    jnp.where(here, term, 0.0)
                    for term in stencil_terms(looked_up[0], looked_up[1], looked_up[2])
                ]
                terms.append((c, w, e, n, s) if side else (c, e, w, n, s))
                if side:
                    for member, value in enumerate((c, e, w, n, s)):
                        step_out[5 * step_no + member] = value
            for d, value in composed(terms, sizes[side], nlon).items():
                out[d + steps] = value
        for q in range(pairs):
            for a in range(2):
                for k in range(2 * steps):
                    d = k - (steps - 1) - a
                    high, low = split(circulant(col_out[d + steps, 2 * q + a : 2 * q + a + 1, :]))
                    at = pl.ds(q * span + k * nlon, nlon)
                    high_out[at, a * nlon : (a + 1) * nlon] = high
                    low_out[at, a * nlon : (a + 1) * nlon] = low
        finish(loads, results, refs)

    return pl.pallas_call(
        kernel,
        in_specs=[pl.BlockSpec(memory_space=pltpu.SMEM)] * 4 + [pl.BlockSpec(memory_space=pl.ANY)],
        out_specs=[pl.BlockSpec(memory_space=pltpu.VMEM)] * 5 + [pl.BlockSpec(memory_space=pl.ANY)] * len(packs),
        out_shape=[jax.ShapeDtypeStruct((2 * steps + 1, size, nlon), F32) for size in sizes]
        + [jax.ShapeDtypeStruct((pairs * span, 2 * nlon), BF16)] * 2
        + [jax.ShapeDtypeStruct((5 * steps, lats + 2 * steps, nlon), F32)]
        + packs,
        scratch_shapes=[pltpu.VMEM((4, size + 2 * steps, nlon), F32) for size in sizes]
        + pack_scratch,
        compiler_params=params(),
        cost_estimate=cost(1),
        name="stencils",
    )(wind_table.T, diffusivity, wind_index, where, covariance)


def columns_operator(
    covariance, halos, stencil, blocks, where, unit, steps, nlon, count, block_at, held=None, ends=False, work=1
):
    rows, cols = covariance.shape
    lats = cols // nlon
    wide = steps * nlon
    size = unit * nlon
    span = 2 * steps * nlon
    pairs = lats // 2
    part = 16
    upper = size - part * (3 * size // (8 * part))

    def kernel(where_ref, stencil_ref, p_ref, *rest):
        halo_refs, rest = rest[: 2 * len(halos)], rest[2 * len(halos) :]
        (b_high, b_low, step_ref), outs, data_ref = rest[:3], rest[3:-1], rest[-1]
        if held is not None:
            outs = outs[1:]
        t_ref = outs[0]
        i = pl.program_id(0)
        col_odd, row_odd = where_ref[2] != 0, where_ref[3] != 0

        @pl.when(i == 0)
        def _():
            data_ref[size:, :wide] = jnp.zeros((size, wide), BF16)
            data_ref[size:, wide + cols :] = jnp.zeros((size, wide), BF16)

        for k in range(len(halos)):
            even_ref, odd_ref = halo_refs[2 * k : 2 * k + 2]
            chosen = i >= 0 if len(halos) == 1 else i == k

            @pl.when(jnp.logical_and(chosen, col_odd))
            def _(even_ref=even_ref, odd_ref=odd_ref):
                data_ref[:size, :wide] = even_ref[...]
                data_ref[:size, wide + cols :] = odd_ref[...]

            @pl.when(jnp.logical_and(chosen, jnp.logical_not(col_odd)))
            def _(even_ref=even_ref, odd_ref=odd_ref):
                data_ref[:size, :wide] = odd_ref[...]
                data_ref[:size, wide + cols :] = even_ref[...]

        data_ref[:upper, wide : wide + cols], data_ref[size : size + upper, wide : wide + cols] = split(
            p_ref[:upper, :]
        )
        weights = [
            [
                lambda at, k=5 * step_no + member: step_ref[k, at : at + 1, :]
                for member in range(5)
            ]
            for step_no in range(steps)
        ]
        starts = list(range(upper, size, part))
        share = -(-len(starts) // (3 * pairs))

        def some_by_steps():
            for _ in range(min(share, len(starts))):
                start = starts.pop(0)
                rows_at = slice(start, start + part)
                planes = []
                for k in range(lats + 2 * steps):
                    if steps <= k < steps + lats:
                        planes.append(p_ref[rows_at, (k - steps) * nlon : (k - steps + 1) * nlon])
                    else:
                        planes.append(data_ref[rows_at, k * nlon : (k + 1) * nlon].astype(F32))
                for k, plane in enumerate(swept(planes, weights)):
                    t_ref[rows_at, k * nlon : (k + 1) * nlon] = plane.astype(BF16)

        for q in range(pairs):
            window = slice((2 * q + 1) * nlon, (2 * q + 1) * nlon + span)
            of = pl.ds(q * span, span)
            total = product(data_ref[:upper, window], b_high[of, :])
            some_by_steps()
            total += product(data_ref[size : size + upper, window], b_high[of, :])
            some_by_steps()
            total += product(data_ref[:upper, window], b_low[of, :])
            some_by_steps()
            for a, k, d in ((0, 2 * q, -steps), (1, 2 * q + 2 * steps + 1, steps)):
                far = slice(k * nlon, (k + 1) * nlon)
                row = stencil_ref[d + steps, 2 * q + a : 2 * q + a + 1, :]
                weight = jnp.sum(row, axis=1, keepdims=True)
                far_values = data_ref[:upper, far].astype(F32) + data_ref[size : size + upper, far].astype(F32)
                value = total[:, a * nlon : (a + 1) * nlon] + weight * far_values
                t_ref[:upper, (2 * q + a) * nlon : (2 * q + a + 1) * nlon] = value.astype(BF16)
        if ends:
            for odd in range(2):
                is_odd = row_odd if odd else jnp.logical_not(row_odd)

                @pl.when(jnp.logical_and(i == 0, is_odd))
                def _(odd=odd):
                    outs[2 - odd][...] = t_ref[:wide, :]

                @pl.when(jnp.logical_and(i == count - 1, is_odd))
                def _(odd=odd):
                    outs[1 + odd][...] = t_ref[size - wide :, :]

    halo_at = (lambda i, at: (i, 0)) if len(halos) == 1 else (lambda i, at: (0, 0))
    in_specs = [
        pl.BlockSpec(stencil.shape, lambda i, at: (0, 0, 0)),
        pl.BlockSpec((size, cols), lambda i, at: (block_at(i, at), 0)),
    ]
    in_specs += [pl.BlockSpec((size, wide), halo_at)] * (2 * len(halos))
    in_specs += [pl.BlockSpec(block.shape, lambda i, at, n=block.ndim: (0,) * n) for block in blocks]
    out_specs = [pl.BlockSpec((size, cols), lambda i, at: (block_at(i, at), 0))]
    out_shape = [jax.ShapeDtypeStruct((rows, cols), BF16)]
    operands = [where, stencil, covariance] + [array for pair in halos for array in pair] + list(blocks)
    aliases = {}
    if ends:
        out_specs += [pl.BlockSpec((wide, cols), lambda i, at: (0, 0))] * 2
        out_shape += [jax.ShapeDtypeStruct((wide, cols), BF16)] * 2
    if held is not None:
        in_specs.append(pl.BlockSpec(memory_space=pl.ANY))
        aliases = {len(operands): 0}
        operands.append(held)
    return pl.pallas_call(
        kernel,
        grid_spec=pltpu.PrefetchScalarGridSpec(
            num_scalar_prefetch=1,
            grid=(count,),
            in_specs=in_specs,
            out_specs=out_specs,
            scratch_shapes=[pltpu.VMEM((2 * size, cols + 2 * wide), BF16)],
        ),
        out_shape=out_shape,
        input_output_aliases=aliases,
        compiler_params=params(),
        cost_estimate=cost(work),
        name="columns_operator",
    )(*operands)


def rows_operator(values, even, odd, stencil, where, steps, nlon, out_dtype, blocks=None, noise=None):
    rows, cols = values.shape
    lat_rows = rows // nlon
    wide = steps * nlon
    size = 2 * nlon
    span = 2 * steps * nlon
    pairs = lat_rows // 2
    group = 2 if pairs % 2 == 0 else 1
    ahead = (steps + 1) // 2
    exact = values.dtype == BF16
    makes = blocks is None
    chunk = min(cols, 256)

    def kernel(where_ref, stencil_ref, x_ref, even_ref, odd_ref, *rest):
        if makes:
            out_ref, a_ref = rest[:2]
        else:
            a_ref, noise_ref, out_ref = rest[:3]
        high_ref, sem = rest[2 if makes else 3 :][:2]
        raw_ref, low_ref = (None, None) if exact else rest[-2:]
        step = pl.program_id(0)

        def load(q):
            here = pl.ds(pl.multiple_of(q * size, size), size)
            there = pl.ds(pl.multiple_of(wide + q * size, nlon), size)
            target = high_ref.at[there, :] if exact else raw_ref.at[here, :]
            return pltpu.make_async_copy(x_ref.at[here, :], target, sem.at[q])

        def ready(q):
            load(q).wait()
            if not exact:
                there = pl.ds(pl.multiple_of(wide + q * size, nlon), size)
                here = pl.ds(pl.multiple_of(q * size, size), size)
                high_ref[there, :], low_ref[there, :] = split(raw_ref[here, :])

        @pl.when(step == 0)
        def _():
            is_odd = where_ref[3]
            at_even = pl.ds(pl.multiple_of((1 - is_odd) * (wide + rows), nlon), wide)
            at_odd = pl.ds(pl.multiple_of(is_odd * (wide + rows), nlon), wide)
            halos = [
                pltpu.make_async_copy(even_ref, high_ref.at[at_even, :], sem.at[pairs]),
                pltpu.make_async_copy(odd_ref, high_ref.at[at_odd, :], sem.at[pairs + 1]),
            ]
            for halo in halos:
                halo.start()
            for q in range(pairs):
                load(q).start()
            if not exact:
                low_ref[:wide, :] = jnp.zeros((wide, cols), BF16)
                low_ref[wide + rows :, :] = jnp.zeros((wide, cols), BF16)
            for halo in halos:
                halo.wait()
            for q in range(min(ahead, pairs)):
                ready(q)

        for j in range(group):
            q = step * group + j + ahead

            @pl.when(q < pairs)
            def _(q=q):
                ready(q)

        row = lambda j, d, a: stencil_ref[d + steps, pl.ds(2 * (step * group + j) + a, 1), :]
        if makes:
            for j in range(group):
                for a in range(2):
                    for k in range(2 * steps):
                        high, low = split(circulant(row(j, k - (steps - 1) - a, a)))
                        top = 2 * j * size + a * nlon
                        a_ref[top : top + nlon, k * nlon : (k + 1) * nlon] = high
                        a_ref[top + size : top + size + nlon, k * nlon : (k + 1) * nlon] = low
        for j in range(group):
            unit = lambda k: pl.multiple_of((2 * (step * group + j) + k) * nlon, nlon)
            weights = [jnp.sum(row(j, d, a), axis=1, keepdims=True) for a, d in ((0, -steps), (1, steps))]
            top = 2 * j * size
            for lane in range(0, cols, chunk):
                lanes = slice(lane, lane + chunk)
                both = product(a_ref[top : top + 2 * size, :], high_ref[pl.ds(unit(1), span), lanes])
                total = both[:size] + both[size:]
                if not exact:
                    total += product(a_ref[top : top + size, :], low_ref[pl.ds(unit(1), span), lanes])
                for a, k in ((0, 0), (1, 2 * steps + 1)):
                    far = high_ref[pl.ds(unit(k), nlon), lanes].astype(F32)
                    if not exact:
                        far += low_ref[pl.ds(unit(k), nlon), lanes].astype(F32)
                    value = total[a * nlon : (a + 1) * nlon, :] + weights[a] * far
                    out_ref[j * size + a * nlon : j * size + (a + 1) * nlon, lanes] = value.astype(out_dtype)
        if noise is not None:
            for a in range(2 * group):
                lat = 2 * group * step + a - where_ref[4]

                @pl.when(jnp.logical_and(lat >= 0, lat < cols // nlon))
                def _(a=a, lat=lat):
                    lanes = pl.ds(pl.multiple_of(lat * nlon, nlon), nlon)
                    eye = lax.broadcasted_iota(jnp.int32, (nlon, nlon), 0) == lax.broadcasted_iota(
                        jnp.int32, (nlon, nlon), 1
                    )
                    added = jnp.where(eye, noise_ref[pl.ds(2 * group * step + a, 1), :], 0.0)
                    out_ref[a * nlon : (a + 1) * nlon, lanes] += added

    in_specs = [pl.BlockSpec(stencil.shape, lambda g, at: (0, 0, 0))] + [pl.BlockSpec(memory_space=pl.ANY)] * 3
    operands = [where, stencil, values, even, odd]
    out_specs = [pl.BlockSpec((group * size, cols), lambda g, at: (g, 0))]
    out_shape = [jax.ShapeDtypeStruct((rows, cols), out_dtype)]
    blocks_spec = pl.BlockSpec((2 * group * size, span), lambda g, at: (g, 0))
    if makes:
        out_specs.append(blocks_spec)
        out_shape.append(jax.ShapeDtypeStruct((2 * rows, span), BF16))
    else:
        in_specs += [blocks_spec, pl.BlockSpec(noise.shape, lambda g, at: (0, 0))]
        operands += [blocks, noise]
    return pl.pallas_call(
        kernel,
        grid_spec=pltpu.PrefetchScalarGridSpec(
            num_scalar_prefetch=1,
            grid=(pairs // group,),
            in_specs=in_specs,
            out_specs=out_specs,
            scratch_shapes=[pltpu.VMEM((rows + 2 * wide, cols), BF16), pltpu.SemaphoreType.DMA((pairs + 2,))]
            + ([] if exact else [pltpu.VMEM((rows, cols), F32), pltpu.VMEM((rows + 2 * wide, cols), BF16)]),
        ),
        out_shape=out_shape,
        compiler_params=params(),
        cost_estimate=cost(1),
        name="rows_operator",
    )(*operands)


def shifted(block, axis, by):
    size = lax.axis_size(axis)
    pairs = [(i, i + by) for i in range(size) if 0 <= i + by < size]
    return lax.ppermute(block, axis, pairs)


def gathered(first, last, axis, dim, unit, halo, own):
    before, after = [], []
    need, hop = halo, 1
    while need > 0:
        take = min(own, need)
        size = first.shape[dim]
        before.insert(0, shifted(lax.slice_in_dim(last, size - take * unit, size, axis=dim), axis, hop))
        after.append(shifted(lax.slice_in_dim(first, 0, take * unit, axis=dim), axis, -hop))
        need, hop = need - take, hop + 1
    join = lambda parts: parts[0] if len(parts) == 1 else jnp.concatenate(parts, axis=dim)
    return join(before), join(after)


def exchanged(block, axis, odd):
    pairs = []
    for i in range(odd, lax.axis_size(axis) - 1, 2):
        pairs += [(i, i + 1), (i + 1, i)]
    return lax.ppermute(block, axis, pairs)


def mirrored(block, odd):
    n_row, n_col = lax.axis_size("row"), lax.axis_size("col")
    pairs = []
    for a in range(n_row):
        for b in range(n_col):
            to = 2 * a + (1 - b % 2) + (1 if (b + odd) % 2 else -1)
            if 0 <= to < n_col:
                pairs.append((a * n_col + b, (b // 2) * n_col + to))
    return lax.ppermute(block, ("row", "col"), pairs)


def body(covariance, noise_var, wind_table, diffusivity, wind_index):
    rows_dev, cols_dev = covariance.shape
    lat_rows, nlon = noise_var.shape
    steps, nlat = wind_index.shape
    lats = cols_dev // nlon
    row_id, col_id = lax.axis_index("row"), lax.axis_index("col")
    own = lat_rows // 4
    fits = lat_rows == 2 * lats and own % 2 == 0 and own >= steps and own <= lats - steps
    if not fits or lax.axis_size("col") != 2 * lax.axis_size("row"):
        return plain_body(covariance, noise_var, wind_table, diffusivity, wind_index)

    near = lat_rows // 2 - own
    middle = lat_rows // 2
    outer, inner, wide = near * nlon, own * nlon, steps * nlon
    pick = lambda parity, even, odd: even + parity * (odd - even)
    col_odd, row_odd = col_id % 2, row_id % 2
    mirror_at, direct_at = pick(col_odd, middle - own, middle), pick(col_odd, middle, middle - own)
    diagonal = col_id * lats - row_id * lat_rows
    where = jnp.stack(
        [
            mirror_at // own,
            direct_at // own,
            col_odd,
            row_odd,
            diagonal,
            row_id * lat_rows,
            col_id * lats,
            mirror_at * nlon,
            pick(col_odd, lats, lats - steps) * nlon,
            pick(col_odd, 2 * lats - steps, 0) * nlon,
            pick(col_odd, lats - own, 0) * nlon,
            pick(col_odd, cols_dev - wide, 0),
            pick(col_odd, 0, cols_dev - wide),
            pick(row_odd, rows_dev - wide, 0),
            pick(row_odd, 0, rows_dev - wide),
        ]
    ).astype(jnp.int32)
    half = outer // 2
    spans = [(0, half, 0), (half, half, half)]
    spans += [(rows_dev - outer, half, outer), (rows_dev - half, half, outer + half), (0, 16, 2 * outer)]
    pieces = [(row, size, (11 + k,), wide, k, there, 0) for row, size, there in spans for k in range(2)]
    pieces += [((13 + k, j * nlon), nlon, 0, cols_dev, k + 2, j * nlon, 0) for k in range(2) for j in range(steps)]
    others = [((8 + k,), wide, (10,), inner, k, 0, nlon) for k in range(2)]
    others += [((7,), inner, (11 + k,), wide, k + 2, 0, 0) for k in range(2)]
    sent = packed(covariance, where, pieces)
    outers, ends = list(sent[:2]), list(sent[2:])
    outers = [exchanged(piece, "col", k) for k, piece in enumerate(outers)]
    ends = [exchanged(piece, "row", k) for k, piece in enumerate(ends)]
    row_s, col_s, *rest = stencils(
        wind_table, diffusivity, wind_index, where, lat_rows, lats, nlon, covariance, others
    )
    col_blocks, mirrors, inners = rest[:3], rest[3:5], rest[5:7]
    mirrors = [mirrored(piece, k) for k, piece in enumerate(mirrors)]

    operator_times_prior, blocks = rows_operator(covariance, *ends, row_s, where, steps, nlon, BF16)
    inners[0] = exchanged(inners[0], "col", 0)
    operator_times_prior, outers, inners[1] = lax.optimization_barrier(
        (operator_times_prior, outers, inners[1])
    )
    inners[1] = exchanged(inners[1], "col", 1)
    mirror, *ends = columns_operator(
        covariance, [outers], col_s, col_blocks, where, near, steps, nlon, 2, lambda i, at: i * (lat_rows // near - 1),
        None, True,
    )
    ends = [exchanged(piece, "row", k) for k, piece in enumerate(ends)]
    (mirror,) = columns_operator(
        covariance, [mirrors, inners], col_s, col_blocks, where, own, steps, nlon, 2, lambda i, at: at[i], mirror, False,
        10 ** 13,
    )
    (predicted_spread_matrix,) = rows_operator(
        mirror, *ends, row_s, where, steps, nlon, F32, blocks, noise_var
    )
    return (predicted_spread_matrix, operator_times_prior)


def plain_body(covariance, noise_var, wind_table, diffusivity, wind_index):
    rows_dev, cols_dev = covariance.shape
    lat_rows, nlon = noise_var.shape
    steps, nlat = wind_index.shape
    lats = cols_dev // nlon
    row_id, col_id = lax.axis_index("row"), lax.axis_index("col")
    sent = covariance.astype(BF16)
    sides = gathered(sent, sent, "col", 1, nlon, steps, lats)
    ends = gathered(sent, sent, "row", 0, nlon, steps, lat_rows)
    firsts = (row_id * lat_rows, col_id * lats)
    where = jnp.stack([0, 0, 1, 1, firsts[1] - firsts[0], *firsts]).astype(jnp.int32)
    row_s, col_s, *col_blocks = stencils(
        wind_table, diffusivity, wind_index, where, lat_rows, lats, nlon, covariance, []
    )
    operator_times_prior, blocks = rows_operator(covariance, *ends, row_s, where, steps, nlon, BF16)
    (mirror,) = columns_operator(
        covariance, [sides], col_s, col_blocks, where, 2, steps, nlon, lat_rows // 2, lambda i, at: i
    )
    ends = gathered(mirror, mirror, "row", 0, nlon, steps, lat_rows)
    (predicted_spread_matrix,) = rows_operator(
        mirror, *ends, row_s, where, steps, nlon, F32, blocks, noise_var
    )
    return (predicted_spread_matrix, operator_times_prior)


def solution(mesh):
    in_specs = (P("row", "col"), P("row", None), P(), P(), P())
    out_specs = (P("row", "col"), P("row", "col"))
    return jax.shard_map(body, mesh=mesh, in_specs=in_specs, out_specs=out_specs, check_vma=False)
```

```python
import functools

import jax
import jax.numpy as jnp
from jax import lax
from jax.experimental import pallas as pl
from jax.experimental.pallas import tpu as pltpu
from jax.sharding import PartitionSpec as P

F32 = jnp.float32
BF16 = jnp.bfloat16
VMEM_LIMIT = 63 * 1024 * 1024


def params():
    return pltpu.CompilerParams(vmem_limit_bytes=VMEM_LIMIT)


def cost(work):
    return pl.CostEstimate(flops=work, bytes_accessed=work, transcendentals=0)


def stencil_terms(zonal_cour, merid_cour, diffuse):
    middle_weight = 1.0 - zonal_cour * zonal_cour - merid_cour * merid_cour - 4.0 * diffuse
    eastward_weight = 0.5 * zonal_cour * zonal_cour - 0.5 * zonal_cour + diffuse
    west_w = 0.5 * zonal_cour * zonal_cour + 0.5 * zonal_cour + diffuse
    north_w = 0.5 * merid_cour * merid_cour - 0.5 * merid_cour + diffuse
    south_w = 0.5 * merid_cour * merid_cour + 0.5 * merid_cour + diffuse
    return middle_weight, eastward_weight, west_w, north_w, south_w


def split(values):
    high = values.astype(BF16)
    return high, (values - high.astype(F32)).astype(BF16)


def circulant(row):
    size = row.shape[1]
    return pltpu.roll(jnp.broadcast_to(row, (size, size)), 0, 1, stride=1, stride_axis=0)


def product(left, right):
    return jnp.dot(left, right, preferred_element_type=F32)


def composed(terms, lats, nlon):
    steps = len(terms)
    padded = lats + 2 * steps
    lane = lax.broadcasted_iota(jnp.int32, (padded, nlon), 1)
    rows = {0: (lane == 0).astype(F32)}
    for step_no in range(steps):
        low, high = step_no + 1, padded - step_no - 1
        c, e, w, n, s = [term[low:high] for term in terms[step_no]]
        size = high - low
        fresh = {}
        for d in range(-step_no - 1, step_no + 2):
            parts = []
            if d in rows:
                here = rows[d][1 : 1 + size]
                parts += [c * here, e * pltpu.roll(here, 1, 1), w * pltpu.roll(here, nlon - 1, 1)]
            if d - 1 in rows:
                parts.append(n * rows[d - 1][2 : 2 + size])
            if d + 1 in rows:
                parts.append(s * rows[d + 1][0:size])
            fresh[d] = functools.reduce(lambda x, y: x + y, parts)
        rows = fresh
    return rows


def swept(planes, weights):
    for step_no, (c, e, w, n, s) in enumerate(weights):
        fresh = []
        for i in range(1, len(planes) - 1):
            at, u = i + step_no, planes[i]
            nlon = u.shape[1]
            fresh.append(
                c(at) * u
                + e(at) * pltpu.roll(u, nlon - 1, 1)
                + w(at) * pltpu.roll(u, 1, 1)
                + n(at) * planes[i + 1]
                + s(at) * planes[i - 1]
            )
        planes = fresh
    return planes


def packing(pieces):
    def placed(piece):
        _, size, _, width, _, _, turn = piece
        return (width, size) if turn else (size, width)

    shapes = {}
    for piece in pieces:
        shape, out = placed(piece), piece[4]
        shapes[out] = (max(piece[5] + shape[0], shapes.get(out, (0,))[0]), shape[1])
    count = len(pieces)
    scratch = [pltpu.VMEM(piece[1:4:2], F32) for piece in pieces]
    scratch += [pltpu.VMEM(placed(piece), BF16) for piece in pieces]
    scratch += [pltpu.SemaphoreType.DMA((count,)), pltpu.SemaphoreType.DMA((count,))]

    def start(where_ref, p_ref, refs):
        first = lambda at: pl.multiple_of(where_ref[at[0]] + sum(at[1:]), 128) if isinstance(at, tuple) else at
        loads = []
        for k, (row, size, col, width, _, _, _) in enumerate(pieces):
            source = p_ref.at[pl.ds(first(row), size), pl.ds(first(col), width)]
            loads.append(pltpu.make_async_copy(source, refs[k], refs[2 * count].at[k]))
            loads[-1].start()
        return loads

    def finish(loads, results, refs):
        stores = []
        for k, piece in enumerate(pieces):
            loads[k].wait()
            got, made, turn, shape = refs[k], refs[count + k], piece[6], placed(piece)
            if turn:
                for a in range(0, shape[0], turn):
                    for b in range(0, shape[1], turn):
                        made[a : a + turn, b : b + turn] = got[b : b + turn, a : a + turn].T.astype(BF16)
            else:
                made[...] = got[...].astype(BF16)
            target = results[piece[4]].at[pl.ds(piece[5], shape[0]), :]
            stores.append(pltpu.make_async_copy(made, target, refs[2 * count + 1].at[k]))
            stores[-1].start()
        for copy in stores:
            copy.wait()

    return [jax.ShapeDtypeStruct(shapes[k], BF16) for k in range(len(shapes))], scratch, start, finish


def packed(covariance, where, pieces):
    out_shape, scratch, start, finish = packing(pieces)

    def kernel(where_ref, p_ref, *refs):
        results, refs = refs[: len(out_shape)], refs[len(out_shape) :]
        finish(start(where_ref, p_ref, refs), results, refs)

    return pl.pallas_call(
        kernel,
        in_specs=[pl.BlockSpec(memory_space=pltpu.SMEM), pl.BlockSpec(memory_space=pl.ANY)],
        out_specs=[pl.BlockSpec(memory_space=pl.ANY)] * len(out_shape),
        out_shape=out_shape,
        scratch_shapes=scratch,
        compiler_params=params(),
        cost_estimate=cost(1),
        name="packed",
    )(where, covariance)


def stencils(wind_table, diffusivity, wind_index, where, lat_rows, lats, nlon, covariance, pieces):
    steps, nlat = wind_index.shape
    sizes = (lat_rows, lats)
    span = 2 * steps * nlon
    pairs = lats // 2
    packs, pack_scratch, start, finish = packing(pieces)

    def kernel(table_ref, diffuse_ref, index_ref, where_ref, p_ref, *refs):
        row_out, col_out, high_out, low_out, step_out = refs[:5]
        results, scratch, refs = refs[5 : 5 + len(packs)], refs[5 + len(packs) :][:2], refs[7 + len(packs) :]
        loads = start(where_ref, p_ref, refs)
        for side, out in enumerate((row_out, col_out)):
            looked_up = scratch[side]
            terms = []
            for step_no in range(steps):
                for i in range(sizes[side] + 2 * steps):
                    lat = where_ref[5 + side] + i - steps
                    inside = jnp.logical_and(lat >= 0, lat < nlat)
                    entry = index_ref[step_no, jnp.clip(lat, 0, nlat - 1)]
                    values = (table_ref[0, entry], table_ref[1, entry], diffuse_ref[entry], inside.astype(F32))
                    for k, value in enumerate(values):
                        looked_up[k, i : i + 1, :] = jnp.full((1, nlon), value, F32)
                here = looked_up[3] > 0.5
                c, e, w, n, s = [
                    jnp.where(here, term, 0.0)
                    for term in stencil_terms(looked_up[0], looked_up[1], looked_up[2])
                ]
                terms.append((c, w, e, n, s) if side else (c, e, w, n, s))
                if side:
                    for member, value in enumerate((c, e, w, n, s)):
                        step_out[5 * step_no + member] = value
            for d, value in composed(terms, sizes[side], nlon).items():
                out[d + steps] = value
        for q in range(pairs):
            for a in range(2):
                for k in range(2 * steps):
                    d = k - (steps - 1) - a
                    high, low = split(circulant(col_out[d + steps, 2 * q + a : 2 * q + a + 1, :]))
                    at = pl.ds(q * span + k * nlon, nlon)
                    high_out[at, a * nlon : (a + 1) * nlon] = high
                    low_out[at, a * nlon : (a + 1) * nlon] = low
        finish(loads, results, refs)

    return pl.pallas_call(
        kernel,
        in_specs=[pl.BlockSpec(memory_space=pltpu.SMEM)] * 4 + [pl.BlockSpec(memory_space=pl.ANY)],
        out_specs=[pl.BlockSpec(memory_space=pltpu.VMEM)] * 5 + [pl.BlockSpec(memory_space=pl.ANY)] * len(packs),
        out_shape=[jax.ShapeDtypeStruct((2 * steps + 1, size, nlon), F32) for size in sizes]
        + [jax.ShapeDtypeStruct((pairs * span, 2 * nlon), BF16)] * 2
        + [jax.ShapeDtypeStruct((5 * steps, lats + 2 * steps, nlon), F32)]
        + packs,
        scratch_shapes=[pltpu.VMEM((4, size + 2 * steps, nlon), F32) for size in sizes]
        + pack_scratch,
        compiler_params=params(),
        cost_estimate=cost(1),
        name="stencils",
    )(wind_table.T, diffusivity, wind_index, where, covariance)


def columns_operator(
    covariance, halos, stencil, blocks, where, unit, steps, nlon, count, block_at, held=None, ends=False, work=1
):
    rows, cols = covariance.shape
    lats = cols // nlon
    wide = steps * nlon
    size = unit * nlon
    span = 2 * steps * nlon
    pairs = lats // 2
    part = nlon // 2
    upper = size - part * (3 * size // (8 * part))

    def kernel(where_ref, stencil_ref, p_ref, *rest):
        halo_groups = []
        for group in halos:
            halo_groups.append(rest[: len(group)])
            rest = rest[len(group) :]
        (b_high, b_low, step_ref), outs, data_ref = rest[:3], rest[3:-1], rest[-1]
        if held is not None:
            outs = outs[1:]
        t_ref = outs[0]
        i = pl.program_id(0)
        col_odd, row_odd = where_ref[2] != 0, where_ref[3] != 0

        @pl.when(i == 0)
        def _():
            data_ref[size:, :wide] = jnp.zeros((size, wide), BF16)
            data_ref[size:, wide + cols :] = jnp.zeros((size, wide), BF16)

        for k, refs in enumerate(halo_groups):
            chosen = i >= 0 if len(halos) == 1 else i == k
            for odd in range(2):
                here = jnp.logical_and(chosen, col_odd if odd else jnp.logical_not(col_odd))
                even_at, odd_at = (0, wide + cols) if odd else (wide + cols, 0)

                @pl.when(here)
                def _(refs=refs, odd_at=odd_at):
                    data_ref[:size, odd_at : odd_at + wide] = refs[1][...]

                for ref, use in ((refs[0], None),) if len(refs) == 2 else ((refs[0], 0), (refs[2], 1)):
                    if use is not None:
                        here_too = jnp.logical_and(here, where_ref[15] == use)

                    @pl.when(here if use is None else here_too)
                    def _(ref=ref, even_at=even_at):
                        data_ref[:size, even_at : even_at + wide] = ref[...]

        data_ref[:upper, wide : wide + cols], data_ref[size : size + upper, wide : wide + cols] = split(
            p_ref[:upper, :]
        )
        weights = [
            [
                lambda at, k=5 * step_no + member: step_ref[k, at : at + 1, :]
                for member in range(5)
            ]
            for step_no in range(steps)
        ]
        starts = list(range(upper, size, part))
        for q in range(max(pairs, len(starts))):
            if q < pairs:
                window = slice((2 * q + 1) * nlon, (2 * q + 1) * nlon + span)
                of = pl.ds(q * span, span)
                total = product(data_ref[:upper, window], b_high[of, :])
                total += product(data_ref[size : size + upper, window], b_high[of, :])
                total += product(data_ref[:upper, window], b_low[of, :])
                for a, k, d in ((0, 2 * q, -steps), (1, 2 * q + 2 * steps + 1, steps)):
                    far = slice(k * nlon, (k + 1) * nlon)
                    row = stencil_ref[d + steps, 2 * q + a : 2 * q + a + 1, :]
                    weight = jnp.sum(row, axis=1, keepdims=True)
                    far_values = data_ref[:upper, far].astype(F32) + data_ref[size : size + upper, far].astype(F32)
                    value = total[:, a * nlon : (a + 1) * nlon] + weight * far_values
                    t_ref[:upper, (2 * q + a) * nlon : (2 * q + a + 1) * nlon] = value.astype(BF16)
            if q < len(starts):
                rows_at = slice(starts[q], starts[q] + part)
                planes = []
                for k in range(lats + 2 * steps):
                    if steps <= k < steps + lats:
                        planes.append(p_ref[rows_at, (k - steps) * nlon : (k - steps + 1) * nlon])
                    else:
                        planes.append(data_ref[rows_at, k * nlon : (k + 1) * nlon].astype(F32))
                for k, plane in enumerate(swept(planes, weights)):
                    t_ref[rows_at, k * nlon : (k + 1) * nlon] = plane.astype(BF16)
        if ends:
            for odd in range(2):
                is_odd = row_odd if odd else jnp.logical_not(row_odd)

                @pl.when(jnp.logical_and(i == 0, is_odd))
                def _(odd=odd):
                    outs[2 - odd][...] = t_ref[:wide, :]

                @pl.when(jnp.logical_and(i == count - 1, is_odd))
                def _(odd=odd):
                    outs[1 + odd][...] = t_ref[size - wide :, :]

    halo_at = (lambda i, at: (i, 0)) if len(halos) == 1 else (lambda i, at: (0, 0))
    in_specs = [
        pl.BlockSpec(stencil.shape, lambda i, at: (0, 0, 0)),
        pl.BlockSpec((size, cols), lambda i, at: (block_at(i, at), 0)),
    ]
    in_specs += [pl.BlockSpec((size, wide), halo_at)] * sum(len(group) for group in halos)
    in_specs += [pl.BlockSpec(block.shape, lambda i, at, n=block.ndim: (0,) * n) for block in blocks]
    out_specs = [pl.BlockSpec((size, cols), lambda i, at: (block_at(i, at), 0))]
    out_shape = [jax.ShapeDtypeStruct((rows, cols), BF16)]
    operands = [where, stencil, covariance] + [array for group in halos for array in group] + list(blocks)
    aliases = {}
    if ends:
        out_specs += [pl.BlockSpec((wide, cols), lambda i, at: (0, 0))] * 2
        out_shape += [jax.ShapeDtypeStruct((wide, cols), BF16)] * 2
    if held is not None:
        in_specs.append(pl.BlockSpec(memory_space=pl.ANY))
        aliases = {len(operands): 0}
        operands.append(held)
    return pl.pallas_call(
        kernel,
        grid_spec=pltpu.PrefetchScalarGridSpec(
            num_scalar_prefetch=1,
            grid=(count,),
            in_specs=in_specs,
            out_specs=out_specs,
            scratch_shapes=[pltpu.VMEM((2 * size, cols + 2 * wide), BF16)],
        ),
        out_shape=out_shape,
        input_output_aliases=aliases,
        compiler_params=params(),
        cost_estimate=cost(work),
        name="columns_operator",
    )(*operands)


def rows_operator(values, even, odd, stencil, where, steps, nlon, out_dtype, blocks=None, noise=None):
    rows, cols = values.shape
    lat_rows = rows // nlon
    wide = steps * nlon
    size = 2 * nlon
    span = 2 * steps * nlon
    pairs = lat_rows // 2
    group = 2 if pairs % 2 == 0 else 1
    ahead = (steps + 1) // 2
    exact = values.dtype == BF16
    makes = blocks is None
    chunk = cols if exact else min(cols, 512)

    def kernel(where_ref, stencil_ref, x_ref, even_ref, odd_ref, *rest):
        if makes:
            out_ref, a_ref = rest[:2]
        else:
            a_ref, noise_ref, out_ref = rest[:3]
        high_ref, sem = rest[2 if makes else 3 :][:2]
        raw_ref, low_ref = (None, None) if exact else rest[-2:]
        step = pl.program_id(0)

        def load(q):
            here = pl.ds(pl.multiple_of(q * size, size), size)
            there = pl.ds(pl.multiple_of(wide + q * size, nlon), size)
            target = high_ref.at[there, :] if exact else raw_ref.at[here, :]
            return pltpu.make_async_copy(x_ref.at[here, :], target, sem.at[q])

        def ready(q):
            load(q).wait()
            if not exact:
                there = pl.ds(pl.multiple_of(wide + q * size, nlon), size)
                here = pl.ds(pl.multiple_of(q * size, size), size)
                high_ref[there, :], low_ref[there, :] = split(raw_ref[here, :])

        @pl.when(step == 0)
        def _():
            is_odd = where_ref[3]
            at_even = pl.ds(pl.multiple_of((1 - is_odd) * (wide + rows), nlon), wide)
            at_odd = pl.ds(pl.multiple_of(is_odd * (wide + rows), nlon), wide)
            halos = [
                pltpu.make_async_copy(even_ref, high_ref.at[at_even, :], sem.at[pairs]),
                pltpu.make_async_copy(odd_ref, high_ref.at[at_odd, :], sem.at[pairs + 1]),
            ]
            for halo in halos:
                halo.start()
            for q in range(pairs):
                load(q).start()
            if not exact:
                low_ref[:wide, :] = jnp.zeros((wide, cols), BF16)
                low_ref[wide + rows :, :] = jnp.zeros((wide, cols), BF16)
            for halo in halos:
                halo.wait()
            for q in range(min(ahead, pairs)):
                ready(q)

        for j in range(group):
            q = step * group + j + ahead

            @pl.when(q < pairs)
            def _(q=q):
                ready(q)

        row = lambda j, d, a: stencil_ref[d + steps, pl.ds(2 * (step * group + j) + a, 1), :]
        if makes:
            for j in range(group):
                for a in range(2):
                    for k in range(2 * steps):
                        high, low = split(circulant(row(j, k - (steps - 1) - a, a)))
                        top = 2 * j * size + a * nlon
                        a_ref[top : top + nlon, k * nlon : (k + 1) * nlon] = high
                        a_ref[top + size : top + size + nlon, k * nlon : (k + 1) * nlon] = low
        for j in range(group):
            unit = lambda k: pl.multiple_of((2 * (step * group + j) + k) * nlon, nlon)
            weights = [jnp.sum(row(j, d, a), axis=1, keepdims=True) for a, d in ((0, -steps), (1, steps))]
            top = 2 * j * size
            for lane in range(0, cols, chunk):
                lanes = slice(lane, lane + chunk)
                both = product(a_ref[top : top + 2 * size, :], high_ref[pl.ds(unit(1), span), lanes])
                total = both[:size] + both[size:]
                if not exact:
                    total += product(a_ref[top : top + size, :], low_ref[pl.ds(unit(1), span), lanes])
                for a, k in ((0, 0), (1, 2 * steps + 1)):
                    far = high_ref[pl.ds(unit(k), nlon), lanes].astype(F32)
                    if not exact:
                        far += low_ref[pl.ds(unit(k), nlon), lanes].astype(F32)
                    value = total[a * nlon : (a + 1) * nlon, :] + weights[a] * far
                    out_ref[j * size + a * nlon : j * size + (a + 1) * nlon, lanes] = value.astype(out_dtype)
        if noise is not None:
            for a in range(2 * group):
                lat = 2 * group * step + a - where_ref[4]

                @pl.when(jnp.logical_and(lat >= 0, lat < cols // nlon))
                def _(a=a, lat=lat):
                    lanes = pl.ds(pl.multiple_of(lat * nlon, nlon), nlon)
                    eye = lax.broadcasted_iota(jnp.int32, (nlon, nlon), 0) == lax.broadcasted_iota(
                        jnp.int32, (nlon, nlon), 1
                    )
                    added = jnp.where(eye, noise_ref[pl.ds(2 * group * step + a, 1), :], 0.0)
                    out_ref[a * nlon : (a + 1) * nlon, lanes] += added

    in_specs = [pl.BlockSpec(stencil.shape, lambda g, at: (0, 0, 0))] + [pl.BlockSpec(memory_space=pl.ANY)] * 3
    operands = [where, stencil, values, even, odd]
    out_specs = [pl.BlockSpec((group * size, cols), lambda g, at: (g, 0))]
    out_shape = [jax.ShapeDtypeStruct((rows, cols), out_dtype)]
    blocks_spec = pl.BlockSpec((2 * group * size, span), lambda g, at: (g, 0))
    if makes:
        out_specs.append(blocks_spec)
        out_shape.append(jax.ShapeDtypeStruct((2 * rows, span), BF16))
    else:
        in_specs += [blocks_spec, pl.BlockSpec(noise.shape, lambda g, at: (0, 0))]
        operands += [blocks, noise]
    return pl.pallas_call(
        kernel,
        grid_spec=pltpu.PrefetchScalarGridSpec(
            num_scalar_prefetch=1,
            grid=(pairs // group,),
            in_specs=in_specs,
            out_specs=out_specs,
            scratch_shapes=[pltpu.VMEM((rows + 2 * wide, cols), BF16), pltpu.SemaphoreType.DMA((pairs + 2,))]
            + ([] if exact else [pltpu.VMEM((rows, cols), F32), pltpu.VMEM((rows + 2 * wide, cols), BF16)]),
        ),
        out_shape=out_shape,
        compiler_params=params(),
        cost_estimate=cost(1),
        name="rows_operator",
    )(*operands)


def shifted(block, axis, by):
    size = lax.axis_size(axis)
    pairs = [(i, i + by) for i in range(size) if 0 <= i + by < size]
    return lax.ppermute(block, axis, pairs)


def gathered(first, last, axis, dim, unit, halo, own):
    before, after = [], []
    need, hop = halo, 1
    while need > 0:
        take = min(own, need)
        size = first.shape[dim]
        before.insert(0, shifted(lax.slice_in_dim(last, size - take * unit, size, axis=dim), axis, hop))
        after.append(shifted(lax.slice_in_dim(first, 0, take * unit, axis=dim), axis, -hop))
        need, hop = need - take, hop + 1
    join = lambda parts: parts[0] if len(parts) == 1 else jnp.concatenate(parts, axis=dim)
    return join(before), join(after)


def exchanged(block, axis, odd):
    pairs = []
    for i in range(odd, lax.axis_size(axis) - 1, 2):
        pairs += [(i, i + 1), (i + 1, i)]
    return lax.ppermute(block, axis, pairs)


def mirrored(block, odd):
    n_row, n_col = lax.axis_size("row"), lax.axis_size("col")
    pairs = []
    for a in range(n_row):
        for b in range(n_col):
            to = 2 * a + (1 - b % 2) + (1 if (b + odd) % 2 else -1)
            here, there = a * n_col + b, (b // 2) * n_col + to
            if 0 <= to < n_col and here != there:
                pairs.append((here, there))
    return lax.ppermute(block, ("row", "col"), pairs)


def body(covariance, noise_var, wind_table, diffusivity, wind_index):
    rows_dev, cols_dev = covariance.shape
    lat_rows, nlon = noise_var.shape
    steps, nlat = wind_index.shape
    lats = cols_dev // nlon
    row_id, col_id = lax.axis_index("row"), lax.axis_index("col")
    own = lat_rows // 4
    fits = lat_rows == 2 * lats and own % 2 == 0 and own >= steps and own <= lats - steps
    if not fits or lax.axis_size("col") != 2 * lax.axis_size("row"):
        return plain_body(covariance, noise_var, wind_table, diffusivity, wind_index)

    near = lat_rows // 2 - own
    middle = lat_rows // 2
    outer, inner, wide = near * nlon, own * nlon, steps * nlon
    pick = lambda parity, even, odd: even + parity * (odd - even)
    col_odd, row_odd = col_id % 2, row_id % 2
    mirror_at, direct_at = pick(col_odd, middle - own, middle), pick(col_odd, middle, middle - own)
    diagonal = col_id * lats - row_id * lat_rows
    where = jnp.stack(
        [
            mirror_at // own,
            direct_at // own,
            col_odd,
            row_odd,
            diagonal,
            row_id * lat_rows,
            col_id * lats,
            mirror_at * nlon,
            pick(col_odd, lats, lats - steps) * nlon,
            pick(col_odd, 2 * lats - steps, 0) * nlon,
            pick(col_odd, lats - own, 0) * nlon,
            pick(col_odd, cols_dev - wide, 0),
            pick(col_odd, 0, cols_dev - wide),
            pick(row_odd, rows_dev - wide, 0),
            pick(row_odd, 0, rows_dev - wide),
            col_id // 2 == row_id,
        ]
    ).astype(jnp.int32)
    half = outer // 2
    spans = [(0, half, 0), (half, half, half)]
    spans += [(rows_dev - outer, half, outer), (rows_dev - half, half, outer + half), (0, 16, 2 * outer)]
    pieces = [(row, size, (11 + k,), wide, k, there, 0) for row, size, there in spans for k in range(2)]
    pieces += [((13 + k, j * nlon), nlon, 0, cols_dev, k + 2, j * nlon, 0) for k in range(2) for j in range(steps)]
    others = [((8 + k,), wide, (10,), inner, k, 0, nlon) for k in range(2)]
    others += [((7,), inner, (11 + k,), wide, k + 2, 0, 0) for k in range(2)]
    sent = packed(covariance, where, pieces)
    outers, ends = list(sent[:2]), list(sent[2:])
    outers = [exchanged(piece, "col", k) for k, piece in enumerate(outers)]
    ends = [exchanged(piece, "row", k) for k, piece in enumerate(ends)]
    row_s, col_s, *rest = stencils(
        wind_table, diffusivity, wind_index, where, lat_rows, lats, nlon, covariance, others
    )
    col_blocks, mirrors, inners = rest[:3], rest[3:5], rest[5:7]
    mirrors = [mirrored(piece, k) for k, piece in enumerate(mirrors)] + [mirrors[0]]

    operator_times_prior, blocks = rows_operator(covariance, *ends, row_s, where, steps, nlon, BF16)
    inners[0] = exchanged(inners[0], "col", 0)
    operator_times_prior, outers, inners[1] = lax.optimization_barrier(
        (operator_times_prior, outers, inners[1])
    )
    inners[1] = exchanged(inners[1], "col", 1)
    mirror, *ends = columns_operator(
        covariance, [outers], col_s, col_blocks, where, near, steps, nlon, 2, lambda i, at: i * (lat_rows // near - 1),
        None, True,
    )
    ends = [exchanged(piece, "row", k) for k, piece in enumerate(ends)]
    (mirror,) = columns_operator(
        covariance, [mirrors, inners], col_s, col_blocks, where, own, steps, nlon, 2, lambda i, at: at[i], mirror, False,
        10 ** 13,
    )
    (predicted_spread_matrix,) = rows_operator(
        mirror, *ends, row_s, where, steps, nlon, F32, blocks, noise_var
    )
    return (predicted_spread_matrix, operator_times_prior)


def plain_body(covariance, noise_var, wind_table, diffusivity, wind_index):
    rows_dev, cols_dev = covariance.shape
    lat_rows, nlon = noise_var.shape
    steps, nlat = wind_index.shape
    lats = cols_dev // nlon
    row_id, col_id = lax.axis_index("row"), lax.axis_index("col")
    sent = covariance.astype(BF16)
    sides = gathered(sent, sent, "col", 1, nlon, steps, lats)
    ends = gathered(sent, sent, "row", 0, nlon, steps, lat_rows)
    firsts = (row_id * lat_rows, col_id * lats)
    where = jnp.stack([0, 0, 1, 1, firsts[1] - firsts[0], *firsts]).astype(jnp.int32)
    row_s, col_s, *col_blocks = stencils(
        wind_table, diffusivity, wind_index, where, lat_rows, lats, nlon, covariance, []
    )
    operator_times_prior, blocks = rows_operator(covariance, *ends, row_s, where, steps, nlon, BF16)
    (mirror,) = columns_operator(
        covariance, [sides], col_s, col_blocks, where, 2, steps, nlon, lat_rows // 2, lambda i, at: i
    )
    ends = gathered(mirror, mirror, "row", 0, nlon, steps, lat_rows)
    (predicted_spread_matrix,) = rows_operator(
        mirror, *ends, row_s, where, steps, nlon, F32, blocks, noise_var
    )
    return (predicted_spread_matrix, operator_times_prior)


def solution(mesh):
    in_specs = (P("row", "col"), P("row", None), P(), P(), P())
    out_specs = (P("row", "col"), P("row", "col"))
    return jax.shard_map(body, mesh=mesh, in_specs=in_specs, out_specs=out_specs, check_vma=False)
```

```python
import functools

import jax
import jax.numpy as jnp
from jax import lax
from jax.experimental import pallas as pl
from jax.experimental.pallas import tpu as pltpu
from jax.sharding import PartitionSpec as P

F32 = jnp.float32
BF16 = jnp.bfloat16
VMEM_LIMIT = 63 * 1024 * 1024


def params():
    return pltpu.CompilerParams(vmem_limit_bytes=VMEM_LIMIT)


def cost(work):
    return pl.CostEstimate(flops=work, bytes_accessed=work, transcendentals=0)


def stencil_terms(zonal_cour, merid_cour, diffuse):
    middle_weight = 1.0 - zonal_cour * zonal_cour - merid_cour * merid_cour - 4.0 * diffuse
    eastward_weight = 0.5 * zonal_cour * zonal_cour - 0.5 * zonal_cour + diffuse
    west_w = 0.5 * zonal_cour * zonal_cour + 0.5 * zonal_cour + diffuse
    north_w = 0.5 * merid_cour * merid_cour - 0.5 * merid_cour + diffuse
    south_w = 0.5 * merid_cour * merid_cour + 0.5 * merid_cour + diffuse
    return middle_weight, eastward_weight, west_w, north_w, south_w


def split(values):
    high = values.astype(BF16)
    return high, (values - high.astype(F32)).astype(BF16)


def circulant(row):
    size = row.shape[1]
    return pltpu.roll(jnp.broadcast_to(row, (size, size)), 0, 1, stride=1, stride_axis=0)


def product(left, right):
    return jnp.dot(left, right, preferred_element_type=F32)


def composed(terms, lats, nlon):
    steps = len(terms)
    padded = lats + 2 * steps
    lane = lax.broadcasted_iota(jnp.int32, (padded, nlon), 1)
    rows = {0: (lane == 0).astype(F32)}
    for step_no in range(steps):
        low, high = step_no + 1, padded - step_no - 1
        c, e, w, n, s = [term[low:high] for term in terms[step_no]]
        size = high - low
        fresh = {}
        for d in range(-step_no - 1, step_no + 2):
            parts = []
            if d in rows:
                here = rows[d][1 : 1 + size]
                parts += [c * here, e * pltpu.roll(here, 1, 1), w * pltpu.roll(here, nlon - 1, 1)]
            if d - 1 in rows:
                parts.append(n * rows[d - 1][2 : 2 + size])
            if d + 1 in rows:
                parts.append(s * rows[d + 1][0:size])
            fresh[d] = functools.reduce(lambda x, y: x + y, parts)
        rows = fresh
    return rows


def swept(planes, weights):
    for step_no, (c, e, w, n, s) in enumerate(weights):
        fresh = []
        for i in range(1, len(planes) - 1):
            at, u = i + step_no, planes[i]
            nlon = u.shape[1]
            fresh.append(
                c(at) * u
                + e(at) * pltpu.roll(u, nlon - 1, 1)
                + w(at) * pltpu.roll(u, 1, 1)
                + n(at) * planes[i + 1]
                + s(at) * planes[i - 1]
            )
        planes = fresh
    return planes


def packing(pieces):
    def placed(piece):
        _, size, _, width, _, _, turn = piece
        return (width, size) if turn else (size, width)

    shapes = {}
    for piece in pieces:
        shape, out = placed(piece), piece[4]
        shapes[out] = (max(piece[5] + shape[0], shapes.get(out, (0,))[0]), shape[1])
    count = len(pieces)
    scratch = [pltpu.VMEM(piece[1:4:2], F32) for piece in pieces]
    scratch += [pltpu.VMEM(placed(piece), BF16) for piece in pieces]
    scratch += [pltpu.SemaphoreType.DMA((count,)), pltpu.SemaphoreType.DMA((count,))]

    def start(where_ref, p_ref, refs):
        first = lambda at: pl.multiple_of(where_ref[at[0]] + sum(at[1:]), 128) if isinstance(at, tuple) else at
        loads = []
        for k, (row, size, col, width, _, _, _) in enumerate(pieces):
            source = p_ref.at[pl.ds(first(row), size), pl.ds(first(col), width)]
            loads.append(pltpu.make_async_copy(source, refs[k], refs[2 * count].at[k]))
            loads[-1].start()
        return loads

    def finish(loads, results, refs):
        stores = []
        for k, piece in enumerate(pieces):
            loads[k].wait()
            got, made, turn, shape = refs[k], refs[count + k], piece[6], placed(piece)
            if turn:
                for a in range(0, shape[0], turn):
                    for b in range(0, shape[1], turn):
                        made[a : a + turn, b : b + turn] = got[b : b + turn, a : a + turn].T.astype(BF16)
            else:
                made[...] = got[...].astype(BF16)
            target = results[piece[4]].at[pl.ds(piece[5], shape[0]), :]
            stores.append(pltpu.make_async_copy(made, target, refs[2 * count + 1].at[k]))
            stores[-1].start()
        for copy in stores:
            copy.wait()

    return [jax.ShapeDtypeStruct(shapes[k], BF16) for k in range(len(shapes))], scratch, start, finish


def packed(covariance, where, pieces):
    out_shape, scratch, start, finish = packing(pieces)

    def kernel(where_ref, p_ref, *refs):
        results, refs = refs[: len(out_shape)], refs[len(out_shape) :]
        finish(start(where_ref, p_ref, refs), results, refs)

    return pl.pallas_call(
        kernel,
        in_specs=[pl.BlockSpec(memory_space=pltpu.SMEM), pl.BlockSpec(memory_space=pl.ANY)],
        out_specs=[pl.BlockSpec(memory_space=pl.ANY)] * len(out_shape),
        out_shape=out_shape,
        scratch_shapes=scratch,
        compiler_params=params(),
        cost_estimate=cost(1),
        name="packed",
    )(where, covariance)


def stencils(wind_table, diffusivity, wind_index, where, lat_rows, lats, nlon, covariance, pieces):
    steps, nlat = wind_index.shape
    sizes = (lat_rows, lats)
    span = 2 * steps * nlon
    pairs = lats // 2
    packs, pack_scratch, start, finish = packing(pieces)

    def kernel(table_ref, diffuse_ref, index_ref, where_ref, p_ref, *refs):
        row_out, col_out, high_out, low_out, step_out = refs[:5]
        results, scratch, refs = refs[5 : 5 + len(packs)], refs[5 + len(packs) :][:2], refs[7 + len(packs) :]
        loads = start(where_ref, p_ref, refs)
        for side, out in enumerate((row_out, col_out)):
            looked_up = scratch[side]
            terms = []
            for step_no in range(steps):
                for i in range(sizes[side] + 2 * steps):
                    lat = where_ref[5 + side] + i - steps
                    inside = jnp.logical_and(lat >= 0, lat < nlat)
                    entry = jnp.where(inside, index_ref[step_no, jnp.clip(lat, 0, nlat - 1)], -1)
                    looked_up[i : i + 1, :] = jnp.full((1, nlon), entry, jnp.int32)
                index = looked_up[...]
                zonal = merid = diffuse = jnp.zeros(index.shape, F32)
                for entry in range(wind_table.shape[0]):
                    here = index == entry
                    zonal = jnp.where(here, table_ref[0, entry], zonal)
                    merid = jnp.where(here, table_ref[1, entry], merid)
                    diffuse = jnp.where(here, diffuse_ref[entry], diffuse)
                c, e, w, n, s = [
                    jnp.where(index >= 0, term, 0.0) for term in stencil_terms(zonal, merid, diffuse)
                ]
                terms.append((c, w, e, n, s) if side else (c, e, w, n, s))
                if side:
                    for member, value in enumerate((c, e, w, n, s)):
                        step_out[5 * step_no + member] = value
            for d, value in composed(terms, sizes[side], nlon).items():
                out[d + steps] = value
        for q in range(pairs):
            for a in range(2):
                for k in range(2 * steps):
                    d = k - (steps - 1) - a
                    high, low = split(circulant(col_out[d + steps, 2 * q + a : 2 * q + a + 1, :]))
                    at = pl.ds(q * span + k * nlon, nlon)
                    high_out[at, a * nlon : (a + 1) * nlon] = high
                    low_out[at, a * nlon : (a + 1) * nlon] = low
        finish(loads, results, refs)

    return pl.pallas_call(
        kernel,
        in_specs=[pl.BlockSpec(memory_space=pltpu.SMEM)] * 4 + [pl.BlockSpec(memory_space=pl.ANY)],
        out_specs=[pl.BlockSpec(memory_space=pltpu.VMEM)] * 5 + [pl.BlockSpec(memory_space=pl.ANY)] * len(packs),
        out_shape=[jax.ShapeDtypeStruct((2 * steps + 1, size, nlon), F32) for size in sizes]
        + [jax.ShapeDtypeStruct((pairs * span, 2 * nlon), BF16)] * 2
        + [jax.ShapeDtypeStruct((5 * steps, lats + 2 * steps, nlon), F32)]
        + packs,
        scratch_shapes=[pltpu.VMEM((size + 2 * steps, nlon), jnp.int32) for size in sizes]
        + pack_scratch,
        compiler_params=params(),
        cost_estimate=cost(1),
        name="stencils",
    )(wind_table.T, diffusivity, wind_index, where, covariance)


def columns_operator(
    covariance, halos, stencil, blocks, where, unit, steps, nlon, count, block_at, held=None, ends=False, work=1
):
    rows, cols = covariance.shape
    lats = cols // nlon
    wide = steps * nlon
    size = unit * nlon
    span = 2 * steps * nlon
    pairs = lats // 2
    part = nlon // 2
    upper = size - part * (3 * size // (8 * part))

    def kernel(where_ref, stencil_ref, p_ref, *rest):
        halo_groups = []
        for group in halos:
            halo_groups.append(rest[: len(group)])
            rest = rest[len(group) :]
        (b_high, b_low, step_ref), outs, data_ref = rest[:3], rest[3:-1], rest[-1]
        if held is not None:
            outs = outs[1:]
        t_ref = outs[0]
        i = pl.program_id(0)
        col_odd, row_odd = where_ref[2] != 0, where_ref[3] != 0

        @pl.when(i == 0)
        def _():
            data_ref[size:, :wide] = jnp.zeros((size, wide), BF16)
            data_ref[size:, wide + cols :] = jnp.zeros((size, wide), BF16)

        for k, refs in enumerate(halo_groups):
            chosen = i >= 0 if len(halos) == 1 else i == k
            for odd in range(2):
                here = jnp.logical_and(chosen, col_odd if odd else jnp.logical_not(col_odd))
                even_at, odd_at = (0, wide + cols) if odd else (wide + cols, 0)

                @pl.when(here)
                def _(refs=refs, odd_at=odd_at):
                    data_ref[:size, odd_at : odd_at + wide] = refs[1][...]

                for ref, use in ((refs[0], None),) if len(refs) == 2 else ((refs[0], 0), (refs[2], 1)):
                    if use is not None:
                        here_too = jnp.logical_and(here, where_ref[15] == use)

                    @pl.when(here if use is None else here_too)
                    def _(ref=ref, even_at=even_at):
                        data_ref[:size, even_at : even_at + wide] = ref[...]

        data_ref[:upper, wide : wide + cols], data_ref[size : size + upper, wide : wide + cols] = split(
            p_ref[:upper, :]
        )
        weights = [
            [
                lambda at, k=5 * step_no + member: step_ref[k, at : at + 1, :]
                for member in range(5)
            ]
            for step_no in range(steps)
        ]
        starts = list(range(upper, size, part))
        for q in range(max(pairs, len(starts))):
            if q < pairs:
                window = slice((2 * q + 1) * nlon, (2 * q + 1) * nlon + span)
                of = pl.ds(q * span, span)
                total = product(data_ref[:upper, window], b_high[of, :])
                total += product(data_ref[size : size + upper, window], b_high[of, :])
                total += product(data_ref[:upper, window], b_low[of, :])
                for a, k, d in ((0, 2 * q, -steps), (1, 2 * q + 2 * steps + 1, steps)):
                    far = slice(k * nlon, (k + 1) * nlon)
                    row = stencil_ref[d + steps, 2 * q + a : 2 * q + a + 1, :]
                    weight = jnp.sum(row, axis=1, keepdims=True)
                    far_values = data_ref[:upper, far].astype(F32) + data_ref[size : size + upper, far].astype(F32)
                    value = total[:, a * nlon : (a + 1) * nlon] + weight * far_values
                    t_ref[:upper, (2 * q + a) * nlon : (2 * q + a + 1) * nlon] = value.astype(BF16)
            if q < len(starts):
                rows_at = slice(starts[q], starts[q] + part)
                planes = []
                for k in range(lats + 2 * steps):
                    if steps <= k < steps + lats:
                        planes.append(p_ref[rows_at, (k - steps) * nlon : (k - steps + 1) * nlon])
                    else:
                        planes.append(data_ref[rows_at, k * nlon : (k + 1) * nlon].astype(F32))
                for k, plane in enumerate(swept(planes, weights)):
                    t_ref[rows_at, k * nlon : (k + 1) * nlon] = plane.astype(BF16)
        if ends:
            for odd in range(2):
                is_odd = row_odd if odd else jnp.logical_not(row_odd)

                @pl.when(jnp.logical_and(i == 0, is_odd))
                def _(odd=odd):
                    outs[2 - odd][...] = t_ref[:wide, :]

                @pl.when(jnp.logical_and(i == count - 1, is_odd))
                def _(odd=odd):
                    outs[1 + odd][...] = t_ref[size - wide :, :]

    halo_at = (lambda i, at: (i, 0)) if len(halos) == 1 else (lambda i, at: (0, 0))
    in_specs = [
        pl.BlockSpec(stencil.shape, lambda i, at: (0, 0, 0)),
        pl.BlockSpec((size, cols), lambda i, at: (block_at(i, at), 0)),
    ]
    in_specs += [pl.BlockSpec((size, wide), halo_at)] * sum(len(group) for group in halos)
    in_specs += [pl.BlockSpec(block.shape, lambda i, at, n=block.ndim: (0,) * n) for block in blocks]
    out_specs = [pl.BlockSpec((size, cols), lambda i, at: (block_at(i, at), 0))]
    out_shape = [jax.ShapeDtypeStruct((rows, cols), BF16)]
    operands = [where, stencil, covariance] + [array for group in halos for array in group] + list(blocks)
    aliases = {}
    if ends:
        out_specs += [pl.BlockSpec((wide, cols), lambda i, at: (0, 0))] * 2
        out_shape += [jax.ShapeDtypeStruct((wide, cols), BF16)] * 2
    if held is not None:
        in_specs.append(pl.BlockSpec(memory_space=pl.ANY))
        aliases = {len(operands): 0}
        operands.append(held)
    return pl.pallas_call(
        kernel,
        grid_spec=pltpu.PrefetchScalarGridSpec(
            num_scalar_prefetch=1,
            grid=(count,),
            in_specs=in_specs,
            out_specs=out_specs,
            scratch_shapes=[pltpu.VMEM((2 * size, cols + 2 * wide), BF16)],
        ),
        out_shape=out_shape,
        input_output_aliases=aliases,
        compiler_params=params(),
        cost_estimate=cost(work),
        name="columns_operator",
    )(*operands)


def rows_operator(values, even, odd, stencil, where, steps, nlon, out_dtype, blocks=None, noise=None):
    rows, cols = values.shape
    lat_rows = rows // nlon
    wide = steps * nlon
    size = 2 * nlon
    span = 2 * steps * nlon
    pairs = lat_rows // 2
    group = 2 if pairs % 2 == 0 else 1
    ahead = (steps + 1) // 2
    exact = values.dtype == BF16
    makes = blocks is None
    chunk = cols if exact else min(cols, 512)

    def kernel(where_ref, stencil_ref, x_ref, even_ref, odd_ref, *rest):
        if makes:
            out_ref, a_ref = rest[:2]
        else:
            a_ref, noise_ref, out_ref = rest[:3]
        high_ref, sem = rest[2 if makes else 3 :][:2]
        raw_ref, low_ref = (None, None) if exact else rest[-2:]
        step = pl.program_id(0)

        def load(q):
            here = pl.ds(pl.multiple_of(q * size, size), size)
            there = pl.ds(pl.multiple_of(wide + q * size, nlon), size)
            target = high_ref.at[there, :] if exact else raw_ref.at[here, :]
            return pltpu.make_async_copy(x_ref.at[here, :], target, sem.at[q])

        def ready(q):
            load(q).wait()
            if not exact:
                there = pl.ds(pl.multiple_of(wide + q * size, nlon), size)
                here = pl.ds(pl.multiple_of(q * size, size), size)
                high_ref[there, :], low_ref[there, :] = split(raw_ref[here, :])

        @pl.when(step == 0)
        def _():
            is_odd = where_ref[3]
            at_even = pl.ds(pl.multiple_of((1 - is_odd) * (wide + rows), nlon), wide)
            at_odd = pl.ds(pl.multiple_of(is_odd * (wide + rows), nlon), wide)
            halos = [
                pltpu.make_async_copy(even_ref, high_ref.at[at_even, :], sem.at[pairs]),
                pltpu.make_async_copy(odd_ref, high_ref.at[at_odd, :], sem.at[pairs + 1]),
            ]
            for halo in halos:
                halo.start()
            for q in range(pairs):
                load(q).start()
            if not exact:
                low_ref[:wide, :] = jnp.zeros((wide, cols), BF16)
                low_ref[wide + rows :, :] = jnp.zeros((wide, cols), BF16)
            for halo in halos:
                halo.wait()
            for q in range(min(ahead, pairs)):
                ready(q)

        for j in range(group):
            q = step * group + j + ahead

            @pl.when(q < pairs)
            def _(q=q):
                ready(q)

        row = lambda j, d, a: stencil_ref[d + steps, pl.ds(2 * (step * group + j) + a, 1), :]
        if makes:
            for j in range(group):
                for a in range(2):
                    for k in range(2 * steps):
                        high, low = split(circulant(row(j, k - (steps - 1) - a, a)))
                        top = 2 * j * size + a * nlon
                        a_ref[top : top + nlon, k * nlon : (k + 1) * nlon] = high
                        a_ref[top + size : top + size + nlon, k * nlon : (k + 1) * nlon] = low
        for j in range(group):
            unit = lambda k: pl.multiple_of((2 * (step * group + j) + k) * nlon, nlon)
            weights = [jnp.sum(row(j, d, a), axis=1, keepdims=True) for a, d in ((0, -steps), (1, steps))]
            top = 2 * j * size
            for lane in range(0, cols, chunk):
                lanes = slice(lane, lane + chunk)
                both = product(a_ref[top : top + 2 * size, :], high_ref[pl.ds(unit(1), span), lanes])
                total = both[:size] + both[size:]
                if not exact:
                    total += product(a_ref[top : top + size, :], low_ref[pl.ds(unit(1), span), lanes])
                for a, k in ((0, 0), (1, 2 * steps + 1)):
                    far = high_ref[pl.ds(unit(k), nlon), lanes].astype(F32)
                    if not exact:
                        far += low_ref[pl.ds(unit(k), nlon), lanes].astype(F32)
                    value = total[a * nlon : (a + 1) * nlon, :] + weights[a] * far
                    out_ref[j * size + a * nlon : j * size + (a + 1) * nlon, lanes] = value.astype(out_dtype)
        if noise is not None:
            for a in range(2 * group):
                lat = 2 * group * step + a - where_ref[4]

                @pl.when(jnp.logical_and(lat >= 0, lat < cols // nlon))
                def _(a=a, lat=lat):
                    lanes = pl.ds(pl.multiple_of(lat * nlon, nlon), nlon)
                    eye = lax.broadcasted_iota(jnp.int32, (nlon, nlon), 0) == lax.broadcasted_iota(
                        jnp.int32, (nlon, nlon), 1
                    )
                    added = jnp.where(eye, noise_ref[pl.ds(2 * group * step + a, 1), :], 0.0)
                    out_ref[a * nlon : (a + 1) * nlon, lanes] += added

    in_specs = [pl.BlockSpec(stencil.shape, lambda g, at: (0, 0, 0))] + [pl.BlockSpec(memory_space=pl.ANY)] * 3
    operands = [where, stencil, values, even, odd]
    out_specs = [pl.BlockSpec((group * size, cols), lambda g, at: (g, 0))]
    out_shape = [jax.ShapeDtypeStruct((rows, cols), out_dtype)]
    blocks_spec = pl.BlockSpec((2 * group * size, span), lambda g, at: (g, 0))
    if makes:
        out_specs.append(blocks_spec)
        out_shape.append(jax.ShapeDtypeStruct((2 * rows, span), BF16))
    else:
        in_specs += [blocks_spec, pl.BlockSpec(noise.shape, lambda g, at: (0, 0))]
        operands += [blocks, noise]
    return pl.pallas_call(
        kernel,
        grid_spec=pltpu.PrefetchScalarGridSpec(
            num_scalar_prefetch=1,
            grid=(pairs // group,),
            in_specs=in_specs,
            out_specs=out_specs,
            scratch_shapes=[pltpu.VMEM((rows + 2 * wide, cols), BF16), pltpu.SemaphoreType.DMA((pairs + 2,))]
            + ([] if exact else [pltpu.VMEM((rows, cols), F32), pltpu.VMEM((rows + 2 * wide, cols), BF16)]),
        ),
        out_shape=out_shape,
        compiler_params=params(),
        cost_estimate=cost(1),
        name="rows_operator",
    )(*operands)


def shifted(block, axis, by):
    size = lax.axis_size(axis)
    pairs = [(i, i + by) for i in range(size) if 0 <= i + by < size]
    return lax.ppermute(block, axis, pairs)


def gathered(first, last, axis, dim, unit, halo, own):
    before, after = [], []
    need, hop = halo, 1
    while need > 0:
        take = min(own, need)
        size = first.shape[dim]
        before.insert(0, shifted(lax.slice_in_dim(last, size - take * unit, size, axis=dim), axis, hop))
        after.append(shifted(lax.slice_in_dim(first, 0, take * unit, axis=dim), axis, -hop))
        need, hop = need - take, hop + 1
    join = lambda parts: parts[0] if len(parts) == 1 else jnp.concatenate(parts, axis=dim)
    return join(before), join(after)


def exchanged(block, axis, odd):
    pairs = []
    for i in range(odd, lax.axis_size(axis) - 1, 2):
        pairs += [(i, i + 1), (i + 1, i)]
    return lax.ppermute(block, axis, pairs)


def mirrored(block, odd):
    n_row, n_col = lax.axis_size("row"), lax.axis_size("col")
    pairs = []
    for a in range(n_row):
        for b in range(n_col):
            to = 2 * a + (1 - b % 2) + (1 if (b + odd) % 2 else -1)
            here, there = a * n_col + b, (b // 2) * n_col + to
            if 0 <= to < n_col and here != there:
                pairs.append((here, there))
    return lax.ppermute(block, ("row", "col"), pairs)


def body(covariance, noise_var, wind_table, diffusivity, wind_index):
    rows_dev, cols_dev = covariance.shape
    lat_rows, nlon = noise_var.shape
    steps, nlat = wind_index.shape
    lats = cols_dev // nlon
    row_id, col_id = lax.axis_index("row"), lax.axis_index("col")
    own = lat_rows // 4
    fits = lat_rows == 2 * lats and own % 2 == 0 and own >= steps and own <= lats - steps
    if not fits or lax.axis_size("col") != 2 * lax.axis_size("row"):
        return plain_body(covariance, noise_var, wind_table, diffusivity, wind_index)

    near = lat_rows // 2 - own
    middle = lat_rows // 2
    outer, inner, wide = near * nlon, own * nlon, steps * nlon
    pick = lambda parity, even, odd: even + parity * (odd - even)
    col_odd, row_odd = col_id % 2, row_id % 2
    mirror_at, direct_at = pick(col_odd, middle - own, middle), pick(col_odd, middle, middle - own)
    diagonal = col_id * lats - row_id * lat_rows
    where = jnp.stack(
        [
            mirror_at // own,
            direct_at // own,
            col_odd,
            row_odd,
            diagonal,
            row_id * lat_rows,
            col_id * lats,
            mirror_at * nlon,
            pick(col_odd, lats, lats - steps) * nlon,
            pick(col_odd, 2 * lats - steps, 0) * nlon,
            pick(col_odd, lats - own, 0) * nlon,
            pick(col_odd, cols_dev - wide, 0),
            pick(col_odd, 0, cols_dev - wide),
            pick(row_odd, rows_dev - wide, 0),
            pick(row_odd, 0, rows_dev - wide),
            col_id // 2 == row_id,
        ]
    ).astype(jnp.int32)
    half = outer // 2
    spans = [(0, half, 0), (half, half, half)]
    spans += [(rows_dev - outer, half, outer), (rows_dev - half, half, outer + half), (0, 16, 2 * outer)]
    pieces = [(row, size, (11 + k,), wide, k, there, 0) for row, size, there in spans for k in range(2)]
    end_pieces = [((13 + k, j * nlon), nlon, 0, cols_dev, k, j * nlon, 0) for k in range(2) for j in range(steps)]
    others = [((8 + k,), wide, (10,), inner, k, 0, nlon) for k in range(2)]
    others += [((7,), inner, (11 + k,), wide, k + 2, 0, 0) for k in range(2)]
    outers = list(packed(covariance, where, pieces))
    later, outers[0] = lax.optimization_barrier((where, outers[0]))
    ends = packed(covariance, later, end_pieces)
    outers = [exchanged(piece, "col", k) for k, piece in enumerate(outers)]
    ends = [exchanged(piece, "row", k) for k, piece in enumerate(ends)]
    row_s, col_s, *rest = stencils(
        wind_table, diffusivity, wind_index, where, lat_rows, lats, nlon, covariance, others
    )
    col_blocks, mirrors, inners = rest[:3], rest[3:5], rest[5:7]
    mirrors = [mirrored(piece, k) for k, piece in enumerate(mirrors)] + [mirrors[0]]

    operator_times_prior, blocks = rows_operator(covariance, *ends, row_s, where, steps, nlon, BF16)
    inners[0] = exchanged(inners[0], "col", 0)
    operator_times_prior, outers, inners[1] = lax.optimization_barrier(
        (operator_times_prior, outers, inners[1])
    )
    inners[1] = exchanged(inners[1], "col", 1)
    mirror, *ends = columns_operator(
        covariance, [outers], col_s, col_blocks, where, near, steps, nlon, 2, lambda i, at: i * (lat_rows // near - 1),
        None, True,
    )
    ends = [exchanged(piece, "row", k) for k, piece in enumerate(ends)]
    (mirror,) = columns_operator(
        covariance, [mirrors, inners], col_s, col_blocks, where, own, steps, nlon, 2, lambda i, at: at[i], mirror, False,
        10 ** 13,
    )
    (predicted_spread_matrix,) = rows_operator(
        mirror, *ends, row_s, where, steps, nlon, F32, blocks, noise_var
    )
    return (predicted_spread_matrix, operator_times_prior)


def plain_body(covariance, noise_var, wind_table, diffusivity, wind_index):
    rows_dev, cols_dev = covariance.shape
    lat_rows, nlon = noise_var.shape
    steps, nlat = wind_index.shape
    lats = cols_dev // nlon
    row_id, col_id = lax.axis_index("row"), lax.axis_index("col")
    sent = covariance.astype(BF16)
    sides = gathered(sent, sent, "col", 1, nlon, steps, lats)
    ends = gathered(sent, sent, "row", 0, nlon, steps, lat_rows)
    firsts = (row_id * lat_rows, col_id * lats)
    where = jnp.stack([0, 0, 1, 1, firsts[1] - firsts[0], *firsts]).astype(jnp.int32)
    row_s, col_s, *col_blocks = stencils(
        wind_table, diffusivity, wind_index, where, lat_rows, lats, nlon, covariance, []
    )
    operator_times_prior, blocks = rows_operator(covariance, *ends, row_s, where, steps, nlon, BF16)
    (mirror,) = columns_operator(
        covariance, [sides], col_s, col_blocks, where, 2, steps, nlon, lat_rows // 2, lambda i, at: i
    )
    ends = gathered(mirror, mirror, "row", 0, nlon, steps, lat_rows)
    (predicted_spread_matrix,) = rows_operator(
        mirror, *ends, row_s, where, steps, nlon, F32, blocks, noise_var
    )
    return (predicted_spread_matrix, operator_times_prior)


def solution(mesh):
    in_specs = (P("row", "col"), P("row", None), P(), P(), P())
    out_specs = (P("row", "col"), P("row", "col"))
    return jax.shard_map(body, mesh=mesh, in_specs=in_specs, out_specs=out_specs, check_vma=False)
```

```python
import functools

import jax
import jax.numpy as jnp
from jax import lax
from jax.experimental import pallas as pl
from jax.experimental.pallas import tpu as pltpu
from jax.sharding import PartitionSpec as P

F32 = jnp.float32
BF16 = jnp.bfloat16
VMEM_LIMIT = 63 * 1024 * 1024


def params():
    return pltpu.CompilerParams(vmem_limit_bytes=VMEM_LIMIT)


def cost(work):
    return pl.CostEstimate(flops=work, bytes_accessed=work, transcendentals=0)


def stencil_terms(zonal_cour, merid_cour, diffuse):
    middle_weight = 1.0 - zonal_cour * zonal_cour - merid_cour * merid_cour - 4.0 * diffuse
    eastward_weight = 0.5 * zonal_cour * zonal_cour - 0.5 * zonal_cour + diffuse
    west_w = 0.5 * zonal_cour * zonal_cour + 0.5 * zonal_cour + diffuse
    north_w = 0.5 * merid_cour * merid_cour - 0.5 * merid_cour + diffuse
    south_w = 0.5 * merid_cour * merid_cour + 0.5 * merid_cour + diffuse
    return middle_weight, eastward_weight, west_w, north_w, south_w


def split(values):
    high = values.astype(BF16)
    return high, (values - high.astype(F32)).astype(BF16)


def circulant(row):
    size = row.shape[1]
    return pltpu.roll(jnp.broadcast_to(row, (size, size)), 0, 1, stride=1, stride_axis=0)


def product(left, right):
    return jnp.dot(left, right, preferred_element_type=F32)


def composed(terms, lats, nlon):
    steps = len(terms)
    padded = lats + 2 * steps
    lane = lax.broadcasted_iota(jnp.int32, (padded, nlon), 1)
    rows = {0: (lane == 0).astype(F32)}
    for step_no in range(steps):
        low, high = step_no + 1, padded - step_no - 1
        c, e, w, n, s = [term[low:high] for term in terms[step_no]]
        size = high - low
        fresh = {}
        for d in range(-step_no - 1, step_no + 2):
            parts = []
            if d in rows:
                here = rows[d][1 : 1 + size]
                parts += [c * here, e * pltpu.roll(here, 1, 1), w * pltpu.roll(here, nlon - 1, 1)]
            if d - 1 in rows:
                parts.append(n * rows[d - 1][2 : 2 + size])
            if d + 1 in rows:
                parts.append(s * rows[d + 1][0:size])
            fresh[d] = functools.reduce(lambda x, y: x + y, parts)
        rows = fresh
    return rows


def swept(planes, weights):
    for step_no, (c, e, w, n, s) in enumerate(weights):
        fresh = []
        for i in range(1, len(planes) - 1):
            at, u = i + step_no, planes[i]
            nlon = u.shape[1]
            fresh.append(
                c(at) * u
                + e(at) * pltpu.roll(u, nlon - 1, 1)
                + w(at) * pltpu.roll(u, 1, 1)
                + n(at) * planes[i + 1]
                + s(at) * planes[i - 1]
            )
        planes = fresh
    return planes


def packing(pieces):
    def placed(piece):
        _, size, _, width, _, _, turn = piece
        return (width, size) if turn else (size, width)

    shapes = {}
    for piece in pieces:
        shape, out = placed(piece), piece[4]
        shapes[out] = (max(piece[5] + shape[0], shapes.get(out, (0,))[0]), shape[1])
    count = len(pieces)
    scratch = [pltpu.VMEM(piece[1:4:2], F32) for piece in pieces]
    scratch += [pltpu.VMEM(placed(piece), BF16) for piece in pieces]
    scratch += [pltpu.SemaphoreType.DMA((count,)), pltpu.SemaphoreType.DMA((count,))]

    def start(where_ref, p_ref, refs):
        first = lambda at: pl.multiple_of(where_ref[at[0]] + sum(at[1:]), 128) if isinstance(at, tuple) else at
        loads = []
        for k, (row, size, col, width, _, _, _) in enumerate(pieces):
            source = p_ref.at[pl.ds(first(row), size), pl.ds(first(col), width)]
            loads.append(pltpu.make_async_copy(source, refs[k], refs[2 * count].at[k]))
            loads[-1].start()
        return loads

    def finish(loads, results, refs):
        stores = []
        for k, piece in enumerate(pieces):
            loads[k].wait()
            got, made, turn, shape = refs[k], refs[count + k], piece[6], placed(piece)
            if turn:
                for a in range(0, shape[0], turn):
                    for b in range(0, shape[1], turn):
                        made[a : a + turn, b : b + turn] = got[b : b + turn, a : a + turn].T.astype(BF16)
            else:
                made[...] = got[...].astype(BF16)
            target = results[piece[4]].at[pl.ds(piece[5], shape[0]), :]
            stores.append(pltpu.make_async_copy(made, target, refs[2 * count + 1].at[k]))
            stores[-1].start()
        for copy in stores:
            copy.wait()

    return [jax.ShapeDtypeStruct(shapes[k], BF16) for k in range(len(shapes))], scratch, start, finish


def packed(covariance, where, pieces):
    out_shape, scratch, start, finish = packing(pieces)

    def kernel(where_ref, p_ref, *refs):
        results, refs = refs[: len(out_shape)], refs[len(out_shape) :]
        finish(start(where_ref, p_ref, refs), results, refs)

    return pl.pallas_call(
        kernel,
        in_specs=[pl.BlockSpec(memory_space=pltpu.SMEM), pl.BlockSpec(memory_space=pl.ANY)],
        out_specs=[pl.BlockSpec(memory_space=pl.ANY)] * len(out_shape),
        out_shape=out_shape,
        scratch_shapes=scratch,
        compiler_params=params(),
        cost_estimate=cost(1),
        name="packed",
    )(where, covariance)


def stencils(wind_table, diffusivity, wind_index, where, lat_rows, lats, nlon, covariance, pieces):
    steps, nlat = wind_index.shape
    sizes = (lat_rows, lats)
    span = 2 * steps * nlon
    pairs = lats // 2
    packs, pack_scratch, start, finish = packing(pieces)

    def kernel(table_ref, diffuse_ref, index_ref, where_ref, p_ref, *refs):
        row_out, col_out, high_out, low_out, step_out = refs[:5]
        results, scratch, refs = refs[5 : 5 + len(packs)], refs[5 + len(packs) :][:2], refs[7 + len(packs) :]
        loads = start(where_ref, p_ref, refs)
        for side, out in enumerate((row_out, col_out)):
            looked_up = scratch[side]
            terms = []
            for step_no in range(steps):
                for i in range(sizes[side] + 2 * steps):
                    lat = where_ref[5 + side] + i - steps
                    inside = jnp.logical_and(lat >= 0, lat < nlat)
                    entry = jnp.where(inside, index_ref[step_no, jnp.clip(lat, 0, nlat - 1)], -1)
                    looked_up[i : i + 1, :] = jnp.full((1, nlon), entry, jnp.int32)
                index = looked_up[...]
                zonal = merid = diffuse = jnp.zeros(index.shape, F32)
                for entry in range(wind_table.shape[0]):
                    here = index == entry
                    zonal = jnp.where(here, table_ref[0, entry], zonal)
                    merid = jnp.where(here, table_ref[1, entry], merid)
                    diffuse = jnp.where(here, diffuse_ref[entry], diffuse)
                c, e, w, n, s = [
                    jnp.where(index >= 0, term, 0.0) for term in stencil_terms(zonal, merid, diffuse)
                ]
                terms.append((c, w, e, n, s) if side else (c, e, w, n, s))
                if side:
                    for member, value in enumerate((c, e, w, n, s)):
                        step_out[5 * step_no + member] = value
            for d, value in composed(terms, sizes[side], nlon).items():
                out[d + steps] = value
        for q in range(pairs):
            for a in range(2):
                for k in range(2 * steps):
                    d = k - (steps - 1) - a
                    high, low = split(circulant(col_out[d + steps, 2 * q + a : 2 * q + a + 1, :]))
                    at = pl.ds(q * span + k * nlon, nlon)
                    high_out[at, a * nlon : (a + 1) * nlon] = high
                    low_out[at, a * nlon : (a + 1) * nlon] = low
        finish(loads, results, refs)

    return pl.pallas_call(
        kernel,
        in_specs=[pl.BlockSpec(memory_space=pltpu.SMEM)] * 4 + [pl.BlockSpec(memory_space=pl.ANY)],
        out_specs=[pl.BlockSpec(memory_space=pltpu.VMEM)] * 5 + [pl.BlockSpec(memory_space=pl.ANY)] * len(packs),
        out_shape=[jax.ShapeDtypeStruct((2 * steps + 1, size, nlon), F32) for size in sizes]
        + [jax.ShapeDtypeStruct((pairs * span, 2 * nlon), BF16)] * 2
        + [jax.ShapeDtypeStruct((5 * steps, lats + 2 * steps, nlon), F32)]
        + packs,
        scratch_shapes=[pltpu.VMEM((size + 2 * steps, nlon), jnp.int32) for size in sizes]
        + pack_scratch,
        compiler_params=params(),
        cost_estimate=cost(1),
        name="stencils",
    )(wind_table.T, diffusivity, wind_index, where, covariance)


def columns_operator(
    covariance, halos, stencil, blocks, where, unit, steps, nlon, count, block_at, held=None, ends=False, work=1
):
    rows, cols = covariance.shape
    lats = cols // nlon
    wide = steps * nlon
    size = unit * nlon
    span = 2 * steps * nlon
    pairs = lats // 2
    part = nlon // 2
    upper = size - part * (3 * size // (8 * part))

    def kernel(where_ref, stencil_ref, p_ref, *rest):
        halo_groups = []
        for group in halos:
            halo_groups.append(rest[: len(group)])
            rest = rest[len(group) :]
        (b_high, b_low, step_ref), outs, data_ref = rest[:3], rest[3:-1], rest[-1]
        if held is not None:
            outs = outs[1:]
        t_ref = outs[0]
        i = pl.program_id(0)
        col_odd, row_odd = where_ref[2] != 0, where_ref[3] != 0

        @pl.when(i == 0)
        def _():
            data_ref[size:, :wide] = jnp.zeros((size, wide), BF16)
            data_ref[size:, wide + cols :] = jnp.zeros((size, wide), BF16)

        for k, refs in enumerate(halo_groups):
            chosen = i >= 0 if len(halos) == 1 else i == k
            for odd in range(2):
                here = jnp.logical_and(chosen, col_odd if odd else jnp.logical_not(col_odd))
                even_at, odd_at = (0, wide + cols) if odd else (wide + cols, 0)

                @pl.when(here)
                def _(refs=refs, odd_at=odd_at):
                    data_ref[:size, odd_at : odd_at + wide] = refs[1][...]

                for ref, use in ((refs[0], None),) if len(refs) == 2 else ((refs[0], 0), (refs[2], 1)):
                    if use is not None:
                        here_too = jnp.logical_and(here, where_ref[15] == use)

                    @pl.when(here if use is None else here_too)
                    def _(ref=ref, even_at=even_at):
                        data_ref[:size, even_at : even_at + wide] = ref[...]

        data_ref[:upper, wide : wide + cols], data_ref[size : size + upper, wide : wide + cols] = split(
            p_ref[:upper, :]
        )
        weights = [
            [
                lambda at, k=5 * step_no + member: step_ref[k, at : at + 1, :]
                for member in range(5)
            ]
            for step_no in range(steps)
        ]
        starts = list(range(upper, size, part))
        for q in range(max(pairs, len(starts))):
            if q < pairs:
                window = slice((2 * q + 1) * nlon, (2 * q + 1) * nlon + span)
                of = pl.ds(q * span, span)
                total = product(data_ref[:upper, window], b_high[of, :])
                total += product(data_ref[size : size + upper, window], b_high[of, :])
                total += product(data_ref[:upper, window], b_low[of, :])
                for a, k, d in ((0, 2 * q, -steps), (1, 2 * q + 2 * steps + 1, steps)):
                    far = slice(k * nlon, (k + 1) * nlon)
                    row = stencil_ref[d + steps, 2 * q + a : 2 * q + a + 1, :]
                    weight = jnp.sum(row, axis=1, keepdims=True)
                    far_values = data_ref[:upper, far].astype(F32) + data_ref[size : size + upper, far].astype(F32)
                    value = total[:, a * nlon : (a + 1) * nlon] + weight * far_values
                    t_ref[:upper, (2 * q + a) * nlon : (2 * q + a + 1) * nlon] = value.astype(BF16)
            if q < len(starts):
                rows_at = slice(starts[q], starts[q] + part)
                planes = []
                for k in range(lats + 2 * steps):
                    if steps <= k < steps + lats:
                        planes.append(p_ref[rows_at, (k - steps) * nlon : (k - steps + 1) * nlon])
                    else:
                        planes.append(data_ref[rows_at, k * nlon : (k + 1) * nlon].astype(F32))
                for k, plane in enumerate(swept(planes, weights)):
                    t_ref[rows_at, k * nlon : (k + 1) * nlon] = plane.astype(BF16)
        if ends:
            for odd in range(2):
                is_odd = row_odd if odd else jnp.logical_not(row_odd)

                @pl.when(jnp.logical_and(i == 0, is_odd))
                def _(odd=odd):
                    outs[2 - odd][...] = t_ref[:wide, :]

                @pl.when(jnp.logical_and(i == count - 1, is_odd))
                def _(odd=odd):
                    outs[1 + odd][...] = t_ref[size - wide :, :]

    members = [member if isinstance(member, tuple) else (member, 0) for group in halos for member in group]
    in_specs = [
        pl.BlockSpec(stencil.shape, lambda i, at: (0, 0, 0)),
        pl.BlockSpec((size, cols), lambda i, at: (block_at(i, at), 0)),
    ]
    for _, block in members:
        halo_at = (lambda i, at: (i, 0)) if len(halos) == 1 else (lambda i, at, block=block: (block, 0))
        in_specs.append(pl.BlockSpec((size, wide), halo_at))
    in_specs += [pl.BlockSpec(block.shape, lambda i, at, n=block.ndim: (0,) * n) for block in blocks]
    out_specs = [pl.BlockSpec((size, cols), lambda i, at: (block_at(i, at), 0))]
    out_shape = [jax.ShapeDtypeStruct((rows, cols), BF16)]
    operands = [where, stencil, covariance] + [array for array, _ in members] + list(blocks)
    aliases = {}
    if ends:
        out_specs += [pl.BlockSpec((wide, cols), lambda i, at: (0, 0))] * 2
        out_shape += [jax.ShapeDtypeStruct((wide, cols), BF16)] * 2
    if held is not None:
        in_specs.append(pl.BlockSpec(memory_space=pl.ANY))
        aliases = {len(operands): 0}
        operands.append(held)
    return pl.pallas_call(
        kernel,
        grid_spec=pltpu.PrefetchScalarGridSpec(
            num_scalar_prefetch=1,
            grid=(count,),
            in_specs=in_specs,
            out_specs=out_specs,
            scratch_shapes=[pltpu.VMEM((2 * size, cols + 2 * wide), BF16)],
        ),
        out_shape=out_shape,
        input_output_aliases=aliases,
        compiler_params=params(),
        cost_estimate=cost(work),
        name="columns_operator",
    )(*operands)


def rows_operator(values, even, odd, stencil, where, steps, nlon, out_dtype, blocks=None, noise=None):
    rows, cols = values.shape
    lat_rows = rows // nlon
    wide = steps * nlon
    size = 2 * nlon
    span = 2 * steps * nlon
    pairs = lat_rows // 2
    group = 2 if pairs % 2 == 0 else 1
    ahead = (steps + 1) // 2
    exact = values.dtype == BF16
    makes = blocks is None
    chunk = cols if exact else min(cols, 512)

    def kernel(where_ref, stencil_ref, x_ref, even_ref, odd_ref, *rest):
        if makes:
            out_ref, a_ref = rest[:2]
        else:
            a_ref, noise_ref, out_ref = rest[:3]
        high_ref, sem = rest[2 if makes else 3 :][:2]
        raw_ref, low_ref = (None, None) if exact else rest[-2:]
        step = pl.program_id(0)

        def load(q):
            here = pl.ds(pl.multiple_of(q * size, size), size)
            there = pl.ds(pl.multiple_of(wide + q * size, nlon), size)
            target = high_ref.at[there, :] if exact else raw_ref.at[here, :]
            return pltpu.make_async_copy(x_ref.at[here, :], target, sem.at[q])

        def ready(q):
            load(q).wait()
            if not exact:
                there = pl.ds(pl.multiple_of(wide + q * size, nlon), size)
                here = pl.ds(pl.multiple_of(q * size, size), size)
                high_ref[there, :], low_ref[there, :] = split(raw_ref[here, :])

        @pl.when(step == 0)
        def _():
            is_odd = where_ref[3]
            at_even = pl.ds(pl.multiple_of((1 - is_odd) * (wide + rows), nlon), wide)
            at_odd = pl.ds(pl.multiple_of(is_odd * (wide + rows), nlon), wide)
            halos = [
                pltpu.make_async_copy(even_ref, high_ref.at[at_even, :], sem.at[pairs]),
                pltpu.make_async_copy(odd_ref, high_ref.at[at_odd, :], sem.at[pairs + 1]),
            ]
            for halo in halos:
                halo.start()
            for q in range(pairs):
                load(q).start()
            if not exact:
                low_ref[:wide, :] = jnp.zeros((wide, cols), BF16)
                low_ref[wide + rows :, :] = jnp.zeros((wide, cols), BF16)
            for halo in halos:
                halo.wait()
            for q in range(min(ahead, pairs)):
                ready(q)

        for j in range(group):
            q = step * group + j + ahead

            @pl.when(q < pairs)
            def _(q=q):
                ready(q)

        row = lambda j, d, a: stencil_ref[d + steps, pl.ds(2 * (step * group + j) + a, 1), :]
        if makes:
            for j in range(group):
                for a in range(2):
                    for k in range(2 * steps):
                        high, low = split(circulant(row(j, k - (steps - 1) - a, a)))
                        top = 2 * j * size + a * nlon
                        a_ref[top : top + nlon, k * nlon : (k + 1) * nlon] = high
                        a_ref[top + size : top + size + nlon, k * nlon : (k + 1) * nlon] = low
        for j in range(group):
            unit = lambda k: pl.multiple_of((2 * (step * group + j) + k) * nlon, nlon)
            weights = [jnp.sum(row(j, d, a), axis=1, keepdims=True) for a, d in ((0, -steps), (1, steps))]
            top = 2 * j * size
            for lane in range(0, cols, chunk):
                lanes = slice(lane, lane + chunk)
                both = product(a_ref[top : top + 2 * size, :], high_ref[pl.ds(unit(1), span), lanes])
                total = both[:size] + both[size:]
                if not exact:
                    total += product(a_ref[top : top + size, :], low_ref[pl.ds(unit(1), span), lanes])
                for a, k in ((0, 0), (1, 2 * steps + 1)):
                    far = high_ref[pl.ds(unit(k), nlon), lanes].astype(F32)
                    if not exact:
                        far += low_ref[pl.ds(unit(k), nlon), lanes].astype(F32)
                    value = total[a * nlon : (a + 1) * nlon, :] + weights[a] * far
                    out_ref[j * size + a * nlon : j * size + (a + 1) * nlon, lanes] = value.astype(out_dtype)
        if noise is not None:
            for a in range(2 * group):
                lat = 2 * group * step + a - where_ref[4]

                @pl.when(jnp.logical_and(lat >= 0, lat < cols // nlon))
                def _(a=a, lat=lat):
                    lanes = pl.ds(pl.multiple_of(lat * nlon, nlon), nlon)
                    eye = lax.broadcasted_iota(jnp.int32, (nlon, nlon), 0) == lax.broadcasted_iota(
                        jnp.int32, (nlon, nlon), 1
                    )
                    added = jnp.where(eye, noise_ref[pl.ds(2 * group * step + a, 1), :], 0.0)
                    out_ref[a * nlon : (a + 1) * nlon, lanes] += added

    in_specs = [pl.BlockSpec(stencil.shape, lambda g, at: (0, 0, 0))] + [pl.BlockSpec(memory_space=pl.ANY)] * 3
    operands = [where, stencil, values, even, odd]
    out_specs = [pl.BlockSpec((group * size, cols), lambda g, at: (g, 0))]
    out_shape = [jax.ShapeDtypeStruct((rows, cols), out_dtype)]
    blocks_spec = pl.BlockSpec((2 * group * size, span), lambda g, at: (g, 0))
    if makes:
        out_specs.append(blocks_spec)
        out_shape.append(jax.ShapeDtypeStruct((2 * rows, span), BF16))
    else:
        in_specs += [blocks_spec, pl.BlockSpec(noise.shape, lambda g, at: (0, 0))]
        operands += [blocks, noise]
    return pl.pallas_call(
        kernel,
        grid_spec=pltpu.PrefetchScalarGridSpec(
            num_scalar_prefetch=1,
            grid=(pairs // group,),
            in_specs=in_specs,
            out_specs=out_specs,
            scratch_shapes=[pltpu.VMEM((rows + 2 * wide, cols), BF16), pltpu.SemaphoreType.DMA((pairs + 2,))]
            + ([] if exact else [pltpu.VMEM((rows, cols), F32), pltpu.VMEM((rows + 2 * wide, cols), BF16)]),
        ),
        out_shape=out_shape,
        compiler_params=params(),
        cost_estimate=cost(1),
        name="rows_operator",
    )(*operands)


def shifted(block, axis, by):
    size = lax.axis_size(axis)
    pairs = [(i, i + by) for i in range(size) if 0 <= i + by < size]
    return lax.ppermute(block, axis, pairs)


def gathered(first, last, axis, dim, unit, halo, own):
    before, after = [], []
    need, hop = halo, 1
    while need > 0:
        take = min(own, need)
        size = first.shape[dim]
        before.insert(0, shifted(lax.slice_in_dim(last, size - take * unit, size, axis=dim), axis, hop))
        after.append(shifted(lax.slice_in_dim(first, 0, take * unit, axis=dim), axis, -hop))
        need, hop = need - take, hop + 1
    join = lambda parts: parts[0] if len(parts) == 1 else jnp.concatenate(parts, axis=dim)
    return join(before), join(after)


def exchanged(block, axis, odd):
    pairs = []
    for i in range(odd, lax.axis_size(axis) - 1, 2):
        pairs += [(i, i + 1), (i + 1, i)]
    return lax.ppermute(block, axis, pairs)


def mirrored(block, odd):
    n_row, n_col = lax.axis_size("row"), lax.axis_size("col")
    pairs = []
    for a in range(n_row):
        for b in range(n_col):
            to = 2 * a + (1 - b % 2) + (1 if (b + odd) % 2 else -1)
            here, there = a * n_col + b, (b // 2) * n_col + to
            if 0 <= to < n_col and here != there:
                pairs.append((here, there))
    return lax.ppermute(block, ("row", "col"), pairs)


def body(covariance, noise_var, wind_table, diffusivity, wind_index):
    rows_dev, cols_dev = covariance.shape
    lat_rows, nlon = noise_var.shape
    steps, nlat = wind_index.shape
    lats = cols_dev // nlon
    row_id, col_id = lax.axis_index("row"), lax.axis_index("col")
    own = lat_rows // 4
    fits = lat_rows == 2 * lats and own % 2 == 0 and own >= steps and own <= lats - steps
    if not fits or lax.axis_size("col") != 2 * lax.axis_size("row"):
        return plain_body(covariance, noise_var, wind_table, diffusivity, wind_index)

    near = lat_rows // 2 - own
    middle = lat_rows // 2
    outer, inner, wide = near * nlon, own * nlon, steps * nlon
    pick = lambda parity, even, odd: even + parity * (odd - even)
    col_odd, row_odd = col_id % 2, row_id % 2
    mirror_at, direct_at = pick(col_odd, middle - own, middle), pick(col_odd, middle, middle - own)
    diagonal = col_id * lats - row_id * lat_rows
    where = jnp.stack(
        [
            mirror_at // own,
            direct_at // own,
            col_odd,
            row_odd,
            diagonal,
            row_id * lat_rows,
            col_id * lats,
            mirror_at * nlon,
            pick(col_odd, lats, lats - steps) * nlon,
            pick(col_odd, 2 * lats - steps, 0) * nlon,
            pick(col_odd, lats - own, 0) * nlon,
            pick(col_odd, cols_dev - wide, 0),
            pick(col_odd, 0, cols_dev - wide),
            pick(row_odd, rows_dev - wide, 0),
            pick(row_odd, 0, rows_dev - wide),
            col_id // 2 == row_id,
        ]
    ).astype(jnp.int32)
    half = outer // 2
    spans = [(0, half, 0), (half, half, half)]
    spans += [(rows_dev - outer, half, outer), (rows_dev - half, half, outer + half)]
    pieces = [(row, size, (11 + k,), wide, k, there, 0) for row, size, there in spans for k in range(2)]
    pieces += [((7,), inner, (11,), wide, 0, 2 * outer, 0), (0, 16, (12,), wide, 1, 2 * outer, 0)]
    end_pieces = [((13 + k, j * nlon), nlon, 0, cols_dev, k, j * nlon, 0) for k in range(2) for j in range(steps)]
    others = [((8 + k,), wide, (10,), inner, k, 0, nlon) for k in range(2)]
    others += [((7,), inner, (12,), wide, 2, 0, 0)]
    outers = list(packed(covariance, where, pieces))
    later, outers[0] = lax.optimization_barrier((where, outers[0]))
    ends = packed(covariance, later, end_pieces)
    outers = [exchanged(piece, "col", k) for k, piece in enumerate(outers)]
    ends = [exchanged(piece, "row", k) for k, piece in enumerate(ends)]
    row_s, col_s, *rest = stencils(
        wind_table, diffusivity, wind_index, where, lat_rows, lats, nlon, covariance, others
    )
    col_blocks, mirrors, inner_odd = rest[:3], rest[3:5], rest[5]
    mirrors = [mirrored(piece, k) for k, piece in enumerate(mirrors)] + [mirrors[0]]

    operator_times_prior, blocks = rows_operator(covariance, *ends, row_s, where, steps, nlon, BF16)
    operator_times_prior, outers, inner_odd = lax.optimization_barrier((operator_times_prior, outers, inner_odd))
    inner_odd = exchanged(inner_odd, "col", 1)
    mirror, *ends = columns_operator(
        covariance, [outers], col_s, col_blocks, where, near, steps, nlon, 2, lambda i, at: i * (lat_rows // near - 1),
        None, True,
    )
    ends = [exchanged(piece, "row", k) for k, piece in enumerate(ends)]
    (mirror,) = columns_operator(
        covariance, [mirrors, [(outers[0], 2 * near // own), inner_odd]], col_s, col_blocks, where, own, steps, nlon, 2, lambda i, at: at[i], mirror, False,
        10 ** 13,
    )
    (predicted_spread_matrix,) = rows_operator(
        mirror, *ends, row_s, where, steps, nlon, F32, blocks, noise_var
    )
    return (predicted_spread_matrix, operator_times_prior)


def plain_body(covariance, noise_var, wind_table, diffusivity, wind_index):
    rows_dev, cols_dev = covariance.shape
    lat_rows, nlon = noise_var.shape
    steps, nlat = wind_index.shape
    lats = cols_dev // nlon
    row_id, col_id = lax.axis_index("row"), lax.axis_index("col")
    sent = covariance.astype(BF16)
    sides = gathered(sent, sent, "col", 1, nlon, steps, lats)
    ends = gathered(sent, sent, "row", 0, nlon, steps, lat_rows)
    firsts = (row_id * lat_rows, col_id * lats)
    where = jnp.stack([0, 0, 1, 1, firsts[1] - firsts[0], *firsts]).astype(jnp.int32)
    row_s, col_s, *col_blocks = stencils(
        wind_table, diffusivity, wind_index, where, lat_rows, lats, nlon, covariance, []
    )
    operator_times_prior, blocks = rows_operator(covariance, *ends, row_s, where, steps, nlon, BF16)
    (mirror,) = columns_operator(
        covariance, [sides], col_s, col_blocks, where, 2, steps, nlon, lat_rows // 2, lambda i, at: i
    )
    ends = gathered(mirror, mirror, "row", 0, nlon, steps, lat_rows)
    (predicted_spread_matrix,) = rows_operator(
        mirror, *ends, row_s, where, steps, nlon, F32, blocks, noise_var
    )
    return (predicted_spread_matrix, operator_times_prior)


def solution(mesh):
    in_specs = (P("row", "col"), P("row", None), P(), P(), P())
    out_specs = (P("row", "col"), P("row", "col"))
    return jax.shard_map(body, mesh=mesh, in_specs=in_specs, out_specs=out_specs, check_vma=False)
```

```python
import functools

import jax
import jax.numpy as jnp
from jax import lax
from jax.experimental import pallas as pl
from jax.experimental.pallas import tpu as pltpu
from jax.sharding import PartitionSpec as P

F32 = jnp.float32
BF16 = jnp.bfloat16
VMEM_LIMIT = 63 * 1024 * 1024


def params():
    return pltpu.CompilerParams(vmem_limit_bytes=VMEM_LIMIT)


def cost(work):
    return pl.CostEstimate(flops=work, bytes_accessed=work, transcendentals=0)


def stencil_terms(zonal_cour, merid_cour, diffuse):
    middle_weight = 1.0 - zonal_cour * zonal_cour - merid_cour * merid_cour - 4.0 * diffuse
    eastward_weight = 0.5 * zonal_cour * zonal_cour - 0.5 * zonal_cour + diffuse
    west_w = 0.5 * zonal_cour * zonal_cour + 0.5 * zonal_cour + diffuse
    north_w = 0.5 * merid_cour * merid_cour - 0.5 * merid_cour + diffuse
    south_w = 0.5 * merid_cour * merid_cour + 0.5 * merid_cour + diffuse
    return middle_weight, eastward_weight, west_w, north_w, south_w


def split(values):
    high = values.astype(BF16)
    return high, (values - high.astype(F32)).astype(BF16)


def circulant(row):
    size = row.shape[1]
    return pltpu.roll(jnp.broadcast_to(row, (size, size)), 0, 1, stride=1, stride_axis=0)


def product(left, right):
    return jnp.dot(left, right, preferred_element_type=F32)


def composed(terms, lats, nlon):
    steps = len(terms)
    padded = lats + 2 * steps
    lane = lax.broadcasted_iota(jnp.int32, (padded, nlon), 1)
    rows = {0: (lane == 0).astype(F32)}
    for step_no in range(steps):
        low, high = step_no + 1, padded - step_no - 1
        c, e, w, n, s = [term[low:high] for term in terms[step_no]]
        size = high - low
        fresh = {}
        for d in range(-step_no - 1, step_no + 2):
            parts = []
            if d in rows:
                here = rows[d][1 : 1 + size]
                parts += [c * here, e * pltpu.roll(here, 1, 1), w * pltpu.roll(here, nlon - 1, 1)]
            if d - 1 in rows:
                parts.append(n * rows[d - 1][2 : 2 + size])
            if d + 1 in rows:
                parts.append(s * rows[d + 1][0:size])
            fresh[d] = functools.reduce(lambda x, y: x + y, parts)
        rows = fresh
    return rows


def swept(planes, weights):
    for step_no, (c, e, w, n, s) in enumerate(weights):
        fresh = []
        for i in range(1, len(planes) - 1):
            at, u = i + step_no, planes[i]
            nlon = u.shape[1]
            fresh.append(
                c(at) * u
                + e(at) * pltpu.roll(u, nlon - 1, 1)
                + w(at) * pltpu.roll(u, 1, 1)
                + n(at) * planes[i + 1]
                + s(at) * planes[i - 1]
            )
        planes = fresh
    return planes


def packing(pieces):
    def placed(piece):
        _, size, _, width, _, _, turn = piece
        return (width, size) if turn else (size, width)

    shapes = {}
    for piece in pieces:
        shape, out = placed(piece), piece[4]
        shapes[out] = (max(piece[5] + shape[0], shapes.get(out, (0,))[0]), shape[1])
    count = len(pieces)
    scratch = [pltpu.VMEM(piece[1:4:2], F32) for piece in pieces]
    scratch += [pltpu.VMEM(placed(piece), BF16) for piece in pieces]
    scratch += [pltpu.SemaphoreType.DMA((count,)), pltpu.SemaphoreType.DMA((count,))]

    def start(where_ref, p_ref, refs):
        first = lambda at: pl.multiple_of(where_ref[at[0]] + sum(at[1:]), 128) if isinstance(at, tuple) else at
        loads = []
        for k, (row, size, col, width, _, _, _) in enumerate(pieces):
            source = p_ref.at[pl.ds(first(row), size), pl.ds(first(col), width)]
            loads.append(pltpu.make_async_copy(source, refs[k], refs[2 * count].at[k]))
            loads[-1].start()
        return loads

    def finish(loads, results, refs):
        stores = []
        for k, piece in enumerate(pieces):
            loads[k].wait()
            got, made, turn, shape = refs[k], refs[count + k], piece[6], placed(piece)
            if turn:
                for a in range(0, shape[0], turn):
                    for b in range(0, shape[1], turn):
                        made[a : a + turn, b : b + turn] = got[b : b + turn, a : a + turn].T.astype(BF16)
            else:
                made[...] = got[...].astype(BF16)
            target = results[piece[4]].at[pl.ds(piece[5], shape[0]), :]
            stores.append(pltpu.make_async_copy(made, target, refs[2 * count + 1].at[k]))
            stores[-1].start()
        for copy in stores:
            copy.wait()

    return [jax.ShapeDtypeStruct(shapes[k], BF16) for k in range(len(shapes))], scratch, start, finish


def packed(covariance, where, pieces):
    out_shape, scratch, start, finish = packing(pieces)

    def kernel(where_ref, p_ref, *refs):
        results, refs = refs[: len(out_shape)], refs[len(out_shape) :]
        finish(start(where_ref, p_ref, refs), results, refs)

    return pl.pallas_call(
        kernel,
        in_specs=[pl.BlockSpec(memory_space=pltpu.SMEM), pl.BlockSpec(memory_space=pl.ANY)],
        out_specs=[pl.BlockSpec(memory_space=pl.ANY)] * len(out_shape),
        out_shape=out_shape,
        scratch_shapes=scratch,
        compiler_params=params(),
        cost_estimate=cost(1),
        name="packed",
    )(where, covariance)


def stencils(wind_table, diffusivity, wind_index, where, lat_rows, lats, nlon, covariance, pieces):
    steps, nlat = wind_index.shape
    sizes = (lat_rows, lats)
    span = 2 * steps * nlon
    pairs = lats // 2
    packs, pack_scratch, start, finish = packing(pieces)

    def kernel(table_ref, diffuse_ref, index_ref, where_ref, p_ref, *refs):
        row_out, col_out, high_out, low_out, step_out = refs[:5]
        results, scratch, refs = refs[5 : 5 + len(packs)], refs[5 + len(packs) :][:2], refs[7 + len(packs) :]
        loads = start(where_ref, p_ref, refs)
        for side, out in enumerate((row_out, col_out)):
            looked_up = scratch[side]
            terms = []
            for step_no in range(steps):
                for i in range(sizes[side] + 2 * steps):
                    lat = where_ref[5 + side] + i - steps
                    inside = jnp.logical_and(lat >= 0, lat < nlat)
                    entry = jnp.where(inside, index_ref[step_no, jnp.clip(lat, 0, nlat - 1)], -1)
                    looked_up[i : i + 1, :] = jnp.full((1, nlon), entry, jnp.int32)
                index = looked_up[...]
                zonal = merid = diffuse = jnp.zeros(index.shape, F32)
                for entry in range(wind_table.shape[0]):
                    here = index == entry
                    zonal = jnp.where(here, table_ref[0, entry], zonal)
                    merid = jnp.where(here, table_ref[1, entry], merid)
                    diffuse = jnp.where(here, diffuse_ref[entry], diffuse)
                c, e, w, n, s = [
                    jnp.where(index >= 0, term, 0.0) for term in stencil_terms(zonal, merid, diffuse)
                ]
                terms.append((c, w, e, n, s) if side else (c, e, w, n, s))
                if side:
                    for member, value in enumerate((c, e, w, n, s)):
                        step_out[5 * step_no + member] = value
            for d, value in composed(terms, sizes[side], nlon).items():
                out[d + steps] = value
        for q in range(pairs):
            for a in range(2):
                for k in range(2 * steps):
                    d = k - (steps - 1) - a
                    high, low = split(circulant(col_out[d + steps, 2 * q + a : 2 * q + a + 1, :]))
                    at = pl.ds(q * span + k * nlon, nlon)
                    high_out[at, a * nlon : (a + 1) * nlon] = high
                    low_out[at, a * nlon : (a + 1) * nlon] = low
        finish(loads, results, refs)

    return pl.pallas_call(
        kernel,
        in_specs=[pl.BlockSpec(memory_space=pltpu.SMEM)] * 4 + [pl.BlockSpec(memory_space=pl.ANY)],
        out_specs=[pl.BlockSpec(memory_space=pltpu.VMEM)] * 5 + [pl.BlockSpec(memory_space=pl.ANY)] * len(packs),
        out_shape=[jax.ShapeDtypeStruct((2 * steps + 1, size, nlon), F32) for size in sizes]
        + [jax.ShapeDtypeStruct((pairs * span, 2 * nlon), BF16)] * 2
        + [jax.ShapeDtypeStruct((5 * steps, lats + 2 * steps, nlon), F32)]
        + packs,
        scratch_shapes=[pltpu.VMEM((size + 2 * steps, nlon), jnp.int32) for size in sizes]
        + pack_scratch,
        compiler_params=params(),
        cost_estimate=cost(1),
        name="stencils",
    )(wind_table.T, diffusivity, wind_index, where, covariance)


def columns_operator(
    covariance, halos, stencil, blocks, where, unit, steps, nlon, count, block_at, held=None, ends=False, work=1
):
    rows, cols = covariance.shape
    lats = cols // nlon
    wide = steps * nlon
    size = unit * nlon
    span = 2 * steps * nlon
    pairs = lats // 2
    part = nlon // 2
    upper = size - part * (3 * size // (8 * part))

    def kernel(where_ref, stencil_ref, p_ref, *rest):
        halo_groups = []
        for group in halos:
            halo_groups.append(rest[: len(group)])
            rest = rest[len(group) :]
        (b_high, b_low, step_ref), outs, data_ref = rest[:3], rest[3:-1], rest[-1]
        if held is not None:
            outs = outs[1:]
        t_ref = outs[0]
        i = pl.program_id(0)
        col_odd, row_odd = where_ref[2] != 0, where_ref[3] != 0

        @pl.when(i == 0)
        def _():
            data_ref[size:, :wide] = jnp.zeros((size, wide), BF16)
            data_ref[size:, wide + cols :] = jnp.zeros((size, wide), BF16)

        for k, refs in enumerate(halo_groups):
            chosen = i >= 0 if len(halos) == 1 else i == k
            for odd in range(2):
                here = jnp.logical_and(chosen, col_odd if odd else jnp.logical_not(col_odd))
                even_at, odd_at = (0, wide + cols) if odd else (wide + cols, 0)

                @pl.when(here)
                def _(refs=refs, odd_at=odd_at):
                    data_ref[:size, odd_at : odd_at + wide] = refs[1][...]

                for ref, use in ((refs[0], None),) if len(refs) == 2 else ((refs[0], 0), (refs[2], 1)):
                    if use is not None:
                        here_too = jnp.logical_and(here, where_ref[15] == use)

                    @pl.when(here if use is None else here_too)
                    def _(ref=ref, even_at=even_at):
                        data_ref[:size, even_at : even_at + wide] = ref[...]

        data_ref[:upper, wide : wide + cols], data_ref[size : size + upper, wide : wide + cols] = split(
            p_ref[:upper, :]
        )
        weights = [
            [
                lambda at, k=5 * step_no + member: step_ref[k, at : at + 1, :]
                for member in range(5)
            ]
            for step_no in range(steps)
        ]
        starts = list(range(upper, size, part))
        for q in range(max(pairs, len(starts))):
            if q < pairs:
                window = slice((2 * q + 1) * nlon, (2 * q + 1) * nlon + span)
                of = pl.ds(q * span, span)
                total = product(data_ref[:upper, window], b_high[of, :])
                total += product(data_ref[size : size + upper, window], b_high[of, :])
                total += product(data_ref[:upper, window], b_low[of, :])
                for a, k, d in ((0, 2 * q, -steps), (1, 2 * q + 2 * steps + 1, steps)):
                    far = slice(k * nlon, (k + 1) * nlon)
                    row = stencil_ref[d + steps, 2 * q + a : 2 * q + a + 1, :]
                    weight = jnp.sum(row, axis=1, keepdims=True)
                    far_values = data_ref[:upper, far].astype(F32) + data_ref[size : size + upper, far].astype(F32)
                    value = total[:, a * nlon : (a + 1) * nlon] + weight * far_values
                    t_ref[:upper, (2 * q + a) * nlon : (2 * q + a + 1) * nlon] = value.astype(BF16)
            if q < len(starts):
                rows_at = slice(starts[q], starts[q] + part)
                planes = []
                for k in range(lats + 2 * steps):
                    if steps <= k < steps + lats:
                        planes.append(p_ref[rows_at, (k - steps) * nlon : (k - steps + 1) * nlon])
                    else:
                        planes.append(data_ref[rows_at, k * nlon : (k + 1) * nlon].astype(F32))
                for k, plane in enumerate(swept(planes, weights)):
                    t_ref[rows_at, k * nlon : (k + 1) * nlon] = plane.astype(BF16)
        if ends:
            for odd in range(2):
                is_odd = row_odd if odd else jnp.logical_not(row_odd)

                @pl.when(jnp.logical_and(i == 0, is_odd))
                def _(odd=odd):
                    outs[2 - odd][...] = t_ref[:wide, :]

                @pl.when(jnp.logical_and(i == count - 1, is_odd))
                def _(odd=odd):
                    outs[1 + odd][...] = t_ref[size - wide :, :]

    halo_at = (lambda i, at: (i, 0)) if len(halos) == 1 else (lambda i, at: (0, 0))
    in_specs = [
        pl.BlockSpec(stencil.shape, lambda i, at: (0, 0, 0)),
        pl.BlockSpec((size, cols), lambda i, at: (block_at(i, at), 0)),
    ]
    in_specs += [pl.BlockSpec((size, wide), halo_at)] * sum(len(group) for group in halos)
    in_specs += [pl.BlockSpec(block.shape, lambda i, at, n=block.ndim: (0,) * n) for block in blocks]
    out_specs = [pl.BlockSpec((size, cols), lambda i, at: (block_at(i, at), 0))]
    out_shape = [jax.ShapeDtypeStruct((rows, cols), BF16)]
    operands = [where, stencil, covariance] + [array for group in halos for array in group] + list(blocks)
    aliases = {}
    if ends:
        out_specs += [pl.BlockSpec((wide, cols), lambda i, at: (0, 0))] * 2
        out_shape += [jax.ShapeDtypeStruct((wide, cols), BF16)] * 2
    if held is not None:
        in_specs.append(pl.BlockSpec(memory_space=pl.ANY))
        aliases = {len(operands): 0}
        operands.append(held)
    return pl.pallas_call(
        kernel,
        grid_spec=pltpu.PrefetchScalarGridSpec(
            num_scalar_prefetch=1,
            grid=(count,),
            in_specs=in_specs,
            out_specs=out_specs,
            scratch_shapes=[pltpu.VMEM((2 * size, cols + 2 * wide), BF16)],
        ),
        out_shape=out_shape,
        input_output_aliases=aliases,
        compiler_params=params(),
        cost_estimate=cost(work),
        name="columns_operator",
    )(*operands)


def rows_operator(values, even, odd, stencil, where, steps, nlon, out_dtype, blocks=None, noise=None):
    rows, cols = values.shape
    lat_rows = rows // nlon
    wide = steps * nlon
    size = 2 * nlon
    span = 2 * steps * nlon
    pairs = lat_rows // 2
    group = 2 if pairs % 2 == 0 else 1
    ahead = (steps + 1) // 2
    exact = values.dtype == BF16
    makes = blocks is None
    chunk = cols if exact else min(cols, 512)

    def kernel(where_ref, stencil_ref, x_ref, even_ref, odd_ref, *rest):
        if makes:
            out_ref, a_ref = rest[:2]
        else:
            a_ref, noise_ref, out_ref = rest[:3]
        high_ref, sem = rest[2 if makes else 3 :][:2]
        raw_ref, low_ref = (None, None) if exact else rest[-2:]
        step = pl.program_id(0)

        def load(q):
            here = pl.ds(pl.multiple_of(q * size, size), size)
            there = pl.ds(pl.multiple_of(wide + q * size, nlon), size)
            target = high_ref.at[there, :] if exact else raw_ref.at[here, :]
            return pltpu.make_async_copy(x_ref.at[here, :], target, sem.at[q])

        def ready(q):
            load(q).wait()
            if not exact:
                there = pl.ds(pl.multiple_of(wide + q * size, nlon), size)
                here = pl.ds(pl.multiple_of(q * size, size), size)
                high_ref[there, :], low_ref[there, :] = split(raw_ref[here, :])

        @pl.when(step == 0)
        def _():
            is_odd = where_ref[3]
            at_even = pl.ds(pl.multiple_of((1 - is_odd) * (wide + rows), nlon), wide)
            at_odd = pl.ds(pl.multiple_of(is_odd * (wide + rows), nlon), wide)
            halos = [
                pltpu.make_async_copy(even_ref, high_ref.at[at_even, :], sem.at[pairs]),
                pltpu.make_async_copy(odd_ref, high_ref.at[at_odd, :], sem.at[pairs + 1]),
            ]
            for halo in halos:
                halo.start()
            for q in range(pairs):
                load(q).start()
            if not exact:
                low_ref[:wide, :] = jnp.zeros((wide, cols), BF16)
                low_ref[wide + rows :, :] = jnp.zeros((wide, cols), BF16)
            for halo in halos:
                halo.wait()
            for q in range(min(ahead, pairs)):
                ready(q)

        for j in range(group):
            q = step * group + j + ahead

            @pl.when(q < pairs)
            def _(q=q):
                ready(q)

        row = lambda j, d, a: stencil_ref[d + steps, pl.ds(2 * (step * group + j) + a, 1), :]
        if makes:
            for j in range(group):
                for a in range(2):
                    for k in range(2 * steps):
                        high, low = split(circulant(row(j, k - (steps - 1) - a, a)))
                        top = 2 * j * size + a * nlon
                        a_ref[top : top + nlon, k * nlon : (k + 1) * nlon] = high
                        a_ref[top + size : top + size + nlon, k * nlon : (k + 1) * nlon] = low
        for j in range(group):
            unit = lambda k: pl.multiple_of((2 * (step * group + j) + k) * nlon, nlon)
            weights = [jnp.sum(row(j, d, a), axis=1, keepdims=True) for a, d in ((0, -steps), (1, steps))]
            top = 2 * j * size
            for lane in range(0, cols, chunk):
                lanes = slice(lane, lane + chunk)
                both = product(a_ref[top : top + 2 * size, :], high_ref[pl.ds(unit(1), span), lanes])
                total = both[:size] + both[size:]
                if not exact:
                    total += product(a_ref[top : top + size, :], low_ref[pl.ds(unit(1), span), lanes])
                for a, k in ((0, 0), (1, 2 * steps + 1)):
                    far = high_ref[pl.ds(unit(k), nlon), lanes].astype(F32)
                    if not exact:
                        far += low_ref[pl.ds(unit(k), nlon), lanes].astype(F32)
                    value = total[a * nlon : (a + 1) * nlon, :] + weights[a] * far
                    out_ref[j * size + a * nlon : j * size + (a + 1) * nlon, lanes] = value.astype(out_dtype)
        if noise is not None:
            for a in range(2 * group):
                lat = 2 * group * step + a - where_ref[4]

                @pl.when(jnp.logical_and(lat >= 0, lat < cols // nlon))
                def _(a=a, lat=lat):
                    lanes = pl.ds(pl.multiple_of(lat * nlon, nlon), nlon)
                    eye = lax.broadcasted_iota(jnp.int32, (nlon, nlon), 0) == lax.broadcasted_iota(
                        jnp.int32, (nlon, nlon), 1
                    )
                    added = jnp.where(eye, noise_ref[pl.ds(2 * group * step + a, 1), :], 0.0)
                    out_ref[a * nlon : (a + 1) * nlon, lanes] += added

    in_specs = [pl.BlockSpec(stencil.shape, lambda g, at: (0, 0, 0))] + [pl.BlockSpec(memory_space=pl.ANY)] * 3
    operands = [where, stencil, values, even, odd]
    out_specs = [pl.BlockSpec((group * size, cols), lambda g, at: (g, 0))]
    out_shape = [jax.ShapeDtypeStruct((rows, cols), out_dtype)]
    blocks_spec = pl.BlockSpec((2 * group * size, span), lambda g, at: (g, 0))
    if makes:
        out_specs.append(blocks_spec)
        out_shape.append(jax.ShapeDtypeStruct((2 * rows, span), BF16))
    else:
        in_specs += [blocks_spec, pl.BlockSpec(noise.shape, lambda g, at: (0, 0))]
        operands += [blocks, noise]
    return pl.pallas_call(
        kernel,
        grid_spec=pltpu.PrefetchScalarGridSpec(
            num_scalar_prefetch=1,
            grid=(pairs // group,),
            in_specs=in_specs,
            out_specs=out_specs,
            scratch_shapes=[pltpu.VMEM((rows + 2 * wide, cols), BF16), pltpu.SemaphoreType.DMA((pairs + 2,))]
            + ([] if exact else [pltpu.VMEM((rows, cols), F32), pltpu.VMEM((rows + 2 * wide, cols), BF16)]),
        ),
        out_shape=out_shape,
        compiler_params=params(),
        cost_estimate=cost(1),
        name="rows_operator",
    )(*operands)


def shifted(block, axis, by):
    size = lax.axis_size(axis)
    pairs = [(i, i + by) for i in range(size) if 0 <= i + by < size]
    return lax.ppermute(block, axis, pairs)


def gathered(first, last, axis, dim, unit, halo, own):
    before, after = [], []
    need, hop = halo, 1
    while need > 0:
        take = min(own, need)
        size = first.shape[dim]
        before.insert(0, shifted(lax.slice_in_dim(last, size - take * unit, size, axis=dim), axis, hop))
        after.append(shifted(lax.slice_in_dim(first, 0, take * unit, axis=dim), axis, -hop))
        need, hop = need - take, hop + 1
    join = lambda parts: parts[0] if len(parts) == 1 else jnp.concatenate(parts, axis=dim)
    return join(before), join(after)


def exchanged(block, axis, odd):
    pairs = []
    for i in range(odd, lax.axis_size(axis) - 1, 2):
        pairs += [(i, i + 1), (i + 1, i)]
    return lax.ppermute(block, axis, pairs)


def mirrored(block, odd):
    n_row, n_col = lax.axis_size("row"), lax.axis_size("col")
    pairs = []
    for a in range(n_row):
        for b in range(n_col):
            to = 2 * a + (1 - b % 2) + (1 if (b + odd) % 2 else -1)
            here, there = a * n_col + b, (b // 2) * n_col + to
            if 0 <= to < n_col and here != there:
                pairs.append((here, there))
    return lax.ppermute(block, ("row", "col"), pairs)


def body(covariance, noise_var, wind_table, diffusivity, wind_index):
    rows_dev, cols_dev = covariance.shape
    lat_rows, nlon = noise_var.shape
    steps, nlat = wind_index.shape
    lats = cols_dev // nlon
    row_id, col_id = lax.axis_index("row"), lax.axis_index("col")
    own = lat_rows // 4
    fits = lat_rows == 2 * lats and own % 2 == 0 and own >= steps and own <= lats - steps
    if not fits or lax.axis_size("col") != 2 * lax.axis_size("row"):
        return plain_body(covariance, noise_var, wind_table, diffusivity, wind_index)

    near = lat_rows // 2 - own
    middle = lat_rows // 2
    outer, inner, wide = near * nlon, own * nlon, steps * nlon
    pick = lambda parity, even, odd: even + parity * (odd - even)
    col_odd, row_odd = col_id % 2, row_id % 2
    mirror_at, direct_at = pick(col_odd, middle - own, middle), pick(col_odd, middle, middle - own)
    diagonal = col_id * lats - row_id * lat_rows
    where = jnp.stack(
        [
            mirror_at // own,
            direct_at // own,
            col_odd,
            row_odd,
            diagonal,
            row_id * lat_rows,
            col_id * lats,
            mirror_at * nlon,
            pick(col_odd, lats, lats - steps) * nlon,
            pick(col_odd, 2 * lats - steps, 0) * nlon,
            pick(col_odd, lats - own, 0) * nlon,
            pick(col_odd, cols_dev - wide, 0),
            pick(col_odd, 0, cols_dev - wide),
            pick(row_odd, rows_dev - wide, 0),
            pick(row_odd, 0, rows_dev - wide),
            col_id // 2 == row_id,
        ]
    ).astype(jnp.int32)
    half = outer // 2
    spans = [(0, half, 0), (half, half, half)]
    spans += [(rows_dev - outer, half, outer), (rows_dev - half, half, outer + half), (0, 16, 2 * outer)]
    pieces = [(row, size, (11 + k,), wide, k, there, 0) for row, size, there in spans for k in range(2)]
    end_pieces = [((13 + k, j * nlon), nlon, 0, cols_dev, k, j * nlon, 0) for k in range(2) for j in range(steps)]
    others = [((8 + k,), wide, (10,), inner, k, 0, nlon) for k in range(2)]
    others += [((7,), inner, (11 + k,), wide, k + 2, 0, 0) for k in range(2)]
    outers = list(packed(covariance, where, pieces))
    later, outers[0] = lax.optimization_barrier((where, outers[0]))
    ends = packed(covariance, later, end_pieces)
    outers = [exchanged(piece, "col", k) for k, piece in enumerate(outers)]
    ends = [exchanged(piece, "row", k) for k, piece in enumerate(ends)]
    row_s, col_s, *rest = stencils(
        wind_table, diffusivity, wind_index, where, lat_rows, lats, nlon, covariance, others
    )
    col_blocks, mirrors, inners = rest[:3], rest[3:5], rest[5:7]
    mirrors = [mirrored(piece, k) for k, piece in enumerate(mirrors)] + [mirrors[0]]

    operator_times_prior, blocks = rows_operator(covariance, *ends, row_s, where, steps, nlon, BF16)
    operator_times_prior, outers, inners = lax.optimization_barrier((operator_times_prior, outers, inners))
    inners = [exchanged(piece, "col", k) for k, piece in enumerate(inners)]
    mirror, *ends = columns_operator(
        covariance, [outers], col_s, col_blocks, where, near, steps, nlon, 2, lambda i, at: i * (lat_rows // near - 1),
        None, True,
    )
    ends = [exchanged(piece, "row", k) for k, piece in enumerate(ends)]
    (mirror,) = columns_operator(
        covariance, [mirrors, inners], col_s, col_blocks, where, own, steps, nlon, 2, lambda i, at: at[i], mirror, False,
        10 ** 13,
    )
    (predicted_spread_matrix,) = rows_operator(
        mirror, *ends, row_s, where, steps, nlon, F32, blocks, noise_var
    )
    return (predicted_spread_matrix, operator_times_prior)


def plain_body(covariance, noise_var, wind_table, diffusivity, wind_index):
    rows_dev, cols_dev = covariance.shape
    lat_rows, nlon = noise_var.shape
    steps, nlat = wind_index.shape
    lats = cols_dev // nlon
    row_id, col_id = lax.axis_index("row"), lax.axis_index("col")
    sent = covariance.astype(BF16)
    sides = gathered(sent, sent, "col", 1, nlon, steps, lats)
    ends = gathered(sent, sent, "row", 0, nlon, steps, lat_rows)
    firsts = (row_id * lat_rows, col_id * lats)
    where = jnp.stack([0, 0, 1, 1, firsts[1] - firsts[0], *firsts]).astype(jnp.int32)
    row_s, col_s, *col_blocks = stencils(
        wind_table, diffusivity, wind_index, where, lat_rows, lats, nlon, covariance, []
    )
    operator_times_prior, blocks = rows_operator(covariance, *ends, row_s, where, steps, nlon, BF16)
    (mirror,) = columns_operator(
        covariance, [sides], col_s, col_blocks, where, 2, steps, nlon, lat_rows // 2, lambda i, at: i
    )
    ends = gathered(mirror, mirror, "row", 0, nlon, steps, lat_rows)
    (predicted_spread_matrix,) = rows_operator(
        mirror, *ends, row_s, where, steps, nlon, F32, blocks, noise_var
    )
    return (predicted_spread_matrix, operator_times_prior)


def solution(mesh):
    in_specs = (P("row", "col"), P("row", None), P(), P(), P())
    out_specs = (P("row", "col"), P("row", "col"))
    return jax.shard_map(body, mesh=mesh, in_specs=in_specs, out_specs=out_specs, check_vma=False)
```

```python
import functools

import jax
import jax.numpy as jnp
from jax import lax
from jax.experimental import pallas as pl
from jax.experimental.pallas import tpu as pltpu
from jax.sharding import PartitionSpec as P

F32 = jnp.float32
BF16 = jnp.bfloat16
VMEM_LIMIT = 63 * 1024 * 1024


def params():
    return pltpu.CompilerParams(vmem_limit_bytes=VMEM_LIMIT)


def cost(work):
    return pl.CostEstimate(flops=work, bytes_accessed=work, transcendentals=0)


def stencil_terms(zonal_cour, merid_cour, diffuse):
    middle_weight = 1.0 - zonal_cour * zonal_cour - merid_cour * merid_cour - 4.0 * diffuse
    eastward_weight = 0.5 * zonal_cour * zonal_cour - 0.5 * zonal_cour + diffuse
    west_w = 0.5 * zonal_cour * zonal_cour + 0.5 * zonal_cour + diffuse
    north_w = 0.5 * merid_cour * merid_cour - 0.5 * merid_cour + diffuse
    south_w = 0.5 * merid_cour * merid_cour + 0.5 * merid_cour + diffuse
    return middle_weight, eastward_weight, west_w, north_w, south_w


def split(values):
    high = values.astype(BF16)
    return high, (values - high.astype(F32)).astype(BF16)


def circulant(row):
    size = row.shape[1]
    return pltpu.roll(jnp.broadcast_to(row, (size, size)), 0, 1, stride=1, stride_axis=0)


def product(left, right):
    return jnp.dot(left, right, preferred_element_type=F32)


def composed(terms, lats, nlon):
    steps = len(terms)
    padded = lats + 2 * steps
    lane = lax.broadcasted_iota(jnp.int32, (padded, nlon), 1)
    rows = {0: (lane == 0).astype(F32)}
    for step_no in range(steps):
        low, high = step_no + 1, padded - step_no - 1
        c, e, w, n, s = [term[low:high] for term in terms[step_no]]
        size = high - low
        fresh = {}
        for d in range(-step_no - 1, step_no + 2):
            parts = []
            if d in rows:
                here = rows[d][1 : 1 + size]
                parts += [c * here, e * pltpu.roll(here, 1, 1), w * pltpu.roll(here, nlon - 1, 1)]
            if d - 1 in rows:
                parts.append(n * rows[d - 1][2 : 2 + size])
            if d + 1 in rows:
                parts.append(s * rows[d + 1][0:size])
            fresh[d] = functools.reduce(lambda x, y: x + y, parts)
        rows = fresh
    return rows


def swept(planes, weights):
    for step_no, (c, e, w, n, s) in enumerate(weights):
        fresh = []
        for i in range(1, len(planes) - 1):
            at, u = i + step_no, planes[i]
            nlon = u.shape[1]
            fresh.append(
                c(at) * u
                + e(at) * pltpu.roll(u, nlon - 1, 1)
                + w(at) * pltpu.roll(u, 1, 1)
                + n(at) * planes[i + 1]
                + s(at) * planes[i - 1]
            )
        planes = fresh
    return planes


def packing(pieces):
    def placed(piece):
        _, size, _, width, _, _, turn = piece
        return (width, size) if turn else (size, width)

    shapes = {}
    for piece in pieces:
        shape, out = placed(piece), piece[4]
        shapes[out] = (max(piece[5] + shape[0], shapes.get(out, (0,))[0]), shape[1])
    count = len(pieces)
    scratch = [pltpu.VMEM(piece[1:4:2], F32) for piece in pieces]
    scratch += [pltpu.VMEM(placed(piece), BF16) for piece in pieces]
    scratch += [pltpu.SemaphoreType.DMA((count,)), pltpu.SemaphoreType.DMA((count,))]

    def start(where_ref, p_ref, refs):
        first = lambda at: pl.multiple_of(where_ref[at[0]] + sum(at[1:]), 128) if isinstance(at, tuple) else at
        loads = []
        for k, (row, size, col, width, _, _, _) in enumerate(pieces):
            source = p_ref.at[pl.ds(first(row), size), pl.ds(first(col), width)]
            loads.append(pltpu.make_async_copy(source, refs[k], refs[2 * count].at[k]))
            loads[-1].start()
        return loads

    def finish(loads, results, refs):
        stores = []
        for k, piece in enumerate(pieces):
            loads[k].wait()
            got, made, turn, shape = refs[k], refs[count + k], piece[6], placed(piece)
            if turn:
                for a in range(0, shape[0], turn):
                    for b in range(0, shape[1], turn):
                        made[a : a + turn, b : b + turn] = got[b : b + turn, a : a + turn].T.astype(BF16)
            else:
                made[...] = got[...].astype(BF16)
            target = results[piece[4]].at[pl.ds(piece[5], shape[0]), :]
            stores.append(pltpu.make_async_copy(made, target, refs[2 * count + 1].at[k]))
            stores[-1].start()
        for copy in stores:
            copy.wait()

    return [jax.ShapeDtypeStruct(shapes[k], BF16) for k in range(len(shapes))], scratch, start, finish


def packed(covariance, where, pieces):
    out_shape, scratch, start, finish = packing(pieces)

    def kernel(where_ref, p_ref, *refs):
        results, refs = refs[: len(out_shape)], refs[len(out_shape) :]
        finish(start(where_ref, p_ref, refs), results, refs)

    return pl.pallas_call(
        kernel,
        in_specs=[pl.BlockSpec(memory_space=pltpu.SMEM), pl.BlockSpec(memory_space=pl.ANY)],
        out_specs=[pl.BlockSpec(memory_space=pl.ANY)] * len(out_shape),
        out_shape=out_shape,
        scratch_shapes=scratch,
        compiler_params=params(),
        cost_estimate=cost(1),
        name="packed",
    )(where, covariance)


def stencils(wind_table, diffusivity, wind_index, where, lat_rows, lats, nlon, covariance, pieces):
    steps, nlat = wind_index.shape
    sizes = (lat_rows, lats)
    span = 2 * steps * nlon
    pairs = lats // 2
    packs, pack_scratch, start, finish = packing(pieces)

    def kernel(table_ref, diffuse_ref, index_ref, where_ref, p_ref, *refs):
        row_out, col_out, high_out, low_out, step_out = refs[:5]
        results, scratch, refs = refs[5 : 5 + len(packs)], refs[5 + len(packs) :][:2], refs[7 + len(packs) :]
        loads = start(where_ref, p_ref, refs)
        for side, out in enumerate((row_out, col_out)):
            looked_up = scratch[side]
            terms = []
            for step_no in range(steps):
                for i in range(sizes[side] + 2 * steps):
                    lat = where_ref[5 + side] + i - steps
                    inside = jnp.logical_and(lat >= 0, lat < nlat)
                    entry = index_ref[step_no, jnp.clip(lat, 0, nlat - 1)]
                    values = (table_ref[0, entry], table_ref[1, entry], diffuse_ref[entry], inside.astype(F32))
                    for k, value in enumerate(values):
                        looked_up[k, i : i + 1, :] = jnp.full((1, nlon), value, F32)
                here = looked_up[3] > 0.5
                c, e, w, n, s = [
                    jnp.where(here, term, 0.0)
                    for term in stencil_terms(looked_up[0], looked_up[1], looked_up[2])
                ]
                terms.append((c, w, e, n, s) if side else (c, e, w, n, s))
                if side:
                    for member, value in enumerate((c, e, w, n, s)):
                        step_out[5 * step_no + member] = value
            for d, value in composed(terms, sizes[side], nlon).items():
                out[d + steps] = value
        for q in range(pairs):
            for a in range(2):
                for k in range(2 * steps):
                    d = k - (steps - 1) - a
                    high, low = split(circulant(col_out[d + steps, 2 * q + a : 2 * q + a + 1, :]))
                    at = pl.ds(q * span + k * nlon, nlon)
                    high_out[at, a * nlon : (a + 1) * nlon] = high
                    low_out[at, a * nlon : (a + 1) * nlon] = low
        finish(loads, results, refs)

    return pl.pallas_call(
        kernel,
        in_specs=[pl.BlockSpec(memory_space=pltpu.SMEM)] * 4 + [pl.BlockSpec(memory_space=pl.ANY)],
        out_specs=[pl.BlockSpec(memory_space=pltpu.VMEM)] * 5 + [pl.BlockSpec(memory_space=pl.ANY)] * len(packs),
        out_shape=[jax.ShapeDtypeStruct((2 * steps + 1, size, nlon), F32) for size in sizes]
        + [jax.ShapeDtypeStruct((pairs * span, 2 * nlon), BF16)] * 2
        + [jax.ShapeDtypeStruct((5 * steps, lats + 2 * steps, nlon), F32)]
        + packs,
        scratch_shapes=[pltpu.VMEM((4, size + 2 * steps, nlon), F32) for size in sizes]
        + pack_scratch,
        compiler_params=params(),
        cost_estimate=cost(1),
        name="stencils",
    )(wind_table.T, diffusivity, wind_index, where, covariance)


def columns_operator(
    covariance, halos, stencil, blocks, where, unit, steps, nlon, count, block_at, held=None, ends=False, work=1
):
    rows, cols = covariance.shape
    lats = cols // nlon
    wide = steps * nlon
    size = unit * nlon
    span = 2 * steps * nlon
    pairs = lats // 2
    part = nlon // 2
    upper = size - part * (size // (2 * part))

    def kernel(where_ref, stencil_ref, p_ref, *rest):
        halo_groups = []
        for group in halos:
            halo_groups.append(rest[: len(group)])
            rest = rest[len(group) :]
        (b_high, b_low, step_ref), outs, data_ref = rest[:3], rest[3:-1], rest[-1]
        if held is not None:
            outs = outs[1:]
        t_ref = outs[0]
        i = pl.program_id(0)
        col_odd, row_odd = where_ref[2] != 0, where_ref[3] != 0

        @pl.when(i == 0)
        def _():
            data_ref[size:, :wide] = jnp.zeros((size, wide), BF16)
            data_ref[size:, wide + cols :] = jnp.zeros((size, wide), BF16)

        for k, refs in enumerate(halo_groups):
            chosen = i >= 0 if len(halos) == 1 else i == k
            for odd in range(2):
                here = jnp.logical_and(chosen, col_odd if odd else jnp.logical_not(col_odd))
                even_at, odd_at = (0, wide + cols) if odd else (wide + cols, 0)

                @pl.when(here)
                def _(refs=refs, odd_at=odd_at):
                    data_ref[:size, odd_at : odd_at + wide] = refs[1][...]

                for ref, use in ((refs[0], None),) if len(refs) == 2 else ((refs[0], 0), (refs[2], 1)):
                    if use is not None:
                        here_too = jnp.logical_and(here, where_ref[15] == use)

                    @pl.when(here if use is None else here_too)
                    def _(ref=ref, even_at=even_at):
                        data_ref[:size, even_at : even_at + wide] = ref[...]

        data_ref[:upper, wide : wide + cols], data_ref[size : size + upper, wide : wide + cols] = split(
            p_ref[:upper, :]
        )
        weights = [
            [
                lambda at, k=5 * step_no + member: step_ref[k, at : at + 1, :]
                for member in range(5)
            ]
            for step_no in range(steps)
        ]
        starts = list(range(upper, size, part))
        for q in range(max(pairs, len(starts))):
            if q < pairs:
                window = slice((2 * q + 1) * nlon, (2 * q + 1) * nlon + span)
                of = pl.ds(q * span, span)
                total = product(data_ref[:upper, window], b_high[of, :])
                total += product(data_ref[size : size + upper, window], b_high[of, :])
                total += product(data_ref[:upper, window], b_low[of, :])
                for a, k, d in ((0, 2 * q, -steps), (1, 2 * q + 2 * steps + 1, steps)):
                    far = slice(k * nlon, (k + 1) * nlon)
                    row = stencil_ref[d + steps, 2 * q + a : 2 * q + a + 1, :]
                    weight = jnp.sum(row, axis=1, keepdims=True)
                    far_values = data_ref[:upper, far].astype(F32) + data_ref[size : size + upper, far].astype(F32)
                    value = total[:, a * nlon : (a + 1) * nlon] + weight * far_values
                    t_ref[:upper, (2 * q + a) * nlon : (2 * q + a + 1) * nlon] = value.astype(BF16)
            if q < len(starts):
                rows_at = slice(starts[q], starts[q] + part)
                planes = []
                for k in range(lats + 2 * steps):
                    if steps <= k < steps + lats:
                        planes.append(p_ref[rows_at, (k - steps) * nlon : (k - steps + 1) * nlon])
                    else:
                        planes.append(data_ref[rows_at, k * nlon : (k + 1) * nlon].astype(F32))
                for k, plane in enumerate(swept(planes, weights)):
                    t_ref[rows_at, k * nlon : (k + 1) * nlon] = plane.astype(BF16)
        if ends:
            for odd in range(2):
                is_odd = row_odd if odd else jnp.logical_not(row_odd)

                @pl.when(jnp.logical_and(i == 0, is_odd))
                def _(odd=odd):
                    outs[2 - odd][...] = t_ref[:wide, :]

                @pl.when(jnp.logical_and(i == count - 1, is_odd))
                def _(odd=odd):
                    outs[1 + odd][...] = t_ref[size - wide :, :]

    halo_at = (lambda i, at: (i, 0)) if len(halos) == 1 else (lambda i, at: (0, 0))
    in_specs = [
        pl.BlockSpec(stencil.shape, lambda i, at: (0, 0, 0)),
        pl.BlockSpec((size, cols), lambda i, at: (block_at(i, at), 0)),
    ]
    in_specs += [pl.BlockSpec((size, wide), halo_at)] * sum(len(group) for group in halos)
    in_specs += [pl.BlockSpec(block.shape, lambda i, at, n=block.ndim: (0,) * n) for block in blocks]
    out_specs = [pl.BlockSpec((size, cols), lambda i, at: (block_at(i, at), 0))]
    out_shape = [jax.ShapeDtypeStruct((rows, cols), BF16)]
    operands = [where, stencil, covariance] + [array for group in halos for array in group] + list(blocks)
    aliases = {}
    if ends:
        out_specs += [pl.BlockSpec((wide, cols), lambda i, at: (0, 0))] * 2
        out_shape += [jax.ShapeDtypeStruct((wide, cols), BF16)] * 2
    if held is not None:
        in_specs.append(pl.BlockSpec(memory_space=pl.ANY))
        aliases = {len(operands): 0}
        operands.append(held)
    return pl.pallas_call(
        kernel,
        grid_spec=pltpu.PrefetchScalarGridSpec(
            num_scalar_prefetch=1,
            grid=(count,),
            in_specs=in_specs,
            out_specs=out_specs,
            scratch_shapes=[pltpu.VMEM((2 * size, cols + 2 * wide), BF16)],
        ),
        out_shape=out_shape,
        input_output_aliases=aliases,
        compiler_params=params(),
        cost_estimate=cost(work),
        name="columns_operator",
    )(*operands)


def rows_operator(values, even, odd, stencil, where, steps, nlon, out_dtype, blocks=None, noise=None):
    rows, cols = values.shape
    lat_rows = rows // nlon
    wide = steps * nlon
    size = 2 * nlon
    span = 2 * steps * nlon
    pairs = lat_rows // 2
    group = 2 if pairs % 2 == 0 else 1
    ahead = (steps + 1) // 2
    exact = values.dtype == BF16
    makes = blocks is None
    chunk = cols if exact else min(cols, 512)

    def kernel(where_ref, stencil_ref, x_ref, even_ref, odd_ref, *rest):
        if makes:
            out_ref, a_ref = rest[:2]
        else:
            a_ref, noise_ref, out_ref = rest[:3]
        high_ref, sem = rest[2 if makes else 3 :][:2]
        raw_ref, low_ref = (None, None) if exact else rest[-2:]
        step = pl.program_id(0)

        def load(q):
            here = pl.ds(pl.multiple_of(q * size, size), size)
            there = pl.ds(pl.multiple_of(wide + q * size, nlon), size)
            target = high_ref.at[there, :] if exact else raw_ref.at[here, :]
            return pltpu.make_async_copy(x_ref.at[here, :], target, sem.at[q])

        def ready(q):
            load(q).wait()
            if not exact:
                there = pl.ds(pl.multiple_of(wide + q * size, nlon), size)
                here = pl.ds(pl.multiple_of(q * size, size), size)
                high_ref[there, :], low_ref[there, :] = split(raw_ref[here, :])

        @pl.when(step == 0)
        def _():
            is_odd = where_ref[3]
            at_even = pl.ds(pl.multiple_of((1 - is_odd) * (wide + rows), nlon), wide)
            at_odd = pl.ds(pl.multiple_of(is_odd * (wide + rows), nlon), wide)
            halos = [
                pltpu.make_async_copy(even_ref, high_ref.at[at_even, :], sem.at[pairs]),
                pltpu.make_async_copy(odd_ref, high_ref.at[at_odd, :], sem.at[pairs + 1]),
            ]
            for halo in halos:
                halo.start()
            for q in range(pairs):
                load(q).start()
            if not exact:
                low_ref[:wide, :] = jnp.zeros((wide, cols), BF16)
                low_ref[wide + rows :, :] = jnp.zeros((wide, cols), BF16)
            for halo in halos:
                halo.wait()
            for q in range(min(ahead, pairs)):
                ready(q)

        for j in range(group):
            q = step * group + j + ahead

            @pl.when(q < pairs)
            def _(q=q):
                ready(q)

        row = lambda j, d, a: stencil_ref[d + steps, pl.ds(2 * (step * group + j) + a, 1), :]
        if makes:
            for j in range(group):
                for a in range(2):
                    for k in range(2 * steps):
                        high, low = split(circulant(row(j, k - (steps - 1) - a, a)))
                        top = 2 * j * size + a * nlon
                        a_ref[top : top + nlon, k * nlon : (k + 1) * nlon] = high
                        a_ref[top + size : top + size + nlon, k * nlon : (k + 1) * nlon] = low
        for j in range(group):
            unit = lambda k: pl.multiple_of((2 * (step * group + j) + k) * nlon, nlon)
            weights = [jnp.sum(row(j, d, a), axis=1, keepdims=True) for a, d in ((0, -steps), (1, steps))]
            top = 2 * j * size
            for lane in range(0, cols, chunk):
                lanes = slice(lane, lane + chunk)
                both = product(a_ref[top : top + 2 * size, :], high_ref[pl.ds(unit(1), span), lanes])
                total = both[:size] + both[size:]
                if not exact:
                    total += product(a_ref[top : top + size, :], low_ref[pl.ds(unit(1), span), lanes])
                for a, k in ((0, 0), (1, 2 * steps + 1)):
                    far = high_ref[pl.ds(unit(k), nlon), lanes].astype(F32)
                    if not exact:
                        far += low_ref[pl.ds(unit(k), nlon), lanes].astype(F32)
                    value = total[a * nlon : (a + 1) * nlon, :] + weights[a] * far
                    out_ref[j * size + a * nlon : j * size + (a + 1) * nlon, lanes] = value.astype(out_dtype)
        if noise is not None:
            for a in range(2 * group):
                lat = 2 * group * step + a - where_ref[4]

                @pl.when(jnp.logical_and(lat >= 0, lat < cols // nlon))
                def _(a=a, lat=lat):
                    lanes = pl.ds(pl.multiple_of(lat * nlon, nlon), nlon)
                    eye = lax.broadcasted_iota(jnp.int32, (nlon, nlon), 0) == lax.broadcasted_iota(
                        jnp.int32, (nlon, nlon), 1
                    )
                    added = jnp.where(eye, noise_ref[pl.ds(2 * group * step + a, 1), :], 0.0)
                    out_ref[a * nlon : (a + 1) * nlon, lanes] += added

    in_specs = [pl.BlockSpec(stencil.shape, lambda g, at: (0, 0, 0))] + [pl.BlockSpec(memory_space=pl.ANY)] * 3
    operands = [where, stencil, values, even, odd]
    out_specs = [pl.BlockSpec((group * size, cols), lambda g, at: (g, 0))]
    out_shape = [jax.ShapeDtypeStruct((rows, cols), out_dtype)]
    blocks_spec = pl.BlockSpec((2 * group * size, span), lambda g, at: (g, 0))
    if makes:
        out_specs.append(blocks_spec)
        out_shape.append(jax.ShapeDtypeStruct((2 * rows, span), BF16))
    else:
        in_specs += [blocks_spec, pl.BlockSpec(noise.shape, lambda g, at: (0, 0))]
        operands += [blocks, noise]
    return pl.pallas_call(
        kernel,
        grid_spec=pltpu.PrefetchScalarGridSpec(
            num_scalar_prefetch=1,
            grid=(pairs // group,),
            in_specs=in_specs,
            out_specs=out_specs,
            scratch_shapes=[pltpu.VMEM((rows + 2 * wide, cols), BF16), pltpu.SemaphoreType.DMA((pairs + 2,))]
            + ([] if exact else [pltpu.VMEM((rows, cols), F32), pltpu.VMEM((rows + 2 * wide, cols), BF16)]),
        ),
        out_shape=out_shape,
        compiler_params=params(),
        cost_estimate=cost(1),
        name="rows_operator",
    )(*operands)


def shifted(block, axis, by):
    size = lax.axis_size(axis)
    pairs = [(i, i + by) for i in range(size) if 0 <= i + by < size]
    return lax.ppermute(block, axis, pairs)


def gathered(first, last, axis, dim, unit, halo, own):
    before, after = [], []
    need, hop = halo, 1
    while need > 0:
        take = min(own, need)
        size = first.shape[dim]
        before.insert(0, shifted(lax.slice_in_dim(last, size - take * unit, size, axis=dim), axis, hop))
        after.append(shifted(lax.slice_in_dim(first, 0, take * unit, axis=dim), axis, -hop))
        need, hop = need - take, hop + 1
    join = lambda parts: parts[0] if len(parts) == 1 else jnp.concatenate(parts, axis=dim)
    return join(before), join(after)


def exchanged(block, axis, odd):
    pairs = []
    for i in range(odd, lax.axis_size(axis) - 1, 2):
        pairs += [(i, i + 1), (i + 1, i)]
    return lax.ppermute(block, axis, pairs)


def mirrored(block, odd):
    n_row, n_col = lax.axis_size("row"), lax.axis_size("col")
    pairs = []
    for a in range(n_row):
        for b in range(n_col):
            to = 2 * a + (1 - b % 2) + (1 if (b + odd) % 2 else -1)
            here, there = a * n_col + b, (b // 2) * n_col + to
            if 0 <= to < n_col and here != there:
                pairs.append((here, there))
    return lax.ppermute(block, ("row", "col"), pairs)


def body(covariance, noise_var, wind_table, diffusivity, wind_index):
    rows_dev, cols_dev = covariance.shape
    lat_rows, nlon = noise_var.shape
    steps, nlat = wind_index.shape
    lats = cols_dev // nlon
    row_id, col_id = lax.axis_index("row"), lax.axis_index("col")
    own = lat_rows // 4
    fits = lat_rows == 2 * lats and own % 2 == 0 and own >= steps and own <= lats - steps
    if not fits or lax.axis_size("col") != 2 * lax.axis_size("row"):
        return plain_body(covariance, noise_var, wind_table, diffusivity, wind_index)

    near = lat_rows // 2 - own
    middle = lat_rows // 2
    outer, inner, wide = near * nlon, own * nlon, steps * nlon
    pick = lambda parity, even, odd: even + parity * (odd - even)
    col_odd, row_odd = col_id % 2, row_id % 2
    mirror_at, direct_at = pick(col_odd, middle - own, middle), pick(col_odd, middle, middle - own)
    diagonal = col_id * lats - row_id * lat_rows
    where = jnp.stack(
        [
            mirror_at // own,
            direct_at // own,
            col_odd,
            row_odd,
            diagonal,
            row_id * lat_rows,
            col_id * lats,
            mirror_at * nlon,
            pick(col_odd, lats, lats - steps) * nlon,
            pick(col_odd, 2 * lats - steps, 0) * nlon,
            pick(col_odd, lats - own, 0) * nlon,
            pick(col_odd, cols_dev - wide, 0),
            pick(col_odd, 0, cols_dev - wide),
            pick(row_odd, rows_dev - wide, 0),
            pick(row_odd, 0, rows_dev - wide),
            col_id // 2 == row_id,
        ]
    ).astype(jnp.int32)
    half = outer // 2
    spans = [(0, half, 0), (half, half, half)]
    spans += [(rows_dev - outer, half, outer), (rows_dev - half, half, outer + half), (0, 16, 2 * outer)]
    pieces = [(row, size, (11 + k,), wide, k, there, 0) for row, size, there in spans for k in range(2)]
    pieces += [((13 + k, j * nlon), nlon, 0, cols_dev, k + 2, j * nlon, 0) for k in range(2) for j in range(steps)]
    others = [((8 + k,), wide, (10,), inner, k, 0, nlon) for k in range(2)]
    others += [((7,), inner, (11 + k,), wide, k + 2, 0, 0) for k in range(2)]
    sent = packed(covariance, where, pieces)
    outers, ends = list(sent[:2]), list(sent[2:])
    outers = [exchanged(piece, "col", k) for k, piece in enumerate(outers)]
    ends = [exchanged(piece, "row", k) for k, piece in enumerate(ends)]
    row_s, col_s, *rest = stencils(
        wind_table, diffusivity, wind_index, where, lat_rows, lats, nlon, covariance, others
    )
    col_blocks, mirrors, inners = rest[:3], rest[3:5], rest[5:7]
    mirrors = [mirrored(piece, k) for k, piece in enumerate(mirrors)] + [mirrors[0]]

    operator_times_prior, blocks = rows_operator(covariance, *ends, row_s, where, steps, nlon, BF16)
    inners[0] = exchanged(inners[0], "col", 0)
    operator_times_prior, outers, inners[1] = lax.optimization_barrier(
        (operator_times_prior, outers, inners[1])
    )
    inners[1] = exchanged(inners[1], "col", 1)
    mirror, *ends = columns_operator(
        covariance, [outers], col_s, col_blocks, where, near, steps, nlon, 2, lambda i, at: i * (lat_rows // near - 1),
        None, True,
    )
    ends = [exchanged(piece, "row", k) for k, piece in enumerate(ends)]
    (mirror,) = columns_operator(
        covariance, [mirrors, inners], col_s, col_blocks, where, own, steps, nlon, 2, lambda i, at: at[i], mirror, False,
        10 ** 13,
    )
    (predicted_spread_matrix,) = rows_operator(
        mirror, *ends, row_s, where, steps, nlon, F32, blocks, noise_var
    )
    return (predicted_spread_matrix, operator_times_prior)


def plain_body(covariance, noise_var, wind_table, diffusivity, wind_index):
    rows_dev, cols_dev = covariance.shape
    lat_rows, nlon = noise_var.shape
    steps, nlat = wind_index.shape
    lats = cols_dev // nlon
    row_id, col_id = lax.axis_index("row"), lax.axis_index("col")
    sent = covariance.astype(BF16)
    sides = gathered(sent, sent, "col", 1, nlon, steps, lats)
    ends = gathered(sent, sent, "row", 0, nlon, steps, lat_rows)
    firsts = (row_id * lat_rows, col_id * lats)
    where = jnp.stack([0, 0, 1, 1, firsts[1] - firsts[0], *firsts]).astype(jnp.int32)
    row_s, col_s, *col_blocks = stencils(
        wind_table, diffusivity, wind_index, where, lat_rows, lats, nlon, covariance, []
    )
    operator_times_prior, blocks = rows_operator(covariance, *ends, row_s, where, steps, nlon, BF16)
    (mirror,) = columns_operator(
        covariance, [sides], col_s, col_blocks, where, 2, steps, nlon, lat_rows // 2, lambda i, at: i
    )
    ends = gathered(mirror, mirror, "row", 0, nlon, steps, lat_rows)
    (predicted_spread_matrix,) = rows_operator(
        mirror, *ends, row_s, where, steps, nlon, F32, blocks, noise_var
    )
    return (predicted_spread_matrix, operator_times_prior)


def solution(mesh):
    in_specs = (P("row", "col"), P("row", None), P(), P(), P())
    out_specs = (P("row", "col"), P("row", "col"))
    return jax.shard_map(body, mesh=mesh, in_specs=in_specs, out_specs=out_specs, check_vma=False)
```

```python
import functools

import jax
import jax.numpy as jnp
from jax import lax
from jax.experimental import pallas as pl
from jax.experimental.pallas import tpu as pltpu
from jax.sharding import PartitionSpec as P

F32 = jnp.float32
BF16 = jnp.bfloat16
VMEM_LIMIT = 63 * 1024 * 1024


def params():
    return pltpu.CompilerParams(vmem_limit_bytes=VMEM_LIMIT)


def cost(work):
    return pl.CostEstimate(flops=work, bytes_accessed=work, transcendentals=0)


def stencil_terms(zonal_cour, merid_cour, diffuse):
    middle_weight = 1.0 - zonal_cour * zonal_cour - merid_cour * merid_cour - 4.0 * diffuse
    eastward_weight = 0.5 * zonal_cour * zonal_cour - 0.5 * zonal_cour + diffuse
    west_w = 0.5 * zonal_cour * zonal_cour + 0.5 * zonal_cour + diffuse
    north_w = 0.5 * merid_cour * merid_cour - 0.5 * merid_cour + diffuse
    south_w = 0.5 * merid_cour * merid_cour + 0.5 * merid_cour + diffuse
    return middle_weight, eastward_weight, west_w, north_w, south_w


def split(values):
    high = values.astype(BF16)
    return high, (values - high.astype(F32)).astype(BF16)


def circulant(row):
    size = row.shape[1]
    return pltpu.roll(jnp.broadcast_to(row, (size, size)), 0, 1, stride=1, stride_axis=0)


def product(left, right):
    return jnp.dot(left, right, preferred_element_type=F32)


def composed(terms, lats, nlon):
    steps = len(terms)
    padded = lats + 2 * steps
    lane = lax.broadcasted_iota(jnp.int32, (padded, nlon), 1)
    rows = {0: (lane == 0).astype(F32)}
    for step_no in range(steps):
        low, high = step_no + 1, padded - step_no - 1
        c, e, w, n, s = [term[low:high] for term in terms[step_no]]
        size = high - low
        fresh = {}
        for d in range(-step_no - 1, step_no + 2):
            parts = []
            if d in rows:
                here = rows[d][1 : 1 + size]
                parts += [c * here, e * pltpu.roll(here, 1, 1), w * pltpu.roll(here, nlon - 1, 1)]
            if d - 1 in rows:
                parts.append(n * rows[d - 1][2 : 2 + size])
            if d + 1 in rows:
                parts.append(s * rows[d + 1][0:size])
            fresh[d] = functools.reduce(lambda x, y: x + y, parts)
        rows = fresh
    return rows


def swept(planes, weights):
    for step_no, (c, e, w, n, s) in enumerate(weights):
        fresh = []
        for i in range(1, len(planes) - 1):
            at, u = i + step_no, planes[i]
            nlon = u.shape[1]
            fresh.append(
                c(at) * u
                + e(at) * pltpu.roll(u, nlon - 1, 1)
                + w(at) * pltpu.roll(u, 1, 1)
                + n(at) * planes[i + 1]
                + s(at) * planes[i - 1]
            )
        planes = fresh
    return planes


def packing(pieces):
    def placed(piece):
        _, size, _, width, _, _, turn = piece
        return (width, size) if turn else (size, width)

    shapes = {}
    for piece in pieces:
        shape, out = placed(piece), piece[4]
        shapes[out] = (max(piece[5] + shape[0], shapes.get(out, (0,))[0]), shape[1])
    count = len(pieces)
    scratch = [pltpu.VMEM(piece[1:4:2], F32) for piece in pieces]
    scratch += [pltpu.VMEM(placed(piece), BF16) for piece in pieces]
    scratch += [pltpu.SemaphoreType.DMA((count,)), pltpu.SemaphoreType.DMA((count,))]

    def start(where_ref, p_ref, refs):
        first = lambda at: pl.multiple_of(where_ref[at[0]] + sum(at[1:]), 128) if isinstance(at, tuple) else at
        loads = []
        for k, (row, size, col, width, _, _, _) in enumerate(pieces):
            source = p_ref.at[pl.ds(first(row), size), pl.ds(first(col), width)]
            loads.append(pltpu.make_async_copy(source, refs[k], refs[2 * count].at[k]))
            loads[-1].start()
        return loads

    def finish(loads, results, refs):
        stores = []
        for k, piece in enumerate(pieces):
            loads[k].wait()
            got, made, turn, shape = refs[k], refs[count + k], piece[6], placed(piece)
            if turn:
                for a in range(0, shape[0], turn):
                    for b in range(0, shape[1], turn):
                        made[a : a + turn, b : b + turn] = got[b : b + turn, a : a + turn].T.astype(BF16)
            else:
                made[...] = got[...].astype(BF16)
            target = results[piece[4]].at[pl.ds(piece[5], shape[0]), :]
            stores.append(pltpu.make_async_copy(made, target, refs[2 * count + 1].at[k]))
            stores[-1].start()
        for copy in stores:
            copy.wait()

    return [jax.ShapeDtypeStruct(shapes[k], BF16) for k in range(len(shapes))], scratch, start, finish


def packed(covariance, where, pieces):
    out_shape, scratch, start, finish = packing(pieces)

    def kernel(where_ref, p_ref, *refs):
        results, refs = refs[: len(out_shape)], refs[len(out_shape) :]
        finish(start(where_ref, p_ref, refs), results, refs)

    return pl.pallas_call(
        kernel,
        in_specs=[pl.BlockSpec(memory_space=pltpu.SMEM), pl.BlockSpec(memory_space=pl.ANY)],
        out_specs=[pl.BlockSpec(memory_space=pl.ANY)] * len(out_shape),
        out_shape=out_shape,
        scratch_shapes=scratch,
        compiler_params=params(),
        cost_estimate=cost(1),
        name="packed",
    )(where, covariance)


def stencils(wind_table, diffusivity, wind_index, where, lat_rows, lats, nlon, covariance, pieces):
    steps, nlat = wind_index.shape
    sizes = (lat_rows, lats)
    span = 2 * steps * nlon
    pairs = lats // 2
    packs, pack_scratch, start, finish = packing(pieces)

    def kernel(table_ref, diffuse_ref, index_ref, where_ref, p_ref, *refs):
        row_out, col_out, high_out, low_out, step_out = refs[:5]
        results, scratch, refs = refs[5 : 5 + len(packs)], refs[5 + len(packs) :][:2], refs[7 + len(packs) :]
        loads = start(where_ref, p_ref, refs)
        for side, out in enumerate((row_out, col_out)):
            looked_up = scratch[side]
            terms = []
            for step_no in range(steps):
                for i in range(sizes[side] + 2 * steps):
                    lat = where_ref[5 + side] + i - steps
                    inside = jnp.logical_and(lat >= 0, lat < nlat)
                    entry = index_ref[step_no, jnp.clip(lat, 0, nlat - 1)]
                    values = (table_ref[0, entry], table_ref[1, entry], diffuse_ref[entry], inside.astype(F32))
                    for k, value in enumerate(values):
                        looked_up[k, i : i + 1, :] = jnp.full((1, nlon), value, F32)
                here = looked_up[3] > 0.5
                c, e, w, n, s = [
                    jnp.where(here, term, 0.0)
                    for term in stencil_terms(looked_up[0], looked_up[1], looked_up[2])
                ]
                terms.append((c, w, e, n, s) if side else (c, e, w, n, s))
                if side:
                    for member, value in enumerate((c, e, w, n, s)):
                        step_out[5 * step_no + member] = value
            for d, value in composed(terms, sizes[side], nlon).items():
                out[d + steps] = value
        for q in range(pairs):
            for a in range(2):
                for k in range(2 * steps):
                    d = k - (steps - 1) - a
                    high, low = split(circulant(col_out[d + steps, 2 * q + a : 2 * q + a + 1, :]))
                    at = pl.ds(q * span + k * nlon, nlon)
                    high_out[at, a * nlon : (a + 1) * nlon] = high
                    low_out[at, a * nlon : (a + 1) * nlon] = low
        finish(loads, results, refs)

    return pl.pallas_call(
        kernel,
        in_specs=[pl.BlockSpec(memory_space=pltpu.SMEM)] * 4 + [pl.BlockSpec(memory_space=pl.ANY)],
        out_specs=[pl.BlockSpec(memory_space=pltpu.VMEM)] * 5 + [pl.BlockSpec(memory_space=pl.ANY)] * len(packs),
        out_shape=[jax.ShapeDtypeStruct((2 * steps + 1, size, nlon), F32) for size in sizes]
        + [jax.ShapeDtypeStruct((pairs * span, 2 * nlon), BF16)] * 2
        + [jax.ShapeDtypeStruct((5 * steps, lats + 2 * steps, nlon), F32)]
        + packs,
        scratch_shapes=[pltpu.VMEM((4, size + 2 * steps, nlon), F32) for size in sizes]
        + pack_scratch,
        compiler_params=params(),
        cost_estimate=cost(1),
        name="stencils",
    )(wind_table.T, diffusivity, wind_index, where, covariance)


def columns_operator(
    covariance, halos, stencil, blocks, where, unit, steps, nlon, count, block_at, held=None, ends=False, work=1
):
    rows, cols = covariance.shape
    lats = cols // nlon
    wide = steps * nlon
    size = unit * nlon
    span = 2 * steps * nlon
    pairs = lats // 2
    part = nlon // 2
    upper = size - part * (size // (4 * part))

    def kernel(where_ref, stencil_ref, p_ref, *rest):
        halo_groups = []
        for group in halos:
            halo_groups.append(rest[: len(group)])
            rest = rest[len(group) :]
        (b_high, b_low, step_ref), outs, data_ref = rest[:3], rest[3:-1], rest[-1]
        if held is not None:
            outs = outs[1:]
        t_ref = outs[0]
        i = pl.program_id(0)
        col_odd, row_odd = where_ref[2] != 0, where_ref[3] != 0

        @pl.when(i == 0)
        def _():
            data_ref[size:, :wide] = jnp.zeros((size, wide), BF16)
            data_ref[size:, wide + cols :] = jnp.zeros((size, wide), BF16)

        for k, refs in enumerate(halo_groups):
            chosen = i >= 0 if len(halos) == 1 else i == k
            for odd in range(2):
                here = jnp.logical_and(chosen, col_odd if odd else jnp.logical_not(col_odd))
                even_at, odd_at = (0, wide + cols) if odd else (wide + cols, 0)

                @pl.when(here)
                def _(refs=refs, odd_at=odd_at):
                    data_ref[:size, odd_at : odd_at + wide] = refs[1][...]

                for ref, use in ((refs[0], None),) if len(refs) == 2 else ((refs[0], 0), (refs[2], 1)):
                    if use is not None:
                        here_too = jnp.logical_and(here, where_ref[15] == use)

                    @pl.when(here if use is None else here_too)
                    def _(ref=ref, even_at=even_at):
                        data_ref[:size, even_at : even_at + wide] = ref[...]

        data_ref[:upper, wide : wide + cols], data_ref[size : size + upper, wide : wide + cols] = split(
            p_ref[:upper, :]
        )
        weights = [
            [
                lambda at, k=5 * step_no + member: step_ref[k, at : at + 1, :]
                for member in range(5)
            ]
            for step_no in range(steps)
        ]
        starts = list(range(upper, size, part))
        for q in range(max(pairs, len(starts))):
            if q < pairs:
                window = slice((2 * q + 1) * nlon, (2 * q + 1) * nlon + span)
                of = pl.ds(q * span, span)
                total = product(data_ref[:upper, window], b_high[of, :])
                total += product(data_ref[size : size + upper, window], b_high[of, :])
                total += product(data_ref[:upper, window], b_low[of, :])
                for a, k, d in ((0, 2 * q, -steps), (1, 2 * q + 2 * steps + 1, steps)):
                    far = slice(k * nlon, (k + 1) * nlon)
                    row = stencil_ref[d + steps, 2 * q + a : 2 * q + a + 1, :]
                    weight = jnp.sum(row, axis=1, keepdims=True)
                    far_values = data_ref[:upper, far].astype(F32) + data_ref[size : size + upper, far].astype(F32)
                    value = total[:, a * nlon : (a + 1) * nlon] + weight * far_values
                    t_ref[:upper, (2 * q + a) * nlon : (2 * q + a + 1) * nlon] = value.astype(BF16)
            if q < len(starts):
                rows_at = slice(starts[q], starts[q] + part)
                planes = []
                for k in range(lats + 2 * steps):
                    if steps <= k < steps + lats:
                        planes.append(p_ref[rows_at, (k - steps) * nlon : (k - steps + 1) * nlon])
                    else:
                        planes.append(data_ref[rows_at, k * nlon : (k + 1) * nlon].astype(F32))
                for k, plane in enumerate(swept(planes, weights)):
                    t_ref[rows_at, k * nlon : (k + 1) * nlon] = plane.astype(BF16)
        if ends:
            for odd in range(2):
                is_odd = row_odd if odd else jnp.logical_not(row_odd)

                @pl.when(jnp.logical_and(i == 0, is_odd))
                def _(odd=odd):
                    outs[2 - odd][...] = t_ref[:wide, :]

                @pl.when(jnp.logical_and(i == count - 1, is_odd))
                def _(odd=odd):
                    outs[1 + odd][...] = t_ref[size - wide :, :]

    halo_at = (lambda i, at: (i, 0)) if len(halos) == 1 else (lambda i, at: (0, 0))
    in_specs = [
        pl.BlockSpec(stencil.shape, lambda i, at: (0, 0, 0)),
        pl.BlockSpec((size, cols), lambda i, at: (block_at(i, at), 0)),
    ]
    in_specs += [pl.BlockSpec((size, wide), halo_at)] * sum(len(group) for group in halos)
    in_specs += [pl.BlockSpec(block.shape, lambda i, at, n=block.ndim: (0,) * n) for block in blocks]
    out_specs = [pl.BlockSpec((size, cols), lambda i, at: (block_at(i, at), 0))]
    out_shape = [jax.ShapeDtypeStruct((rows, cols), BF16)]
    operands = [where, stencil, covariance] + [array for group in halos for array in group] + list(blocks)
    aliases = {}
    if ends:
        out_specs += [pl.BlockSpec((wide, cols), lambda i, at: (0, 0))] * 2
        out_shape += [jax.ShapeDtypeStruct((wide, cols), BF16)] * 2
    if held is not None:
        in_specs.append(pl.BlockSpec(memory_space=pl.ANY))
        aliases = {len(operands): 0}
        operands.append(held)
    return pl.pallas_call(
        kernel,
        grid_spec=pltpu.PrefetchScalarGridSpec(
            num_scalar_prefetch=1,
            grid=(count,),
            in_specs=in_specs,
            out_specs=out_specs,
            scratch_shapes=[pltpu.VMEM((2 * size, cols + 2 * wide), BF16)],
        ),
        out_shape=out_shape,
        input_output_aliases=aliases,
        compiler_params=params(),
        cost_estimate=cost(work),
        name="columns_operator",
    )(*operands)


def rows_operator(values, even, odd, stencil, where, steps, nlon, out_dtype, blocks=None, noise=None):
    rows, cols = values.shape
    lat_rows = rows // nlon
    wide = steps * nlon
    size = 2 * nlon
    span = 2 * steps * nlon
    pairs = lat_rows // 2
    group = 2 if pairs % 2 == 0 else 1
    ahead = (steps + 1) // 2
    exact = values.dtype == BF16
    makes = blocks is None
    chunk = cols if exact else min(cols, 512)

    def kernel(where_ref, stencil_ref, x_ref, even_ref, odd_ref, *rest):
        if makes:
            out_ref, a_ref = rest[:2]
        else:
            a_ref, noise_ref, out_ref = rest[:3]
        high_ref, sem = rest[2 if makes else 3 :][:2]
        raw_ref, low_ref = (None, None) if exact else rest[-2:]
        step = pl.program_id(0)

        def load(q):
            here = pl.ds(pl.multiple_of(q * size, size), size)
            there = pl.ds(pl.multiple_of(wide + q * size, nlon), size)
            target = high_ref.at[there, :] if exact else raw_ref.at[here, :]
            return pltpu.make_async_copy(x_ref.at[here, :], target, sem.at[q])

        def ready(q):
            load(q).wait()
            if not exact:
                there = pl.ds(pl.multiple_of(wide + q * size, nlon), size)
                here = pl.ds(pl.multiple_of(q * size, size), size)
                high_ref[there, :], low_ref[there, :] = split(raw_ref[here, :])

        @pl.when(step == 0)
        def _():
            is_odd = where_ref[3]
            at_even = pl.ds(pl.multiple_of((1 - is_odd) * (wide + rows), nlon), wide)
            at_odd = pl.ds(pl.multiple_of(is_odd * (wide + rows), nlon), wide)
            halos = [
                pltpu.make_async_copy(even_ref, high_ref.at[at_even, :], sem.at[pairs]),
                pltpu.make_async_copy(odd_ref, high_ref.at[at_odd, :], sem.at[pairs + 1]),
            ]
            for halo in halos:
                halo.start()
            for q in range(pairs):
                load(q).start()
            if not exact:
                low_ref[:wide, :] = jnp.zeros((wide, cols), BF16)
                low_ref[wide + rows :, :] = jnp.zeros((wide, cols), BF16)
            for halo in halos:
                halo.wait()
            for q in range(min(ahead, pairs)):
                ready(q)

        for j in range(group):
            q = step * group + j + ahead

            @pl.when(q < pairs)
            def _(q=q):
                ready(q)

        row = lambda j, d, a: stencil_ref[d + steps, pl.ds(2 * (step * group + j) + a, 1), :]
        if makes:
            for j in range(group):
                for a in range(2):
                    for k in range(2 * steps):
                        high, low = split(circulant(row(j, k - (steps - 1) - a, a)))
                        top = 2 * j * size + a * nlon
                        a_ref[top : top + nlon, k * nlon : (k + 1) * nlon] = high
                        a_ref[top + size : top + size + nlon, k * nlon : (k + 1) * nlon] = low
        for j in range(group):
            unit = lambda k: pl.multiple_of((2 * (step * group + j) + k) * nlon, nlon)
            weights = [jnp.sum(row(j, d, a), axis=1, keepdims=True) for a, d in ((0, -steps), (1, steps))]
            top = 2 * j * size
            for lane in range(0, cols, chunk):
                lanes = slice(lane, lane + chunk)
                both = product(a_ref[top : top + 2 * size, :], high_ref[pl.ds(unit(1), span), lanes])
                total = both[:size] + both[size:]
                if not exact:
                    total += product(a_ref[top : top + size, :], low_ref[pl.ds(unit(1), span), lanes])
                for a, k in ((0, 0), (1, 2 * steps + 1)):
                    far = high_ref[pl.ds(unit(k), nlon), lanes].astype(F32)
                    if not exact:
                        far += low_ref[pl.ds(unit(k), nlon), lanes].astype(F32)
                    value = total[a * nlon : (a + 1) * nlon, :] + weights[a] * far
                    out_ref[j * size + a * nlon : j * size + (a + 1) * nlon, lanes] = value.astype(out_dtype)
        if noise is not None:
            for a in range(2 * group):
                lat = 2 * group * step + a - where_ref[4]

                @pl.when(jnp.logical_and(lat >= 0, lat < cols // nlon))
                def _(a=a, lat=lat):
                    lanes = pl.ds(pl.multiple_of(lat * nlon, nlon), nlon)
                    eye = lax.broadcasted_iota(jnp.int32, (nlon, nlon), 0) == lax.broadcasted_iota(
                        jnp.int32, (nlon, nlon), 1
                    )
                    added = jnp.where(eye, noise_ref[pl.ds(2 * group * step + a, 1), :], 0.0)
                    out_ref[a * nlon : (a + 1) * nlon, lanes] += added

    in_specs = [pl.BlockSpec(stencil.shape, lambda g, at: (0, 0, 0))] + [pl.BlockSpec(memory_space=pl.ANY)] * 3
    operands = [where, stencil, values, even, odd]
    out_specs = [pl.BlockSpec((group * size, cols), lambda g, at: (g, 0))]
    out_shape = [jax.ShapeDtypeStruct((rows, cols), out_dtype)]
    blocks_spec = pl.BlockSpec((2 * group * size, span), lambda g, at: (g, 0))
    if makes:
        out_specs.append(blocks_spec)
        out_shape.append(jax.ShapeDtypeStruct((2 * rows, span), BF16))
    else:
        in_specs += [blocks_spec, pl.BlockSpec(noise.shape, lambda g, at: (0, 0))]
        operands += [blocks, noise]
    return pl.pallas_call(
        kernel,
        grid_spec=pltpu.PrefetchScalarGridSpec(
            num_scalar_prefetch=1,
            grid=(pairs // group,),
            in_specs=in_specs,
            out_specs=out_specs,
            scratch_shapes=[pltpu.VMEM((rows + 2 * wide, cols), BF16), pltpu.SemaphoreType.DMA((pairs + 2,))]
            + ([] if exact else [pltpu.VMEM((rows, cols), F32), pltpu.VMEM((rows + 2 * wide, cols), BF16)]),
        ),
        out_shape=out_shape,
        compiler_params=params(),
        cost_estimate=cost(1),
        name="rows_operator",
    )(*operands)


def shifted(block, axis, by):
    size = lax.axis_size(axis)
    pairs = [(i, i + by) for i in range(size) if 0 <= i + by < size]
    return lax.ppermute(block, axis, pairs)


def gathered(first, last, axis, dim, unit, halo, own):
    before, after = [], []
    need, hop = halo, 1
    while need > 0:
        take = min(own, need)
        size = first.shape[dim]
        before.insert(0, shifted(lax.slice_in_dim(last, size - take * unit, size, axis=dim), axis, hop))
        after.append(shifted(lax.slice_in_dim(first, 0, take * unit, axis=dim), axis, -hop))
        need, hop = need - take, hop + 1
    join = lambda parts: parts[0] if len(parts) == 1 else jnp.concatenate(parts, axis=dim)
    return join(before), join(after)


def exchanged(block, axis, odd):
    pairs = []
    for i in range(odd, lax.axis_size(axis) - 1, 2):
        pairs += [(i, i + 1), (i + 1, i)]
    return lax.ppermute(block, axis, pairs)


def mirrored(block, odd):
    n_row, n_col = lax.axis_size("row"), lax.axis_size("col")
    pairs = []
    for a in range(n_row):
        for b in range(n_col):
            to = 2 * a + (1 - b % 2) + (1 if (b + odd) % 2 else -1)
            here, there = a * n_col + b, (b // 2) * n_col + to
            if 0 <= to < n_col and here != there:
                pairs.append((here, there))
    return lax.ppermute(block, ("row", "col"), pairs)


def body(covariance, noise_var, wind_table, diffusivity, wind_index):
    rows_dev, cols_dev = covariance.shape
    lat_rows, nlon = noise_var.shape
    steps, nlat = wind_index.shape
    lats = cols_dev // nlon
    row_id, col_id = lax.axis_index("row"), lax.axis_index("col")
    own = lat_rows // 4
    fits = lat_rows == 2 * lats and own % 2 == 0 and own >= steps and own <= lats - steps
    if not fits or lax.axis_size("col") != 2 * lax.axis_size("row"):
        return plain_body(covariance, noise_var, wind_table, diffusivity, wind_index)

    near = lat_rows // 2 - own
    middle = lat_rows // 2
    outer, inner, wide = near * nlon, own * nlon, steps * nlon
    pick = lambda parity, even, odd: even + parity * (odd - even)
    col_odd, row_odd = col_id % 2, row_id % 2
    mirror_at, direct_at = pick(col_odd, middle - own, middle), pick(col_odd, middle, middle - own)
    diagonal = col_id * lats - row_id * lat_rows
    where = jnp.stack(
        [
            mirror_at // own,
            direct_at // own,
            col_odd,
            row_odd,
            diagonal,
            row_id * lat_rows,
            col_id * lats,
            mirror_at * nlon,
            pick(col_odd, lats, lats - steps) * nlon,
            pick(col_odd, 2 * lats - steps, 0) * nlon,
            pick(col_odd, lats - own, 0) * nlon,
            pick(col_odd, cols_dev - wide, 0),
            pick(col_odd, 0, cols_dev - wide),
            pick(row_odd, rows_dev - wide, 0),
            pick(row_odd, 0, rows_dev - wide),
            col_id // 2 == row_id,
        ]
    ).astype(jnp.int32)
    half = outer // 2
    spans = [(0, half, 0), (half, half, half)]
    spans += [(rows_dev - outer, half, outer), (rows_dev - half, half, outer + half), (0, 16, 2 * outer)]
    pieces = [(row, size, (11 + k,), wide, k, there, 0) for row, size, there in spans for k in range(2)]
    pieces += [((13 + k, j * nlon), nlon, 0, cols_dev, k + 2, j * nlon, 0) for k in range(2) for j in range(steps)]
    others = [((8 + k,), wide, (10,), inner, k, 0, nlon) for k in range(2)]
    others += [((7,), inner, (11 + k,), wide, k + 2, 0, 0) for k in range(2)]
    sent = packed(covariance, where, pieces)
    outers, ends = list(sent[:2]), list(sent[2:])
    outers = [exchanged(piece, "col", k) for k, piece in enumerate(outers)]
    ends = [exchanged(piece, "row", k) for k, piece in enumerate(ends)]
    row_s, col_s, *rest = stencils(
        wind_table, diffusivity, wind_index, where, lat_rows, lats, nlon, covariance, others
    )
    col_blocks, mirrors, inners = rest[:3], rest[3:5], rest[5:7]
    mirrors = [mirrored(piece, k) for k, piece in enumerate(mirrors)] + [mirrors[0]]

    operator_times_prior, blocks = rows_operator(covariance, *ends, row_s, where, steps, nlon, BF16)
    inners[0] = exchanged(inners[0], "col", 0)
    operator_times_prior, outers, inners[1] = lax.optimization_barrier(
        (operator_times_prior, outers, inners[1])
    )
    inners[1] = exchanged(inners[1], "col", 1)
    mirror, *ends = columns_operator(
        covariance, [outers], col_s, col_blocks, where, near, steps, nlon, 2, lambda i, at: i * (lat_rows // near - 1),
        None, True,
    )
    ends = [exchanged(piece, "row", k) for k, piece in enumerate(ends)]
    (mirror,) = columns_operator(
        covariance, [mirrors, inners], col_s, col_blocks, where, own, steps, nlon, 2, lambda i, at: at[i], mirror, False,
        10 ** 13,
    )
    (predicted_spread_matrix,) = rows_operator(
        mirror, *ends, row_s, where, steps, nlon, F32, blocks, noise_var
    )
    return (predicted_spread_matrix, operator_times_prior)


def plain_body(covariance, noise_var, wind_table, diffusivity, wind_index):
    rows_dev, cols_dev = covariance.shape
    lat_rows, nlon = noise_var.shape
    steps, nlat = wind_index.shape
    lats = cols_dev // nlon
    row_id, col_id = lax.axis_index("row"), lax.axis_index("col")
    sent = covariance.astype(BF16)
    sides = gathered(sent, sent, "col", 1, nlon, steps, lats)
    ends = gathered(sent, sent, "row", 0, nlon, steps, lat_rows)
    firsts = (row_id * lat_rows, col_id * lats)
    where = jnp.stack([0, 0, 1, 1, firsts[1] - firsts[0], *firsts]).astype(jnp.int32)
    row_s, col_s, *col_blocks = stencils(
        wind_table, diffusivity, wind_index, where, lat_rows, lats, nlon, covariance, []
    )
    operator_times_prior, blocks = rows_operator(covariance, *ends, row_s, where, steps, nlon, BF16)
    (mirror,) = columns_operator(
        covariance, [sides], col_s, col_blocks, where, 2, steps, nlon, lat_rows // 2, lambda i, at: i
    )
    ends = gathered(mirror, mirror, "row", 0, nlon, steps, lat_rows)
    (predicted_spread_matrix,) = rows_operator(
        mirror, *ends, row_s, where, steps, nlon, F32, blocks, noise_var
    )
    return (predicted_spread_matrix, operator_times_prior)


def solution(mesh):
    in_specs = (P("row", "col"), P("row", None), P(), P(), P())
    out_specs = (P("row", "col"), P("row", "col"))
    return jax.shard_map(body, mesh=mesh, in_specs=in_specs, out_specs=out_specs, check_vma=False)
```

```python
import functools

import jax
import jax.numpy as jnp
from jax import lax
from jax.experimental import pallas as pl
from jax.experimental.pallas import tpu as pltpu
from jax.sharding import PartitionSpec as P

F32 = jnp.float32
BF16 = jnp.bfloat16
VMEM_LIMIT = 63 * 1024 * 1024


def params():
    return pltpu.CompilerParams(vmem_limit_bytes=VMEM_LIMIT)


def cost(work):
    return pl.CostEstimate(flops=work, bytes_accessed=work, transcendentals=0)


def stencil_terms(zonal_cour, merid_cour, diffuse):
    middle_weight = 1.0 - zonal_cour * zonal_cour - merid_cour * merid_cour - 4.0 * diffuse
    eastward_weight = 0.5 * zonal_cour * zonal_cour - 0.5 * zonal_cour + diffuse
    west_w = 0.5 * zonal_cour * zonal_cour + 0.5 * zonal_cour + diffuse
    north_w = 0.5 * merid_cour * merid_cour - 0.5 * merid_cour + diffuse
    south_w = 0.5 * merid_cour * merid_cour + 0.5 * merid_cour + diffuse
    return middle_weight, eastward_weight, west_w, north_w, south_w


def split(values):
    high = values.astype(BF16)
    return high, (values - high.astype(F32)).astype(BF16)


def circulant(row):
    size = row.shape[1]
    return pltpu.roll(jnp.broadcast_to(row, (size, size)), 0, 1, stride=1, stride_axis=0)


def product(left, right):
    return jnp.dot(left, right, preferred_element_type=F32)


def composed(terms, lats, nlon):
    steps = len(terms)
    padded = lats + 2 * steps
    lane = lax.broadcasted_iota(jnp.int32, (padded, nlon), 1)
    rows = {0: (lane == 0).astype(F32)}
    for step_no in range(steps):
        low, high = step_no + 1, padded - step_no - 1
        c, e, w, n, s = [term[low:high] for term in terms[step_no]]
        size = high - low
        fresh = {}
        for d in range(-step_no - 1, step_no + 2):
            parts = []
            if d in rows:
                here = rows[d][1 : 1 + size]
                parts += [c * here, e * pltpu.roll(here, 1, 1), w * pltpu.roll(here, nlon - 1, 1)]
            if d - 1 in rows:
                parts.append(n * rows[d - 1][2 : 2 + size])
            if d + 1 in rows:
                parts.append(s * rows[d + 1][0:size])
            fresh[d] = functools.reduce(lambda x, y: x + y, parts)
        rows = fresh
    return rows


def swept(planes, weights):
    for step_no, (c, e, w, n, s) in enumerate(weights):
        fresh = []
        for i in range(1, len(planes) - 1):
            at, u = i + step_no, planes[i]
            nlon = u.shape[1]
            fresh.append(
                c(at) * u
                + e(at) * pltpu.roll(u, nlon - 1, 1)
                + w(at) * pltpu.roll(u, 1, 1)
                + n(at) * planes[i + 1]
                + s(at) * planes[i - 1]
            )
        planes = fresh
    return planes


def packing(pieces):
    def placed(piece):
        _, size, _, width, _, _, turn = piece
        return (width, size) if turn else (size, width)

    shapes = {}
    for piece in pieces:
        shape, out = placed(piece), piece[4]
        shapes[out] = (max(piece[5] + shape[0], shapes.get(out, (0,))[0]), shape[1])
    count = len(pieces)
    scratch = [pltpu.VMEM(piece[1:4:2], F32) for piece in pieces]
    scratch += [pltpu.VMEM(placed(piece), BF16) for piece in pieces]
    scratch += [pltpu.SemaphoreType.DMA((count,)), pltpu.SemaphoreType.DMA((count,))]

    def start(where_ref, p_ref, refs):
        first = lambda at: pl.multiple_of(where_ref[at[0]] + sum(at[1:]), 128) if isinstance(at, tuple) else at
        loads = []
        for k, (row, size, col, width, _, _, _) in enumerate(pieces):
            source = p_ref.at[pl.ds(first(row), size), pl.ds(first(col), width)]
            loads.append(pltpu.make_async_copy(source, refs[k], refs[2 * count].at[k]))
            loads[-1].start()
        return loads

    def finish(loads, results, refs):
        stores = []
        for k, piece in enumerate(pieces):
            loads[k].wait()
            got, made, turn, shape = refs[k], refs[count + k], piece[6], placed(piece)
            if turn:
                for a in range(0, shape[0], turn):
                    for b in range(0, shape[1], turn):
                        made[a : a + turn, b : b + turn] = got[b : b + turn, a : a + turn].T.astype(BF16)
            else:
                made[...] = got[...].astype(BF16)
            target = results[piece[4]].at[pl.ds(piece[5], shape[0]), :]
            stores.append(pltpu.make_async_copy(made, target, refs[2 * count + 1].at[k]))
            stores[-1].start()
        for copy in stores:
            copy.wait()

    return [jax.ShapeDtypeStruct(shapes[k], BF16) for k in range(len(shapes))], scratch, start, finish


def packed(covariance, where, pieces):
    out_shape, scratch, start, finish = packing(pieces)

    def kernel(where_ref, p_ref, *refs):
        results, refs = refs[: len(out_shape)], refs[len(out_shape) :]
        finish(start(where_ref, p_ref, refs), results, refs)

    return pl.pallas_call(
        kernel,
        in_specs=[pl.BlockSpec(memory_space=pltpu.SMEM), pl.BlockSpec(memory_space=pl.ANY)],
        out_specs=[pl.BlockSpec(memory_space=pl.ANY)] * len(out_shape),
        out_shape=out_shape,
        scratch_shapes=scratch,
        compiler_params=params(),
        cost_estimate=cost(1),
        name="packed",
    )(where, covariance)


def stencils(wind_table, diffusivity, wind_index, where, lat_rows, lats, nlon, covariance, pieces):
    steps, nlat = wind_index.shape
    sizes = (lat_rows, lats)
    span = 2 * steps * nlon
    pairs = lats // 2
    packs, pack_scratch, start, finish = packing(pieces)

    def kernel(table_ref, diffuse_ref, index_ref, where_ref, p_ref, *refs):
        row_out, col_out, high_out, low_out, step_out = refs[:5]
        results, scratch, refs = refs[5 : 5 + len(packs)], refs[5 + len(packs) :][:2], refs[7 + len(packs) :]
        loads = start(where_ref, p_ref, refs)
        for side, out in enumerate((row_out, col_out)):
            looked_up = scratch[side]
            terms = []
            for step_no in range(steps):
                for i in range(sizes[side] + 2 * steps):
                    lat = where_ref[5 + side] + i - steps
                    inside = jnp.logical_and(lat >= 0, lat < nlat)
                    entry = index_ref[step_no, jnp.clip(lat, 0, nlat - 1)]
                    values = (table_ref[0, entry], table_ref[1, entry], diffuse_ref[entry], inside.astype(F32))
                    for k, value in enumerate(values):
                        looked_up[k, i : i + 1, :] = jnp.full((1, nlon), value, F32)
                here = looked_up[3] > 0.5
                c, e, w, n, s = [
                    jnp.where(here, term, 0.0)
                    for term in stencil_terms(looked_up[0], looked_up[1], looked_up[2])
                ]
                terms.append((c, w, e, n, s) if side else (c, e, w, n, s))
                if side:
                    for member, value in enumerate((c, e, w, n, s)):
                        step_out[5 * step_no + member] = value
            for d, value in composed(terms, sizes[side], nlon).items():
                out[d + steps] = value
        for q in range(pairs):
            for a in range(2):
                for k in range(2 * steps):
                    d = k - (steps - 1) - a
                    high, low = split(circulant(col_out[d + steps, 2 * q + a : 2 * q + a + 1, :]))
                    at = pl.ds(q * span + k * nlon, nlon)
                    high_out[at, a * nlon : (a + 1) * nlon] = high
                    low_out[at, a * nlon : (a + 1) * nlon] = low
        finish(loads, results, refs)

    return pl.pallas_call(
        kernel,
        in_specs=[pl.BlockSpec(memory_space=pltpu.SMEM)] * 4 + [pl.BlockSpec(memory_space=pl.ANY)],
        out_specs=[pl.BlockSpec(memory_space=pltpu.VMEM)] * 5 + [pl.BlockSpec(memory_space=pl.ANY)] * len(packs),
        out_shape=[jax.ShapeDtypeStruct((2 * steps + 1, size, nlon), F32) for size in sizes]
        + [jax.ShapeDtypeStruct((pairs * span, 2 * nlon), BF16)] * 2
        + [jax.ShapeDtypeStruct((5 * steps, lats + 2 * steps, nlon), F32)]
        + packs,
        scratch_shapes=[pltpu.VMEM((4, size + 2 * steps, nlon), F32) for size in sizes]
        + pack_scratch,
        compiler_params=params(),
        cost_estimate=cost(1),
        name="stencils",
    )(wind_table.T, diffusivity, wind_index, where, covariance)


def columns_operator(
    covariance, halos, stencil, blocks, where, unit, steps, nlon, count, block_at, held=None, ends=False, work=1
):
    rows, cols = covariance.shape
    lats = cols // nlon
    wide = steps * nlon
    size = unit * nlon
    span = 2 * steps * nlon
    pairs = lats // 2
    part = nlon // 2
    upper = size - part * (3 * size // (8 * part))

    def kernel(where_ref, stencil_ref, p_ref, *rest):
        halo_refs, rest = rest[: 2 * len(halos)], rest[2 * len(halos) :]
        (b_high, b_low, step_ref), outs, data_ref = rest[:3], rest[3:-1], rest[-1]
        if held is not None:
            outs = outs[1:]
        t_ref = outs[0]
        i = pl.program_id(0)
        col_odd, row_odd = where_ref[2] != 0, where_ref[3] != 0

        @pl.when(i == 0)
        def _():
            data_ref[size:, :wide] = jnp.zeros((size, wide), BF16)
            data_ref[size:, wide + cols :] = jnp.zeros((size, wide), BF16)

        for k in range(len(halos)):
            even_ref, odd_ref = halo_refs[2 * k : 2 * k + 2]
            chosen = i >= 0 if len(halos) == 1 else i == k

            @pl.when(jnp.logical_and(chosen, col_odd))
            def _(even_ref=even_ref, odd_ref=odd_ref):
                data_ref[:size, :wide] = even_ref[...]
                data_ref[:size, wide + cols :] = odd_ref[...]

            @pl.when(jnp.logical_and(chosen, jnp.logical_not(col_odd)))
            def _(even_ref=even_ref, odd_ref=odd_ref):
                data_ref[:size, :wide] = odd_ref[...]
                data_ref[:size, wide + cols :] = even_ref[...]

        data_ref[:upper, wide : wide + cols], data_ref[size : size + upper, wide : wide + cols] = split(
            p_ref[:upper, :]
        )
        weights = [
            [
                lambda at, k=5 * step_no + member: step_ref[k, at : at + 1, :]
                for member in range(5)
            ]
            for step_no in range(steps)
        ]
        starts = list(range(upper, size, part))
        for q in range(max(pairs, len(starts))):
            if q < pairs:
                window = slice((2 * q + 1) * nlon, (2 * q + 1) * nlon + span)
                of = pl.ds(q * span, span)
                total = product(data_ref[:upper, window], b_high[of, :])
                total += product(data_ref[size : size + upper, window], b_high[of, :])
                total += product(data_ref[:upper, window], b_low[of, :])
                for a, k, d in ((0, 2 * q, -steps), (1, 2 * q + 2 * steps + 1, steps)):
                    far = slice(k * nlon, (k + 1) * nlon)
                    row = stencil_ref[d + steps, 2 * q + a : 2 * q + a + 1, :]
                    weight = jnp.sum(row, axis=1, keepdims=True)
                    far_values = data_ref[:upper, far].astype(F32) + data_ref[size : size + upper, far].astype(F32)
                    value = total[:, a * nlon : (a + 1) * nlon] + weight * far_values
                    t_ref[:upper, (2 * q + a) * nlon : (2 * q + a + 1) * nlon] = value.astype(BF16)
            if q < len(starts):
                rows_at = slice(starts[q], starts[q] + part)
                planes = []
                for k in range(lats + 2 * steps):
                    if steps <= k < steps + lats:
                        planes.append(p_ref[rows_at, (k - steps) * nlon : (k - steps + 1) * nlon])
                    else:
                        planes.append(data_ref[rows_at, k * nlon : (k + 1) * nlon].astype(F32))
                for k, plane in enumerate(swept(planes, weights)):
                    t_ref[rows_at, k * nlon : (k + 1) * nlon] = plane.astype(BF16)
        if ends:
            for odd in range(2):
                is_odd = row_odd if odd else jnp.logical_not(row_odd)

                @pl.when(jnp.logical_and(i == 0, is_odd))
                def _(odd=odd):
                    outs[2 - odd][...] = t_ref[:wide, :]

                @pl.when(jnp.logical_and(i == count - 1, is_odd))
                def _(odd=odd):
                    outs[1 + odd][...] = t_ref[size - wide :, :]

    halo_at = (lambda i, at: (i, 0)) if len(halos) == 1 else (lambda i, at: (0, 0))
    in_specs = [
        pl.BlockSpec(stencil.shape, lambda i, at: (0, 0, 0)),
        pl.BlockSpec((size, cols), lambda i, at: (block_at(i, at), 0)),
    ]
    in_specs += [pl.BlockSpec((size, wide), halo_at)] * (2 * len(halos))
    in_specs += [pl.BlockSpec(block.shape, lambda i, at, n=block.ndim: (0,) * n) for block in blocks]
    out_specs = [pl.BlockSpec((size, cols), lambda i, at: (block_at(i, at), 0))]
    out_shape = [jax.ShapeDtypeStruct((rows, cols), BF16)]
    operands = [where, stencil, covariance] + [array for pair in halos for array in pair] + list(blocks)
    aliases = {}
    if ends:
        out_specs += [pl.BlockSpec((wide, cols), lambda i, at: (0, 0))] * 2
        out_shape += [jax.ShapeDtypeStruct((wide, cols), BF16)] * 2
    if held is not None:
        in_specs.append(pl.BlockSpec(memory_space=pl.ANY))
        aliases = {len(operands): 0}
        operands.append(held)
    return pl.pallas_call(
        kernel,
        grid_spec=pltpu.PrefetchScalarGridSpec(
            num_scalar_prefetch=1,
            grid=(count,),
            in_specs=in_specs,
            out_specs=out_specs,
            scratch_shapes=[pltpu.VMEM((2 * size, cols + 2 * wide), BF16)],
        ),
        out_shape=out_shape,
        input_output_aliases=aliases,
        compiler_params=params(),
        cost_estimate=cost(work),
        name="columns_operator",
    )(*operands)


def rows_operator(values, even, odd, stencil, where, steps, nlon, out_dtype, blocks=None, noise=None):
    rows, cols = values.shape
    lat_rows = rows // nlon
    wide = steps * nlon
    size = 2 * nlon
    span = 2 * steps * nlon
    pairs = lat_rows // 2
    group = 2 if pairs % 2 == 0 else 1
    ahead = (steps + 1) // 2
    exact = values.dtype == BF16
    makes = blocks is None
    chunk = min(cols, 256)

    def kernel(where_ref, stencil_ref, x_ref, even_ref, odd_ref, *rest):
        if makes:
            out_ref, a_ref = rest[:2]
        else:
            a_ref, noise_ref, out_ref = rest[:3]
        high_ref, sem = rest[2 if makes else 3 :][:2]
        raw_ref, low_ref = (None, None) if exact else rest[-2:]
        step = pl.program_id(0)

        def load(q):
            here = pl.ds(pl.multiple_of(q * size, size), size)
            there = pl.ds(pl.multiple_of(wide + q * size, nlon), size)
            target = high_ref.at[there, :] if exact else raw_ref.at[here, :]
            return pltpu.make_async_copy(x_ref.at[here, :], target, sem.at[q])

        def ready(q):
            load(q).wait()
            if not exact:
                there = pl.ds(pl.multiple_of(wide + q * size, nlon), size)
                here = pl.ds(pl.multiple_of(q * size, size), size)
                high_ref[there, :], low_ref[there, :] = split(raw_ref[here, :])

        def ends():
            is_odd = where_ref[3]
            at_even = pl.ds(pl.multiple_of((1 - is_odd) * (wide + rows), nlon), wide)
            at_odd = pl.ds(pl.multiple_of(is_odd * (wide + rows), nlon), wide)
            return [
                pltpu.make_async_copy(even_ref, high_ref.at[at_even, :], sem.at[pairs]),
                pltpu.make_async_copy(odd_ref, high_ref.at[at_odd, :], sem.at[pairs + 1]),
            ]

        @pl.when(step == 0)
        def _():
            halos = ends()
            for halo in halos:
                halo.start()
            for q in range(pairs):
                load(q).start()
            if not exact:
                low_ref[:wide, :] = jnp.zeros((wide, cols), BF16)
                low_ref[wide + rows :, :] = jnp.zeros((wide, cols), BF16)

        row = lambda j, d, a: stencil_ref[d + steps, pl.ds(2 * (step * group + j) + a, 1), :]
        if makes:
            for j in range(group):
                for a in range(2):
                    for k in range(2 * steps):
                        high, low = split(circulant(row(j, k - (steps - 1) - a, a)))
                        top = 2 * j * size + a * nlon
                        a_ref[top : top + nlon, k * nlon : (k + 1) * nlon] = high
                        a_ref[top + size : top + size + nlon, k * nlon : (k + 1) * nlon] = low
        @pl.when(step == 0)
        def _():
            for halo in ends():
                halo.wait()
            for q in range(min(ahead, pairs)):
                ready(q)

        for j in range(group):
            q = step * group + j + ahead

            @pl.when(q < pairs)
            def _(q=q):
                ready(q)

        for j in range(group):
            unit = lambda k: pl.multiple_of((2 * (step * group + j) + k) * nlon, nlon)
            weights = [jnp.sum(row(j, d, a), axis=1, keepdims=True) for a, d in ((0, -steps), (1, steps))]
            top = 2 * j * size
            for lane in range(0, cols, chunk):
                lanes = slice(lane, lane + chunk)
                both = product(a_ref[top : top + 2 * size, :], high_ref[pl.ds(unit(1), span), lanes])
                total = both[:size] + both[size:]
                if not exact:
                    total += product(a_ref[top : top + size, :], low_ref[pl.ds(unit(1), span), lanes])
                for a, k in ((0, 0), (1, 2 * steps + 1)):
                    far = high_ref[pl.ds(unit(k), nlon), lanes].astype(F32)
                    if not exact:
                        far += low_ref[pl.ds(unit(k), nlon), lanes].astype(F32)
                    value = total[a * nlon : (a + 1) * nlon, :] + weights[a] * far
                    out_ref[j * size + a * nlon : j * size + (a + 1) * nlon, lanes] = value.astype(out_dtype)
        if noise is not None:
            for a in range(2 * group):
                lat = 2 * group * step + a - where_ref[4]

                @pl.when(jnp.logical_and(lat >= 0, lat < cols // nlon))
                def _(a=a, lat=lat):
                    lanes = pl.ds(pl.multiple_of(lat * nlon, nlon), nlon)
                    eye = lax.broadcasted_iota(jnp.int32, (nlon, nlon), 0) == lax.broadcasted_iota(
                        jnp.int32, (nlon, nlon), 1
                    )
                    added = jnp.where(eye, noise_ref[pl.ds(2 * group * step + a, 1), :], 0.0)
                    out_ref[a * nlon : (a + 1) * nlon, lanes] += added

    in_specs = [pl.BlockSpec(stencil.shape, lambda g, at: (0, 0, 0))] + [pl.BlockSpec(memory_space=pl.ANY)] * 3
    operands = [where, stencil, values, even, odd]
    out_specs = [pl.BlockSpec((group * size, cols), lambda g, at: (g, 0))]
    out_shape = [jax.ShapeDtypeStruct((rows, cols), out_dtype)]
    blocks_spec = pl.BlockSpec((2 * group * size, span), lambda g, at: (g, 0))
    if makes:
        out_specs.append(blocks_spec)
        out_shape.append(jax.ShapeDtypeStruct((2 * rows, span), BF16))
    else:
        in_specs += [blocks_spec, pl.BlockSpec(noise.shape, lambda g, at: (0, 0))]
        operands += [blocks, noise]
    return pl.pallas_call(
        kernel,
        grid_spec=pltpu.PrefetchScalarGridSpec(
            num_scalar_prefetch=1,
            grid=(pairs // group,),
            in_specs=in_specs,
            out_specs=out_specs,
            scratch_shapes=[pltpu.VMEM((rows + 2 * wide, cols), BF16), pltpu.SemaphoreType.DMA((pairs + 2,))]
            + ([] if exact else [pltpu.VMEM((rows, cols), F32), pltpu.VMEM((rows + 2 * wide, cols), BF16)]),
        ),
        out_shape=out_shape,
        compiler_params=params(),
        cost_estimate=cost(1),
        name="rows_operator",
    )(*operands)


def shifted(block, axis, by):
    size = lax.axis_size(axis)
    pairs = [(i, i + by) for i in range(size) if 0 <= i + by < size]
    return lax.ppermute(block, axis, pairs)


def gathered(first, last, axis, dim, unit, halo, own):
    before, after = [], []
    need, hop = halo, 1
    while need > 0:
        take = min(own, need)
        size = first.shape[dim]
        before.insert(0, shifted(lax.slice_in_dim(last, size - take * unit, size, axis=dim), axis, hop))
        after.append(shifted(lax.slice_in_dim(first, 0, take * unit, axis=dim), axis, -hop))
        need, hop = need - take, hop + 1
    join = lambda parts: parts[0] if len(parts) == 1 else jnp.concatenate(parts, axis=dim)
    return join(before), join(after)


def exchanged(block, axis, odd):
    pairs = []
    for i in range(odd, lax.axis_size(axis) - 1, 2):
        pairs += [(i, i + 1), (i + 1, i)]
    return lax.ppermute(block, axis, pairs)


def mirrored(block, odd):
    n_row, n_col = lax.axis_size("row"), lax.axis_size("col")
    pairs = []
    for a in range(n_row):
        for b in range(n_col):
            to = 2 * a + (1 - b % 2) + (1 if (b + odd) % 2 else -1)
            if 0 <= to < n_col:
                pairs.append((a * n_col + b, (b // 2) * n_col + to))
    return lax.ppermute(block, ("row", "col"), pairs)


def body(covariance, noise_var, wind_table, diffusivity, wind_index):
    rows_dev, cols_dev = covariance.shape
    lat_rows, nlon = noise_var.shape
    steps, nlat = wind_index.shape
    lats = cols_dev // nlon
    row_id, col_id = lax.axis_index("row"), lax.axis_index("col")
    own = lat_rows // 4
    fits = lat_rows == 2 * lats and own % 2 == 0 and own >= steps and own <= lats - steps
    if not fits or lax.axis_size("col") != 2 * lax.axis_size("row"):
        return plain_body(covariance, noise_var, wind_table, diffusivity, wind_index)

    near = lat_rows // 2 - own
    middle = lat_rows // 2
    outer, inner, wide = near * nlon, own * nlon, steps * nlon
    pick = lambda parity, even, odd: even + parity * (odd - even)
    col_odd, row_odd = col_id % 2, row_id % 2
    mirror_at, direct_at = pick(col_odd, middle - own, middle), pick(col_odd, middle, middle - own)
    diagonal = col_id * lats - row_id * lat_rows
    where = jnp.stack(
        [
            mirror_at // own,
            direct_at // own,
            col_odd,
            row_odd,
            diagonal,
            row_id * lat_rows,
            col_id * lats,
            mirror_at * nlon,
            pick(col_odd, lats, lats - steps) * nlon,
            pick(col_odd, 2 * lats - steps, 0) * nlon,
            pick(col_odd, lats - own, 0) * nlon,
            pick(col_odd, cols_dev - wide, 0),
            pick(col_odd, 0, cols_dev - wide),
            pick(row_odd, rows_dev - wide, 0),
            pick(row_odd, 0, rows_dev - wide),
        ]
    ).astype(jnp.int32)
    half = outer // 2
    spans = [(0, half, 0), (half, half, half)]
    spans += [(rows_dev - outer, half, outer), (rows_dev - half, half, outer + half), (0, 16, 2 * outer)]
    pieces = [(row, size, (11 + k,), wide, k, there, 0) for row, size, there in spans for k in range(2)]
    pieces += [((13 + k, j * nlon), nlon, 0, cols_dev, k + 2, j * nlon, 0) for k in range(2) for j in range(steps)]
    others = [((8 + k,), wide, (10,), inner, k, 0, nlon) for k in range(2)]
    others += [((7,), inner, (11 + k,), wide, k + 2, 0, 0) for k in range(2)]
    sent = packed(covariance, where, pieces)
    outers, ends = list(sent[:2]), list(sent[2:])
    outers = [exchanged(piece, "col", k) for k, piece in enumerate(outers)]
    ends = [exchanged(piece, "row", k) for k, piece in enumerate(ends)]
    row_s, col_s, *rest = stencils(
        wind_table, diffusivity, wind_index, where, lat_rows, lats, nlon, covariance, others
    )
    col_blocks, mirrors, inners = rest[:3], rest[3:5], rest[5:7]
    mirrors = [mirrored(piece, k) for k, piece in enumerate(mirrors)]

    operator_times_prior, blocks = rows_operator(covariance, *ends, row_s, where, steps, nlon, BF16)
    inners[0] = exchanged(inners[0], "col", 0)
    operator_times_prior, outers, inners[1] = lax.optimization_barrier(
        (operator_times_prior, outers, inners[1])
    )
    inners[1] = exchanged(inners[1], "col", 1)
    mirror, *ends = columns_operator(
        covariance, [outers], col_s, col_blocks, where, near, steps, nlon, 2, lambda i, at: i * (lat_rows // near - 1),
        None, True,
    )
    ends = [exchanged(piece, "row", k) for k, piece in enumerate(ends)]
    (mirror,) = columns_operator(
        covariance, [mirrors, inners], col_s, col_blocks, where, own, steps, nlon, 2, lambda i, at: at[i], mirror, False,
        10 ** 13,
    )
    (predicted_spread_matrix,) = rows_operator(
        mirror, *ends, row_s, where, steps, nlon, F32, blocks, noise_var
    )
    return (predicted_spread_matrix, operator_times_prior)


def plain_body(covariance, noise_var, wind_table, diffusivity, wind_index):
    rows_dev, cols_dev = covariance.shape
    lat_rows, nlon = noise_var.shape
    steps, nlat = wind_index.shape
    lats = cols_dev // nlon
    row_id, col_id = lax.axis_index("row"), lax.axis_index("col")
    sent = covariance.astype(BF16)
    sides = gathered(sent, sent, "col", 1, nlon, steps, lats)
    ends = gathered(sent, sent, "row", 0, nlon, steps, lat_rows)
    firsts = (row_id * lat_rows, col_id * lats)
    where = jnp.stack([0, 0, 1, 1, firsts[1] - firsts[0], *firsts]).astype(jnp.int32)
    row_s, col_s, *col_blocks = stencils(
        wind_table, diffusivity, wind_index, where, lat_rows, lats, nlon, covariance, []
    )
    operator_times_prior, blocks = rows_operator(covariance, *ends, row_s, where, steps, nlon, BF16)
    (mirror,) = columns_operator(
        covariance, [sides], col_s, col_blocks, where, 2, steps, nlon, lat_rows // 2, lambda i, at: i
    )
    ends = gathered(mirror, mirror, "row", 0, nlon, steps, lat_rows)
    (predicted_spread_matrix,) = rows_operator(
        mirror, *ends, row_s, where, steps, nlon, F32, blocks, noise_var
    )
    return (predicted_spread_matrix, operator_times_prior)


def solution(mesh):
    in_specs = (P("row", "col"), P("row", None), P(), P(), P())
    out_specs = (P("row", "col"), P("row", "col"))
    return jax.shard_map(body, mesh=mesh, in_specs=in_specs, out_specs=out_specs, check_vma=False)
```
